32 devices in a mesh: parts: 2 (over x), store: 8 (over z, y), tensor: 2 (over core).
Axes of the slice: x: 2, y: 2, z: 4, core: 2. Of those that a mesh axis runs over, the one named last changes fastest.
Arguments:
- x_in: bfloat16 [2, 256, 8192], P(None, ('parts', 'store'), 'tensor'), parts along dimension 1, may hold values from -6 to 6
- q_base: bfloat16 [2, 256, 8192], P(None, ('parts', 'store'), 'tensor'), parts along dimension 1, may hold values from -120 to 120
- k_new: bfloat16 [2, 256, 1024], P(None, ('parts', 'store'), 'tensor'), parts along dimension 1, may hold values from -4.2 to 4.2
- v_new: bfloat16 [2, 256, 1024], P(None, ('parts', 'store'), 'tensor'), parts along dimension 1, may hold values from -6 to 6
- cache_k: bfloat16 [256, 512, 1024], P(('parts', 'store'), None, 'tensor'), parts along dimension 0, may hold values from -4 to 4
- cache_v: bfloat16 [256, 512, 1024], P(('parts', 'store'), None, 'tensor'), parts along dimension 0, may hold values from -6 to 6
- lengths: int32 [256], P(('parts', 'store')), parts along dimension 0, may hold values from 1 to 512, 16384 in all
- adapter_ids: int32 [256], P(('parts', 'store')), parts along dimension 0, may hold values from 0 to 63, as said below
- slot_of: int32 [128], P('parts'), parts along dimension 0, may hold values from 0 to 63, as said below
- a_query: bfloat16 [8192, 64, 16], P(None, 'store'), may hold values from -0.0625 to 0.0625
- b_query: bfloat16 [64, 16, 8192], P('store', None, 'tensor'), may hold values from -0.75 to 0.75
- a_output: bfloat16 [8192, 64, 16], P(None, 'store'), may hold values from -0.0625 to 0.0625
- b_output: bfloat16 [64, 16, 8192], P('store', None, 'tensor'), may hold values from -0.75 to 0.75
Outputs:
- attn_out: bfloat16 [2, 256, 8192], P(None, ('parts', 'store'), 'tensor'), parts along dimension 1
- adapter_out: bfloat16 [2, 256, 8192], P(None, ('parts', 'store'), 'tensor'), parts along dimension 1
The draws below stay inside these ranges and needn't reach their ends.
There are 2 independent parts, one for each index of `parts`. The reference program is written for one: setup_inputs(seed, part) draws one part's arguments, and reference() takes and returns one part's arrays. A program takes and returns all parts, laid end to end along the dimension named above; an argument that names none is the same for every part. Nothing has to cross between parts.
Inputs may be any that keep to these rules, and one draw needn't show every extreme that they name: `adapter_ids`: each row names an adapter of the store. In every aligned block of 16 rows (the rows of one device), at most 2 rows name adapters whose slot lies in one aligned block of 8 slots, and in every draw one such slot block is named by exactly 2 rows of every row block. `slot_of`: A permutation: each slot holds one adapter. The lengths of the 128 rows of one part sum to 16384; each part is drawn for itself, so the whole array over all parts sums to that times the number of parts. One row of each part has length exactly 512.
All inputs are finite; a program needn't handle non-finite values. No bound on the sum of `lengths` on one device may be relied on, other than what follows from the above.
Results may differ from the reference program's by a relative error of at most 0.008.
Values may be sent and summed in bfloat16 or wider, within the bound.
No kernel may reach another device: no remote copies, remote signals or barrier semaphores. Data moves between devices by JAX's collectives and lax.ppermute only.
A program may use at most 128 MiB of HBM per device.

```python
import math
import jax
import jax.numpy as jnp
import numpy as np
from jax import lax

D = 8192
H = 64
KVH = 8
HD = 128
R = 16
CAP = 2
ROWS_DEV = 16
MAXLEN = 512
ADAPT_DEV = 8
ROWS = 128
NADAPT = 64


def adapter_slots(key):
    return jax.random.permutation(jax.random.fold_in(key, 11), NADAPT).astype(jnp.int32)


def draw_slot_of(key, part):
    return adapter_slots(key)


def draw_adapter_ids(key, part):
    shuffle = adapter_slots(key)
    key = jax.random.fold_in(key, 2)
    owner_count = NADAPT // ADAPT_DEV
    inverse = jnp.zeros((NADAPT,), jnp.int32).at[shuffle].set(jnp.arange(NADAPT, dtype=jnp.int32))
    hot_owner = jax.random.randint(jax.random.fold_in(key, 1), (), 0, owner_count)
    entries = jnp.arange(owner_count * CAP, dtype=jnp.int32)
    entry_owner = entries // CAP

    def one_block(block_key):
        rank_order = jax.random.permutation(jax.random.fold_in(block_key, 1), owner_count * CAP).astype(jnp.int32)
        scores = rank_order - jnp.where(entry_owner == hot_owner, owner_count * CAP, 0)
        chosen = jnp.argsort(scores, stable=True)[:ROWS_DEV]
        picked = entry_owner[chosen]
        picked = picked[jax.random.permutation(jax.random.fold_in(block_key, 2), ROWS_DEV)]
        within = jax.random.randint(jax.random.fold_in(block_key, 3), (ROWS_DEV,), 0, ADAPT_DEV)
        return inverse[picked * ADAPT_DEV + within]
    block_keys = jax.random.split(jax.random.fold_in(key, 5), ROWS // ROWS_DEV)
    return jax.vmap(one_block)(block_keys).reshape(ROWS).astype(jnp.int32)


def draw_q_base(key, part):
    key = jax.random.fold_in(key, 3)
    base_draw = jnp.clip(jax.random.normal(key, (2, ROWS, H * HD), jnp.float32), -4.0, 4.0)
    return base_draw.astype(jnp.bfloat16)


def draw_cache_k(key, part):
    key = jax.random.fold_in(key, 4)
    keys_draw = jnp.clip(jax.random.normal(key, (ROWS, MAXLEN, KVH * HD), jnp.float32), -4.0, 4.0)
    return keys_draw.astype(jnp.bfloat16)


def draw_k_new(key, part):
    key = jax.random.fold_in(key, 5)
    keys_draw = jnp.clip(jax.random.normal(key, (2, ROWS, KVH * HD), jnp.float32), -4.0, 4.0)
    return keys_draw.astype(jnp.bfloat16)


def block_levels(stream_key, extent, pieces, least, largest):
    loudness = 1.0
    for axis_at, blocks in pieces:
        draws = jax.random.uniform(jax.random.fold_in(jax.random.fold_in(stream_key, 6), axis_at), (blocks,), jnp.float32, least / len(pieces), largest / len(pieces))
        loudness = loudness * jnp.repeat(jnp.exp(draws), extent[axis_at] // blocks).reshape((-1,) + (1,) * (len(extent) - 1 - axis_at))
    return loudness


def profile(amount, total, limit, slope):
    weights = [(1 << 20) // math.isqrt(grade ** slope) + 1 for grade in range(2, amount + 1)]
    spare, given = total - limit - (amount - 1), [1] * (amount - 1)
    while spare > 0:
        free = [i for i in range(amount - 1) if given[i] < limit]
        pool, remaining = sum([weights[i] for i in free]), spare
        for i in free:
            addition = min(limit - given[i], max(1, remaining * weights[i] // pool), spare)
            given[i] = given[i] + addition
            spare = spare - addition
    return np.array([limit] + given)


def ragged_sizes(rng, amount, total, bound, skew):
    if amount == 2:
        one = jax.random.randint(rng, (), max(1, total - bound), min(bound, total - 1) + 1)
        return jnp.stack([one, total - one])
    sizes = jnp.asarray(profile(amount, total, bound, skew), jnp.int32)
    twos = (amount - 1) // 2
    donor, receiver = sizes[1:1 + 2 * twos:2], sizes[2:2 + 2 * twos:2]
    slack = jnp.minimum(donor - 1, bound - receiver)
    shifted = jax.random.randint(jax.random.fold_in(rng, 1), (twos,), 0, 1 << 20) % (slack + 1)
    sizes = sizes.at[1:1 + 2 * twos:2].set(donor - shifted).at[2:2 + 2 * twos:2].set(receiver + shifted)
    return sizes[jax.random.permutation(jax.random.fold_in(rng, 2), amount)]


def bell_draw(own_key, extent, scale, most, cuts=(), kind=jnp.bfloat16):
    result = jax.random.normal(own_key, extent, jnp.float32) * scale
    if len(cuts) > 0:
        result = block_levels(own_key, extent, cuts, -0.22, 0.18) * result
    return jnp.clip(result, min=-most, max=most).astype(kind)


def setup_inputs(seed: int = 0, part: int = 0) -> dict:
    splits = jax.random.split(jax.random.key(seed), 14)
    own_keys = jax.random.split(jax.random.fold_in(splits[13], part), 14)
    x_in = bell_draw(own_keys[0], (2, ROWS, D), 1.0, 6.0, ((1, 8), (2, 2)))
    q_base = draw_q_base(jax.random.fold_in(jax.random.fold_in(splits[13], part), 71), part)
    k_new = draw_k_new(jax.random.fold_in(jax.random.fold_in(splits[13], part), 71), part)
    v_new = bell_draw(own_keys[3], (2, ROWS, KVH * HD), 1.0, 6.0, ((1, 8), (2, 2)))
    cache_k = draw_cache_k(jax.random.fold_in(jax.random.fold_in(splits[13], part), 71), part)
    cache_v = bell_draw(own_keys[5], (ROWS, MAXLEN, KVH * HD), 1.0, 6.0, ((0, 8), (2, 2)))
    lengths = ragged_sizes(own_keys[6], ROWS, ROWS * MAXLEN // 4, MAXLEN, 2).astype(jnp.int32)
    adapter_ids = draw_adapter_ids(jax.random.fold_in(jax.random.fold_in(splits[13], part), 71), part)
    slot_of = draw_slot_of(jax.random.fold_in(jax.random.fold_in(splits[13], part), 71), part)
    a_query = bell_draw(splits[9], (D, NADAPT, R), D ** -0.5, 0.0625, ((1, 8),))
    b_query = bell_draw(splits[10], (NADAPT, R, H * HD), 64 ** -0.5, 0.75, ((0, 8), (2, 2)))
    a_output = bell_draw(splits[11], (H * HD, NADAPT, R), (H * HD) ** -0.5, 0.0625, ((1, 8),))
    b_output = bell_draw(splits[12], (NADAPT, R, D), 64 ** -0.5, 0.75, ((0, 8), (2, 2)))
    return {"x_in": x_in, "q_base": q_base, "k_new": k_new, "v_new": v_new, "cache_k": cache_k, "cache_v": cache_v, "lengths": lengths, "adapter_ids": adapter_ids, "slot_of": slot_of, "a_query": a_query, "b_query": b_query, "a_output": a_output, "b_output": b_output}


def adapter_term(activations, a_store, b_store, slot_rows):
    a_rows = jnp.take(a_store, slot_rows, axis=1)
    low_rank = jnp.einsum('srw,wrk->srk', activations.astype(jnp.float32), a_rows.astype(jnp.float32)).astype(jnp.bfloat16)
    b_rows = jnp.take(b_store, slot_rows, axis=0)
    product = jnp.einsum('srk,rkq->srq', low_rank.astype(jnp.float32), b_rows.astype(jnp.float32))
    return (2.0 * product).astype(jnp.bfloat16)

def attend_row(items):
    queries, keys_row, values_row, new_keys, new_values, length_row = items
    scale = 1.0 / math.sqrt(HD)
    query_f = queries.astype(jnp.float32)
    cached = jnp.einsum('sgjd,lgd->sgjl', query_f, keys_row.astype(jnp.float32)) * scale
    valid = jnp.arange(MAXLEN, dtype=jnp.int32) < length_row
    cached = jnp.where(valid[None, None, None, :], cached, -jnp.inf)
    fresh = jnp.einsum('sgjd,tgd->sgjt', query_f, new_keys.astype(jnp.float32)) * scale
    steps_ok = jnp.arange(2, dtype=jnp.int32)[None, :] <= jnp.arange(2, dtype=jnp.int32)[:, None]
    fresh = jnp.where(steps_ok[:, None, None, :], fresh, -jnp.inf)
    top = jnp.maximum(lax.optimization_barrier(jnp.max(cached, axis=-1)), lax.optimization_barrier(jnp.max(fresh, axis=-1)))[..., None]
    cached_exp = jnp.exp(cached - top)
    fresh_exp = jnp.exp(fresh - top)
    total = lax.optimization_barrier(jnp.sum(cached_exp, axis=-1, keepdims=True)) + lax.optimization_barrier(jnp.sum(fresh_exp, axis=-1, keepdims=True))
    weight_cached = (cached_exp / total).astype(jnp.bfloat16)
    weight_fresh = (fresh_exp / total).astype(jnp.bfloat16)
    mixed = jnp.einsum('sgjl,lgd->sgjd', weight_cached.astype(jnp.float32), values_row.astype(jnp.float32))
    mixed = mixed + jnp.einsum('sgjt,tgd->sgjd', weight_fresh.astype(jnp.float32), new_values.astype(jnp.float32))
    return mixed.astype(jnp.bfloat16)

def reference(x_in, q_base, k_new, v_new, cache_k, cache_v, lengths, adapter_ids, slot_of, a_query, b_query, a_output, b_output):
    slot_rows = jnp.take(slot_of, adapter_ids).astype(jnp.int32)
    delta_query = adapter_term(x_in, a_query, b_query, slot_rows)
    query = (q_base.astype(jnp.float32) + delta_query.astype(jnp.float32)).astype(jnp.bfloat16)
    groups = H // KVH
    grouped = query.reshape(2, ROWS, KVH, groups, HD).transpose(1, 0, 2, 3, 4)
    keys_all = cache_k.reshape(ROWS, MAXLEN, KVH, HD)
    values_all = cache_v.reshape(ROWS, MAXLEN, KVH, HD)
    new_keys = k_new.reshape(2, ROWS, KVH, HD).transpose(1, 0, 2, 3)
    new_values = v_new.reshape(2, ROWS, KVH, HD).transpose(1, 0, 2, 3)
    mixed = lax.map(attend_row, (grouped, keys_all, values_all, new_keys, new_values, lengths))
    attn_out = mixed.transpose(1, 0, 2, 3, 4).reshape(2, ROWS, H * HD)
    adapter_out = adapter_term(attn_out, a_output, b_output, slot_rows)
    return (attn_out, adapter_out)
```

```python
import functools
import math

import jax
import jax.numpy as jnp
from jax import lax
from jax.experimental import pallas as pl
from jax.experimental.pallas import tpu as pltpu
from jax.sharding import PartitionSpec as P

HD = 128
CAP = 2
STEPS = 2
CHUNK = 128
QUAD = 4
BF16 = jnp.bfloat16
F32 = jnp.float32
I32 = jnp.int32
VMEM = pl.BlockSpec(memory_space=pltpu.VMEM)
SMEM = pl.BlockSpec(memory_space=pltpu.SMEM)
ANY = pl.BlockSpec(memory_space=pl.ANY)


def iota(shape, dim):
    return lax.broadcasted_iota(I32, shape, dim)


def one_hot(hits):
    return jnp.where(hits, 1.0, 0.0).astype(BF16)


def stacked(ref, heads, wide):
    return jnp.concatenate(
        [ref[s, :, c * wide : (c + 1) * wide] for c in range(heads) for s in range(STEPS)], axis=0
    )


def pack_matrix(row_at, owners, heads, rows):
    items = CAP * STEPS
    block = heads * items
    shape = (block, heads * STEPS * rows)
    at = iota(shape, 0)
    col = iota(shape, 1)
    base = (at // items) * (STEPS * rows) + (at % STEPS) * rows
    first = (at // STEPS) % CAP == 0
    parts = []
    for i in range(owners):
        row = jnp.where(first, row_at[i * CAP], row_at[i * CAP + 1])
        parts.append(one_hot((col == base + row) & (row >= 0)))
    return jnp.concatenate(parts, axis=0)


def unpack_matrix(place_of, owners, heads, rows):
    items = CAP * STEPS
    block = heads * items
    shape = (rows, owners * block)
    at = iota(shape, 0)
    col = iota(shape, 1)
    spot = jnp.zeros(shape, I32)
    for r in range(rows):
        place = place_of[r]
        spot = jnp.where(at == r, (place // CAP) * block + (place % CAP) * STEPS, spot)
    return jnp.concatenate(
        [one_hot(col == spot + (c * items + s)) for c in range(heads) for s in range(STEPS)], axis=0
    )


def regroup_matrix(owners, heads):
    items = CAP * STEPS
    total = owners * heads * items
    at = iota((total, total), 0)
    col = iota((total, total), 1)
    head = at // (owners * items)
    owner = (at // items) % owners
    return one_hot(col == owner * (heads * items) + head * items + at % items)


def ungroup_matrix(owners, heads):
    items = CAP * STEPS
    total = owners * heads * items
    at = iota((total, total), 0)
    col = iota((total, total), 1)
    owner = at // (heads * items)
    head = (at // items) % heads
    return one_hot(col == head * (owners * items) + owner * items + at % items)


def exact(matrix, values):
    return jnp.dot(matrix, values, preferred_element_type=F32).astype(BF16)


def dispatch_kernel(owners, heads, adapt, rank, me, ids, slot_of, lengths, x_ref, *refs):
    place_of, row_at, slot_at, order, *blocks = refs
    rows = x_ref.shape[1]
    wide = x_ref.shape[2] // heads
    for p in range(owners * CAP):
        row_at[p] = -1
        slot_at[p] = -1
    for r in range(rows):
        slot = slot_of[ids[r]]
        relative = (slot // adapt) ^ me[0]
        taken = jnp.where(row_at[relative * CAP] >= 0, 1, 0)
        place = relative * CAP + taken
        row_at[place] = r
        slot_at[place] = slot % adapt
        place_of[r] = place
    sizes = [lengths[r] for r in range(rows)]
    for r in range(rows):
        ahead = jnp.int32(0)
        for q in range(rows):
            if q != r:
                longer = sizes[q] >= sizes[r] if q < r else sizes[q] > sizes[r]
                ahead = ahead + jnp.where(longer, 1, 0)
        order[ahead] = r
    items = CAP * STEPS
    block = heads * items
    packed = exact(pack_matrix(row_at, owners, heads, rows), stacked(x_ref, heads, wide))
    at = iota((block, adapt * rank), 0)
    lane_slot = iota((block, adapt * rank), 1) // rank
    first = (at // STEPS) % CAP == 0
    for i in range(owners):
        blocks[i][:, :wide] = packed[i * block : (i + 1) * block]
        slot = jnp.where(first, slot_at[i * CAP], slot_at[i * CAP + 1])
        blocks[i][:, wide:] = one_hot(lane_slot == slot)


def project_kernel(owners, heads, wide, first, a_ref, *refs):
    if first:
        blocks, (part_ref, mask_ref) = refs[:owners], refs[owners:]
    else:
        blocks, (mask_in, part_ref) = refs[:owners], refs[owners:]
    grouped = regroup_matrix(owners, heads)
    items = owners * CAP * STEPS
    arrived = jnp.concatenate([b[:, :wide] for b in blocks], axis=0)
    arrived = exact(grouped, arrived)
    if first:
        masks = jnp.concatenate([b[:, wide:] for b in blocks], axis=0)
        mask = jnp.dot(grouped[:items], masks, preferred_element_type=F32)
        mask_ref[...] = mask
    else:
        mask = mask_in[...]
    total = jnp.zeros(mask.shape, F32)
    for c in range(heads):
        total = total + lax.dot_general(
            arrived[c * items : (c + 1) * items],
            a_ref[:, c * wide : (c + 1) * wide],
            (((1,), (1,)), ((), ())),
            preferred_element_type=F32,
        )
    part_ref[...] = total * mask


def expand_kernel(owners, heads, wide, mine, other, b_ref, *blocks):
    low_rank = (mine[...] + other[...]).astype(BF16)
    pieces = []
    for c in range(heads):
        product = jnp.dot(
            low_rank, b_ref[:, c * wide : (c + 1) * wide], preferred_element_type=F32
        )
        pieces.append((2.0 * product).astype(BF16))
    back = exact(ungroup_matrix(owners, heads), jnp.concatenate(pieces, axis=0))
    block = heads * CAP * STEPS
    for i in range(owners):
        blocks[i][...] = back[i * block : (i + 1) * block]


def attend_kernel(
    owners, heads, place_of, row_at, order, lengths, q_ref, kn_ref, vn_ref, k_any, v_any, *refs
):
    blocks = refs[:owners]
    out_ref = refs[owners]
    outgoing = refs[owners + 1 : 2 * owners + 1]
    k_buf, v_buf, q_buf, o_buf, k_sem, v_sem = refs[2 * owners + 1 :]
    rows = q_ref.shape[1]
    wide = q_ref.shape[2] // heads
    groups = wide // HD
    span = STEPS * groups
    width = heads * HD
    sizes = k_any.shape[1] // CHUNK

    def copies(row, amount):
        part = pl.ds(0, amount * CHUNK)
        return (
            pltpu.make_async_copy(k_any.at[row, part], k_buf.at[row, part], k_sem.at[row]),
            pltpu.make_async_copy(v_any.at[row, part], v_buf.at[row, part], v_sem.at[row]),
        )

    def per_quad(action):
        def body(quad, carry):
            longest = lengths[order[quad * QUAD]]
            amount = (longest + CHUNK - 1) // CHUNK
            for size in range(1, sizes + 1):

                @pl.when(amount == size)
                def _():
                    action([order[quad * QUAD + j] for j in range(QUAD)], size)

            return carry

        lax.fori_loop(0, rows // QUAD, body, 0)

    def begin(rows_in, size):
        for row in rows_in:
            for copy in copies(row, size):
                copy.start()

    per_quad(begin)

    delta = jnp.dot(
        unpack_matrix(place_of, owners, heads, rows),
        jnp.concatenate([b[...] for b in blocks], axis=0),
        preferred_element_type=F32,
    )
    query = (stacked(q_ref, heads, wide).astype(F32) + delta).astype(BF16).astype(F32)
    for c in range(heads):
        for s in range(STEPS):
            top = (c * STEPS + s) * rows
            for j in range(groups):
                q_buf[pl.ds(c * span + s * groups + j, rows, stride=heads * span), :] = query[
                    top : top + rows, j * HD : (j + 1) * HD
                ]

    scale = 1.0 / math.sqrt(HD)
    new_keys = jnp.concatenate([kn_ref[t] for t in range(STEPS)], axis=0)
    new_values = jnp.concatenate([vn_ref[t] for t in range(STEPS)], axis=0)
    total = heads * span
    diagonal = iota((total, width), 0) // span == iota((total, width), 1) // HD
    fresh_shape = (total, STEPS * rows)
    step_of = (iota(fresh_shape, 0) // groups) % STEPS
    fresh_at = iota(fresh_shape, 1)
    in_time = fresh_at // rows <= step_of
    contract = (((1,), (1,)), ((), ()))

    def attend(rows_in, size):
        for row in rows_in:
            for copy in copies(row, size):
                copy.wait()
        length_now = size * CHUNK
        position = iota((total, length_now), 1)
        for row in rows_in:
            start = pl.multiple_of(row * total, total)
            one = q_buf[pl.ds(start, total), :].astype(BF16)
            spread = jnp.where(diagonal, jnp.concatenate([one] * heads, axis=1), jnp.zeros((), BF16))
            keys = k_buf[row, :length_now, :]
            values = v_buf[row, :length_now, :]
            cached = lax.dot_general(spread, keys, contract, preferred_element_type=F32) * scale
            cached = jnp.where(position < lengths[row], cached, -jnp.inf)
            fresh = lax.dot_general(spread, new_keys, contract, preferred_element_type=F32) * scale
            fresh = jnp.where(in_time & (fresh_at % rows == row), fresh, -jnp.inf)
            top = jnp.maximum(
                jnp.max(cached, axis=1, keepdims=True), jnp.max(fresh, axis=1, keepdims=True)
            )
            cached = jnp.exp(cached - top)
            fresh = jnp.exp(fresh - top)
            norm = jnp.sum(cached, axis=1, keepdims=True) + jnp.sum(fresh, axis=1, keepdims=True)
            share = 1.0 / norm
            mixed = jnp.dot((cached * share).astype(BF16), values, preferred_element_type=F32)
            mixed = mixed + jnp.dot(
                (fresh * share).astype(BF16), new_values, preferred_element_type=F32
            )
            o_buf[pl.ds(start, total), :] = jnp.concatenate(
                [
                    mixed[c * span : (c + 1) * span, c * HD : (c + 1) * HD]
                    for c in range(heads)
                ],
                axis=0,
            )

    per_quad(attend)

    results = []
    for c in range(heads):
        for s in range(STEPS):
            tiles = [
                o_buf[pl.ds(c * span + s * groups + j, rows, stride=heads * span), :].astype(BF16)
                for j in range(groups)
            ]
            piece = jnp.concatenate(tiles, axis=1)
            out_ref[s, :, c * wide : (c + 1) * wide] = piece
            results.append(piece)
    packed = exact(pack_matrix(row_at, owners, heads, rows), jnp.concatenate(results, axis=0))
    block = heads * CAP * STEPS
    for i in range(owners):
        outgoing[i][...] = packed[i * block : (i + 1) * block]


def collect_kernel(owners, heads, place_of, *refs):
    blocks, out_ref = refs[:owners], refs[owners]
    rows = out_ref.shape[1]
    wide = out_ref.shape[2] // heads
    arrived = jnp.concatenate([b[...] for b in blocks], axis=0)
    values = exact(unpack_matrix(place_of, owners, heads, rows), arrived)
    for c in range(heads):
        for s in range(STEPS):
            top = (c * STEPS + s) * rows
            out_ref[s, :, c * wide : (c + 1) * wide] = values[top : top + rows]


def exchange(blocks):
    owners = len(blocks)
    arrived = [blocks[0]] + [None] * (owners - 1)
    for i in range(owners - 1, 0, -1):
        arrived[i] = lax.ppermute(blocks[i], "store", [(s, s ^ i) for s in range(owners)])
    return arrived


def swap_cores(part):
    return lax.ppermute(part, "tensor", [(0, 1), (1, 0)])


def shards(
    x_in,
    q_base,
    k_new,
    v_new,
    cache_k,
    cache_v,
    lengths,
    adapter_ids,
    slot_of,
    a_query,
    b_query,
    a_output,
    b_output,
):
    owners = lax.axis_size("store")
    rows = x_in.shape[1]
    width = x_in.shape[2]
    heads = cache_k.shape[2] // HD
    wide = width // heads
    adapt, rank = a_query.shape[1:]
    lanes = adapt * rank
    block = heads * CAP * STEPS
    items = owners * CAP * STEPS
    me = lax.axis_index("store").astype(I32).reshape(1)
    core = lax.axis_index("tensor")

    def half(a_store):
        flat = jnp.transpose(a_store, (1, 2, 0)).reshape(lanes, a_store.shape[0])
        return lax.dynamic_slice(flat, (0, core * width), (lanes, width))

    shape = jax.ShapeDtypeStruct
    small = pltpu.CompilerParams(vmem_limit_bytes=16 * 1024 * 1024)

    place_of, row_at, _, order, *blocks = pl.pallas_call(
        functools.partial(dispatch_kernel, owners, heads, adapt, rank),
        out_shape=[
            shape((rows,), I32),
            shape((owners * CAP,), I32),
            shape((owners * CAP,), I32),
            shape((rows,), I32),
        ]
        + [shape((block, wide + lanes), BF16)] * owners,
        in_specs=[SMEM] * 4 + [VMEM],
        out_specs=[SMEM] * 4 + [VMEM] * owners,
        compiler_params=small,
        name="dispatch",
    )(me, adapter_ids, slot_of, lengths, x_in)

    arrived = exchange(blocks)
    part, mask = pl.pallas_call(
        functools.partial(project_kernel, owners, heads, wide, True),
        out_shape=[shape((items, lanes), F32)] * 2,
        in_specs=[VMEM] * (owners + 1),
        out_specs=[VMEM] * 2,
        compiler_params=small,
        name="project_query",
    )(half(a_query), *arrived)

    def expand(part, b_store, name):
        return pl.pallas_call(
            functools.partial(expand_kernel, owners, heads, wide),
            out_shape=[shape((block, wide), BF16)] * owners,
            in_specs=[VMEM] * 3,
            out_specs=[VMEM] * owners,
            compiler_params=small,
            name=name,
        )(part, swap_cores(part), b_store.reshape(lanes, width))

    returned = exchange(expand(part, b_query, "expand_query"))

    attn_out, *outgoing = pl.pallas_call(
        functools.partial(attend_kernel, owners, heads),
        out_shape=[shape((STEPS, rows, width), BF16)] + [shape((block, wide), BF16)] * owners,
        in_specs=[SMEM] * 4 + [VMEM] * 3 + [ANY] * 2 + [VMEM] * owners,
        out_specs=[VMEM] * (owners + 1),
        scratch_shapes=[
            pltpu.VMEM(cache_k.shape, BF16),
            pltpu.VMEM(cache_v.shape, BF16),
            pltpu.VMEM((rows * STEPS * width // HD, HD), F32),
            pltpu.VMEM((rows * STEPS * width // HD, HD), F32),
            pltpu.SemaphoreType.DMA((rows,)),
            pltpu.SemaphoreType.DMA((rows,)),
        ],
        compiler_params=pltpu.CompilerParams(vmem_limit_bytes=32 * 1024 * 1024),
        name="attend",
    )(place_of, row_at, order, lengths, q_base, k_new, v_new, cache_k, cache_v, *returned)

    arrived = exchange(outgoing)
    part = pl.pallas_call(
        functools.partial(project_kernel, owners, heads, wide, False),
        out_shape=shape((items, lanes), F32),
        in_specs=[VMEM] * (owners + 2),
        out_specs=VMEM,
        compiler_params=small,
        name="project_output",
    )(half(a_output), *arrived, mask)
    returned = exchange(expand(part, b_output, "expand_output"))
    adapter_out = pl.pallas_call(
        functools.partial(collect_kernel, owners, heads),
        out_shape=shape((STEPS, rows, width), BF16),
        in_specs=[SMEM] + [VMEM] * owners,
        out_specs=VMEM,
        compiler_params=small,
        name="collect",
    )(place_of, *returned)
    return (attn_out, adapter_out)


def solution(mesh):
    in_specs = (
        P(None, ("parts", "store"), "tensor"),
        P(None, ("parts", "store"), "tensor"),
        P(None, ("parts", "store"), "tensor"),
        P(None, ("parts", "store"), "tensor"),
        P(("parts", "store"), None, "tensor"),
        P(("parts", "store"), None, "tensor"),
        P(("parts", "store")),
        P(("parts", "store")),
        P("parts"),
        P(None, "store", None),
        P("store", None, "tensor"),
        P(None, "store", None),
        P("store", None, "tensor"),
    )
    out_specs = (P(None, ("parts", "store"), "tensor"), P(None, ("parts", "store"), "tensor"))
    return jax.shard_map(shards, mesh=mesh, in_specs=in_specs, out_specs=out_specs, check_vma=False)
```

```python
import functools
import math

import jax
import jax.numpy as jnp
from jax import lax
from jax.experimental import pallas as pl
from jax.experimental.pallas import tpu as pltpu
from jax.sharding import PartitionSpec as P

HD = 128
CAP = 2
STEPS = 2
CHUNK = 128
QUAD = 4
BF16 = jnp.bfloat16
F32 = jnp.float32
I32 = jnp.int32
VMEM = pl.BlockSpec(memory_space=pltpu.VMEM)
SMEM = pl.BlockSpec(memory_space=pltpu.SMEM)
HBM = pl.BlockSpec(memory_space=pltpu.HBM)


def iota(shape, dim):
    return lax.broadcasted_iota(I32, shape, dim)


def one_hot(hits):
    return jnp.where(hits, 1.0, 0.0).astype(BF16)


def stacked(ref, heads, wide):
    return jnp.concatenate(
        [ref[s, :, c * wide : (c + 1) * wide] for c in range(heads) for s in range(STEPS)], axis=0
    )


def pack_matrix(row_at, owners, heads, rows):
    items = CAP * STEPS
    block = heads * items
    shape = (block, heads * STEPS * rows)
    at = iota(shape, 0)
    col = iota(shape, 1)
    base = (at // items) * (STEPS * rows) + (at % STEPS) * rows
    first = (at // STEPS) % CAP == 0
    parts = []
    for i in range(owners):
        row = jnp.where(first, row_at[i * CAP], row_at[i * CAP + 1])
        parts.append(one_hot((col == base + row) & (row >= 0)))
    return jnp.concatenate(parts, axis=0)


def unpack_matrix(place_of, owners, heads, rows):
    items = CAP * STEPS
    block = heads * items
    shape = (rows, owners * block)
    at = iota(shape, 0)
    col = iota(shape, 1)
    spot = jnp.zeros(shape, I32)
    for r in range(rows):
        place = place_of[r]
        spot = jnp.where(at == r, (place // CAP) * block + (place % CAP) * STEPS, spot)
    return jnp.concatenate(
        [one_hot(col == spot + (c * items + s)) for c in range(heads) for s in range(STEPS)], axis=0
    )


def regroup_matrix(owners, heads):
    items = CAP * STEPS
    total = owners * heads * items
    at = iota((total, total), 0)
    col = iota((total, total), 1)
    head = at // (owners * items)
    owner = (at // items) % owners
    return one_hot(col == owner * (heads * items) + head * items + at % items)


def ungroup_matrix(owners, heads):
    items = CAP * STEPS
    total = owners * heads * items
    at = iota((total, total), 0)
    col = iota((total, total), 1)
    owner = at // (heads * items)
    head = (at // items) % heads
    return one_hot(col == head * (owners * items) + owner * items + at % items)


def exact(matrix, values):
    return jnp.dot(matrix, values, preferred_element_type=F32).astype(BF16)


def dispatch_kernel(
    owners,
    heads,
    adapt,
    rank,
    ids_hbm,
    slot_of_hbm,
    lengths_hbm,
    x_hbm,
    place_of,
    row_at,
    order,
    blocks,
    slot_at,
    ids,
    slot_of,
    lengths,
    x_ref,
    sems,
):
    sources = (ids_hbm, slot_of_hbm, lengths_hbm, x_hbm)
    targets = (ids, slot_of, lengths, x_ref)
    copies = [pltpu.make_async_copy(a, b, sems.at[k]) for k, (a, b) in enumerate(zip(sources, targets))]
    for copy in copies:
        copy.start()
    rows = x_ref.shape[1]
    wide = x_ref.shape[2] // heads
    for copy in copies[:3]:
        copy.wait()
    for p in range(owners * CAP):
        row_at[p] = -1
        slot_at[p] = -1
    for r in range(rows):
        slot = slot_of[ids[r]]
        relative = slot // adapt
        taken = jnp.where(row_at[relative * CAP] >= 0, 1, 0)
        place = relative * CAP + taken
        row_at[place] = r
        slot_at[place] = slot % adapt
        place_of[r] = place
    sizes = [lengths[r] for r in range(rows)]
    for r in range(rows):
        ahead = jnp.int32(0)
        for q in range(rows):
            if q != r:
                longer = sizes[q] >= sizes[r] if q < r else sizes[q] > sizes[r]
                ahead = ahead + jnp.where(longer, 1, 0)
        order[ahead] = r
    items = CAP * STEPS
    block = heads * items
    copies[3].wait()
    packed = exact(pack_matrix(row_at, owners, heads, rows), stacked(x_ref, heads, wide))
    at = iota((block, adapt * rank), 0)
    lane_slot = iota((block, adapt * rank), 1) // rank
    first = (at // STEPS) % CAP == 0
    for i in range(owners):
        blocks[i, :, :wide] = packed[i * block : (i + 1) * block]
        slot = jnp.where(first, slot_at[i * CAP], slot_at[i * CAP + 1])
        blocks[i, :, wide:] = one_hot(lane_slot == slot)


def project_kernel(owners, heads, wide, first, a_ref, blocks, *refs):
    if first:
        part_ref, mask_ref = refs
    else:
        mask_in, part_ref = refs
    grouped = regroup_matrix(owners, heads)
    items = owners * CAP * STEPS
    arrived = jnp.concatenate([blocks[i, :, :wide] for i in range(owners)], axis=0)
    arrived = exact(grouped, arrived)
    if first:
        masks = jnp.concatenate([blocks[i, :, wide:] for i in range(owners)], axis=0)
        mask = jnp.dot(grouped[:items], masks, preferred_element_type=F32)
        mask_ref[...] = mask
    else:
        mask = mask_in[...]
    total = jnp.zeros(mask.shape, F32)
    for c in range(heads):
        total = total + lax.dot_general(
            arrived[c * items : (c + 1) * items],
            a_ref[:, c * wide : (c + 1) * wide],
            (((1,), (1,)), ((), ())),
            preferred_element_type=F32,
        )
    part_ref[...] = total * mask


def expand_kernel(owners, heads, wide, mine, other, b_ref, blocks):
    low_rank = (mine[...] + other[...]).astype(BF16)
    pieces = []
    for c in range(heads):
        product = jnp.dot(
            low_rank, b_ref[:, c * wide : (c + 1) * wide], preferred_element_type=F32
        )
        pieces.append((2.0 * product).astype(BF16))
    back = exact(ungroup_matrix(owners, heads), jnp.concatenate(pieces, axis=0))
    block = heads * CAP * STEPS
    for i in range(owners):
        blocks[i] = back[i * block : (i + 1) * block]


def attend_kernel(
    owners,
    heads,
    place_of,
    row_at,
    order,
    lengths,
    q_ref,
    kn_ref,
    vn_ref,
    k_any,
    v_any,
    blocks,
    out_ref,
    outgoing,
    k_buf,
    v_buf,
    q_buf,
    o_buf,
    k_sem,
    v_sem,
):
    rows = q_ref.shape[1]
    wide = q_ref.shape[2] // heads
    groups = wide // HD
    span = STEPS * groups
    width = heads * HD
    sizes = k_any.shape[1] // CHUNK

    def copies(row, amount):
        part = pl.ds(0, amount * CHUNK)
        return (
            pltpu.make_async_copy(k_any.at[row, part], k_buf.at[row, part], k_sem.at[row]),
            pltpu.make_async_copy(v_any.at[row, part], v_buf.at[row, part], v_sem.at[row]),
        )

    def per_quad(action):
        def body(quad, carry):
            longest = lengths[order[quad * QUAD]]
            amount = (longest + CHUNK - 1) // CHUNK
            for size in range(1, sizes + 1):

                @pl.when(amount == size)
                def _():
                    action([order[quad * QUAD + j] for j in range(QUAD)], size)

            return carry

        lax.fori_loop(0, rows // QUAD, body, 0)

    def begin(rows_in, size):
        for row in rows_in:
            for copy in copies(row, size):
                copy.start()

    per_quad(begin)

    delta = jnp.dot(
        unpack_matrix(place_of, owners, heads, rows),
        jnp.concatenate([blocks[i] for i in range(owners)], axis=0),
        preferred_element_type=F32,
    )
    query = (stacked(q_ref, heads, wide).astype(F32) + delta).astype(BF16).astype(F32)
    for c in range(heads):
        for s in range(STEPS):
            top = (c * STEPS + s) * rows
            for j in range(groups):
                q_buf[pl.ds(c * span + s * groups + j, rows, stride=heads * span), :] = query[
                    top : top + rows, j * HD : (j + 1) * HD
                ]

    scale = 1.0 / math.sqrt(HD)
    new_keys = jnp.concatenate([kn_ref[t] for t in range(STEPS)], axis=0)
    new_values = jnp.concatenate([vn_ref[t] for t in range(STEPS)], axis=0)
    total = heads * span
    diagonal = iota((total, width), 0) // span == iota((total, width), 1) // HD
    fresh_shape = (total, STEPS * rows)
    step_of = (iota(fresh_shape, 0) // groups) % STEPS
    fresh_at = iota(fresh_shape, 1)
    in_time = fresh_at // rows <= step_of
    contract = (((1,), (1,)), ((), ()))

    def attend(rows_in, size):
        for row in rows_in:
            for copy in copies(row, size):
                copy.wait()
        length_now = size * CHUNK
        position = iota((total, length_now), 1)
        for row in rows_in:
            start = pl.multiple_of(row * total, total)
            one = q_buf[pl.ds(start, total), :].astype(BF16)
            spread = jnp.where(diagonal, jnp.concatenate([one] * heads, axis=1), jnp.zeros((), BF16))
            keys = k_buf[row, :length_now, :]
            values = v_buf[row, :length_now, :]
            cached = lax.dot_general(spread, keys, contract, preferred_element_type=F32) * scale
            cached = jnp.where(position < lengths[row], cached, -jnp.inf)
            fresh = lax.dot_general(spread, new_keys, contract, preferred_element_type=F32) * scale
            fresh = jnp.where(in_time & (fresh_at % rows == row), fresh, -jnp.inf)
            top = jnp.maximum(
                jnp.max(cached, axis=1, keepdims=True), jnp.max(fresh, axis=1, keepdims=True)
            )
            cached = jnp.exp(cached - top)
            fresh = jnp.exp(fresh - top)
            norm = jnp.sum(cached, axis=1, keepdims=True) + jnp.sum(fresh, axis=1, keepdims=True)
            share = 1.0 / norm
            mixed = jnp.dot((cached * share).astype(BF16), values, preferred_element_type=F32)
            mixed = mixed + jnp.dot(
                (fresh * share).astype(BF16), new_values, preferred_element_type=F32
            )
            o_buf[pl.ds(start, total), :] = jnp.concatenate(
                [
                    mixed[c * span : (c + 1) * span, c * HD : (c + 1) * HD]
                    for c in range(heads)
                ],
                axis=0,
            )

    per_quad(attend)

    results = []
    for c in range(heads):
        for s in range(STEPS):
            tiles = [
                o_buf[pl.ds(c * span + s * groups + j, rows, stride=heads * span), :].astype(BF16)
                for j in range(groups)
            ]
            piece = jnp.concatenate(tiles, axis=1)
            out_ref[s, :, c * wide : (c + 1) * wide] = piece
            results.append(piece)
    packed = exact(pack_matrix(row_at, owners, heads, rows), jnp.concatenate(results, axis=0))
    block = heads * CAP * STEPS
    for i in range(owners):
        outgoing[i] = packed[i * block : (i + 1) * block]


def collect_kernel(owners, heads, place_of, blocks, out_ref):
    rows = out_ref.shape[1]
    wide = out_ref.shape[2] // heads
    arrived = jnp.concatenate([blocks[i] for i in range(owners)], axis=0)
    values = exact(unpack_matrix(place_of, owners, heads, rows), arrived)
    for c in range(heads):
        for s in range(STEPS):
            top = (c * STEPS + s) * rows
            out_ref[s, :, c * wide : (c + 1) * wide] = values[top : top + rows]


def exchange(blocks):
    return lax.all_to_all(blocks, "store", split_axis=0, concat_axis=0, tiled=True)


def swap_cores(part):
    return lax.ppermute(part, "tensor", [(0, 1), (1, 0)])


def shards(
    x_in,
    q_base,
    k_new,
    v_new,
    cache_k,
    cache_v,
    lengths,
    adapter_ids,
    slot_of,
    a_query,
    b_query,
    a_output,
    b_output,
):
    owners = lax.axis_size("store")
    rows = x_in.shape[1]
    width = x_in.shape[2]
    heads = cache_k.shape[2] // HD
    wide = width // heads
    adapt, rank = a_query.shape[1:]
    lanes = adapt * rank
    block = heads * CAP * STEPS
    items = owners * CAP * STEPS
    core = lax.axis_index("tensor")

    def half(a_store):
        flat = jnp.transpose(a_store, (1, 2, 0)).reshape(lanes, a_store.shape[0])
        return lax.dynamic_slice(flat, (0, core * width), (lanes, width))

    shape = jax.ShapeDtypeStruct
    small = pltpu.CompilerParams(vmem_limit_bytes=16 * 1024 * 1024)

    sent = shape((owners, block, wide), BF16)
    place_of, row_at, order, blocks = pl.pallas_call(
        functools.partial(dispatch_kernel, owners, heads, adapt, rank),
        out_shape=[
            shape((rows,), I32),
            shape((owners * CAP,), I32),
            shape((rows,), I32),
            shape((owners, block, wide + lanes), BF16),
        ],
        in_specs=[HBM] * 4,
        out_specs=[SMEM] * 3 + [VMEM],
        scratch_shapes=[
            pltpu.SMEM((owners * CAP,), I32),
            pltpu.SMEM(adapter_ids.shape, I32),
            pltpu.SMEM(slot_of.shape, I32),
            pltpu.SMEM(lengths.shape, I32),
            pltpu.VMEM(x_in.shape, BF16),
            pltpu.SemaphoreType.DMA((4,)),
        ],
        compiler_params=small,
        name="dispatch",
    )(adapter_ids, slot_of, lengths, x_in)

    arrived = exchange(blocks)
    part, mask = pl.pallas_call(
        functools.partial(project_kernel, owners, heads, wide, True),
        out_shape=[shape((items, lanes), F32)] * 2,
        in_specs=[VMEM] * 2,
        out_specs=[VMEM] * 2,
        compiler_params=small,
        name="project_query",
    )(half(a_query), arrived)

    def expand(part, b_store, name):
        return pl.pallas_call(
            functools.partial(expand_kernel, owners, heads, wide),
            out_shape=sent,
            in_specs=[VMEM] * 3,
            out_specs=VMEM,
            compiler_params=small,
            name=name,
        )(part, swap_cores(part), b_store.reshape(lanes, width))

    returned = exchange(expand(part, b_query, "expand_query"))

    attn_out, outgoing = pl.pallas_call(
        functools.partial(attend_kernel, owners, heads),
        out_shape=[shape((STEPS, rows, width), BF16), sent],
        in_specs=[SMEM] * 4 + [VMEM] * 3 + [HBM] * 2 + [VMEM],
        out_specs=[VMEM] * 2,
        scratch_shapes=[
            pltpu.VMEM(cache_k.shape, BF16),
            pltpu.VMEM(cache_v.shape, BF16),
            pltpu.VMEM((rows * STEPS * width // HD, HD), F32),
            pltpu.VMEM((rows * STEPS * width // HD, HD), F32),
            pltpu.SemaphoreType.DMA((rows,)),
            pltpu.SemaphoreType.DMA((rows,)),
        ],
        compiler_params=pltpu.CompilerParams(vmem_limit_bytes=32 * 1024 * 1024),
        name="attend",
    )(place_of, row_at, order, lengths, q_base, k_new, v_new, cache_k, cache_v, returned)

    arrived = exchange(outgoing)
    part = pl.pallas_call(
        functools.partial(project_kernel, owners, heads, wide, False),
        out_shape=shape((items, lanes), F32),
        in_specs=[VMEM] * 3,
        out_specs=VMEM,
        compiler_params=small,
        name="project_output",
    )(half(a_output), arrived, mask)
    returned = exchange(expand(part, b_output, "expand_output"))
    adapter_out = pl.pallas_call(
        functools.partial(collect_kernel, owners, heads),
        out_shape=shape((STEPS, rows, width), BF16),
        in_specs=[SMEM, VMEM],
        out_specs=VMEM,
        compiler_params=small,
        name="collect",
    )(place_of, returned)
    return (attn_out, adapter_out)


def solution(mesh):
    in_specs = (
        P(None, ("parts", "store"), "tensor"),
        P(None, ("parts", "store"), "tensor"),
        P(None, ("parts", "store"), "tensor"),
        P(None, ("parts", "store"), "tensor"),
        P(("parts", "store"), None, "tensor"),
        P(("parts", "store"), None, "tensor"),
        P(("parts", "store")),
        P(("parts", "store")),
        P("parts"),
        P(None, "store", None),
        P("store", None, "tensor"),
        P(None, "store", None),
        P("store", None, "tensor"),
    )
    out_specs = (P(None, ("parts", "store"), "tensor"), P(None, ("parts", "store"), "tensor"))
    return jax.shard_map(shards, mesh=mesh, in_specs=in_specs, out_specs=out_specs, check_vma=False)
```

```python
import functools
import math

import jax
import jax.numpy as jnp
from jax import lax
from jax.experimental import pallas as pl
from jax.experimental.pallas import tpu as pltpu
from jax.sharding import PartitionSpec as P

HD = 128
CAP = 2
STEPS = 2
CHUNK = 128
QUAD = 4
BF16 = jnp.bfloat16
F32 = jnp.float32
I32 = jnp.int32
VMEM = pl.BlockSpec(memory_space=pltpu.VMEM)
SMEM = pl.BlockSpec(memory_space=pltpu.SMEM)
HBM = pl.BlockSpec(memory_space=pltpu.HBM)


def iota(shape, dim):
    return lax.broadcasted_iota(I32, shape, dim)


def one_hot(hits):
    return jnp.where(hits, 1.0, 0.0).astype(BF16)


def stacked(ref, heads, wide):
    return jnp.concatenate(
        [ref[s, :, c * wide : (c + 1) * wide] for c in range(heads) for s in range(STEPS)], axis=0
    )


def pack_matrix(row_at, owners, heads, rows, by_row):
    items = CAP * STEPS
    block = heads * items
    shape = (block, heads * STEPS * rows)
    at = iota(shape, 0)
    col = iota(shape, 1)
    head_step = (at // items) * STEPS + at % STEPS
    base = head_step if by_row else head_step * rows
    factor = heads * STEPS if by_row else 1
    first = (at // STEPS) % CAP == 0
    parts = []
    for i in range(owners):
        row = jnp.where(first, row_at[i * CAP], row_at[i * CAP + 1])
        parts.append(one_hot((col == base + row * factor) & (row >= 0)))
    return jnp.concatenate(parts, axis=0)


def unpack_matrix(place_of, owners, heads, rows, by_row):
    items = CAP * STEPS
    block = heads * items
    pairs = heads * STEPS
    if by_row:
        shape = (pairs, owners * block)
        at = iota(shape, 0)
        col = iota(shape, 1) - ((at // STEPS) * items + at % STEPS)
        parts = []
        for r in range(rows):
            place = place_of[r]
            parts.append(one_hot(col == (place // CAP) * block + (place % CAP) * STEPS))
        return jnp.concatenate(parts, axis=0)
    shape = (rows, owners * block)
    at = iota(shape, 0)
    col = iota(shape, 1)
    spot = jnp.zeros(shape, I32)
    for r in range(rows):
        place = place_of[r]
        spot = jnp.where(at == r, (place // CAP) * block + (place % CAP) * STEPS, spot)
    return jnp.concatenate(
        [one_hot(col == spot + (c * items + s)) for c in range(heads) for s in range(STEPS)], axis=0
    )


def by_row_matrix(heads, rows):
    pairs = heads * STEPS
    at = iota((pairs * rows, pairs * rows), 0)
    col = iota((pairs * rows, pairs * rows), 1)
    return one_hot(col == (at % pairs) * rows + at // pairs)


def by_pair_matrix(heads, rows):
    pairs = heads * STEPS
    at = iota((pairs * rows, pairs * rows), 0)
    col = iota((pairs * rows, pairs * rows), 1)
    return one_hot(col == (at % rows) * pairs + at // rows)


def regroup_matrix(owners, heads):
    items = CAP * STEPS
    total = owners * heads * items
    at = iota((total, total), 0)
    col = iota((total, total), 1)
    head = at // (owners * items)
    owner = (at // items) % owners
    return one_hot(col == owner * (heads * items) + head * items + at % items)


def ungroup_matrix(owners, heads):
    items = CAP * STEPS
    total = owners * heads * items
    at = iota((total, total), 0)
    col = iota((total, total), 1)
    owner = at // (heads * items)
    head = (at // items) % heads
    return one_hot(col == head * (owners * items) + owner * items + at % items)


def exact(matrix, values):
    return jnp.dot(matrix, values, preferred_element_type=F32).astype(BF16)


def dispatch_kernel(
    owners,
    heads,
    adapt,
    rank,
    ids_hbm,
    slot_of_hbm,
    x_hbm,
    place_of,
    row_at,
    blocks,
    slot_at,
    ids,
    slot_of,
    x_ref,
    sems,
):
    pairs = ((ids_hbm, ids), (slot_of_hbm, slot_of), (x_hbm, x_ref))
    copies = [pltpu.make_async_copy(a, b, sems.at[k]) for k, (a, b) in enumerate(pairs)]
    for copy in copies:
        copy.start()
    rows = x_ref.shape[1]
    wide = x_ref.shape[2] // heads
    for copy in copies[:2]:
        copy.wait()
    for p in range(owners * CAP):
        row_at[p] = -1
        slot_at[p] = -1
    for r in range(rows):
        slot = slot_of[ids[r]]
        relative = slot // adapt
        taken = jnp.where(row_at[relative * CAP] >= 0, 1, 0)
        place = relative * CAP + taken
        row_at[place] = r
        slot_at[place] = slot % adapt
        place_of[r] = place
    items = CAP * STEPS
    block = heads * items
    copies[2].wait()
    packed = exact(pack_matrix(row_at, owners, heads, rows, False), stacked(x_ref, heads, wide))
    at = iota((block, adapt * rank), 0)
    lane_slot = iota((block, adapt * rank), 1) // rank
    first = (at // STEPS) % CAP == 0
    for i in range(owners):
        blocks[i, :, :wide] = packed[i * block : (i + 1) * block]
        slot = jnp.where(first, slot_at[i * CAP], slot_at[i * CAP + 1])
        blocks[i, :, wide:] = one_hot(lane_slot == slot)


def project_kernel(owners, heads, wide, first, a_ref, blocks, *refs):
    if first:
        after, part_ref, mask_ref = refs
    else:
        mask_in, part_ref = refs
    grouped = regroup_matrix(owners, heads)
    items = owners * CAP * STEPS
    arrived = jnp.concatenate([blocks[i, :, :wide] for i in range(owners)], axis=0)
    arrived = exact(grouped, arrived)
    if first:
        masks = jnp.concatenate([blocks[i, :, wide:] for i in range(owners)], axis=0)
        mask = jnp.dot(grouped[:items], masks, preferred_element_type=F32)
        mask_ref[...] = mask
    else:
        mask = mask_in[...]
    total = jnp.zeros(mask.shape, F32)
    for c in range(heads):
        total = total + lax.dot_general(
            arrived[c * items : (c + 1) * items],
            a_ref[:, c * wide : (c + 1) * wide],
            (((1,), (1,)), ((), ())),
            preferred_element_type=F32,
        )
    part_ref[...] = total * mask


def expand_kernel(owners, heads, wide, mine, other, b_ref, blocks):
    low_rank = (mine[...] + other[...]).astype(BF16)
    pieces = []
    for c in range(heads):
        product = jnp.dot(
            low_rank, b_ref[:, c * wide : (c + 1) * wide], preferred_element_type=F32
        )
        pieces.append((2.0 * product).astype(BF16))
    back = exact(ungroup_matrix(owners, heads), jnp.concatenate(pieces, axis=0))
    block = heads * CAP * STEPS
    for i in range(owners):
        blocks[i] = back[i * block : (i + 1) * block]


def quads(order, lengths, rows, sizes, action):
    def body(quad, carry):
        longest = lengths[order[quad * QUAD]]
        amount = (longest + CHUNK - 1) // CHUNK
        for size in range(1, sizes + 1):

            @pl.when(amount == size)
            def _():
                action([order[quad * QUAD + j] for j in range(QUAD)], size)

        return carry

    lax.fori_loop(0, rows // QUAD, body, 0)


def prefetch_kernel(after, lengths_hbm, k_hbm, v_hbm, order, k_out, v_out, lengths, k_sem, v_sem):
    pltpu.sync_copy(lengths_hbm, lengths)
    rows = k_hbm.shape[0]
    sizes = [lengths[r] for r in range(rows)]
    for r in range(rows):
        ahead = jnp.int32(0)
        for q in range(rows):
            if q != r:
                longer = sizes[q] >= sizes[r] if q < r else sizes[q] > sizes[r]
                ahead = ahead + jnp.where(longer, 1, 0)
        order[ahead] = r

    def copies(row, size):
        part = pl.ds(0, size * CHUNK)
        return (
            pltpu.make_async_copy(k_hbm.at[row, part], k_out.at[row, part], k_sem.at[row]),
            pltpu.make_async_copy(v_hbm.at[row, part], v_out.at[row, part], v_sem.at[row]),
        )

    def begin(rows_in, size):
        for row in rows_in:
            for copy in copies(row, size):
                copy.start()

    def finish(rows_in, size):
        for row in rows_in:
            for copy in copies(row, size):
                copy.wait()

    chunks = k_hbm.shape[1] // CHUNK
    quads(order, lengths, rows, chunks, begin)
    quads(order, lengths, rows, chunks, finish)


def attend_kernel(
    owners,
    heads,
    place_of,
    row_at,
    order,
    lengths,
    q_ref,
    kn_ref,
    vn_ref,
    k_ref,
    v_ref,
    blocks,
    out_ref,
    outgoing,
    q_buf,
    o_buf,
):
    rows = q_ref.shape[1]
    wide = q_ref.shape[2] // heads
    groups = wide // HD
    pairs = heads * STEPS
    total = groups * pairs
    width = heads * HD

    delta = jnp.dot(
        unpack_matrix(place_of, owners, heads, rows, True),
        jnp.concatenate([blocks[i] for i in range(owners)], axis=0),
        preferred_element_type=F32,
    )
    base = jnp.dot(
        by_row_matrix(heads, rows), stacked(q_ref, heads, wide), preferred_element_type=F32
    )
    q_buf[...] = base + delta

    factor = math.log2(math.e) / math.sqrt(HD)
    new_keys = jnp.concatenate([kn_ref[t] for t in range(STEPS)], axis=0)
    new_values = jnp.concatenate([vn_ref[t] for t in range(STEPS)], axis=0)
    diagonal = (iota((total, width), 0) // STEPS) % heads == iota((total, width), 1) // HD
    own_head = [(iota((total, HD), 0) // STEPS) % heads == c for c in range(heads)]
    fresh_shape = (total, STEPS * rows)
    fresh_at = iota(fresh_shape, 1)
    in_time = fresh_at // rows <= iota(fresh_shape, 0) % STEPS
    contract = (((1,), (1,)), ((), ()))

    def attend(rows_in, size):
        extent = size * CHUNK
        position = iota((total, extent), 1)
        results = []
        for row in rows_in:
            start = pl.multiple_of(row * pairs, pairs)
            flat = q_buf[pl.ds(start, pairs), :]
            one = jnp.concatenate(
                [flat[:, j * HD : (j + 1) * HD] for j in range(groups)], axis=0
            ).astype(BF16)
            spread = jnp.where(diagonal, jnp.concatenate([one] * heads, axis=1), jnp.zeros((), BF16))
            cached = lax.dot_general(
                spread, k_ref[row, :extent, :], contract, preferred_element_type=F32
            )
            cached = jnp.where(position < lengths[row], cached, -jnp.inf)
            fresh = lax.dot_general(spread, new_keys, contract, preferred_element_type=F32)
            fresh = jnp.where(in_time & (fresh_at % rows == row), fresh, -jnp.inf)
            top = jnp.maximum(
                jnp.max(cached, axis=1, keepdims=True), jnp.max(fresh, axis=1, keepdims=True)
            )
            cached = jnp.exp2((cached - top) * factor)
            fresh = jnp.exp2((fresh - top) * factor)
            norm = jnp.sum(cached, axis=1, keepdims=True) + jnp.sum(fresh, axis=1, keepdims=True)
            mixed = jnp.dot(
                cached.astype(BF16), v_ref[row, :extent, :], preferred_element_type=F32
            ) + jnp.dot(fresh.astype(BF16), new_values, preferred_element_type=F32)
            own = jnp.zeros((total, HD), F32)
            for c in range(heads):
                own = jnp.where(own_head[c], mixed[:, c * HD : (c + 1) * HD], own)
            results.append((start, own / norm))
        for start, own in results:
            o_buf[pl.ds(start, pairs), :] = jnp.concatenate(
                [own[j * pairs : (j + 1) * pairs] for j in range(groups)], axis=1
            )

    quads(order, lengths, rows, k_ref.shape[1] // CHUNK, attend)

    mixed = o_buf[...].astype(BF16)
    packed = exact(pack_matrix(row_at, owners, heads, rows, True), mixed)
    block = heads * CAP * STEPS
    for i in range(owners):
        outgoing[i] = packed[i * block : (i + 1) * block]
    final = exact(by_pair_matrix(heads, rows), mixed)
    for c in range(heads):
        for s in range(STEPS):
            at = (c * STEPS + s) * rows
            out_ref[s, :, c * wide : (c + 1) * wide] = final[at : at + rows]


def collect_kernel(owners, heads, place_of, blocks, out_ref):
    rows = out_ref.shape[1]
    wide = out_ref.shape[2] // heads
    arrived = jnp.concatenate([blocks[i] for i in range(owners)], axis=0)
    values = exact(unpack_matrix(place_of, owners, heads, rows, False), arrived)
    for c in range(heads):
        for s in range(STEPS):
            top = (c * STEPS + s) * rows
            out_ref[s, :, c * wide : (c + 1) * wide] = values[top : top + rows]


def exchange(blocks):
    return lax.all_to_all(blocks, "store", split_axis=0, concat_axis=0, tiled=True)


def in_hbm(array):
    return pltpu.with_memory_space_constraint(array, pltpu.HBM)


def in_vmem(array):
    return pltpu.with_memory_space_constraint(array, pltpu.VMEM)


def swap_cores(part):
    return lax.ppermute(part, "tensor", [(0, 1), (1, 0)])


def shards(
    x_in,
    q_base,
    k_new,
    v_new,
    cache_k,
    cache_v,
    lengths,
    adapter_ids,
    slot_of,
    a_query,
    b_query,
    a_output,
    b_output,
):
    owners = lax.axis_size("store")
    rows = x_in.shape[1]
    width = x_in.shape[2]
    heads = cache_k.shape[2] // HD
    wide = width // heads
    adapt, rank = a_query.shape[1:]
    lanes = adapt * rank
    block = heads * CAP * STEPS
    items = owners * CAP * STEPS
    core = lax.axis_index("tensor")

    def half(a_store):
        flat = jnp.transpose(a_store, (1, 2, 0)).reshape(lanes, a_store.shape[0])
        return lax.dynamic_slice(flat, (0, core * width), (lanes, width))

    shape = jax.ShapeDtypeStruct
    small = pltpu.CompilerParams(vmem_limit_bytes=16 * 1024 * 1024)

    sent = shape((owners, block, wide), BF16)
    place_of, row_at, blocks = pl.pallas_call(
        functools.partial(dispatch_kernel, owners, heads, adapt, rank),
        out_shape=[
            shape((rows,), I32),
            shape((owners * CAP,), I32),
            shape((owners, block, wide + lanes), BF16),
        ],
        in_specs=[HBM] * 3,
        out_specs=[SMEM] * 2 + [VMEM],
        scratch_shapes=[
            pltpu.SMEM((owners * CAP,), I32),
            pltpu.SMEM(adapter_ids.shape, I32),
            pltpu.SMEM(slot_of.shape, I32),
            pltpu.VMEM(x_in.shape, BF16),
            pltpu.SemaphoreType.DMA((3,)),
        ],
        compiler_params=small,
        name="dispatch",
    )(in_hbm(adapter_ids), in_hbm(slot_of), in_hbm(x_in))

    order, keys, values = pl.pallas_call(
        prefetch_kernel,
        out_shape=[
            shape((rows,), I32),
            pltpu.VMEM(cache_k.shape, BF16),
            pltpu.VMEM(cache_v.shape, BF16),
        ],
        in_specs=[SMEM] + [HBM] * 3,
        out_specs=[SMEM, VMEM, VMEM],
        scratch_shapes=[
            pltpu.SMEM(lengths.shape, I32),
            pltpu.SemaphoreType.DMA((rows,)),
            pltpu.SemaphoreType.DMA((rows,)),
        ],
        compiler_params=small,
        cost_estimate=pl.CostEstimate(flops=0, bytes_accessed=8 * 1024 * 1024, transcendentals=0),
        name="prefetch",
    )(place_of, in_hbm(lengths), in_hbm(cache_k), in_hbm(cache_v))

    arrived = exchange(blocks)
    part, mask = pl.pallas_call(
        functools.partial(project_kernel, owners, heads, wide, True),
        out_shape=[shape((items, lanes), F32)] * 2,
        in_specs=[VMEM] * 2 + [SMEM],
        out_specs=[VMEM] * 2,
        compiler_params=small,
        name="project_query",
    )(half(a_query), arrived, order)

    def expand(part, b_store, name):
        return pl.pallas_call(
            functools.partial(expand_kernel, owners, heads, wide),
            out_shape=sent,
            in_specs=[VMEM] * 3,
            out_specs=VMEM,
            compiler_params=small,
            name=name,
        )(part, swap_cores(part), b_store.reshape(lanes, width))

    returned = exchange(expand(part, b_query, "expand_query"))

    attn_out, outgoing = pl.pallas_call(
        functools.partial(attend_kernel, owners, heads),
        out_shape=[shape((STEPS, rows, width), BF16), sent],
        in_specs=[SMEM] * 4 + [VMEM] * 6,
        out_specs=[VMEM] * 2,
        scratch_shapes=[
            pltpu.VMEM((rows * STEPS * heads, wide), F32),
            pltpu.VMEM((rows * STEPS * heads, wide), F32),
        ],
        compiler_params=pltpu.CompilerParams(vmem_limit_bytes=24 * 1024 * 1024),
        name="attend",
    )(place_of, row_at, order, lengths, q_base, k_new, v_new, in_vmem(keys), in_vmem(values), returned)

    arrived = exchange(outgoing)
    part = pl.pallas_call(
        functools.partial(project_kernel, owners, heads, wide, False),
        out_shape=shape((items, lanes), F32),
        in_specs=[VMEM] * 3,
        out_specs=VMEM,
        compiler_params=small,
        name="project_output",
    )(half(a_output), arrived, mask)
    returned = exchange(expand(part, b_output, "expand_output"))
    adapter_out = pl.pallas_call(
        functools.partial(collect_kernel, owners, heads),
        out_shape=shape((STEPS, rows, width), BF16),
        in_specs=[SMEM, VMEM],
        out_specs=VMEM,
        compiler_params=small,
        name="collect",
    )(place_of, returned)
    return (attn_out, adapter_out)


def solution(mesh):
    in_specs = (
        P(None, ("parts", "store"), "tensor"),
        P(None, ("parts", "store"), "tensor"),
        P(None, ("parts", "store"), "tensor"),
        P(None, ("parts", "store"), "tensor"),
        P(("parts", "store"), None, "tensor"),
        P(("parts", "store"), None, "tensor"),
        P(("parts", "store")),
        P(("parts", "store")),
        P("parts"),
        P(None, "store", None),
        P("store", None, "tensor"),
        P(None, "store", None),
        P("store", None, "tensor"),
    )
    out_specs = (P(None, ("parts", "store"), "tensor"), P(None, ("parts", "store"), "tensor"))
    return jax.shard_map(shards, mesh=mesh, in_specs=in_specs, out_specs=out_specs, check_vma=False)
```

```python
import functools
import math

import jax
import jax.numpy as jnp
from jax import lax
from jax.experimental import pallas as pl
from jax.experimental.pallas import tpu as pltpu
from jax.sharding import PartitionSpec as P

HD = 128
CAP = 2
STEPS = 2
CHUNK = 128
QUAD = 4
BF16 = jnp.bfloat16
F32 = jnp.float32
I32 = jnp.int32
VMEM = pl.BlockSpec(memory_space=pltpu.VMEM)
SMEM = pl.BlockSpec(memory_space=pltpu.SMEM)
HBM = pl.BlockSpec(memory_space=pltpu.HBM)


def iota(shape, dim):
    return lax.broadcasted_iota(I32, shape, dim)


def one_hot(hits):
    return jnp.where(hits, 1.0, 0.0).astype(BF16)


def stacked(ref, heads, wide):
    return jnp.concatenate(
        [ref[s, :, c * wide : (c + 1) * wide] for c in range(heads) for s in range(STEPS)], axis=0
    )


def pack_matrix(row_at, owners, heads, rows, by_row):
    items = CAP * STEPS
    block = heads * items
    shape = (block, heads * STEPS * rows)
    at = iota(shape, 0)
    col = iota(shape, 1)
    head_step = (at // items) * STEPS + at % STEPS
    base = head_step if by_row else head_step * rows
    factor = heads * STEPS if by_row else 1
    first = (at // STEPS) % CAP == 0
    parts = []
    for i in range(owners):
        row = jnp.where(first, row_at[i * CAP], row_at[i * CAP + 1])
        parts.append(one_hot((col == base + row * factor) & (row >= 0)))
    return jnp.concatenate(parts, axis=0)


def unpack_matrix(place_of, owners, heads, rows, by_row):
    items = CAP * STEPS
    block = heads * items
    pairs = heads * STEPS
    if by_row:
        shape = (pairs, owners * block)
        at = iota(shape, 0)
        col = iota(shape, 1) - ((at // STEPS) * items + at % STEPS)
        parts = []
        for r in range(rows):
            place = place_of[r]
            parts.append(one_hot(col == (place // CAP) * block + (place % CAP) * STEPS))
        return jnp.concatenate(parts, axis=0)
    shape = (rows, owners * block)
    at = iota(shape, 0)
    col = iota(shape, 1)
    spot = jnp.zeros(shape, I32)
    for r in range(rows):
        place = place_of[r]
        spot = jnp.where(at == r, (place // CAP) * block + (place % CAP) * STEPS, spot)
    return jnp.concatenate(
        [one_hot(col == spot + (c * items + s)) for c in range(heads) for s in range(STEPS)], axis=0
    )


def by_row_matrix(heads, rows):
    pairs = heads * STEPS
    at = iota((pairs * rows, pairs * rows), 0)
    col = iota((pairs * rows, pairs * rows), 1)
    return one_hot(col == (at % pairs) * rows + at // pairs)


def by_pair_matrix(heads, rows):
    pairs = heads * STEPS
    at = iota((pairs * rows, pairs * rows), 0)
    col = iota((pairs * rows, pairs * rows), 1)
    return one_hot(col == (at % rows) * pairs + at // rows)


def regroup_matrix(owners, heads):
    items = CAP * STEPS
    total = owners * heads * items
    at = iota((total, total), 0)
    col = iota((total, total), 1)
    head = at // (owners * items)
    owner = (at // items) % owners
    return one_hot(col == owner * (heads * items) + head * items + at % items)


def ungroup_matrix(owners, heads):
    items = CAP * STEPS
    total = owners * heads * items
    at = iota((total, total), 0)
    col = iota((total, total), 1)
    owner = at // (heads * items)
    head = (at // items) % heads
    return one_hot(col == head * (owners * items) + owner * items + at % items)


def exact(matrix, values):
    return jnp.dot(matrix, values, preferred_element_type=F32).astype(BF16)


def dispatch_kernel(
    owners,
    heads,
    adapt,
    rank,
    ids_hbm,
    slot_of_hbm,
    lengths_hbm,
    x_hbm,
    place_of,
    row_at,
    order,
    blocks,
    slot_at,
    ids,
    slot_of,
    lengths,
    x_ref,
    sems,
):
    pairs = ((ids_hbm, ids), (slot_of_hbm, slot_of), (lengths_hbm, lengths), (x_hbm, x_ref))
    copies = [pltpu.make_async_copy(a, b, sems.at[k]) for k, (a, b) in enumerate(pairs)]
    for copy in copies:
        copy.start()
    rows = x_ref.shape[1]
    wide = x_ref.shape[2] // heads
    for copy in copies[:3]:
        copy.wait()
    for p in range(owners * CAP):
        row_at[p] = -1
        slot_at[p] = -1
    for r in range(rows):
        slot = slot_of[ids[r]]
        relative = slot // adapt
        taken = jnp.where(row_at[relative * CAP] >= 0, 1, 0)
        place = relative * CAP + taken
        row_at[place] = r
        slot_at[place] = slot % adapt
        place_of[r] = place
    sizes = [lengths[r] for r in range(rows)]
    for r in range(rows):
        ahead = jnp.int32(0)
        for q in range(rows):
            if q != r:
                shorter = sizes[q] <= sizes[r] if q < r else sizes[q] < sizes[r]
                ahead = ahead + jnp.where(shorter, 1, 0)
        order[ahead] = r
    items = CAP * STEPS
    block = heads * items
    copies[3].wait()
    packed = exact(pack_matrix(row_at, owners, heads, rows, False), stacked(x_ref, heads, wide))
    at = iota((block, adapt * rank), 0)
    lane_slot = iota((block, adapt * rank), 1) // rank
    first = (at // STEPS) % CAP == 0
    for i in range(owners):
        blocks[i, :, :wide] = packed[i * block : (i + 1) * block]
        slot = jnp.where(first, slot_at[i * CAP], slot_at[i * CAP + 1])
        blocks[i, :, wide:] = one_hot(lane_slot == slot)


def project_kernel(owners, heads, wide, first, core, a_ref, blocks, *refs):
    if first:
        part_ref, mask_ref = refs
    else:
        mask_in, part_ref = refs
    grouped = regroup_matrix(owners, heads)
    items = owners * CAP * STEPS
    arrived = jnp.concatenate([blocks[i, :, :wide] for i in range(owners)], axis=0)
    arrived = exact(grouped, arrived)
    if first:
        masks = jnp.concatenate([blocks[i, :, wide:] for i in range(owners)], axis=0)
        mask = jnp.dot(grouped[:items], masks, preferred_element_type=F32)
        mask_ref[...] = mask
    else:
        mask = mask_in[...]
    total = jnp.zeros(mask.shape, F32)
    for c in range(heads):
        total = total + lax.dot_general(
            arrived[c * items : (c + 1) * items],
            a_ref[:, pl.ds(pl.multiple_of(core[0] * heads * wide + c * wide, wide), wide)],
            (((1,), (1,)), ((), ())),
            preferred_element_type=F32,
        )
    part_ref[...] = total * mask


def expand_kernel(owners, heads, wide, mine, other, b_ref, blocks):
    low_rank = (mine[...] + other[...]).astype(BF16)
    pieces = []
    for c in range(heads):
        product = jnp.dot(
            low_rank, b_ref[:, c * wide : (c + 1) * wide], preferred_element_type=F32
        )
        pieces.append((2.0 * product).astype(BF16))
    back = exact(ungroup_matrix(owners, heads), jnp.concatenate(pieces, axis=0))
    block = heads * CAP * STEPS
    for i in range(owners):
        blocks[i] = back[i * block : (i + 1) * block]


def quads(order, lengths, rows, sizes, action):
    def body(quad, carry):
        longest = lengths[order[quad * QUAD + QUAD - 1]]
        amount = (longest + CHUNK - 1) // CHUNK
        for size in range(1, sizes + 1):

            @pl.when(amount == size)
            def _():
                action([order[quad * QUAD + j] for j in range(QUAD)], size)

        return carry

    lax.fori_loop(0, rows // QUAD, body, 0)


def attend_kernel(
    owners,
    heads,
    place_of,
    row_at,
    order,
    lengths,
    q_ref,
    kn_ref,
    vn_ref,
    k_hbm,
    v_hbm,
    blocks,
    out_ref,
    outgoing,
    k_ref,
    v_ref,
    q_buf,
    o_buf,
    k_sem,
    v_sem,
):
    rows = q_ref.shape[1]

    def copies(row, size):
        part = pl.ds(0, size * CHUNK)
        return (
            pltpu.make_async_copy(k_hbm.at[row, part], k_ref.at[row, part], k_sem.at[row]),
            pltpu.make_async_copy(v_hbm.at[row, part], v_ref.at[row, part], v_sem.at[row]),
        )

    def begin(rows_in, size):
        for row in rows_in:
            for copy in copies(row, size):
                copy.start()

    chunks = k_hbm.shape[1] // CHUNK
    quads(order, lengths, rows, chunks, begin)

    wide = q_ref.shape[2] // heads
    groups = wide // HD
    pairs = heads * STEPS
    total = groups * pairs
    width = heads * HD

    delta = jnp.dot(
        unpack_matrix(place_of, owners, heads, rows, True),
        jnp.concatenate([blocks[i] for i in range(owners)], axis=0),
        preferred_element_type=F32,
    )
    base = jnp.dot(
        by_row_matrix(heads, rows), stacked(q_ref, heads, wide), preferred_element_type=F32
    )
    q_buf[...] = base + delta

    factor = math.log2(math.e) / math.sqrt(HD)
    new_keys = jnp.concatenate([kn_ref[t] for t in range(STEPS)], axis=0)
    new_values = jnp.concatenate([vn_ref[t] for t in range(STEPS)], axis=0)
    diagonal = (iota((total, width), 0) // STEPS) % heads == iota((total, width), 1) // HD
    own_head = [(iota((total, HD), 0) // STEPS) % heads == c for c in range(heads)]
    fresh_shape = (total, STEPS * rows)
    fresh_at = iota(fresh_shape, 1)
    in_time = fresh_at // rows <= iota(fresh_shape, 0) % STEPS
    contract = (((1,), (1,)), ((), ()))

    def attend(rows_in, size):
        for row in rows_in:
            for copy in copies(row, size):
                copy.wait()
        extent = size * CHUNK
        position = iota((total, extent), 1)
        results = []
        for row in rows_in:
            start = pl.multiple_of(row * pairs, pairs)
            flat = q_buf[pl.ds(start, pairs), :]
            one = jnp.concatenate(
                [flat[:, j * HD : (j + 1) * HD] for j in range(groups)], axis=0
            ).astype(BF16)
            spread = jnp.where(diagonal, jnp.concatenate([one] * heads, axis=1), jnp.zeros((), BF16))
            cached = lax.dot_general(
                spread, k_ref[row, :extent, :], contract, preferred_element_type=F32
            )
            cached = jnp.where(position < lengths[row], cached, -jnp.inf)
            fresh = lax.dot_general(spread, new_keys, contract, preferred_element_type=F32)
            fresh = jnp.where(in_time & (fresh_at % rows == row), fresh, -jnp.inf)
            top = jnp.maximum(
                jnp.max(cached, axis=1, keepdims=True), jnp.max(fresh, axis=1, keepdims=True)
            )
            cached = jnp.exp2((cached - top) * factor)
            fresh = jnp.exp2((fresh - top) * factor)
            norm = jnp.sum(cached, axis=1, keepdims=True) + jnp.sum(fresh, axis=1, keepdims=True)
            mixed = jnp.dot(
                cached.astype(BF16), v_ref[row, :extent, :], preferred_element_type=F32
            ) + jnp.dot(fresh.astype(BF16), new_values, preferred_element_type=F32)
            own = jnp.zeros((total, HD), F32)
            for c in range(heads):
                own = jnp.where(own_head[c], mixed[:, c * HD : (c + 1) * HD], own)
            results.append((start, own / norm))
        for start, own in results:
            o_buf[pl.ds(start, pairs), :] = jnp.concatenate(
                [own[j * pairs : (j + 1) * pairs] for j in range(groups)], axis=1
            )

    quads(order, lengths, rows, chunks, attend)

    mixed = o_buf[...].astype(BF16)
    packed = exact(pack_matrix(row_at, owners, heads, rows, True), mixed)
    block = heads * CAP * STEPS
    for i in range(owners):
        outgoing[i] = packed[i * block : (i + 1) * block]
    final = exact(by_pair_matrix(heads, rows), mixed)
    for c in range(heads):
        for s in range(STEPS):
            at = (c * STEPS + s) * rows
            out_ref[s, :, c * wide : (c + 1) * wide] = final[at : at + rows]


def collect_kernel(owners, heads, place_of, blocks, out_ref):
    rows = out_ref.shape[1]
    wide = out_ref.shape[2] // heads
    arrived = jnp.concatenate([blocks[i] for i in range(owners)], axis=0)
    values = exact(unpack_matrix(place_of, owners, heads, rows, False), arrived)
    for c in range(heads):
        for s in range(STEPS):
            top = (c * STEPS + s) * rows
            out_ref[s, :, c * wide : (c + 1) * wide] = values[top : top + rows]


def exchange(blocks):
    return lax.all_to_all(blocks, "store", split_axis=0, concat_axis=0, tiled=True)


def in_hbm(array):
    return pltpu.with_memory_space_constraint(array, pltpu.HBM)


def swap_cores(part):
    return lax.ppermute(part, "tensor", [(0, 1), (1, 0)])


def shards(
    x_in,
    q_base,
    k_new,
    v_new,
    cache_k,
    cache_v,
    lengths,
    adapter_ids,
    slot_of,
    a_query,
    b_query,
    a_output,
    b_output,
):
    owners = lax.axis_size("store")
    rows = x_in.shape[1]
    width = x_in.shape[2]
    heads = cache_k.shape[2] // HD
    wide = width // heads
    adapt, rank = a_query.shape[1:]
    lanes = adapt * rank
    block = heads * CAP * STEPS
    items = owners * CAP * STEPS
    core = lax.axis_index("tensor").astype(I32).reshape(1)

    def flat(a_store):
        return jnp.transpose(a_store, (1, 2, 0)).reshape(lanes, a_store.shape[0])

    shape = jax.ShapeDtypeStruct
    small = pltpu.CompilerParams(vmem_limit_bytes=16 * 1024 * 1024)

    sent = shape((owners, block, wide), BF16)
    place_of, row_at, order, blocks = pl.pallas_call(
        functools.partial(dispatch_kernel, owners, heads, adapt, rank),
        out_shape=[
            shape((rows,), I32),
            shape((owners * CAP,), I32),
            shape((rows,), I32),
            shape((owners, block, wide + lanes), BF16),
        ],
        in_specs=[HBM] * 4,
        out_specs=[SMEM] * 3 + [VMEM],
        scratch_shapes=[
            pltpu.SMEM((owners * CAP,), I32),
            pltpu.SMEM(adapter_ids.shape, I32),
            pltpu.SMEM(slot_of.shape, I32),
            pltpu.SMEM(lengths.shape, I32),
            pltpu.VMEM(x_in.shape, BF16),
            pltpu.SemaphoreType.DMA((4,)),
        ],
        compiler_params=small,
        name="dispatch",
    )(in_hbm(adapter_ids), in_hbm(slot_of), in_hbm(lengths), in_hbm(x_in))

    arrived = exchange(blocks)
    part, mask = pl.pallas_call(
        functools.partial(project_kernel, owners, heads, wide, True),
        out_shape=[shape((items, lanes), F32)] * 2,
        in_specs=[SMEM] + [VMEM] * 2,
        out_specs=[VMEM] * 2,
        compiler_params=small,
        name="project_query",
    )(core, flat(a_query), arrived)

    def expand(part, b_store, name):
        return pl.pallas_call(
            functools.partial(expand_kernel, owners, heads, wide),
            out_shape=sent,
            in_specs=[VMEM] * 3,
            out_specs=VMEM,
            compiler_params=small,
            name=name,
        )(part, swap_cores(part), b_store.reshape(lanes, width))

    returned = exchange(expand(part, b_query, "expand_query"))

    attn_out, outgoing = pl.pallas_call(
        functools.partial(attend_kernel, owners, heads),
        out_shape=[shape((STEPS, rows, width), BF16), sent],
        in_specs=[SMEM] * 4 + [VMEM] * 3 + [HBM] * 2 + [VMEM],
        out_specs=[VMEM] * 2,
        scratch_shapes=[
            pltpu.VMEM(cache_k.shape, BF16),
            pltpu.VMEM(cache_v.shape, BF16),
            pltpu.VMEM((rows * STEPS * heads, wide), F32),
            pltpu.VMEM((rows * STEPS * heads, wide), F32),
            pltpu.SemaphoreType.DMA((rows,)),
            pltpu.SemaphoreType.DMA((rows,)),
        ],
        compiler_params=pltpu.CompilerParams(vmem_limit_bytes=32 * 1024 * 1024),
        name="attend",
    )(place_of, row_at, order, lengths, q_base, k_new, v_new, in_hbm(cache_k), in_hbm(cache_v), returned)

    arrived = exchange(outgoing)
    part = pl.pallas_call(
        functools.partial(project_kernel, owners, heads, wide, False),
        out_shape=shape((items, lanes), F32),
        in_specs=[SMEM] + [VMEM] * 3,
        out_specs=VMEM,
        compiler_params=small,
        name="project_output",
    )(core, flat(a_output), arrived, mask)
    returned = exchange(expand(part, b_output, "expand_output"))
    adapter_out = pl.pallas_call(
        functools.partial(collect_kernel, owners, heads),
        out_shape=shape((STEPS, rows, width), BF16),
        in_specs=[SMEM, VMEM],
        out_specs=VMEM,
        compiler_params=small,
        name="collect",
    )(place_of, returned)
    return (attn_out, adapter_out)


def solution(mesh):
    in_specs = (
        P(None, ("parts", "store"), "tensor"),
        P(None, ("parts", "store"), "tensor"),
        P(None, ("parts", "store"), "tensor"),
        P(None, ("parts", "store"), "tensor"),
        P(("parts", "store"), None, "tensor"),
        P(("parts", "store"), None, "tensor"),
        P(("parts", "store")),
        P(("parts", "store")),
        P("parts"),
        P(None, "store", None),
        P("store", None, "tensor"),
        P(None, "store", None),
        P("store", None, "tensor"),
    )
    out_specs = (P(None, ("parts", "store"), "tensor"), P(None, ("parts", "store"), "tensor"))
    return jax.shard_map(shards, mesh=mesh, in_specs=in_specs, out_specs=out_specs, check_vma=False)
```

```python
import functools
import math

import jax
import jax.numpy as jnp
from jax import lax
from jax.experimental import pallas as pl
from jax.experimental.pallas import tpu as pltpu
from jax.sharding import PartitionSpec as P

HD = 128
CAP = 2
STEPS = 2
CHUNK = 128
QUAD = 4
BF16 = jnp.bfloat16
F32 = jnp.float32
I32 = jnp.int32
VMEM = pl.BlockSpec(memory_space=pltpu.VMEM)
SMEM = pl.BlockSpec(memory_space=pltpu.SMEM)
HBM = pl.BlockSpec(memory_space=pltpu.HBM)


def iota(shape, dim):
    return lax.broadcasted_iota(I32, shape, dim)


def over(x, n):
    return lax.shift_right_logical(x, jnp.full_like(x, n.bit_length() - 1)) if n & (n - 1) == 0 else x // n


def rest(x, n):
    return x & (n - 1) if n & (n - 1) == 0 else x % n


def one_hot(hits):
    return jnp.where(hits, 1.0, 0.0).astype(BF16)


def stacked(ref, heads, wide):
    return jnp.concatenate(
        [ref[s, :, c * wide : (c + 1) * wide] for c in range(heads) for s in range(STEPS)], axis=0
    )


def pack_matrix(meta, owners, heads, rows, by_row):
    items = CAP * STEPS
    block = heads * items
    shape = (block, heads * STEPS * rows)
    at = iota(shape, 0)
    col = iota(shape, 1)
    head_step = over(at, items) * STEPS + rest(at, STEPS)
    offset = col - (head_step if by_row else head_step * rows)
    factor = heads * STEPS if by_row else 1
    first = rest(over(at, STEPS), CAP) == 0
    if not by_row:
        offset = jnp.where((offset >= 0) & (offset < rows), offset, -1)
    parts = []
    for i in range(owners):
        here = [meta[rows + i * CAP + k] for k in range(CAP)]
        spots = [jnp.where(h >= 0, h * factor, -rows * factor * heads * STEPS * 2) for h in here]
        parts.append(one_hot(offset == jnp.where(first, spots[0], spots[1])))
    return jnp.concatenate(parts, axis=0)


def unpack_matrix(meta, owners, heads, rows, by_row):
    items = CAP * STEPS
    block = heads * items
    pairs = heads * STEPS
    spots = [over(meta[r], CAP) * block + rest(meta[r], CAP) * STEPS for r in range(rows)]
    if by_row:
        shape = (pairs, owners * block)
        at = iota(shape, 0)
        col = iota(shape, 1) - (over(at, STEPS) * items + rest(at, STEPS))
        return jnp.concatenate([one_hot(col == spots[r]) for r in range(rows)], axis=0)
    shape = (rows, owners * block)
    at = iota(shape, 0)
    col = iota(shape, 1)
    spot = jnp.zeros(shape, I32)
    for r in range(rows):
        spot = jnp.where(at == r, spots[r], spot)
    offset = col - spot
    return jnp.concatenate(
        [one_hot(offset == c * items + s) for c in range(heads) for s in range(STEPS)], axis=0
    )


def by_row_matrix(heads, rows):
    pairs = heads * STEPS
    shape = (pairs * rows, pairs * rows)
    at = iota(shape, 0)
    return one_hot(iota(shape, 1) == rest(at, pairs) * rows + over(at, pairs))


def by_pair_matrix(heads, rows):
    pairs = heads * STEPS
    shape = (pairs * rows, pairs * rows)
    at = iota(shape, 0)
    return one_hot(iota(shape, 1) == rest(at, rows) * pairs + over(at, rows))


def regroup_matrix(owners, heads):
    items = CAP * STEPS
    total = owners * heads * items
    at = iota((total, total), 0)
    head = over(at, owners * items)
    owner = rest(over(at, items), owners)
    return one_hot(
        iota((total, total), 1) == owner * (heads * items) + head * items + rest(at, items)
    )


def ungroup_matrix(owners, heads):
    items = CAP * STEPS
    total = owners * heads * items
    at = iota((total, total), 0)
    owner = over(at, heads * items)
    head = rest(over(at, items), heads)
    return one_hot(
        iota((total, total), 1) == head * (owners * items) + owner * items + rest(at, items)
    )


def exact(matrix, values):
    return jnp.dot(matrix, values, preferred_element_type=F32).astype(BF16)


def dispatch_kernel(
    owners,
    heads,
    adapt,
    rank,
    ids_hbm,
    slot_of_hbm,
    lengths_hbm,
    x_hbm,
    meta,
    blocks,
    slot_at,
    ids,
    slot_of,
    lengths,
    x_ref,
    sems,
):
    pairs = ((ids_hbm, ids), (slot_of_hbm, slot_of), (lengths_hbm, lengths), (x_hbm, x_ref))
    copies = [pltpu.make_async_copy(a, b, sems.at[k]) for k, (a, b) in enumerate(pairs)]
    for copy in copies:
        copy.start()
    rows = x_ref.shape[1]
    wide = x_ref.shape[2] // heads
    for copy in copies[:3]:
        copy.wait()
    row_at = rows
    order = rows + owners * CAP
    spans = order + rows
    for p in range(owners * CAP):
        meta[row_at + p] = -1
        slot_at[p] = -1
    for r in range(rows):
        slot = slot_of[ids[r]]
        first = over(slot, adapt) * CAP
        place = first + jnp.where(meta[row_at + first] >= 0, 1, 0)
        meta[row_at + place] = r
        slot_at[place] = rest(slot, adapt)
        meta[r] = place
    sizes = [lengths[r] for r in range(rows)]
    for r in range(rows):
        ahead = jnp.int32(0)
        for q in range(rows):
            if q != r:
                shorter = sizes[q] <= sizes[r] if q < r else sizes[q] < sizes[r]
                ahead = ahead + jnp.where(shorter, 1, 0)
        meta[order + ahead] = r
        meta[spans + r] = sizes[r]
    items = CAP * STEPS
    block = heads * items
    copies[3].wait()
    packed = exact(pack_matrix(meta, owners, heads, rows, False), stacked(x_ref, heads, wide))
    at = iota((block, adapt * rank), 0)
    lane_slot = over(iota((block, adapt * rank), 1), rank)
    first = rest(over(at, STEPS), CAP) == 0
    for i in range(owners):
        blocks[i, :, :wide] = packed[i * block : (i + 1) * block]
        slot = jnp.where(first, slot_at[i * CAP], slot_at[i * CAP + 1])
        blocks[i, :, wide:] = one_hot(lane_slot == slot)


def project_kernel(owners, heads, wide, first, a_ref, blocks, *refs):
    core = lax.axis_index("tensor")
    if first:
        part_ref, mask_ref = refs
    else:
        mask_in, part_ref = refs
    grouped = regroup_matrix(owners, heads)
    items = owners * CAP * STEPS
    arrived = jnp.concatenate([blocks[i, :, :wide] for i in range(owners)], axis=0)
    arrived = exact(grouped, arrived)
    if first:
        masks = jnp.concatenate([blocks[i, :, wide:] for i in range(owners)], axis=0)
        mask = jnp.dot(grouped[:items], masks, preferred_element_type=F32)
        mask_ref[...] = mask
    else:
        mask = mask_in[...]
    total = jnp.zeros(mask.shape, F32)
    for c in range(heads):
        total = total + lax.dot_general(
            arrived[c * items : (c + 1) * items],
            a_ref[:, pl.ds(pl.multiple_of(core * (heads * wide) + c * wide, wide), wide)],
            (((1,), (1,)), ((), ())),
            preferred_element_type=F32,
        )
    part_ref[...] = total * mask


def expand_kernel(owners, heads, wide, mine, other, b_ref, blocks):
    low_rank = (mine[...] + other[...]).astype(BF16)
    pieces = []
    for c in range(heads):
        product = jnp.dot(
            low_rank, b_ref[:, c * wide : (c + 1) * wide], preferred_element_type=F32
        )
        pieces.append((2.0 * product).astype(BF16))
    back = exact(ungroup_matrix(owners, heads), jnp.concatenate(pieces, axis=0))
    block = heads * CAP * STEPS
    for i in range(owners):
        blocks[i] = back[i * block : (i + 1) * block]


def quads(row_of, span_of, rows, sizes, action):
    def body(quad, carry):
        amount = over(span_of(row_of(quad * QUAD + QUAD - 1)) + (CHUNK - 1), CHUNK)
        for size in range(1, sizes + 1):

            @pl.when(amount == size)
            def _():
                action([row_of(quad * QUAD + j) for j in range(QUAD)], size)

        return carry

    lax.fori_loop(0, rows // QUAD, body, 0)


def attend_kernel(
    owners,
    heads,
    meta,
    q_hbm,
    kn_hbm,
    vn_hbm,
    k_hbm,
    v_hbm,
    blocks,
    out_ref,
    outgoing,
    q_ref,
    kn_ref,
    vn_ref,
    k_ref,
    v_ref,
    mask_ref,
    q_buf,
    o_buf,
    k_sem,
    v_sem,
    sems,
):
    rows = q_hbm.shape[1]
    wide = q_hbm.shape[2] // heads
    groups = wide // HD
    pairs = heads * STEPS
    total = groups * pairs
    width = heads * HD
    fresh_rows = STEPS * rows

    singles = [pltpu.make_async_copy(q_hbm, q_ref, sems.at[0])]
    for k, (source, target) in enumerate(((kn_hbm, kn_ref), (vn_hbm, vn_ref))):
        for t in range(STEPS):
            part = target.at[pl.ds(t * rows, rows)]
            singles.append(pltpu.make_async_copy(source.at[t], part, sems.at[1 + k * STEPS + t]))
    for copy in singles:
        copy.start()

    def row_of(place):
        return meta[rows + owners * CAP + place]

    def span_of(row):
        return meta[2 * rows + owners * CAP + row]

    def copies(row, size):
        part = pl.ds(0, size * CHUNK)
        return (
            pltpu.make_async_copy(k_hbm.at[row, part], k_ref.at[row, part], k_sem.at[row]),
            pltpu.make_async_copy(v_hbm.at[row, part], v_ref.at[row, part], v_sem.at[row]),
        )

    def begin(rows_in, size):
        for row in rows_in:
            for copy in copies(row, size):
                copy.start()

    chunks = k_hbm.shape[1] // CHUNK
    quads(row_of, span_of, rows, chunks, begin)

    head_at = rest(over(iota((total, width), 0), STEPS), heads)
    mask_ref[...] = one_hot(head_at == over(iota((total, width), 1), HD))
    head_own = rest(over(iota((total, HD), 0), STEPS), heads)
    blank = jnp.zeros((CHUNK - fresh_rows, width), BF16)
    kn_ref[fresh_rows:, :] = blank
    vn_ref[fresh_rows:, :] = blank

    delta = jnp.dot(
        unpack_matrix(meta, owners, heads, rows, True),
        jnp.concatenate([blocks[i] for i in range(owners)], axis=0),
        preferred_element_type=F32,
    )
    by_row = by_row_matrix(heads, rows)
    for copy in singles:
        copy.wait()
    base = jnp.dot(by_row, stacked(q_ref, heads, wide), preferred_element_type=F32)
    q_buf[...] = base + delta

    factor = math.log2(math.e) / math.sqrt(HD)
    fresh_shape = (total, CHUNK)
    fresh_at = iota(fresh_shape, 1)
    fresh_step = over(fresh_at, rows)
    fresh_row = jnp.where(fresh_step <= rest(iota(fresh_shape, 0), STEPS), rest(fresh_at, rows), rows)
    contract = (((1,), (1,)), ((), ()))

    def attend(rows_in, size):
        for row in rows_in:
            for copy in copies(row, size):
                copy.wait()
        extent = size * CHUNK
        position = iota((total, extent), 1)
        results = []
        for row in rows_in:
            start = pl.multiple_of(row * pairs, pairs)
            flat = q_buf[pl.ds(start, pairs), :]
            one = jnp.concatenate(
                [flat[:, j * HD : (j + 1) * HD] for j in range(groups)], axis=0
            ).astype(BF16)
            spread = jnp.concatenate([one] * heads, axis=1) * mask_ref[...]
            cached = lax.dot_general(
                spread, k_ref[row, :extent, :], contract, preferred_element_type=F32
            )
            cached = jnp.where(position < span_of(row), cached, -jnp.inf)
            fresh = lax.dot_general(spread, kn_ref[...], contract, preferred_element_type=F32)
            fresh = jnp.where(fresh_row == row, fresh, -jnp.inf)
            scores = jnp.concatenate([cached, fresh], axis=1)
            top = jnp.max(scores, axis=1, keepdims=True)
            weights = jnp.exp2((scores - top) * factor)
            norm = jnp.sum(weights, axis=1, keepdims=True)
            weights = weights.astype(BF16)
            mixed = jnp.dot(
                weights[:, :extent], v_ref[row, :extent, :], preferred_element_type=F32
            ) + jnp.dot(weights[:, extent:], vn_ref[...], preferred_element_type=F32)
            own = mixed[:, :HD]
            for c in range(1, heads):
                own = jnp.where(head_own == c, mixed[:, c * HD : (c + 1) * HD], own)
            results.append((start, own * (1.0 / norm)))
        for start, own in results:
            o_buf[pl.ds(start, pairs), :] = jnp.concatenate(
                [own[j * pairs : (j + 1) * pairs] for j in range(groups)], axis=1
            )

    quads(row_of, span_of, rows, chunks, attend)

    mixed = o_buf[...].astype(BF16)
    packed = exact(pack_matrix(meta, owners, heads, rows, True), mixed)
    block = heads * CAP * STEPS
    for i in range(owners):
        outgoing[i] = packed[i * block : (i + 1) * block]
    final = exact(by_pair_matrix(heads, rows), mixed)
    for c in range(heads):
        for s in range(STEPS):
            at = (c * STEPS + s) * rows
            out_ref[s, :, c * wide : (c + 1) * wide] = final[at : at + rows]


def collect_kernel(owners, heads, meta, blocks, out_ref):
    rows = out_ref.shape[1]
    wide = out_ref.shape[2] // heads
    arrived = jnp.concatenate([blocks[i] for i in range(owners)], axis=0)
    values = exact(unpack_matrix(meta, owners, heads, rows, False), arrived)
    for c in range(heads):
        for s in range(STEPS):
            top = (c * STEPS + s) * rows
            out_ref[s, :, c * wide : (c + 1) * wide] = values[top : top + rows]


def exchange(blocks):
    return lax.all_to_all(blocks, "store", split_axis=0, concat_axis=0, tiled=True)


def in_hbm(array):
    return pltpu.with_memory_space_constraint(array, pltpu.HBM)


def swap_cores(part):
    return lax.ppermute(part, "tensor", [(0, 1), (1, 0)])


def shards(
    x_in,
    q_base,
    k_new,
    v_new,
    cache_k,
    cache_v,
    lengths,
    adapter_ids,
    slot_of,
    a_query,
    b_query,
    a_output,
    b_output,
):
    owners = lax.axis_size("store")
    rows = x_in.shape[1]
    width = x_in.shape[2]
    heads = cache_k.shape[2] // HD
    wide = width // heads
    adapt, rank = a_query.shape[1:]
    lanes = adapt * rank
    block = heads * CAP * STEPS
    items = owners * CAP * STEPS
    def flat(a_store):
        return jnp.transpose(a_store, (1, 2, 0)).reshape(lanes, a_store.shape[0])

    shape = jax.ShapeDtypeStruct
    small = pltpu.CompilerParams(vmem_limit_bytes=16 * 1024 * 1024)

    sent = shape((owners, block, wide), BF16)
    meta, blocks = pl.pallas_call(
        functools.partial(dispatch_kernel, owners, heads, adapt, rank),
        out_shape=[
            shape((3 * rows + owners * CAP,), I32),
            shape((owners, block, wide + lanes), BF16),
        ],
        in_specs=[HBM] * 4,
        out_specs=[SMEM, VMEM],
        scratch_shapes=[
            pltpu.SMEM((owners * CAP,), I32),
            pltpu.SMEM(adapter_ids.shape, I32),
            pltpu.SMEM(slot_of.shape, I32),
            pltpu.SMEM(lengths.shape, I32),
            pltpu.VMEM(x_in.shape, BF16),
            pltpu.SemaphoreType.DMA((4,)),
        ],
        compiler_params=small,
        name="dispatch",
    )(in_hbm(adapter_ids), in_hbm(slot_of), in_hbm(lengths), in_hbm(x_in))

    arrived = exchange(blocks)
    part, mask = pl.pallas_call(
        functools.partial(project_kernel, owners, heads, wide, True),
        out_shape=[shape((items, lanes), F32)] * 2,
        in_specs=[VMEM] * 2,
        out_specs=[VMEM] * 2,
        compiler_params=small,
        name="project_query",
    )(flat(a_query), arrived)

    def expand(part, b_store, name):
        return pl.pallas_call(
            functools.partial(expand_kernel, owners, heads, wide),
            out_shape=sent,
            in_specs=[VMEM] * 3,
            out_specs=VMEM,
            compiler_params=small,
            name=name,
        )(part, swap_cores(part), b_store.reshape(lanes, width))

    returned = exchange(expand(part, b_query, "expand_query"))

    attn_out, outgoing = pl.pallas_call(
        functools.partial(attend_kernel, owners, heads),
        out_shape=[pltpu.VMEM((STEPS, rows, width), BF16), sent],
        in_specs=[SMEM] + [HBM] * 5 + [VMEM],
        out_specs=[VMEM] * 2,
        scratch_shapes=[
            pltpu.VMEM(q_base.shape, BF16),
            pltpu.VMEM((CHUNK, heads * HD), BF16),
            pltpu.VMEM((CHUNK, heads * HD), BF16),
            pltpu.VMEM(cache_k.shape, BF16),
            pltpu.VMEM(cache_v.shape, BF16),
            pltpu.VMEM((STEPS * wide // HD * heads, heads * HD), BF16),
            pltpu.VMEM((rows * STEPS * heads, wide), F32),
            pltpu.VMEM((rows * STEPS * heads, wide), F32),
            pltpu.SemaphoreType.DMA((rows,)),
            pltpu.SemaphoreType.DMA((rows,)),
            pltpu.SemaphoreType.DMA((1 + 2 * STEPS,)),
        ],
        compiler_params=pltpu.CompilerParams(vmem_limit_bytes=32 * 1024 * 1024),
        name="attend",
    )(meta, *map(in_hbm, (q_base, k_new, v_new, cache_k, cache_v)), returned)

    arrived = exchange(outgoing)
    part = pl.pallas_call(
        functools.partial(project_kernel, owners, heads, wide, False),
        out_shape=shape((items, lanes), F32),
        in_specs=[VMEM] * 3,
        out_specs=VMEM,
        compiler_params=small,
        name="project_output",
    )(flat(a_output), arrived, mask)
    returned = exchange(expand(part, b_output, "expand_output"))
    adapter_out = pl.pallas_call(
        functools.partial(collect_kernel, owners, heads),
        out_shape=shape((STEPS, rows, width), BF16),
        in_specs=[SMEM, VMEM],
        out_specs=VMEM,
        compiler_params=small,
        name="collect",
    )(meta, returned)
    return (attn_out, adapter_out)


def solution(mesh):
    in_specs = (
        P(None, ("parts", "store"), "tensor"),
        P(None, ("parts", "store"), "tensor"),
        P(None, ("parts", "store"), "tensor"),
        P(None, ("parts", "store"), "tensor"),
        P(("parts", "store"), None, "tensor"),
        P(("parts", "store"), None, "tensor"),
        P(("parts", "store")),
        P(("parts", "store")),
        P("parts"),
        P(None, "store", None),
        P("store", None, "tensor"),
        P(None, "store", None),
        P("store", None, "tensor"),
    )
    out_specs = (P(None, ("parts", "store"), "tensor"), P(None, ("parts", "store"), "tensor"))
    return jax.shard_map(shards, mesh=mesh, in_specs=in_specs, out_specs=out_specs, check_vma=False)
```

```python
import functools
import math

import jax
import jax.numpy as jnp
from jax import lax
from jax.experimental import pallas as pl
from jax.experimental.pallas import tpu as pltpu
from jax.sharding import PartitionSpec as P

HD = 128
CAP = 2
STEPS = 2
CHUNK = 128
QUAD = 4
BF16 = jnp.bfloat16
F32 = jnp.float32
I32 = jnp.int32
VMEM = pl.BlockSpec(memory_space=pltpu.VMEM)
SMEM = pl.BlockSpec(memory_space=pltpu.SMEM)
HBM = pl.BlockSpec(memory_space=pltpu.HBM)


def iota(shape, dim):
    return lax.broadcasted_iota(I32, shape, dim)


def over(x, n):
    return lax.shift_right_logical(x, jnp.full_like(x, n.bit_length() - 1)) if n & (n - 1) == 0 else x // n


def rest(x, n):
    return x & (n - 1) if n & (n - 1) == 0 else x % n


def one_hot(hits):
    return jnp.where(hits, 1.0, 0.0).astype(BF16)


def stacked(ref, heads, wide):
    return jnp.concatenate(
        [ref[s, :, c * wide : (c + 1) * wide] for c in range(heads) for s in range(STEPS)], axis=0
    )


def pack_matrix(meta, owners, heads, rows, by_row):
    items = CAP * STEPS
    block = heads * items
    shape = (block, heads * STEPS * rows)
    at = iota(shape, 0)
    col = iota(shape, 1)
    head_step = over(at, items) * STEPS + rest(at, STEPS)
    offset = col - (head_step if by_row else head_step * rows)
    factor = heads * STEPS if by_row else 1
    first = rest(over(at, STEPS), CAP) == 0
    if not by_row:
        offset = jnp.where((offset >= 0) & (offset < rows), offset, -1)
    parts = []
    for i in range(owners):
        here = [meta[rows + i * CAP + k] for k in range(CAP)]
        spots = [jnp.where(h >= 0, h * factor, -rows * factor * heads * STEPS * 2) for h in here]
        parts.append(one_hot(offset == jnp.where(first, spots[0], spots[1])))
    return jnp.concatenate(parts, axis=0)


def unpack_matrix(meta, owners, heads, rows, by_row):
    items = CAP * STEPS
    block = heads * items
    pairs = heads * STEPS
    spots = [over(meta[r], CAP) * block + rest(meta[r], CAP) * STEPS for r in range(rows)]
    if by_row:
        shape = (pairs, owners * block)
        at = iota(shape, 0)
        col = iota(shape, 1) - (over(at, STEPS) * items + rest(at, STEPS))
        return jnp.concatenate([one_hot(col == spots[r]) for r in range(rows)], axis=0)
    shape = (rows, owners * block)
    at = iota(shape, 0)
    col = iota(shape, 1)
    spot = jnp.zeros(shape, I32)
    for r in range(rows):
        spot = jnp.where(at == r, spots[r], spot)
    offset = col - spot
    return jnp.concatenate(
        [one_hot(offset == c * items + s) for c in range(heads) for s in range(STEPS)], axis=0
    )


def by_row_matrix(heads, rows):
    pairs = heads * STEPS
    shape = (pairs * rows, pairs * rows)
    at = iota(shape, 0)
    return one_hot(iota(shape, 1) == rest(at, pairs) * rows + over(at, pairs))


def by_pair_matrix(heads, rows):
    pairs = heads * STEPS
    shape = (pairs * rows, pairs * rows)
    at = iota(shape, 0)
    return one_hot(iota(shape, 1) == rest(at, rows) * pairs + over(at, rows))


def regroup_matrix(owners, heads):
    items = CAP * STEPS
    total = owners * heads * items
    at = iota((total, total), 0)
    head = over(at, owners * items)
    owner = rest(over(at, items), owners)
    return one_hot(
        iota((total, total), 1) == owner * (heads * items) + head * items + rest(at, items)
    )


def ungroup_matrix(owners, heads):
    items = CAP * STEPS
    total = owners * heads * items
    at = iota((total, total), 0)
    owner = over(at, heads * items)
    head = rest(over(at, items), heads)
    return one_hot(
        iota((total, total), 1) == head * (owners * items) + owner * items + rest(at, items)
    )


def in_order(arrived, crossed):
    return [b for a, c in zip(arrived, crossed) for b in (a[0], c[...])]


def exact(matrix, values):
    return jnp.dot(matrix, values, preferred_element_type=F32).astype(BF16)


def dispatch_kernel(
    owners,
    heads,
    adapt,
    rank,
    ids_hbm,
    slot_of_hbm,
    lengths_hbm,
    x_hbm,
    meta,
    *refs,
):
    outgoing = refs[: owners // 2]
    slot_at, ids, slot_of, lengths, x_ref, sems = refs[owners // 2 :]
    pairs = ((ids_hbm, ids), (slot_of_hbm, slot_of), (lengths_hbm, lengths), (x_hbm, x_ref))
    copies = [pltpu.make_async_copy(a, b, sems.at[k]) for k, (a, b) in enumerate(pairs)]
    for copy in copies:
        copy.start()
    rows = x_ref.shape[1]
    wide = x_ref.shape[2] // heads
    for copy in copies[:3]:
        copy.wait()
    me = lax.axis_index("store")
    row_at = rows
    order = rows + owners * CAP
    spans = order + rows
    for p in range(owners * CAP):
        meta[row_at + p] = -1
        slot_at[p] = -1
    for r in range(rows):
        slot = slot_of[ids[r]]
        first = (over(slot, adapt) ^ me) * CAP
        place = first + jnp.where(meta[row_at + first] >= 0, 1, 0)
        meta[row_at + place] = r
        slot_at[place] = rest(slot, adapt)
        meta[r] = place
    sizes = [lengths[r] for r in range(rows)]
    for r in range(rows):
        ahead = jnp.int32(0)
        for q in range(rows):
            if q != r:
                shorter = sizes[q] <= sizes[r] if q < r else sizes[q] < sizes[r]
                ahead = ahead + jnp.where(shorter, 1, 0)
        meta[order + ahead] = r
        meta[spans + r] = sizes[r]
    items = CAP * STEPS
    block = heads * items
    copies[3].wait()
    packed = exact(pack_matrix(meta, owners, heads, rows, False), stacked(x_ref, heads, wide))
    at = iota((block, adapt * rank), 0)
    lane_slot = over(iota((block, adapt * rank), 1), rank)
    first = rest(over(at, STEPS), CAP) == 0
    for i in range(owners):
        outgoing[i // 2][i % 2, :, :wide] = packed[i * block : (i + 1) * block]
        slot = jnp.where(first, slot_at[i * CAP], slot_at[i * CAP + 1])
        outgoing[i // 2][i % 2, :, wide:] = one_hot(lane_slot == slot)


def project_kernel(owners, heads, wide, first, a_ref, *refs):
    blocks = in_order(refs[: owners // 2], refs[owners // 2 : owners])
    refs = refs[owners:]
    core = lax.axis_index("tensor")
    if first:
        part_ref, mask_ref = refs
    else:
        mask_in, part_ref = refs
    grouped = regroup_matrix(owners, heads)
    items = owners * CAP * STEPS
    arrived = jnp.concatenate([b[:, :wide] for b in blocks], axis=0)
    arrived = exact(grouped, arrived)
    if first:
        masks = jnp.concatenate([b[:, wide:] for b in blocks], axis=0)
        mask = jnp.dot(grouped[:items], masks, preferred_element_type=F32)
        mask_ref[...] = mask
    else:
        mask = mask_in[...]
    total = jnp.zeros(mask.shape, F32)
    for c in range(heads):
        total = total + lax.dot_general(
            arrived[c * items : (c + 1) * items],
            a_ref[:, pl.ds(pl.multiple_of(core * (heads * wide) + c * wide, wide), wide)],
            (((1,), (1,)), ((), ())),
            preferred_element_type=F32,
        )
    part_ref[...] = total * mask


def expand_kernel(owners, heads, wide, mine, other, b_ref, *outgoing):
    low_rank = (mine[...] + other[...]).astype(BF16)
    pieces = []
    for c in range(heads):
        product = jnp.dot(
            low_rank, b_ref[:, c * wide : (c + 1) * wide], preferred_element_type=F32
        )
        pieces.append((2.0 * product).astype(BF16))
    back = exact(ungroup_matrix(owners, heads), jnp.concatenate(pieces, axis=0))
    block = heads * CAP * STEPS
    for i in range(owners):
        outgoing[i // 2][i % 2] = back[i * block : (i + 1) * block]


def quads(row_of, span_of, rows, sizes, action):
    def body(quad, carry):
        amount = over(span_of(row_of(quad * QUAD + QUAD - 1)) + (CHUNK - 1), CHUNK)
        for size in range(1, sizes + 1):

            @pl.when(amount == size)
            def _():
                action([row_of(quad * QUAD + j) for j in range(QUAD)], size)

        return carry

    lax.fori_loop(0, rows // QUAD, body, 0)


def attend_kernel(
    owners,
    heads,
    meta,
    q_hbm,
    kn_hbm,
    vn_hbm,
    k_hbm,
    v_hbm,
    *refs,
):
    blocks = in_order(refs[: owners // 2], refs[owners // 2 : owners])
    out_ref = refs[owners]
    outgoing = refs[owners + 1 : owners + 1 + owners // 2]
    q_ref, kn_ref, vn_ref, k_ref, v_ref, mask_ref, q_buf, o_buf, k_sem, v_sem, sems = refs[
        owners + 1 + owners // 2 :
    ]
    rows = q_hbm.shape[1]
    wide = q_hbm.shape[2] // heads
    groups = wide // HD
    pairs = heads * STEPS
    total = groups * pairs
    width = heads * HD
    fresh_rows = STEPS * rows

    singles = [pltpu.make_async_copy(q_hbm, q_ref, sems.at[0])]
    for k, (source, target) in enumerate(((kn_hbm, kn_ref), (vn_hbm, vn_ref))):
        for t in range(STEPS):
            part = target.at[pl.ds(t * rows, rows)]
            singles.append(pltpu.make_async_copy(source.at[t], part, sems.at[1 + k * STEPS + t]))
    for copy in singles:
        copy.start()

    def row_of(place):
        return meta[rows + owners * CAP + place]

    def span_of(row):
        return meta[2 * rows + owners * CAP + row]

    def copies(row, size):
        part = pl.ds(0, size * CHUNK)
        return (
            pltpu.make_async_copy(k_hbm.at[row, part], k_ref.at[row, part], k_sem.at[row]),
            pltpu.make_async_copy(v_hbm.at[row, part], v_ref.at[row, part], v_sem.at[row]),
        )

    def begin(rows_in, size):
        for row in rows_in:
            for copy in copies(row, size):
                copy.start()

    chunks = k_hbm.shape[1] // CHUNK
    quads(row_of, span_of, rows, chunks, begin)

    head_at = rest(over(iota((total, width), 0), STEPS), heads)
    mask_ref[...] = one_hot(head_at == over(iota((total, width), 1), HD))
    head_own = rest(over(iota((total, HD), 0), STEPS), heads)
    blank = jnp.zeros((CHUNK - fresh_rows, width), BF16)
    kn_ref[fresh_rows:, :] = blank
    vn_ref[fresh_rows:, :] = blank

    delta = jnp.dot(
        unpack_matrix(meta, owners, heads, rows, True),
        jnp.concatenate(blocks, axis=0),
        preferred_element_type=F32,
    )
    by_row = by_row_matrix(heads, rows)
    for copy in singles:
        copy.wait()
    base = jnp.dot(by_row, stacked(q_ref, heads, wide), preferred_element_type=F32)
    q_buf[...] = base + delta

    factor = math.log2(math.e) / math.sqrt(HD)
    fresh_shape = (total, CHUNK)
    fresh_at = iota(fresh_shape, 1)
    fresh_step = over(fresh_at, rows)
    fresh_row = jnp.where(fresh_step <= rest(iota(fresh_shape, 0), STEPS), rest(fresh_at, rows), rows)
    contract = (((1,), (1,)), ((), ()))

    def attend(rows_in, size):
        for row in rows_in:
            for copy in copies(row, size):
                copy.wait()
        extent = size * CHUNK
        position = iota((total, extent), 1)
        results = []
        for row in rows_in:
            start = pl.multiple_of(row * pairs, pairs)
            flat = q_buf[pl.ds(start, pairs), :]
            one = jnp.concatenate(
                [flat[:, j * HD : (j + 1) * HD] for j in range(groups)], axis=0
            ).astype(BF16)
            spread = jnp.concatenate([one] * heads, axis=1) * mask_ref[...]
            cached = lax.dot_general(
                spread, k_ref[row, :extent, :], contract, preferred_element_type=F32
            )
            cached = jnp.where(position < span_of(row), cached, -jnp.inf)
            fresh = lax.dot_general(spread, kn_ref[...], contract, preferred_element_type=F32)
            fresh = jnp.where(fresh_row == row, fresh, -jnp.inf)
            scores = jnp.concatenate([cached, fresh], axis=1)
            top = jnp.max(scores, axis=1, keepdims=True)
            weights = jnp.exp2((scores - top) * factor)
            norm = jnp.sum(weights, axis=1, keepdims=True)
            weights = weights.astype(BF16)
            mixed = jnp.dot(
                weights[:, :extent], v_ref[row, :extent, :], preferred_element_type=F32
            ) + jnp.dot(weights[:, extent:], vn_ref[...], preferred_element_type=F32)
            own = mixed[:, :HD]
            for c in range(1, heads):
                own = jnp.where(head_own == c, mixed[:, c * HD : (c + 1) * HD], own)
            results.append((start, own * (1.0 / norm)))
        for start, own in results:
            o_buf[pl.ds(start, pairs), :] = jnp.concatenate(
                [own[j * pairs : (j + 1) * pairs] for j in range(groups)], axis=1
            )

    quads(row_of, span_of, rows, chunks, attend)

    mixed = o_buf[...].astype(BF16)
    packed = exact(pack_matrix(meta, owners, heads, rows, True), mixed)
    block = heads * CAP * STEPS
    for i in range(owners):
        outgoing[i // 2][i % 2] = packed[i * block : (i + 1) * block]
    final = exact(by_pair_matrix(heads, rows), mixed)
    for c in range(heads):
        for s in range(STEPS):
            at = (c * STEPS + s) * rows
            out_ref[s, :, c * wide : (c + 1) * wide] = final[at : at + rows]


def collect_kernel(owners, heads, meta, *refs):
    blocks = in_order(refs[: owners // 2], refs[owners // 2 : owners])
    out_ref = refs[owners]
    rows = out_ref.shape[1]
    wide = out_ref.shape[2] // heads
    arrived = jnp.concatenate(blocks, axis=0)
    values = exact(unpack_matrix(meta, owners, heads, rows, False), arrived)
    for c in range(heads):
        for s in range(STEPS):
            top = (c * STEPS + s) * rows
            out_ref[s, :, c * wide : (c + 1) * wide] = values[top : top + rows]


def exchange(pairs):
    owners = 2 * len(pairs)
    arrived = [pairs[0]] + [
        lax.ppermute(pair, "store", [(s, s ^ (2 * k)) for s in range(owners)])
        for k, pair in enumerate(pairs)
        if k > 0
    ]
    crossed = [lax.ppermute(pair[1], "store", [(s, s ^ 1) for s in range(owners)]) for pair in arrived]
    return arrived + crossed


def in_hbm(array):
    return pltpu.with_memory_space_constraint(array, pltpu.HBM)


def swap_cores(part):
    return lax.ppermute(part, "tensor", [(0, 1), (1, 0)])


def shards(
    x_in,
    q_base,
    k_new,
    v_new,
    cache_k,
    cache_v,
    lengths,
    adapter_ids,
    slot_of,
    a_query,
    b_query,
    a_output,
    b_output,
):
    owners = lax.axis_size("store")
    rows = x_in.shape[1]
    width = x_in.shape[2]
    heads = cache_k.shape[2] // HD
    wide = width // heads
    adapt, rank = a_query.shape[1:]
    lanes = adapt * rank
    block = heads * CAP * STEPS
    items = owners * CAP * STEPS
    def flat(a_store):
        return jnp.transpose(a_store, (1, 2, 0)).reshape(lanes, a_store.shape[0])

    shape = jax.ShapeDtypeStruct
    small = pltpu.CompilerParams(vmem_limit_bytes=16 * 1024 * 1024)

    sent = [shape((2, block, wide), BF16)] * (owners // 2)
    meta, *blocks = pl.pallas_call(
        functools.partial(dispatch_kernel, owners, heads, adapt, rank),
        out_shape=[
            shape((3 * rows + owners * CAP,), I32),
        ]
        + [shape((2, block, wide + lanes), BF16)] * (owners // 2),
        in_specs=[HBM] * 4,
        out_specs=[SMEM] + [VMEM] * (owners // 2),
        scratch_shapes=[
            pltpu.SMEM((owners * CAP,), I32),
            pltpu.SMEM(adapter_ids.shape, I32),
            pltpu.SMEM(slot_of.shape, I32),
            pltpu.SMEM(lengths.shape, I32),
            pltpu.VMEM(x_in.shape, BF16),
            pltpu.SemaphoreType.DMA((4,)),
        ],
        compiler_params=small,
        name="dispatch",
    )(in_hbm(adapter_ids), in_hbm(slot_of), in_hbm(lengths), in_hbm(x_in))

    arrived = exchange(blocks)
    part, mask = pl.pallas_call(
        functools.partial(project_kernel, owners, heads, wide, True),
        out_shape=[shape((items, lanes), F32)] * 2,
        in_specs=[VMEM] * (owners + 1),
        out_specs=[VMEM] * 2,
        compiler_params=small,
        name="project_query",
    )(flat(a_query), *arrived)

    def expand(part, b_store, name):
        return pl.pallas_call(
            functools.partial(expand_kernel, owners, heads, wide),
            out_shape=sent,
            in_specs=[VMEM] * 3,
            out_specs=[VMEM] * (owners // 2),
            compiler_params=small,
            name=name,
        )(part, swap_cores(part), b_store.reshape(lanes, width))

    returned = exchange(expand(part, b_query, "expand_query"))

    attn_out, *outgoing = pl.pallas_call(
        functools.partial(attend_kernel, owners, heads),
        out_shape=[shape((STEPS, rows, width), BF16)] + sent,
        in_specs=[SMEM] + [HBM] * 5 + [VMEM] * owners,
        out_specs=[VMEM] * (1 + owners // 2),
        scratch_shapes=[
            pltpu.VMEM(q_base.shape, BF16),
            pltpu.VMEM((CHUNK, heads * HD), BF16),
            pltpu.VMEM((CHUNK, heads * HD), BF16),
            pltpu.VMEM(cache_k.shape, BF16),
            pltpu.VMEM(cache_v.shape, BF16),
            pltpu.VMEM((STEPS * wide // HD * heads, heads * HD), BF16),
            pltpu.VMEM((rows * STEPS * heads, wide), F32),
            pltpu.VMEM((rows * STEPS * heads, wide), F32),
            pltpu.SemaphoreType.DMA((rows,)),
            pltpu.SemaphoreType.DMA((rows,)),
            pltpu.SemaphoreType.DMA((1 + 2 * STEPS,)),
        ],
        compiler_params=pltpu.CompilerParams(vmem_limit_bytes=32 * 1024 * 1024),
        name="attend",
    )(meta, *map(in_hbm, (q_base, k_new, v_new, cache_k, cache_v)), *returned)

    arrived = exchange(outgoing)
    part = pl.pallas_call(
        functools.partial(project_kernel, owners, heads, wide, False),
        out_shape=shape((items, lanes), F32),
        in_specs=[VMEM] * (owners + 2),
        out_specs=VMEM,
        compiler_params=small,
        name="project_output",
    )(flat(a_output), *arrived, mask)
    returned = exchange(expand(part, b_output, "expand_output"))
    adapter_out = pl.pallas_call(
        functools.partial(collect_kernel, owners, heads),
        out_shape=shape((STEPS, rows, width), BF16),
        in_specs=[SMEM] + [VMEM] * owners,
        out_specs=VMEM,
        compiler_params=small,
        name="collect",
    )(meta, *returned)
    return (attn_out, adapter_out)


def solution(mesh):
    in_specs = (
        P(None, ("parts", "store"), "tensor"),
        P(None, ("parts", "store"), "tensor"),
        P(None, ("parts", "store"), "tensor"),
        P(None, ("parts", "store"), "tensor"),
        P(("parts", "store"), None, "tensor"),
        P(("parts", "store"), None, "tensor"),
        P(("parts", "store")),
        P(("parts", "store")),
        P("parts"),
        P(None, "store", None),
        P("store", None, "tensor"),
        P(None, "store", None),
        P("store", None, "tensor"),
    )
    out_specs = (P(None, ("parts", "store"), "tensor"), P(None, ("parts", "store"), "tensor"))
    return jax.shard_map(shards, mesh=mesh, in_specs=in_specs, out_specs=out_specs, check_vma=False)
```

```python
import functools
import math

import jax
import jax.numpy as jnp
from jax import lax
from jax.experimental import pallas as pl
from jax.experimental.pallas import tpu as pltpu
from jax.sharding import PartitionSpec as P

HD = 128
CAP = 2
STEPS = 2
CHUNK = 128
QUAD = 4
BF16 = jnp.bfloat16
F32 = jnp.float32
I32 = jnp.int32
VMEM = pl.BlockSpec(memory_space=pltpu.VMEM)
SMEM = pl.BlockSpec(memory_space=pltpu.SMEM)
HBM = pl.BlockSpec(memory_space=pltpu.HBM)


def iota(shape, dim):
    return lax.broadcasted_iota(I32, shape, dim)


def over(x, n):
    return lax.shift_right_logical(x, jnp.full_like(x, n.bit_length() - 1)) if n & (n - 1) == 0 else x // n


def rest(x, n):
    return x & (n - 1) if n & (n - 1) == 0 else x % n


def one_hot(hits):
    return jnp.where(hits, 1.0, 0.0).astype(BF16)


def stacked(ref, heads, wide):
    return jnp.concatenate(
        [ref[s, :, c * wide : (c + 1) * wide] for c in range(heads) for s in range(STEPS)], axis=0
    )


def pack_matrix(meta, owners, heads, rows, by_row):
    items = CAP * STEPS
    block = heads * items
    shape = (block, heads * STEPS * rows)
    at = iota(shape, 0)
    col = iota(shape, 1)
    head_step = over(at, items) * STEPS + rest(at, STEPS)
    offset = col - (head_step if by_row else head_step * rows)
    factor = heads * STEPS if by_row else 1
    first = rest(over(at, STEPS), CAP) == 0
    if not by_row:
        offset = jnp.where((offset >= 0) & (offset < rows), offset, -1)
    parts = []
    for i in range(owners):
        here = [meta[rows + i * CAP + k] for k in range(CAP)]
        spots = [jnp.where(h >= 0, h * factor, -rows * factor * heads * STEPS * 2) for h in here]
        parts.append(one_hot(offset == jnp.where(first, spots[0], spots[1])))
    return jnp.concatenate(parts, axis=0)


def unpack_matrix(meta, owners, heads, rows, by_row):
    items = CAP * STEPS
    block = heads * items
    pairs = heads * STEPS
    spots = [over(meta[r], CAP) * block + rest(meta[r], CAP) * STEPS for r in range(rows)]
    if by_row:
        shape = (pairs, owners * block)
        at = iota(shape, 0)
        col = iota(shape, 1) - (over(at, STEPS) * items + rest(at, STEPS))
        return jnp.concatenate([one_hot(col == spots[r]) for r in range(rows)], axis=0)
    shape = (rows, owners * block)
    at = iota(shape, 0)
    col = iota(shape, 1)
    spot = jnp.zeros(shape, I32)
    for r in range(rows):
        spot = jnp.where(at == r, spots[r], spot)
    offset = col - spot
    return jnp.concatenate(
        [one_hot(offset == c * items + s) for c in range(heads) for s in range(STEPS)], axis=0
    )


def by_row_matrix(heads, rows):
    pairs = heads * STEPS
    shape = (pairs * rows, pairs * rows)
    at = iota(shape, 0)
    return one_hot(iota(shape, 1) == rest(at, pairs) * rows + over(at, pairs))


def by_pair_matrix(heads, rows):
    pairs = heads * STEPS
    shape = (pairs * rows, pairs * rows)
    at = iota(shape, 0)
    return one_hot(iota(shape, 1) == rest(at, rows) * pairs + over(at, rows))


def regroup_matrix(owners, heads):
    items = CAP * STEPS
    total = owners * heads * items
    at = iota((total, total), 0)
    head = over(at, owners * items)
    owner = rest(over(at, items), owners)
    return one_hot(
        iota((total, total), 1) == owner * (heads * items) + head * items + rest(at, items)
    )


def ungroup_matrix(owners, heads):
    items = CAP * STEPS
    total = owners * heads * items
    at = iota((total, total), 0)
    owner = over(at, heads * items)
    head = rest(over(at, items), heads)
    return one_hot(
        iota((total, total), 1) == head * (owners * items) + owner * items + rest(at, items)
    )


def exact(matrix, values):
    return jnp.dot(matrix, values, preferred_element_type=F32).astype(BF16)


def dispatch_kernel(
    owners,
    heads,
    adapt,
    rank,
    ids_hbm,
    slot_of_hbm,
    lengths_hbm,
    x_hbm,
    a_hbm,
    b_hbm,
    meta,
    blocks,
    a_out,
    b_out,
    slot_at,
    ids,
    slot_of,
    lengths,
    x_ref,
    sems,
):
    width = x_hbm.shape[2]
    start = pl.multiple_of(lax.axis_index("tensor") * width, width)
    pairs = (
        (ids_hbm, ids),
        (slot_of_hbm, slot_of),
        (lengths_hbm, lengths),
        (x_hbm, x_ref),
        (a_hbm.at[:, pl.ds(start, width)], a_out),
        (b_hbm, b_out),
    )
    copies = [pltpu.make_async_copy(a, b, sems.at[k]) for k, (a, b) in enumerate(pairs)]
    for copy in copies:
        copy.start()
    rows = x_ref.shape[1]
    wide = x_ref.shape[2] // heads
    for copy in copies[:3]:
        copy.wait()
    row_at = rows
    order = rows + owners * CAP
    spans = order + rows
    for p in range(owners * CAP):
        meta[row_at + p] = -1
        slot_at[p] = -1
    for r in range(rows):
        slot = slot_of[ids[r]]
        first = over(slot, adapt) * CAP
        place = first + jnp.where(meta[row_at + first] >= 0, 1, 0)
        meta[row_at + place] = r
        slot_at[place] = rest(slot, adapt)
        meta[r] = place
    sizes = [lengths[r] for r in range(rows)]
    for r in range(rows):
        ahead = jnp.int32(0)
        for q in range(rows):
            if q != r:
                shorter = sizes[q] <= sizes[r] if q < r else sizes[q] < sizes[r]
                ahead = ahead + jnp.where(shorter, 1, 0)
        meta[order + ahead] = r
        meta[spans + r] = sizes[r]
    items = CAP * STEPS
    block = heads * items
    copies[3].wait()
    packed = exact(pack_matrix(meta, owners, heads, rows, False), stacked(x_ref, heads, wide))
    at = iota((block, adapt * rank), 0)
    lane_slot = over(iota((block, adapt * rank), 1), rank)
    first = rest(over(at, STEPS), CAP) == 0
    for i in range(owners):
        blocks[i, :, :wide] = packed[i * block : (i + 1) * block]
        slot = jnp.where(first, slot_at[i * CAP], slot_at[i * CAP + 1])
        blocks[i, :, wide:] = one_hot(lane_slot == slot)
    for copy in copies[4:]:
        copy.wait()


def project_kernel(owners, heads, wide, first, a_ref, blocks, *refs):
    core = lax.axis_index("tensor") if a_ref.shape[1] > heads * wide else 0
    if first:
        part_ref, mask_ref = refs
    else:
        mask_in, part_ref = refs
    grouped = regroup_matrix(owners, heads)
    items = owners * CAP * STEPS
    arrived = jnp.concatenate([blocks[i, :, :wide] for i in range(owners)], axis=0)
    arrived = exact(grouped, arrived)
    if first:
        masks = jnp.concatenate([blocks[i, :, wide:] for i in range(owners)], axis=0)
        mask = jnp.dot(grouped[:items], masks, preferred_element_type=F32)
        mask_ref[...] = mask
    else:
        mask = mask_in[...]
    total = jnp.zeros(mask.shape, F32)
    for c in range(heads):
        total = total + lax.dot_general(
            arrived[c * items : (c + 1) * items],
            a_ref[:, pl.ds(pl.multiple_of(core * (heads * wide) + c * wide, wide), wide)],
            (((1,), (1,)), ((), ())),
            preferred_element_type=F32,
        )
    part_ref[...] = total * mask


def expand_kernel(owners, heads, wide, mine, other, b_ref, blocks):
    low_rank = (mine[...] + other[...]).astype(BF16)
    pieces = []
    for c in range(heads):
        product = jnp.dot(
            low_rank, b_ref[:, c * wide : (c + 1) * wide], preferred_element_type=F32
        )
        pieces.append((2.0 * product).astype(BF16))
    back = exact(ungroup_matrix(owners, heads), jnp.concatenate(pieces, axis=0))
    block = heads * CAP * STEPS
    for i in range(owners):
        blocks[i] = back[i * block : (i + 1) * block]


def quads(row_of, span_of, rows, sizes, action):
    def body(quad, carry):
        amount = over(span_of(row_of(quad * QUAD + QUAD - 1)) + (CHUNK - 1), CHUNK)
        for size in range(1, sizes + 1):

            @pl.when(amount == size)
            def _():
                action([row_of(quad * QUAD + j) for j in range(QUAD)], size)

        return carry

    lax.fori_loop(0, rows // QUAD, body, 0)


def attend_kernel(
    owners,
    heads,
    meta,
    q_hbm,
    kn_hbm,
    vn_hbm,
    k_hbm,
    v_hbm,
    blocks,
    out_hbm,
    outgoing,
    q_ref,
    kn_ref,
    vn_ref,
    k_ref,
    v_ref,
    mask_ref,
    q_buf,
    o_buf,
    k_sem,
    v_sem,
    sems,
):
    rows = q_hbm.shape[1]
    wide = q_hbm.shape[2] // heads
    groups = wide // HD
    pairs = heads * STEPS
    total = groups * pairs
    width = heads * HD
    fresh_rows = STEPS * rows

    singles = [pltpu.make_async_copy(q_hbm, q_ref, sems.at[0])]
    for k, (source, target) in enumerate(((kn_hbm, kn_ref), (vn_hbm, vn_ref))):
        for t in range(STEPS):
            part = target.at[pl.ds(t * rows, rows)]
            singles.append(pltpu.make_async_copy(source.at[t], part, sems.at[1 + k * STEPS + t]))
    for copy in singles:
        copy.start()

    def row_of(place):
        return meta[rows + owners * CAP + place]

    def span_of(row):
        return meta[2 * rows + owners * CAP + row]

    def copies(row, size):
        part = pl.ds(0, size * CHUNK)
        return (
            pltpu.make_async_copy(k_hbm.at[row, part], k_ref.at[row, part], k_sem.at[row]),
            pltpu.make_async_copy(v_hbm.at[row, part], v_ref.at[row, part], v_sem.at[row]),
        )

    def begin(rows_in, size):
        for row in rows_in:
            for copy in copies(row, size):
                copy.start()

    chunks = k_hbm.shape[1] // CHUNK
    quads(row_of, span_of, rows, chunks, begin)

    head_at = rest(over(iota((total, width), 0), STEPS), heads)
    mask_ref[...] = one_hot(head_at == over(iota((total, width), 1), HD))
    head_own = rest(over(iota((QUAD * total, HD), 0), STEPS), heads)
    blank = jnp.zeros((CHUNK - fresh_rows, width), BF16)
    kn_ref[fresh_rows:, :] = blank
    vn_ref[fresh_rows:, :] = blank

    delta = jnp.dot(
        unpack_matrix(meta, owners, heads, rows, True),
        jnp.concatenate([blocks[i] for i in range(owners)], axis=0),
        preferred_element_type=F32,
    )
    by_row = by_row_matrix(heads, rows)
    for copy in singles:
        copy.wait()
    base = jnp.dot(by_row, stacked(q_ref, heads, wide), preferred_element_type=F32)
    q_buf[...] = base + delta

    factor = math.log2(math.e) / math.sqrt(HD)
    fresh_shape = (total, CHUNK)
    fresh_at = iota(fresh_shape, 1)
    fresh_step = over(fresh_at, rows)
    fresh_row = jnp.where(fresh_step <= rest(iota(fresh_shape, 0), STEPS), rest(fresh_at, rows), rows)
    contract = (((1,), (1,)), ((), ()))

    def attend(rows_in, size):
        for row in rows_in:
            for copy in copies(row, size):
                copy.wait()
        extent = size * CHUNK
        position = iota((total, extent), 1)
        starts = [pl.multiple_of(row * pairs, pairs) for row in rows_in]
        spreads = []
        for start in starts:
            flat = q_buf[pl.ds(start, pairs), :]
            one = jnp.concatenate(
                [flat[:, j * HD : (j + 1) * HD] for j in range(groups)], axis=0
            ).astype(BF16)
            spreads.append(jnp.concatenate([one] * heads, axis=1) * mask_ref[...])
        cached = [
            lax.dot_general(spread, k_ref[row, :extent, :], contract, preferred_element_type=F32)
            for row, spread in zip(rows_in, spreads)
        ]
        fresh = lax.dot_general(
            jnp.concatenate(spreads, axis=0), kn_ref[...], contract, preferred_element_type=F32
        )
        scores = jnp.concatenate(
            [
                jnp.concatenate(
                    [
                        jnp.where(position < span_of(row), cached[k], -jnp.inf),
                        jnp.where(fresh_row == row, fresh[k * total : (k + 1) * total], -jnp.inf),
                    ],
                    axis=1,
                )
                for k, row in enumerate(rows_in)
            ],
            axis=0,
        )
        top = jnp.max(scores, axis=1, keepdims=True)
        weights = jnp.exp2((scores - top) * factor)
        share = 1.0 / jnp.sum(weights, axis=1, keepdims=True)
        weights = weights.astype(BF16)
        mixed = jnp.dot(weights[:, extent:], vn_ref[...], preferred_element_type=F32)
        mixed = mixed + jnp.concatenate(
            [
                jnp.dot(
                    weights[k * total : (k + 1) * total, :extent],
                    v_ref[row, :extent, :],
                    preferred_element_type=F32,
                )
                for k, row in enumerate(rows_in)
            ],
            axis=0,
        )
        own = mixed[:, :HD]
        for c in range(1, heads):
            own = jnp.where(head_own == c, mixed[:, c * HD : (c + 1) * HD], own)
        own = own * share
        for k, start in enumerate(starts):
            one = own[k * total : (k + 1) * total]
            o_buf[pl.ds(start, pairs), :] = jnp.concatenate(
                [one[j * pairs : (j + 1) * pairs] for j in range(groups)], axis=1
            )

    quads(row_of, span_of, rows, chunks, attend)

    mixed = o_buf[...].astype(BF16)
    final = exact(by_pair_matrix(heads, rows), mixed)
    for c in range(heads):
        for s in range(STEPS):
            at = (c * STEPS + s) * rows
            q_ref[s, :, c * wide : (c + 1) * wide] = final[at : at + rows]
    result = pltpu.make_async_copy(q_ref, out_hbm, sems.at[0])
    result.start()
    packed = exact(pack_matrix(meta, owners, heads, rows, True), mixed)
    block = heads * CAP * STEPS
    for i in range(owners):
        outgoing[i] = packed[i * block : (i + 1) * block]
    result.wait()


def collect_kernel(owners, heads, meta, blocks, out_hbm, out_ref, sems):
    rows = out_ref.shape[1]
    wide = out_ref.shape[2] // heads
    span = STEPS * rows
    arrived = jnp.concatenate([blocks[i] for i in range(owners)], axis=0)
    spread = unpack_matrix(meta, owners, heads, rows, False)
    copies = []
    for c in range(heads):
        values = exact(spread[c * span : (c + 1) * span], arrived)
        for s in range(STEPS):
            out_ref[s, :, c * wide : (c + 1) * wide] = values[s * rows : (s + 1) * rows]
        part = (slice(None), slice(None), pl.ds(c * wide, wide))
        copies.append(pltpu.make_async_copy(out_ref.at[part], out_hbm.at[part], sems.at[c]))
        copies[-1].start()
    for copy in copies:
        copy.wait()


def exchange(blocks):
    return lax.all_to_all(blocks, "store", split_axis=0, concat_axis=0, tiled=True)


def in_hbm(array):
    return pltpu.with_memory_space_constraint(array, pltpu.HBM)


def swap_cores(part):
    return lax.ppermute(part, "tensor", [(0, 1), (1, 0)])


def shards(
    x_in,
    q_base,
    k_new,
    v_new,
    cache_k,
    cache_v,
    lengths,
    adapter_ids,
    slot_of,
    a_query,
    b_query,
    a_output,
    b_output,
):
    owners = lax.axis_size("store")
    rows = x_in.shape[1]
    width = x_in.shape[2]
    heads = cache_k.shape[2] // HD
    wide = width // heads
    adapt, rank = a_query.shape[1:]
    lanes = adapt * rank
    block = heads * CAP * STEPS
    items = owners * CAP * STEPS
    def flat(a_store):
        return jnp.transpose(a_store, (1, 2, 0)).reshape(lanes, a_store.shape[0])

    shape = jax.ShapeDtypeStruct
    small = pltpu.CompilerParams(vmem_limit_bytes=16 * 1024 * 1024)

    sent = shape((owners, block, wide), BF16)
    meta, blocks, a_near, b_near = pl.pallas_call(
        functools.partial(dispatch_kernel, owners, heads, adapt, rank),
        out_shape=[
            shape((3 * rows + owners * CAP,), I32),
            shape((owners, block, wide + lanes), BF16),
            pltpu.VMEM((lanes, width), BF16),
            pltpu.VMEM((lanes, width), BF16),
        ],
        in_specs=[HBM] * 6,
        out_specs=[SMEM] + [VMEM] * 3,
        scratch_shapes=[
            pltpu.SMEM((owners * CAP,), I32),
            pltpu.SMEM(adapter_ids.shape, I32),
            pltpu.SMEM(slot_of.shape, I32),
            pltpu.SMEM(lengths.shape, I32),
            pltpu.VMEM(x_in.shape, BF16),
            pltpu.SemaphoreType.DMA((6,)),
        ],
        compiler_params=small,
        name="dispatch",
    )(
        *map(in_hbm, (adapter_ids, slot_of, lengths, x_in, flat(a_query))),
        in_hbm(b_query.reshape(lanes, width)),
    )

    arrived = exchange(blocks)
    part, mask = pl.pallas_call(
        functools.partial(project_kernel, owners, heads, wide, True),
        out_shape=[shape((items, lanes), F32)] * 2,
        in_specs=[VMEM] * 2,
        out_specs=[VMEM] * 2,
        compiler_params=small,
        name="project_query",
    )(a_near, arrived)

    def expand(part, b_store, name):
        return pl.pallas_call(
            functools.partial(expand_kernel, owners, heads, wide),
            out_shape=sent,
            in_specs=[VMEM] * 3,
            out_specs=VMEM,
            compiler_params=small,
            name=name,
        )(part, swap_cores(part), b_store)

    returned = exchange(expand(part, b_near, "expand_query"))

    attn_out, outgoing = pl.pallas_call(
        functools.partial(attend_kernel, owners, heads),
        out_shape=[shape((STEPS, rows, width), BF16), sent],
        in_specs=[SMEM] + [HBM] * 5 + [VMEM],
        out_specs=[HBM, VMEM],
        scratch_shapes=[
            pltpu.VMEM(q_base.shape, BF16),
            pltpu.VMEM((CHUNK, heads * HD), BF16),
            pltpu.VMEM((CHUNK, heads * HD), BF16),
            pltpu.VMEM(cache_k.shape, BF16),
            pltpu.VMEM(cache_v.shape, BF16),
            pltpu.VMEM((STEPS * wide // HD * heads, heads * HD), BF16),
            pltpu.VMEM((rows * STEPS * heads, wide), F32),
            pltpu.VMEM((rows * STEPS * heads, wide), F32),
            pltpu.SemaphoreType.DMA((rows,)),
            pltpu.SemaphoreType.DMA((rows,)),
            pltpu.SemaphoreType.DMA((1 + 2 * STEPS,)),
        ],
        compiler_params=pltpu.CompilerParams(vmem_limit_bytes=32 * 1024 * 1024),
        name="attend",
    )(meta, *map(in_hbm, (q_base, k_new, v_new, cache_k, cache_v)), returned)

    arrived = exchange(outgoing)
    part = pl.pallas_call(
        functools.partial(project_kernel, owners, heads, wide, False),
        out_shape=shape((items, lanes), F32),
        in_specs=[VMEM] * 3,
        out_specs=VMEM,
        compiler_params=small,
        name="project_output",
    )(flat(a_output), arrived, mask)
    returned = exchange(expand(part, b_output.reshape(lanes, width), "expand_output"))
    adapter_out = pl.pallas_call(
        functools.partial(collect_kernel, owners, heads),
        out_shape=shape((STEPS, rows, width), BF16),
        in_specs=[SMEM, VMEM],
        out_specs=HBM,
        scratch_shapes=[
            pltpu.VMEM((STEPS, rows, width), BF16),
            pltpu.SemaphoreType.DMA((heads,)),
        ],
        compiler_params=small,
        name="collect",
    )(meta, returned)
    return (attn_out, adapter_out)


def solution(mesh):
    in_specs = (
        P(None, ("parts", "store"), "tensor"),
        P(None, ("parts", "store"), "tensor"),
        P(None, ("parts", "store"), "tensor"),
        P(None, ("parts", "store"), "tensor"),
        P(("parts", "store"), None, "tensor"),
        P(("parts", "store"), None, "tensor"),
        P(("parts", "store")),
        P(("parts", "store")),
        P("parts"),
        P(None, "store", None),
        P("store", None, "tensor"),
        P(None, "store", None),
        P("store", None, "tensor"),
    )
    out_specs = (P(None, ("parts", "store"), "tensor"), P(None, ("parts", "store"), "tensor"))
    return jax.shard_map(shards, mesh=mesh, in_specs=in_specs, out_specs=out_specs, check_vma=False)
```

```python
import functools
import math

import jax
import jax.numpy as jnp
from jax import lax
from jax.experimental import pallas as pl
from jax.experimental.pallas import tpu as pltpu
from jax.sharding import PartitionSpec as P

HD = 128
CAP = 2
STEPS = 2
CHUNK = 128
QUAD = 4
BF16 = jnp.bfloat16
F32 = jnp.float32
I32 = jnp.int32
VMEM = pl.BlockSpec(memory_space=pltpu.VMEM)
SMEM = pl.BlockSpec(memory_space=pltpu.SMEM)
HBM = pl.BlockSpec(memory_space=pltpu.HBM)


def iota(shape, dim):
    return lax.broadcasted_iota(I32, shape, dim)


def over(x, n):
    return lax.shift_right_logical(x, jnp.full_like(x, n.bit_length() - 1)) if n & (n - 1) == 0 else x // n


def rest(x, n):
    return x & (n - 1) if n & (n - 1) == 0 else x % n


def one_hot(hits):
    return jnp.where(hits, 1.0, 0.0).astype(BF16)


def stacked(ref, heads, wide):
    return jnp.concatenate(
        [ref[s, :, c * wide : (c + 1) * wide] for c in range(heads) for s in range(STEPS)], axis=0
    )


def gather_matrix(meta, base, owners, heads, rows):
    pairs = heads * STEPS
    shape = (pairs, pairs * rows)
    offset = iota(shape, 1) - iota(shape, 0) * rows
    parts = []
    for i in range(owners):
        row = meta[base + i]
        parts.append(one_hot(offset == jnp.where(row >= 0, row, -rows * pairs)))
    return jnp.concatenate(parts, axis=0)


def scatter_matrix(meta, owners, heads, rows):
    pairs = heads * STEPS
    shape = (rows, CAP * owners * pairs)
    at = iota(shape, 0)
    spot = jnp.zeros(shape, I32)
    for r in range(rows):
        spot = jnp.where(at == r, meta[r] * pairs, spot)
    offset = iota(shape, 1) - spot
    return jnp.concatenate([one_hot(offset == pair) for pair in range(pairs)], axis=0)


def regroup_matrix(owners, heads):
    total = owners * heads * STEPS
    at = iota((total, total), 0)
    head = over(at, owners * STEPS)
    owner = rest(over(at, STEPS), owners)
    return one_hot(
        iota((total, total), 1) == owner * (heads * STEPS) + head * STEPS + rest(at, STEPS)
    )


def ungroup_matrix(owners, heads):
    total = owners * heads * STEPS
    at = iota((total, total), 0)
    owner = over(at, heads * STEPS)
    head = rest(over(at, STEPS), heads)
    return one_hot(
        iota((total, total), 1) == head * (owners * STEPS) + owner * STEPS + rest(at, STEPS)
    )


def exact(matrix, values):
    return jnp.dot(matrix, values, preferred_element_type=F32).astype(BF16)


def dispatch_kernel(
    owners,
    heads,
    adapt,
    rank,
    ids_hbm,
    slot_of_hbm,
    lengths_hbm,
    x_hbm,
    meta,
    first_out,
    second_out,
    slot_at,
    ids,
    slot_of,
    lengths,
    x_ref,
    sems,
):
    pairs = (
        (ids_hbm, ids),
        (slot_of_hbm, slot_of),
        (lengths_hbm, lengths),
        (x_hbm, x_ref),
    )
    copies = [pltpu.make_async_copy(a, b, sems.at[k]) for k, (a, b) in enumerate(pairs)]
    for copy in copies:
        copy.start()
    rows = x_ref.shape[1]
    wide = x_ref.shape[2] // heads
    for copy in copies[:3]:
        copy.wait()
    places = owners * CAP
    row_at = rows
    order = rows + places
    spans = rows + 2 * places
    for p in range(places):
        meta[row_at + p] = -1
        meta[spans + p] = 0
        slot_at[p] = -1
    for r in range(rows):
        slot = slot_of[ids[r]]
        owner = over(slot, adapt)
        place = owner + jnp.where(meta[row_at + owner] >= 0, owners, 0)
        meta[row_at + place] = r
        meta[spans + place] = lengths[r]
        slot_at[place] = rest(slot, adapt)
        meta[r] = place
    for k in range(CAP):
        sizes = [meta[spans + k * owners + i] for i in range(owners)]
        for r in range(owners):
            ahead = jnp.int32(0)
            for q in range(owners):
                if q != r:
                    shorter = sizes[q] <= sizes[r] if q < r else sizes[q] < sizes[r]
                    ahead = ahead + jnp.where(shorter, 1, 0)
            meta[order + k * owners + ahead] = r
    copies[3].wait()
    block = heads * STEPS
    values = stacked(x_ref, heads, wide)
    lane_slot = over(iota((block, adapt * rank), 1), rank)
    for k, out in enumerate((first_out, second_out)):
        base = k * owners
        packed = exact(gather_matrix(meta, row_at + base, owners, heads, rows), values)
        for i in range(owners):
            out[i, :, :wide] = packed[i * block : (i + 1) * block]
            out[i, :, wide:] = one_hot(lane_slot == slot_at[base + i])


def project_kernel(owners, heads, wide, first, a_hbm, blocks, *refs):
    if first:
        part_ref, mask_ref, a_ref, sem = refs
    else:
        mask_in, part_ref, a_ref, sem = refs
    width = heads * wide
    start = pl.multiple_of(lax.axis_index("tensor") * width, width)
    store = pltpu.make_async_copy(a_hbm.at[:, pl.ds(start, width)], a_ref, sem)
    store.start()
    grouped = regroup_matrix(owners, heads)
    items = owners * STEPS
    arrived = jnp.concatenate([blocks[i, :, :wide] for i in range(owners)], axis=0)
    arrived = exact(grouped, arrived)
    if first:
        masks = jnp.concatenate([blocks[i, :, wide:] for i in range(owners)], axis=0)
        mask = jnp.dot(grouped[:items], masks, preferred_element_type=F32)
        mask_ref[...] = mask
    else:
        mask = mask_in[...]
    store.wait()
    total = jnp.zeros(mask.shape, F32)
    for c in range(heads):
        total = total + lax.dot_general(
            arrived[c * items : (c + 1) * items],
            a_ref[:, c * wide : (c + 1) * wide],
            (((1,), (1,)), ((), ())),
            preferred_element_type=F32,
        )
    part_ref[...] = total * mask


def expand_kernel(owners, heads, wide, mine, other, b_hbm, blocks, b_ref, sem):
    store = pltpu.make_async_copy(b_hbm, b_ref, sem)
    store.start()
    low_rank = (mine[...] + other[...]).astype(BF16)
    matrix = ungroup_matrix(owners, heads)
    store.wait()
    pieces = []
    for c in range(heads):
        product = jnp.dot(
            low_rank, b_ref[:, c * wide : (c + 1) * wide], preferred_element_type=F32
        )
        pieces.append((2.0 * product).astype(BF16))
    back = exact(matrix, jnp.concatenate(pieces, axis=0))
    block = heads * STEPS
    for i in range(owners):
        blocks[i] = back[i * block : (i + 1) * block]


def quads(row_of, span_of, rows, sizes, action):
    def body(quad, carry):
        amount = over(span_of(row_of(quad * QUAD + QUAD - 1)) + (CHUNK - 1), CHUNK)
        for size in range(1, sizes + 1):

            @pl.when(amount == size)
            def _():
                action([row_of(quad * QUAD + j) for j in range(QUAD)], size)

        return carry

    lax.fori_loop(0, rows // QUAD, body, 0)


def attend_kernel(
    owners,
    heads,
    chain,
    meta,
    q_hbm,
    kn_hbm,
    vn_hbm,
    k_hbm,
    v_hbm,
    blocks,
    outgoing,
    q_ref,
    kn_ref,
    vn_ref,
    k_ref,
    v_ref,
    mask_ref,
    q_buf,
    o_buf,
    k_sem,
    v_sem,
    sems,
):
    rows = q_hbm.shape[1]
    wide = q_hbm.shape[2] // heads
    groups = wide // HD
    pairs = heads * STEPS
    total = groups * pairs
    width = heads * HD
    fresh_rows = STEPS * rows

    singles = [pltpu.make_async_copy(q_hbm, q_ref, sems.at[0])]
    for k, (source, target) in enumerate(((kn_hbm, kn_ref), (vn_hbm, vn_ref))):
        for t in range(STEPS):
            part = target.at[pl.ds(t * rows, rows)]
            singles.append(pltpu.make_async_copy(source.at[t], part, sems.at[1 + k * STEPS + t]))
    for copy in singles:
        copy.start()

    places = owners * CAP
    own_base = chain * owners

    def slot_at(place):
        return meta[rows + places + own_base + place]

    def span_of(slot):
        return meta[rows + 2 * places + own_base + slot]

    def row_of(slot):
        return jnp.maximum(meta[rows + own_base + slot], 0)

    def copies(slot, size):
        part = pl.ds(0, size * CHUNK)
        row = row_of(slot)
        return (
            pltpu.make_async_copy(k_hbm.at[row, part], k_ref.at[slot, part], k_sem.at[slot]),
            pltpu.make_async_copy(v_hbm.at[row, part], v_ref.at[slot, part], v_sem.at[slot]),
        )

    def begin(slots, size):
        for slot in slots:
            for copy in copies(slot, size):
                copy.start()

    chunks = k_hbm.shape[1] // CHUNK
    quads(slot_at, span_of, owners, chunks, begin)

    head_at = rest(over(iota((total, width), 0), STEPS), heads)
    mask_ref[...] = one_hot(head_at == over(iota((total, width), 1), HD))
    head_own = rest(over(iota((QUAD * total, HD), 0), STEPS), heads)
    blank = jnp.zeros((CHUNK - fresh_rows, width), BF16)
    kn_ref[fresh_rows:, :] = blank
    vn_ref[fresh_rows:, :] = blank

    o_buf[...] = jnp.zeros(o_buf.shape, F32)
    delta = jnp.concatenate([blocks[i] for i in range(owners)], axis=0).astype(F32)
    gather = gather_matrix(meta, rows + own_base, owners, heads, rows)
    for copy in singles:
        copy.wait()
    q_buf[...] = jnp.dot(gather, stacked(q_ref, heads, wide), preferred_element_type=F32) + delta

    factor = math.log2(math.e) / math.sqrt(HD)
    fresh_shape = (total, CHUNK)
    fresh_at = iota(fresh_shape, 1)
    fresh_step = over(fresh_at, rows)
    fresh_row = jnp.where(fresh_step <= rest(iota(fresh_shape, 0), STEPS), rest(fresh_at, rows), rows)
    contract = (((1,), (1,)), ((), ()))

    def attend(slots, size):
        for slot in slots:
            for copy in copies(slot, size):
                copy.wait()
        extent = size * CHUNK
        position = iota((total, extent), 1)
        starts = [pl.multiple_of(slot * pairs, pairs) for slot in slots]
        spreads = []
        for start in starts:
            flat = q_buf[pl.ds(start, pairs), :]
            one = jnp.concatenate(
                [flat[:, j * HD : (j + 1) * HD] for j in range(groups)], axis=0
            ).astype(BF16)
            spreads.append(jnp.concatenate([one] * heads, axis=1) * mask_ref[...])
        cached = [
            lax.dot_general(spread, k_ref[slot, :extent, :], contract, preferred_element_type=F32)
            for slot, spread in zip(slots, spreads)
        ]
        fresh = lax.dot_general(
            jnp.concatenate(spreads, axis=0), kn_ref[...], contract, preferred_element_type=F32
        )
        scores = jnp.concatenate(
            [
                jnp.concatenate(
                    [
                        jnp.where(position < span_of(slot), cached[k], -jnp.inf),
                        jnp.where(fresh_row == row_of(slot), fresh[k * total : (k + 1) * total], -jnp.inf),
                    ],
                    axis=1,
                )
                for k, slot in enumerate(slots)
            ],
            axis=0,
        )
        top = jnp.max(scores, axis=1, keepdims=True)
        weights = jnp.exp2((scores - top) * factor)
        share = 1.0 / jnp.sum(weights, axis=1, keepdims=True)
        weights = weights.astype(BF16)
        mixed = jnp.dot(weights[:, extent:], vn_ref[...], preferred_element_type=F32)
        mixed = mixed + jnp.concatenate(
            [
                jnp.dot(
                    weights[k * total : (k + 1) * total, :extent],
                    v_ref[slot, :extent, :],
                    preferred_element_type=F32,
                )
                for k, slot in enumerate(slots)
            ],
            axis=0,
        )
        own = mixed[:, :HD]
        for c in range(1, heads):
            own = jnp.where(head_own == c, mixed[:, c * HD : (c + 1) * HD], own)
        own = own * share
        for k, start in enumerate(starts):
            one = own[k * total : (k + 1) * total]
            o_buf[pl.ds(start, pairs), :] = jnp.concatenate(
                [one[j * pairs : (j + 1) * pairs] for j in range(groups)], axis=1
            )

    quads(slot_at, span_of, owners, chunks, attend)

    mixed = o_buf[...].astype(BF16)
    for i in range(owners):
        outgoing[i] = mixed[i * pairs : (i + 1) * pairs]


def collect_kernel(owners, heads, meta, first, second, out_hbm, out_ref, sems):
    rows = out_ref.shape[1]
    wide = out_ref.shape[2] // heads
    span = STEPS * rows
    arrived = jnp.concatenate([b[i] for b in (first, second) for i in range(owners)], axis=0)
    spread = scatter_matrix(meta, owners, heads, rows)
    copies = []
    for c in range(heads):
        values = exact(spread[c * span : (c + 1) * span], arrived)
        for s in range(STEPS):
            out_ref[s, :, c * wide : (c + 1) * wide] = values[s * rows : (s + 1) * rows]
        part = (slice(None), slice(None), pl.ds(c * wide, wide))
        copies.append(pltpu.make_async_copy(out_ref.at[part], out_hbm.at[part], sems.at[c]))
        copies[-1].start()
    for copy in copies:
        copy.wait()


def exchange(blocks):
    return lax.all_to_all(blocks, "store", split_axis=0, concat_axis=0, tiled=True)


def in_hbm(array):
    return pltpu.with_memory_space_constraint(array, pltpu.HBM)


def swap_cores(part):
    return lax.ppermute(part, "tensor", [(0, 1), (1, 0)])


def shards(
    x_in,
    q_base,
    k_new,
    v_new,
    cache_k,
    cache_v,
    lengths,
    adapter_ids,
    slot_of,
    a_query,
    b_query,
    a_output,
    b_output,
):
    owners = lax.axis_size("store")
    rows = x_in.shape[1]
    width = x_in.shape[2]
    heads = cache_k.shape[2] // HD
    wide = width // heads
    adapt, rank = a_query.shape[1:]
    lanes = adapt * rank
    block = heads * STEPS
    items = owners * STEPS

    def flat(a_store):
        return in_hbm(jnp.transpose(a_store, (1, 2, 0)).reshape(lanes, a_store.shape[0]))

    shape = jax.ShapeDtypeStruct
    small = pltpu.CompilerParams(vmem_limit_bytes=16 * 1024 * 1024)
    sent = shape((owners, block, wide), BF16)
    marked = shape((owners, block, wide + lanes), BF16)
    meta, *chains = pl.pallas_call(
        functools.partial(dispatch_kernel, owners, heads, adapt, rank),
        out_shape=[shape((rows + 3 * owners * CAP,), I32), marked, marked],
        in_specs=[HBM] * 4,
        out_specs=[SMEM] + [VMEM] * 2,
        scratch_shapes=[
            pltpu.SMEM((owners * CAP,), I32),
            pltpu.SMEM(adapter_ids.shape, I32),
            pltpu.SMEM(slot_of.shape, I32),
            pltpu.SMEM(lengths.shape, I32),
            pltpu.VMEM(x_in.shape, BF16),
            pltpu.SemaphoreType.DMA((4,)),
        ],
        compiler_params=small,
        name="dispatch",
    )(*map(in_hbm, (adapter_ids, slot_of, lengths, x_in)))

    store_scratch = [pltpu.VMEM((lanes, width), BF16), pltpu.SemaphoreType.DMA(())]

    def expand(part, b_store, name):
        return pl.pallas_call(
            functools.partial(expand_kernel, owners, heads, wide),
            out_shape=sent,
            in_specs=[VMEM] * 2 + [HBM],
            out_specs=VMEM,
            scratch_shapes=store_scratch,
            compiler_params=small,
            name=name,
        )(part, swap_cores(part), in_hbm(b_store.reshape(lanes, width)))

    def attend(chain, returned):
        return pl.pallas_call(
            functools.partial(attend_kernel, owners, heads, chain),
            out_shape=sent,
            in_specs=[SMEM] + [HBM] * 5 + [VMEM],
            out_specs=VMEM,
            scratch_shapes=[
                pltpu.VMEM(q_base.shape, BF16),
                pltpu.VMEM((CHUNK, heads * HD), BF16),
                pltpu.VMEM((CHUNK, heads * HD), BF16),
                pltpu.VMEM((owners,) + cache_k.shape[1:], BF16),
                pltpu.VMEM((owners,) + cache_v.shape[1:], BF16),
                pltpu.VMEM((STEPS * wide // HD * heads, heads * HD), BF16),
                pltpu.VMEM((owners * block, wide), F32),
                pltpu.VMEM((owners * block, wide), F32),
                pltpu.SemaphoreType.DMA((owners,)),
                pltpu.SemaphoreType.DMA((owners,)),
                pltpu.SemaphoreType.DMA((1 + 2 * STEPS,)),
            ],
            compiler_params=pltpu.CompilerParams(vmem_limit_bytes=32 * 1024 * 1024),
            name=f"attend_{chain}",
        )(meta, *map(in_hbm, (q_base, k_new, v_new, cache_k, cache_v)), returned)

    def collect(blocks, name):
        return pl.pallas_call(
            functools.partial(collect_kernel, owners, heads),
            out_shape=shape((STEPS, rows, width), BF16),
            in_specs=[SMEM] + [VMEM] * CAP,
            out_specs=HBM,
            scratch_shapes=[
                pltpu.VMEM((STEPS, rows, width), BF16),
                pltpu.SemaphoreType.DMA((heads,)),
            ],
            compiler_params=small,
            name=name,
        )(meta, *blocks)

    attended, finished = [], []
    for chain, blocks in enumerate(chains):
        part, mask = pl.pallas_call(
            functools.partial(project_kernel, owners, heads, wide, True),
            out_shape=[shape((items, lanes), F32)] * 2,
            in_specs=[HBM, VMEM],
            out_specs=[VMEM] * 2,
            scratch_shapes=store_scratch,
            compiler_params=small,
            name=f"project_query_{chain}",
        )(flat(a_query), exchange(blocks))
        returned = exchange(expand(part, b_query, f"expand_query_{chain}"))
        outgoing = attend(chain, returned)
        attended.append(outgoing)
        part = pl.pallas_call(
            functools.partial(project_kernel, owners, heads, wide, False),
            out_shape=shape((items, lanes), F32),
            in_specs=[HBM] + [VMEM] * 2,
            out_specs=VMEM,
            scratch_shapes=store_scratch,
            compiler_params=small,
            name=f"project_output_{chain}",
        )(flat(a_output), exchange(outgoing), mask)
        finished.append(exchange(expand(part, b_output, f"expand_output_{chain}")))
    return (collect(attended, "collect_attended"), collect(finished, "collect_adapters"))


def solution(mesh):
    in_specs = (
        P(None, ("parts", "store"), "tensor"),
        P(None, ("parts", "store"), "tensor"),
        P(None, ("parts", "store"), "tensor"),
        P(None, ("parts", "store"), "tensor"),
        P(("parts", "store"), None, "tensor"),
        P(("parts", "store"), None, "tensor"),
        P(("parts", "store")),
        P(("parts", "store")),
        P("parts"),
        P(None, "store", None),
        P("store", None, "tensor"),
        P(None, "store", None),
        P("store", None, "tensor"),
    )
    out_specs = (P(None, ("parts", "store"), "tensor"), P(None, ("parts", "store"), "tensor"))
    return jax.shard_map(shards, mesh=mesh, in_specs=in_specs, out_specs=out_specs, check_vma=False)
```

```python
import functools
import math

import jax
import jax.numpy as jnp
from jax import lax
from jax.experimental import pallas as pl
from jax.experimental.pallas import tpu as pltpu
from jax.sharding import PartitionSpec as P

HD = 128
CAP = 2
STEPS = 2
CHUNK = 128
QUAD = 4
BF16 = jnp.bfloat16
F32 = jnp.float32
I32 = jnp.int32
VMEM = pl.BlockSpec(memory_space=pltpu.VMEM)
SMEM = pl.BlockSpec(memory_space=pltpu.SMEM)
HBM = pl.BlockSpec(memory_space=pltpu.HBM)


def iota(shape, dim):
    return lax.broadcasted_iota(I32, shape, dim)


def over(x, n):
    return lax.shift_right_logical(x, jnp.full_like(x, n.bit_length() - 1)) if n & (n - 1) == 0 else x // n


def rest(x, n):
    return x & (n - 1) if n & (n - 1) == 0 else x % n


def one_hot(hits):
    return jnp.where(hits, 1.0, 0.0).astype(BF16)


def stacked(ref, heads, wide):
    return jnp.concatenate(
        [ref[s, :, c * wide : (c + 1) * wide] for c in range(heads) for s in range(STEPS)], axis=0
    )


def pack_matrix(meta, owners, heads, rows, by_row):
    items = CAP * STEPS
    block = heads * items
    shape = (block, heads * STEPS * rows)
    at = iota(shape, 0)
    col = iota(shape, 1)
    head_step = over(at, items) * STEPS + rest(at, STEPS)
    offset = col - (head_step if by_row else head_step * rows)
    factor = heads * STEPS if by_row else 1
    first = rest(over(at, STEPS), CAP) == 0
    if not by_row:
        offset = jnp.where((offset >= 0) & (offset < rows), offset, -1)
    parts = []
    for i in range(owners):
        here = [meta[rows + i * CAP + k] for k in range(CAP)]
        spots = [jnp.where(h >= 0, h * factor, -rows * factor * heads * STEPS * 2) for h in here]
        parts.append(one_hot(offset == jnp.where(first, spots[0], spots[1])))
    return jnp.concatenate(parts, axis=0)


def unpack_matrix(meta, owners, heads, rows, by_row):
    items = CAP * STEPS
    block = heads * items
    pairs = heads * STEPS
    spots = [over(meta[r], CAP) * block + rest(meta[r], CAP) * STEPS for r in range(rows)]
    if by_row:
        shape = (pairs, owners * block)
        at = iota(shape, 0)
        col = iota(shape, 1) - (over(at, STEPS) * items + rest(at, STEPS))
        return jnp.concatenate([one_hot(col == spots[r]) for r in range(rows)], axis=0)
    shape = (rows, owners * block)
    at = iota(shape, 0)
    col = iota(shape, 1)
    spot = jnp.zeros(shape, I32)
    for r in range(rows):
        spot = jnp.where(at == r, spots[r], spot)
    offset = col - spot
    return jnp.concatenate(
        [one_hot(offset == c * items + s) for c in range(heads) for s in range(STEPS)], axis=0
    )


def by_row_matrix(heads, rows):
    pairs = heads * STEPS
    shape = (pairs * rows, pairs * rows)
    at = iota(shape, 0)
    return one_hot(iota(shape, 1) == rest(at, pairs) * rows + over(at, pairs))


def by_pair_matrix(heads, rows):
    pairs = heads * STEPS
    shape = (pairs * rows, pairs * rows)
    at = iota(shape, 0)
    return one_hot(iota(shape, 1) == rest(at, rows) * pairs + over(at, rows))


def regroup_matrix(owners, heads):
    items = CAP * STEPS
    total = owners * heads * items
    at = iota((total, total), 0)
    head = over(at, owners * items)
    owner = rest(over(at, items), owners)
    return one_hot(
        iota((total, total), 1) == owner * (heads * items) + head * items + rest(at, items)
    )


def ungroup_matrix(owners, heads):
    items = CAP * STEPS
    total = owners * heads * items
    at = iota((total, total), 0)
    owner = over(at, heads * items)
    head = rest(over(at, items), heads)
    return one_hot(
        iota((total, total), 1) == head * (owners * items) + owner * items + rest(at, items)
    )


def in_order(arrived, crossed):
    return [b for k in range(crossed.shape[0]) for b in (arrived[k, 0], crossed[k])]


def exact(matrix, values):
    return jnp.dot(matrix, values, preferred_element_type=F32).astype(BF16)


def dispatch_kernel(
    owners,
    heads,
    adapt,
    rank,
    ids_hbm,
    slot_of_hbm,
    lengths_hbm,
    x_hbm,
    a_hbm,
    b_hbm,
    meta,
    blocks,
    a_out,
    b_out,
    slot_at,
    ids,
    slot_of,
    lengths,
    x_ref,
    sems,
):
    width = x_hbm.shape[2]
    start = pl.multiple_of(lax.axis_index("tensor") * width, width)
    pairs = (
        (ids_hbm, ids),
        (slot_of_hbm, slot_of),
        (lengths_hbm, lengths),
        (x_hbm, x_ref),
        (a_hbm.at[:, pl.ds(start, width)], a_out),
        (b_hbm, b_out),
    )
    copies = [pltpu.make_async_copy(a, b, sems.at[k]) for k, (a, b) in enumerate(pairs)]
    for copy in copies:
        copy.start()
    rows = x_ref.shape[1]
    wide = x_ref.shape[2] // heads
    for copy in copies[:3]:
        copy.wait()
    parity = rest(lax.axis_index("store"), 2)
    row_at = rows
    order = rows + owners * CAP
    spans = order + rows
    for p in range(owners * CAP):
        meta[row_at + p] = -1
        slot_at[p] = -1
    for r in range(rows):
        slot = slot_of[ids[r]]
        first = (over(slot, adapt) ^ parity) * CAP
        place = first + jnp.where(meta[row_at + first] >= 0, 1, 0)
        meta[row_at + place] = r
        slot_at[place] = rest(slot, adapt)
        meta[r] = place
    sizes = [lengths[r] for r in range(rows)]
    for r in range(rows):
        ahead = jnp.int32(0)
        for q in range(rows):
            if q != r:
                shorter = sizes[q] <= sizes[r] if q < r else sizes[q] < sizes[r]
                ahead = ahead + jnp.where(shorter, 1, 0)
        meta[order + ahead] = r
        meta[spans + r] = sizes[r]
    items = CAP * STEPS
    block = heads * items
    copies[3].wait()
    packed = exact(pack_matrix(meta, owners, heads, rows, False), stacked(x_ref, heads, wide))
    at = iota((block, adapt * rank), 0)
    lane_slot = over(iota((block, adapt * rank), 1), rank)
    first = rest(over(at, STEPS), CAP) == 0
    for i in range(owners):
        blocks[i, :, :wide] = packed[i * block : (i + 1) * block]
        slot = jnp.where(first, slot_at[i * CAP], slot_at[i * CAP + 1])
        blocks[i, :, wide:] = one_hot(lane_slot == slot)
    for copy in copies[4:]:
        copy.wait()


def project_kernel(owners, heads, wide, first, a_ref, arrived, crossed, *refs):
    blocks = in_order(arrived, crossed)
    core = lax.axis_index("tensor") if a_ref.shape[1] > heads * wide else 0
    if first:
        part_ref, mask_ref = refs
    else:
        mask_in, part_ref = refs
    grouped = regroup_matrix(owners, heads)
    items = owners * CAP * STEPS
    arrived = jnp.concatenate([b[:, :wide] for b in blocks], axis=0)
    arrived = exact(grouped, arrived)
    if first:
        masks = jnp.concatenate([b[:, wide:] for b in blocks], axis=0)
        mask = jnp.dot(grouped[:items], masks, preferred_element_type=F32)
        mask_ref[...] = mask
    else:
        mask = mask_in[...]
    total = jnp.zeros(mask.shape, F32)
    for c in range(heads):
        total = total + lax.dot_general(
            arrived[c * items : (c + 1) * items],
            a_ref[:, pl.ds(pl.multiple_of(core * (heads * wide) + c * wide, wide), wide)],
            (((1,), (1,)), ((), ())),
            preferred_element_type=F32,
        )
    part_ref[...] = total * mask


def expand_kernel(owners, heads, wide, mine, other, b_ref, blocks):
    low_rank = (mine[...] + other[...]).astype(BF16)
    pieces = []
    for c in range(heads):
        product = jnp.dot(
            low_rank, b_ref[:, c * wide : (c + 1) * wide], preferred_element_type=F32
        )
        pieces.append((2.0 * product).astype(BF16))
    back = exact(ungroup_matrix(owners, heads), jnp.concatenate(pieces, axis=0))
    block = heads * CAP * STEPS
    for i in range(owners):
        blocks[i] = back[i * block : (i + 1) * block]


def quads(row_of, span_of, rows, sizes, action):
    def body(quad, carry):
        amount = over(span_of(row_of(quad * QUAD + QUAD - 1)) + (CHUNK - 1), CHUNK)
        for size in range(1, sizes + 1):

            @pl.when(amount == size)
            def _():
                action([row_of(quad * QUAD + j) for j in range(QUAD)], size)

        return carry

    lax.fori_loop(0, rows // QUAD, body, 0)


def attend_kernel(
    owners,
    heads,
    meta,
    q_hbm,
    kn_hbm,
    vn_hbm,
    k_hbm,
    v_hbm,
    arrived,
    crossed,
    out_hbm,
    outgoing,
    q_ref,
    kn_ref,
    vn_ref,
    k_ref,
    v_ref,
    mask_ref,
    q_buf,
    o_buf,
    k_sem,
    v_sem,
    sems,
):
    rows = q_hbm.shape[1]
    wide = q_hbm.shape[2] // heads
    groups = wide // HD
    pairs = heads * STEPS
    total = groups * pairs
    width = heads * HD
    fresh_rows = STEPS * rows

    singles = [pltpu.make_async_copy(q_hbm, q_ref, sems.at[0])]
    for k, (source, target) in enumerate(((kn_hbm, kn_ref), (vn_hbm, vn_ref))):
        for t in range(STEPS):
            part = target.at[pl.ds(t * rows, rows)]
            singles.append(pltpu.make_async_copy(source.at[t], part, sems.at[1 + k * STEPS + t]))
    for copy in singles:
        copy.start()

    def row_of(place):
        return meta[rows + owners * CAP + place]

    def span_of(row):
        return meta[2 * rows + owners * CAP + row]

    def copies(row, size):
        part = pl.ds(0, size * CHUNK)
        return (
            pltpu.make_async_copy(k_hbm.at[row, part], k_ref.at[row, part], k_sem.at[row]),
            pltpu.make_async_copy(v_hbm.at[row, part], v_ref.at[row, part], v_sem.at[row]),
        )

    def begin(rows_in, size):
        for row in rows_in:
            for copy in copies(row, size):
                copy.start()

    chunks = k_hbm.shape[1] // CHUNK
    quads(row_of, span_of, rows, chunks, begin)

    head_at = rest(over(iota((total, width), 0), STEPS), heads)
    mask_ref[...] = one_hot(head_at == over(iota((total, width), 1), HD))
    head_own = rest(over(iota((QUAD * total, HD), 0), STEPS), heads)
    blank = jnp.zeros((CHUNK - fresh_rows, width), BF16)
    kn_ref[fresh_rows:, :] = blank
    vn_ref[fresh_rows:, :] = blank

    delta = jnp.dot(
        unpack_matrix(meta, owners, heads, rows, True),
        jnp.concatenate(in_order(arrived, crossed), axis=0),
        preferred_element_type=F32,
    )
    by_row = by_row_matrix(heads, rows)
    for copy in singles:
        copy.wait()
    base = jnp.dot(by_row, stacked(q_ref, heads, wide), preferred_element_type=F32)
    q_buf[...] = base + delta

    factor = math.log2(math.e) / math.sqrt(HD)
    fresh_shape = (total, CHUNK)
    fresh_at = iota(fresh_shape, 1)
    fresh_step = over(fresh_at, rows)
    fresh_row = jnp.where(fresh_step <= rest(iota(fresh_shape, 0), STEPS), rest(fresh_at, rows), rows)
    contract = (((1,), (1,)), ((), ()))

    def attend(rows_in, size):
        for row in rows_in:
            for copy in copies(row, size):
                copy.wait()
        extent = size * CHUNK
        position = iota((total, extent), 1)
        starts = [pl.multiple_of(row * pairs, pairs) for row in rows_in]
        spreads = []
        for start in starts:
            flat = q_buf[pl.ds(start, pairs), :]
            one = jnp.concatenate(
                [flat[:, j * HD : (j + 1) * HD] for j in range(groups)], axis=0
            ).astype(BF16)
            spreads.append(jnp.concatenate([one] * heads, axis=1) * mask_ref[...])
        cached = [
            lax.dot_general(spread, k_ref[row, :extent, :], contract, preferred_element_type=F32)
            for row, spread in zip(rows_in, spreads)
        ]
        fresh = lax.dot_general(
            jnp.concatenate(spreads, axis=0), kn_ref[...], contract, preferred_element_type=F32
        )
        scores = jnp.concatenate(
            [
                jnp.concatenate(
                    [
                        jnp.where(position < span_of(row), cached[k], -jnp.inf),
                        jnp.where(fresh_row == row, fresh[k * total : (k + 1) * total], -jnp.inf),
                    ],
                    axis=1,
                )
                for k, row in enumerate(rows_in)
            ],
            axis=0,
        )
        top = jnp.max(scores, axis=1, keepdims=True)
        weights = jnp.exp2((scores - top) * factor)
        share = 1.0 / jnp.sum(weights, axis=1, keepdims=True)
        weights = weights.astype(BF16)
        mixed = jnp.dot(weights[:, extent:], vn_ref[...], preferred_element_type=F32)
        mixed = mixed + jnp.concatenate(
            [
                jnp.dot(
                    weights[k * total : (k + 1) * total, :extent],
                    v_ref[row, :extent, :],
                    preferred_element_type=F32,
                )
                for k, row in enumerate(rows_in)
            ],
            axis=0,
        )
        own = mixed[:, :HD]
        for c in range(1, heads):
            own = jnp.where(head_own == c, mixed[:, c * HD : (c + 1) * HD], own)
        own = own * share
        for k, start in enumerate(starts):
            one = own[k * total : (k + 1) * total]
            o_buf[pl.ds(start, pairs), :] = jnp.concatenate(
                [one[j * pairs : (j + 1) * pairs] for j in range(groups)], axis=1
            )

    quads(row_of, span_of, rows, chunks, attend)

    mixed = o_buf[...].astype(BF16)
    final = exact(by_pair_matrix(heads, rows), mixed)
    for c in range(heads):
        for s in range(STEPS):
            at = (c * STEPS + s) * rows
            q_ref[s, :, c * wide : (c + 1) * wide] = final[at : at + rows]
    result = pltpu.make_async_copy(q_ref, out_hbm, sems.at[0])
    result.start()
    packed = exact(pack_matrix(meta, owners, heads, rows, True), mixed)
    block = heads * CAP * STEPS
    for i in range(owners):
        outgoing[i] = packed[i * block : (i + 1) * block]
    result.wait()


def collect_kernel(owners, heads, meta, straight, crossed, out_hbm, out_ref, sems):
    rows = out_ref.shape[1]
    wide = out_ref.shape[2] // heads
    span = STEPS * rows
    arrived = jnp.concatenate(in_order(straight, crossed), axis=0)
    spread = unpack_matrix(meta, owners, heads, rows, False)
    copies = []
    for c in range(heads):
        values = exact(spread[c * span : (c + 1) * span], arrived)
        for s in range(STEPS):
            out_ref[s, :, c * wide : (c + 1) * wide] = values[s * rows : (s + 1) * rows]
        part = (slice(None), slice(None), pl.ds(c * wide, wide))
        copies.append(pltpu.make_async_copy(out_ref.at[part], out_hbm.at[part], sems.at[c]))
        copies[-1].start()
    for copy in copies:
        copy.wait()


def exchange(blocks):
    owners = blocks.shape[0]
    paired = blocks.reshape((owners // 2, 2) + blocks.shape[1:])
    groups = [list(range(parity, owners, 2)) for parity in range(2)]
    arrived = lax.all_to_all(
        paired, "store", split_axis=0, concat_axis=0, axis_index_groups=groups, tiled=True
    )
    crossed = lax.ppermute(arrived[:, 1], "store", [(s, s ^ 1) for s in range(owners)])
    return arrived, crossed


def in_hbm(array):
    return pltpu.with_memory_space_constraint(array, pltpu.HBM)


def swap_cores(part):
    return lax.ppermute(part, "tensor", [(0, 1), (1, 0)])


def shards(
    x_in,
    q_base,
    k_new,
    v_new,
    cache_k,
    cache_v,
    lengths,
    adapter_ids,
    slot_of,
    a_query,
    b_query,
    a_output,
    b_output,
):
    owners = lax.axis_size("store")
    rows = x_in.shape[1]
    width = x_in.shape[2]
    heads = cache_k.shape[2] // HD
    wide = width // heads
    adapt, rank = a_query.shape[1:]
    lanes = adapt * rank
    block = heads * CAP * STEPS
    items = owners * CAP * STEPS
    def flat(a_store):
        return jnp.transpose(a_store, (1, 2, 0)).reshape(lanes, a_store.shape[0])

    shape = jax.ShapeDtypeStruct
    small = pltpu.CompilerParams(vmem_limit_bytes=16 * 1024 * 1024)

    sent = shape((owners, block, wide), BF16)
    meta, blocks, a_near, b_near = pl.pallas_call(
        functools.partial(dispatch_kernel, owners, heads, adapt, rank),
        out_shape=[
            shape((3 * rows + owners * CAP,), I32),
            shape((owners, block, wide + lanes), BF16),
            pltpu.VMEM((lanes, width), BF16),
            pltpu.VMEM((lanes, width), BF16),
        ],
        in_specs=[HBM] * 6,
        out_specs=[SMEM] + [VMEM] * 3,
        scratch_shapes=[
            pltpu.SMEM((owners * CAP,), I32),
            pltpu.SMEM(adapter_ids.shape, I32),
            pltpu.SMEM(slot_of.shape, I32),
            pltpu.SMEM(lengths.shape, I32),
            pltpu.VMEM(x_in.shape, BF16),
            pltpu.SemaphoreType.DMA((6,)),
        ],
        compiler_params=small,
        name="dispatch",
    )(
        *map(in_hbm, (adapter_ids, slot_of, lengths, x_in, flat(a_query))),
        in_hbm(b_query.reshape(lanes, width)),
    )

    arrived = exchange(blocks)
    part, mask = pl.pallas_call(
        functools.partial(project_kernel, owners, heads, wide, True),
        out_shape=[shape((items, lanes), F32)] * 2,
        in_specs=[VMEM] * 3,
        out_specs=[VMEM] * 2,
        compiler_params=small,
        name="project_query",
    )(a_near, *arrived)

    def expand(part, b_store, name):
        return pl.pallas_call(
            functools.partial(expand_kernel, owners, heads, wide),
            out_shape=sent,
            in_specs=[VMEM] * 3,
            out_specs=VMEM,
            compiler_params=small,
            name=name,
        )(part, swap_cores(part), b_store)

    returned = exchange(expand(part, b_near, "expand_query"))

    attn_out, outgoing = pl.pallas_call(
        functools.partial(attend_kernel, owners, heads),
        out_shape=[shape((STEPS, rows, width), BF16), sent],
        in_specs=[SMEM] + [HBM] * 5 + [VMEM] * 2,
        out_specs=[HBM, VMEM],
        scratch_shapes=[
            pltpu.VMEM(q_base.shape, BF16),
            pltpu.VMEM((CHUNK, heads * HD), BF16),
            pltpu.VMEM((CHUNK, heads * HD), BF16),
            pltpu.VMEM(cache_k.shape, BF16),
            pltpu.VMEM(cache_v.shape, BF16),
            pltpu.VMEM((STEPS * wide // HD * heads, heads * HD), BF16),
            pltpu.VMEM((rows * STEPS * heads, wide), F32),
            pltpu.VMEM((rows * STEPS * heads, wide), F32),
            pltpu.SemaphoreType.DMA((rows,)),
            pltpu.SemaphoreType.DMA((rows,)),
            pltpu.SemaphoreType.DMA((1 + 2 * STEPS,)),
        ],
        compiler_params=pltpu.CompilerParams(vmem_limit_bytes=32 * 1024 * 1024),
        name="attend",
    )(meta, *map(in_hbm, (q_base, k_new, v_new, cache_k, cache_v)), *returned)

    arrived = exchange(outgoing)
    part = pl.pallas_call(
        functools.partial(project_kernel, owners, heads, wide, False),
        out_shape=shape((items, lanes), F32),
        in_specs=[VMEM] * 4,
        out_specs=VMEM,
        compiler_params=small,
        name="project_output",
    )(flat(a_output), *arrived, mask)
    returned = exchange(expand(part, b_output.reshape(lanes, width), "expand_output"))
    adapter_out = pl.pallas_call(
        functools.partial(collect_kernel, owners, heads),
        out_shape=shape((STEPS, rows, width), BF16),
        in_specs=[SMEM] + [VMEM] * 2,
        out_specs=HBM,
        scratch_shapes=[
            pltpu.VMEM((STEPS, rows, width), BF16),
            pltpu.SemaphoreType.DMA((heads,)),
        ],
        compiler_params=small,
        name="collect",
    )(meta, *returned)
    return (attn_out, adapter_out)


def solution(mesh):
    in_specs = (
        P(None, ("parts", "store"), "tensor"),
        P(None, ("parts", "store"), "tensor"),
        P(None, ("parts", "store"), "tensor"),
        P(None, ("parts", "store"), "tensor"),
        P(("parts", "store"), None, "tensor"),
        P(("parts", "store"), None, "tensor"),
        P(("parts", "store")),
        P(("parts", "store")),
        P("parts"),
        P(None, "store", None),
        P("store", None, "tensor"),
        P(None, "store", None),
        P("store", None, "tensor"),
    )
    out_specs = (P(None, ("parts", "store"), "tensor"), P(None, ("parts", "store"), "tensor"))
    return jax.shard_map(shards, mesh=mesh, in_specs=in_specs, out_specs=out_specs, check_vma=False)
```

```python
import functools
import math

import jax
import jax.numpy as jnp
from jax import lax
from jax.experimental import pallas as pl
from jax.experimental.pallas import tpu as pltpu
from jax.sharding import PartitionSpec as P

HD = 128
CAP = 2
STEPS = 2
CHUNK = 128
QUAD = 4
BF16 = jnp.bfloat16
F32 = jnp.float32
I32 = jnp.int32
VMEM = pl.BlockSpec(memory_space=pltpu.VMEM)
SMEM = pl.BlockSpec(memory_space=pltpu.SMEM)
HBM = pl.BlockSpec(memory_space=pltpu.HBM)


def iota(shape, dim):
    return lax.broadcasted_iota(I32, shape, dim)


def over(x, n):
    return lax.shift_right_logical(x, jnp.full_like(x, n.bit_length() - 1)) if n & (n - 1) == 0 else x // n


def rest(x, n):
    return x & (n - 1) if n & (n - 1) == 0 else x % n


def one_hot(hits):
    return jnp.where(hits, 1.0, 0.0).astype(BF16)


def stacked(ref, heads, wide):
    return jnp.concatenate(
        [ref[s, :, c * wide : (c + 1) * wide] for c in range(heads) for s in range(STEPS)], axis=0
    )


def pack_matrix(meta, owners, heads, rows, by_row):
    items = CAP * STEPS
    block = heads * items
    shape = (block, heads * STEPS * rows)
    at = iota(shape, 0)
    col = iota(shape, 1)
    head_step = over(at, items) * STEPS + rest(at, STEPS)
    offset = col - (head_step if by_row else head_step * rows)
    factor = heads * STEPS if by_row else 1
    first = rest(over(at, STEPS), CAP) == 0
    if not by_row:
        offset = jnp.where((offset >= 0) & (offset < rows), offset, -1)
    parts = []
    for i in range(owners):
        here = [meta[rows + i * CAP + k] for k in range(CAP)]
        spots = [jnp.where(h >= 0, h * factor, -rows * factor * heads * STEPS * 2) for h in here]
        parts.append(one_hot(offset == jnp.where(first, spots[0], spots[1])))
    return jnp.concatenate(parts, axis=0)


def unpack_matrix(meta, owners, heads, rows, by_row):
    items = CAP * STEPS
    block = heads * items
    pairs = heads * STEPS
    spots = [over(meta[r], CAP) * block + rest(meta[r], CAP) * STEPS for r in range(rows)]
    if by_row:
        shape = (pairs, owners * block)
        at = iota(shape, 0)
        col = iota(shape, 1) - (over(at, STEPS) * items + rest(at, STEPS))
        return jnp.concatenate([one_hot(col == spots[r]) for r in range(rows)], axis=0)
    shape = (rows, owners * block)
    at = iota(shape, 0)
    col = iota(shape, 1)
    spot = jnp.zeros(shape, I32)
    for r in range(rows):
        spot = jnp.where(at == r, spots[r], spot)
    offset = col - spot
    return jnp.concatenate(
        [one_hot(offset == c * items + s) for c in range(heads) for s in range(STEPS)], axis=0
    )


def by_row_matrix(heads, rows):
    pairs = heads * STEPS
    shape = (pairs * rows, pairs * rows)
    at = iota(shape, 0)
    return one_hot(iota(shape, 1) == rest(at, pairs) * rows + over(at, pairs))


def by_pair_matrix(heads, rows):
    pairs = heads * STEPS
    shape = (pairs * rows, pairs * rows)
    at = iota(shape, 0)
    return one_hot(iota(shape, 1) == rest(at, rows) * pairs + over(at, rows))


def regroup_matrix(owners, heads):
    items = CAP * STEPS
    total = owners * heads * items
    at = iota((total, total), 0)
    head = over(at, owners * items)
    owner = rest(over(at, items), owners)
    return one_hot(
        iota((total, total), 1) == owner * (heads * items) + head * items + rest(at, items)
    )


def ungroup_matrix(owners, heads):
    items = CAP * STEPS
    total = owners * heads * items
    at = iota((total, total), 0)
    owner = over(at, heads * items)
    head = rest(over(at, items), heads)
    return one_hot(
        iota((total, total), 1) == head * (owners * items) + owner * items + rest(at, items)
    )


def exact(matrix, values):
    return jnp.dot(matrix, values, preferred_element_type=F32).astype(BF16)


def dispatch_kernel(
    owners,
    heads,
    adapt,
    rank,
    ids_hbm,
    slot_of_hbm,
    lengths_hbm,
    x_hbm,
    a_hbm,
    b_hbm,
    meta,
    blocks,
    a_out,
    b_out,
    slot_at,
    ids,
    slot_of,
    lengths,
    x_ref,
    sems,
):
    width = x_hbm.shape[2]
    start = pl.multiple_of(lax.axis_index("tensor") * width, width)
    pairs = (
        (ids_hbm, ids),
        (slot_of_hbm, slot_of),
        (lengths_hbm, lengths),
        (x_hbm, x_ref),
        (a_hbm.at[:, pl.ds(start, width)], a_out),
        (b_hbm, b_out),
    )
    copies = [pltpu.make_async_copy(a, b, sems.at[k]) for k, (a, b) in enumerate(pairs)]
    for copy in copies:
        copy.start()
    rows = x_ref.shape[1]
    wide = x_ref.shape[2] // heads
    for copy in copies[:3]:
        copy.wait()
    me = lax.axis_index("store")
    row_at = rows
    order = rows + owners * CAP
    spans = order + rows
    for p in range(owners * CAP):
        meta[row_at + p] = -1
        slot_at[p] = -1
    for r in range(rows):
        slot = slot_of[ids[r]]
        first = (over(slot, adapt) ^ me) * CAP
        place = first + jnp.where(meta[row_at + first] >= 0, 1, 0)
        meta[row_at + place] = r
        slot_at[place] = rest(slot, adapt)
        meta[r] = place
    sizes = [lengths[r] for r in range(rows)]
    for r in range(rows):
        ahead = jnp.int32(0)
        for q in range(rows):
            if q != r:
                shorter = sizes[q] <= sizes[r] if q < r else sizes[q] < sizes[r]
                ahead = ahead + jnp.where(shorter, 1, 0)
        meta[order + ahead] = r
        meta[spans + r] = sizes[r]
    items = CAP * STEPS
    block = heads * items
    copies[3].wait()
    packed = exact(pack_matrix(meta, owners, heads, rows, False), stacked(x_ref, heads, wide))
    at = iota((block, adapt * rank), 0)
    lane_slot = over(iota((block, adapt * rank), 1), rank)
    first = rest(over(at, STEPS), CAP) == 0
    for i in range(owners):
        blocks[i, :, :wide] = packed[i * block : (i + 1) * block]
        slot = jnp.where(first, slot_at[i * CAP], slot_at[i * CAP + 1])
        blocks[i, :, wide:] = one_hot(lane_slot == slot)
    for copy in copies[4:]:
        copy.wait()


def project_kernel(owners, heads, wide, first, a_ref, blocks, *refs):
    core = lax.axis_index("tensor") if a_ref.shape[1] > heads * wide else 0
    if first:
        part_ref, mask_ref = refs
    else:
        mask_in, part_ref = refs
    grouped = regroup_matrix(owners, heads)
    items = owners * CAP * STEPS
    arrived = jnp.concatenate([blocks[i, :, :wide] for i in range(owners)], axis=0)
    arrived = exact(grouped, arrived)
    if first:
        masks = jnp.concatenate([blocks[i, :, wide:] for i in range(owners)], axis=0)
        mask = jnp.dot(grouped[:items], masks, preferred_element_type=F32)
        mask_ref[...] = mask
    else:
        mask = mask_in[...]
    total = jnp.zeros(mask.shape, F32)
    for c in range(heads):
        total = total + lax.dot_general(
            arrived[c * items : (c + 1) * items],
            a_ref[:, pl.ds(pl.multiple_of(core * (heads * wide) + c * wide, wide), wide)],
            (((1,), (1,)), ((), ())),
            preferred_element_type=F32,
        )
    part_ref[...] = total * mask


def expand_kernel(owners, heads, wide, mine, other, b_ref, blocks):
    low_rank = (mine[...] + other[...]).astype(BF16)
    pieces = []
    for c in range(heads):
        product = jnp.dot(
            low_rank, b_ref[:, c * wide : (c + 1) * wide], preferred_element_type=F32
        )
        pieces.append((2.0 * product).astype(BF16))
    back = exact(ungroup_matrix(owners, heads), jnp.concatenate(pieces, axis=0))
    block = heads * CAP * STEPS
    for i in range(owners):
        blocks[i] = back[i * block : (i + 1) * block]


def quads(row_of, span_of, rows, sizes, action):
    def body(quad, carry):
        amount = over(span_of(row_of(quad * QUAD + QUAD - 1)) + (CHUNK - 1), CHUNK)
        for size in range(1, sizes + 1):

            @pl.when(amount == size)
            def _():
                action([row_of(quad * QUAD + j) for j in range(QUAD)], size)

        return carry

    lax.fori_loop(0, rows // QUAD, body, 0)


def attend_kernel(
    owners,
    heads,
    meta,
    q_hbm,
    kn_hbm,
    vn_hbm,
    k_hbm,
    v_hbm,
    blocks,
    out_hbm,
    outgoing,
    q_ref,
    kn_ref,
    vn_ref,
    k_ref,
    v_ref,
    mask_ref,
    q_buf,
    o_buf,
    k_sem,
    v_sem,
    sems,
):
    rows = q_hbm.shape[1]
    wide = q_hbm.shape[2] // heads
    groups = wide // HD
    pairs = heads * STEPS
    total = groups * pairs
    width = heads * HD
    fresh_rows = STEPS * rows

    singles = [pltpu.make_async_copy(q_hbm, q_ref, sems.at[0])]
    for k, (source, target) in enumerate(((kn_hbm, kn_ref), (vn_hbm, vn_ref))):
        for t in range(STEPS):
            part = target.at[pl.ds(t * rows, rows)]
            singles.append(pltpu.make_async_copy(source.at[t], part, sems.at[1 + k * STEPS + t]))
    for copy in singles:
        copy.start()

    def row_of(place):
        return meta[rows + owners * CAP + place]

    def span_of(row):
        return meta[2 * rows + owners * CAP + row]

    def copies(row, size):
        part = pl.ds(0, size * CHUNK)
        return (
            pltpu.make_async_copy(k_hbm.at[row, part], k_ref.at[row, part], k_sem.at[row]),
            pltpu.make_async_copy(v_hbm.at[row, part], v_ref.at[row, part], v_sem.at[row]),
        )

    def begin(rows_in, size):
        for row in rows_in:
            for copy in copies(row, size):
                copy.start()

    chunks = k_hbm.shape[1] // CHUNK
    quads(row_of, span_of, rows, chunks, begin)

    head_at = rest(over(iota((total, width), 0), STEPS), heads)
    mask_ref[...] = one_hot(head_at == over(iota((total, width), 1), HD))
    head_own = rest(over(iota((QUAD * total, HD), 0), STEPS), heads)
    blank = jnp.zeros((CHUNK - fresh_rows, width), BF16)
    kn_ref[fresh_rows:, :] = blank
    vn_ref[fresh_rows:, :] = blank

    delta = jnp.dot(
        unpack_matrix(meta, owners, heads, rows, True),
        jnp.concatenate([blocks[i] for i in range(owners)], axis=0),
        preferred_element_type=F32,
    )
    by_row = by_row_matrix(heads, rows)
    for copy in singles:
        copy.wait()
    base = jnp.dot(by_row, stacked(q_ref, heads, wide), preferred_element_type=F32)
    q_buf[...] = base + delta

    factor = math.log2(math.e) / math.sqrt(HD)
    fresh_shape = (total, CHUNK)
    fresh_at = iota(fresh_shape, 1)
    fresh_step = over(fresh_at, rows)
    fresh_row = jnp.where(fresh_step <= rest(iota(fresh_shape, 0), STEPS), rest(fresh_at, rows), rows)
    contract = (((1,), (1,)), ((), ()))

    def attend(rows_in, size):
        for row in rows_in:
            for copy in copies(row, size):
                copy.wait()
        extent = size * CHUNK
        position = iota((total, extent), 1)
        starts = [pl.multiple_of(row * pairs, pairs) for row in rows_in]
        spreads = []
        for start in starts:
            flat = q_buf[pl.ds(start, pairs), :]
            one = jnp.concatenate(
                [flat[:, j * HD : (j + 1) * HD] for j in range(groups)], axis=0
            ).astype(BF16)
            spreads.append(jnp.concatenate([one] * heads, axis=1) * mask_ref[...])
        cached = [
            lax.dot_general(spread, k_ref[row, :extent, :], contract, preferred_element_type=F32)
            for row, spread in zip(rows_in, spreads)
        ]
        fresh = lax.dot_general(
            jnp.concatenate(spreads, axis=0), kn_ref[...], contract, preferred_element_type=F32
        )
        scores = jnp.concatenate(
            [
                jnp.concatenate(
                    [
                        jnp.where(position < span_of(row), cached[k], -jnp.inf),
                        jnp.where(fresh_row == row, fresh[k * total : (k + 1) * total], -jnp.inf),
                    ],
                    axis=1,
                )
                for k, row in enumerate(rows_in)
            ],
            axis=0,
        )
        top = jnp.max(scores, axis=1, keepdims=True)
        weights = jnp.exp2((scores - top) * factor)
        share = 1.0 / jnp.sum(weights, axis=1, keepdims=True)
        weights = weights.astype(BF16)
        mixed = jnp.dot(weights[:, extent:], vn_ref[...], preferred_element_type=F32)
        mixed = mixed + jnp.concatenate(
            [
                jnp.dot(
                    weights[k * total : (k + 1) * total, :extent],
                    v_ref[row, :extent, :],
                    preferred_element_type=F32,
                )
                for k, row in enumerate(rows_in)
            ],
            axis=0,
        )
        own = mixed[:, :HD]
        for c in range(1, heads):
            own = jnp.where(head_own == c, mixed[:, c * HD : (c + 1) * HD], own)
        own = own * share
        for k, start in enumerate(starts):
            one = own[k * total : (k + 1) * total]
            o_buf[pl.ds(start, pairs), :] = jnp.concatenate(
                [one[j * pairs : (j + 1) * pairs] for j in range(groups)], axis=1
            )

    quads(row_of, span_of, rows, chunks, attend)

    mixed = o_buf[...].astype(BF16)
    final = exact(by_pair_matrix(heads, rows), mixed)
    for c in range(heads):
        for s in range(STEPS):
            at = (c * STEPS + s) * rows
            q_ref[s, :, c * wide : (c + 1) * wide] = final[at : at + rows]
    result = pltpu.make_async_copy(q_ref, out_hbm, sems.at[0])
    result.start()
    packed = exact(pack_matrix(meta, owners, heads, rows, True), mixed)
    block = heads * CAP * STEPS
    for i in range(owners):
        outgoing[i] = packed[i * block : (i + 1) * block]
    result.wait()


def collect_kernel(owners, heads, meta, blocks, out_hbm, out_ref, sems):
    rows = out_ref.shape[1]
    wide = out_ref.shape[2] // heads
    span = STEPS * rows
    arrived = jnp.concatenate([blocks[i] for i in range(owners)], axis=0)
    spread = unpack_matrix(meta, owners, heads, rows, False)
    copies = []
    for c in range(heads):
        values = exact(spread[c * span : (c + 1) * span], arrived)
        for s in range(STEPS):
            out_ref[s, :, c * wide : (c + 1) * wide] = values[s * rows : (s + 1) * rows]
        part = (slice(None), slice(None), pl.ds(c * wide, wide))
        copies.append(pltpu.make_async_copy(out_ref.at[part], out_hbm.at[part], sems.at[c]))
        copies[-1].start()
    for copy in copies:
        copy.wait()


def exchange(blocks):
    owners = blocks.shape[0]
    arrived = [blocks[0]]
    for i in range(1, owners):
        arrived.append(lax.ppermute(blocks[i], "store", [(s, s ^ i) for s in range(owners)]))
    return jnp.stack(arrived)


def in_hbm(array):
    return pltpu.with_memory_space_constraint(array, pltpu.HBM)


def swap_cores(part):
    return lax.ppermute(part, "tensor", [(0, 1), (1, 0)])


def shards(
    x_in,
    q_base,
    k_new,
    v_new,
    cache_k,
    cache_v,
    lengths,
    adapter_ids,
    slot_of,
    a_query,
    b_query,
    a_output,
    b_output,
):
    owners = lax.axis_size("store")
    rows = x_in.shape[1]
    width = x_in.shape[2]
    heads = cache_k.shape[2] // HD
    wide = width // heads
    adapt, rank = a_query.shape[1:]
    lanes = adapt * rank
    block = heads * CAP * STEPS
    items = owners * CAP * STEPS
    def flat(a_store):
        return jnp.transpose(a_store, (1, 2, 0)).reshape(lanes, a_store.shape[0])

    shape = jax.ShapeDtypeStruct
    small = pltpu.CompilerParams(vmem_limit_bytes=16 * 1024 * 1024)

    sent = shape((owners, block, wide), BF16)
    meta, blocks, a_near, b_near = pl.pallas_call(
        functools.partial(dispatch_kernel, owners, heads, adapt, rank),
        out_shape=[
            shape((3 * rows + owners * CAP,), I32),
            shape((owners, block, wide + lanes), BF16),
            pltpu.VMEM((lanes, width), BF16),
            pltpu.VMEM((lanes, width), BF16),
        ],
        in_specs=[HBM] * 6,
        out_specs=[SMEM] + [VMEM] * 3,
        scratch_shapes=[
            pltpu.SMEM((owners * CAP,), I32),
            pltpu.SMEM(adapter_ids.shape, I32),
            pltpu.SMEM(slot_of.shape, I32),
            pltpu.SMEM(lengths.shape, I32),
            pltpu.VMEM(x_in.shape, BF16),
            pltpu.SemaphoreType.DMA((6,)),
        ],
        compiler_params=small,
        name="dispatch",
    )(
        *map(in_hbm, (adapter_ids, slot_of, lengths, x_in, flat(a_query))),
        in_hbm(b_query.reshape(lanes, width)),
    )

    arrived = exchange(blocks)
    part, mask = pl.pallas_call(
        functools.partial(project_kernel, owners, heads, wide, True),
        out_shape=[shape((items, lanes), F32)] * 2,
        in_specs=[VMEM] * 2,
        out_specs=[VMEM] * 2,
        compiler_params=small,
        name="project_query",
    )(a_near, arrived)

    def expand(part, b_store, name):
        return pl.pallas_call(
            functools.partial(expand_kernel, owners, heads, wide),
            out_shape=sent,
            in_specs=[VMEM] * 3,
            out_specs=VMEM,
            compiler_params=small,
            name=name,
        )(part, swap_cores(part), b_store)

    returned = exchange(expand(part, b_near, "expand_query"))

    attn_out, outgoing = pl.pallas_call(
        functools.partial(attend_kernel, owners, heads),
        out_shape=[shape((STEPS, rows, width), BF16), sent],
        in_specs=[SMEM] + [HBM] * 5 + [VMEM],
        out_specs=[HBM, VMEM],
        scratch_shapes=[
            pltpu.VMEM(q_base.shape, BF16),
            pltpu.VMEM((CHUNK, heads * HD), BF16),
            pltpu.VMEM((CHUNK, heads * HD), BF16),
            pltpu.VMEM(cache_k.shape, BF16),
            pltpu.VMEM(cache_v.shape, BF16),
            pltpu.VMEM((STEPS * wide // HD * heads, heads * HD), BF16),
            pltpu.VMEM((rows * STEPS * heads, wide), F32),
            pltpu.VMEM((rows * STEPS * heads, wide), F32),
            pltpu.SemaphoreType.DMA((rows,)),
            pltpu.SemaphoreType.DMA((rows,)),
            pltpu.SemaphoreType.DMA((1 + 2 * STEPS,)),
        ],
        compiler_params=pltpu.CompilerParams(vmem_limit_bytes=32 * 1024 * 1024),
        name="attend",
    )(meta, *map(in_hbm, (q_base, k_new, v_new, cache_k, cache_v)), returned)

    arrived = exchange(outgoing)
    part = pl.pallas_call(
        functools.partial(project_kernel, owners, heads, wide, False),
        out_shape=shape((items, lanes), F32),
        in_specs=[VMEM] * 3,
        out_specs=VMEM,
        compiler_params=small,
        name="project_output",
    )(flat(a_output), arrived, mask)
    returned = exchange(expand(part, b_output.reshape(lanes, width), "expand_output"))
    adapter_out = pl.pallas_call(
        functools.partial(collect_kernel, owners, heads),
        out_shape=shape((STEPS, rows, width), BF16),
        in_specs=[SMEM, VMEM],
        out_specs=HBM,
        scratch_shapes=[
            pltpu.VMEM((STEPS, rows, width), BF16),
            pltpu.SemaphoreType.DMA((heads,)),
        ],
        compiler_params=small,
        name="collect",
    )(meta, returned)
    return (attn_out, adapter_out)


def solution(mesh):
    in_specs = (
        P(None, ("parts", "store"), "tensor"),
        P(None, ("parts", "store"), "tensor"),
        P(None, ("parts", "store"), "tensor"),
        P(None, ("parts", "store"), "tensor"),
        P(("parts", "store"), None, "tensor"),
        P(("parts", "store"), None, "tensor"),
        P(("parts", "store")),
        P(("parts", "store")),
        P("parts"),
        P(None, "store", None),
        P("store", None, "tensor"),
        P(None, "store", None),
        P("store", None, "tensor"),
    )
    out_specs = (P(None, ("parts", "store"), "tensor"), P(None, ("parts", "store"), "tensor"))
    return jax.shard_map(shards, mesh=mesh, in_specs=in_specs, out_specs=out_specs, check_vma=False)
```

```python
import functools
import math

import jax
import jax.numpy as jnp
from jax import lax
from jax.experimental import pallas as pl
from jax.experimental.pallas import tpu as pltpu
from jax.sharding import PartitionSpec as P

HD = 128
CAP = 2
STEPS = 2
CHUNK = 128
BF16 = jnp.bfloat16
F32 = jnp.float32
I32 = jnp.int32
VMEM = pl.BlockSpec(memory_space=pltpu.VMEM)
SMEM = pl.BlockSpec(memory_space=pltpu.SMEM)
HBM = pl.BlockSpec(memory_space=pltpu.HBM)


def iota(shape, dim):
    return lax.broadcasted_iota(I32, shape, dim)


def over(x, n):
    return lax.shift_right_logical(x, jnp.full_like(x, n.bit_length() - 1)) if n & (n - 1) == 0 else x // n


def rest(x, n):
    return x & (n - 1) if n & (n - 1) == 0 else x % n


def one_hot(hits):
    return jnp.where(hits, 1.0, 0.0).astype(BF16)


def stacked(ref, heads, wide):
    return jnp.concatenate(
        [ref[s, :, c * wide : (c + 1) * wide] for c in range(heads) for s in range(STEPS)], axis=0
    )


def pack_matrix(meta, owners, heads, rows, by_row):
    items = CAP * STEPS
    block = heads * items
    shape = (block, heads * STEPS * rows)
    at = iota(shape, 0)
    col = iota(shape, 1)
    head_step = over(at, items) * STEPS + rest(at, STEPS)
    offset = col - (head_step if by_row else head_step * rows)
    factor = heads * STEPS if by_row else 1
    first = rest(over(at, STEPS), CAP) == 0
    if not by_row:
        offset = jnp.where((offset >= 0) & (offset < rows), offset, -1)
    parts = []
    for i in range(owners):
        here = [meta[rows + i * CAP + k] for k in range(CAP)]
        spots = [jnp.where(h >= 0, h * factor, -rows * factor * heads * STEPS * 2) for h in here]
        parts.append(one_hot(offset == jnp.where(first, spots[0], spots[1])))
    return jnp.concatenate(parts, axis=0)


def unpack_matrix(meta, owners, heads, rows, by_row):
    items = CAP * STEPS
    block = heads * items
    pairs = heads * STEPS
    spots = [over(meta[r], CAP) * block + rest(meta[r], CAP) * STEPS for r in range(rows)]
    if by_row:
        shape = (pairs, owners * block)
        at = iota(shape, 0)
        col = iota(shape, 1) - (over(at, STEPS) * items + rest(at, STEPS))
        return jnp.concatenate([one_hot(col == spots[r]) for r in range(rows)], axis=0)
    shape = (rows, owners * block)
    at = iota(shape, 0)
    col = iota(shape, 1)
    spot = jnp.zeros(shape, I32)
    for r in range(rows):
        spot = jnp.where(at == r, spots[r], spot)
    offset = col - spot
    return jnp.concatenate(
        [one_hot(offset == c * items + s) for c in range(heads) for s in range(STEPS)], axis=0
    )


def by_row_matrix(heads, rows):
    pairs = heads * STEPS
    shape = (pairs * rows, pairs * rows)
    at = iota(shape, 0)
    return one_hot(iota(shape, 1) == rest(at, pairs) * rows + over(at, pairs))


def by_pair_matrix(heads, rows):
    pairs = heads * STEPS
    shape = (pairs * rows, pairs * rows)
    at = iota(shape, 0)
    return one_hot(iota(shape, 1) == rest(at, rows) * pairs + over(at, rows))


def regroup_matrix(owners, heads):
    items = CAP * STEPS
    total = owners * heads * items
    at = iota((total, total), 0)
    head = over(at, owners * items)
    owner = rest(over(at, items), owners)
    return one_hot(
        iota((total, total), 1) == owner * (heads * items) + head * items + rest(at, items)
    )


def ungroup_matrix(owners, heads):
    items = CAP * STEPS
    total = owners * heads * items
    at = iota((total, total), 0)
    owner = over(at, heads * items)
    head = rest(over(at, items), heads)
    return one_hot(
        iota((total, total), 1) == head * (owners * items) + owner * items + rest(at, items)
    )


def exact(matrix, values):
    return jnp.dot(matrix, values, preferred_element_type=F32).astype(BF16)


def dispatch_kernel(
    owners,
    heads,
    adapt,
    rank,
    ids_hbm,
    slot_of_hbm,
    lengths_hbm,
    x_hbm,
    a_hbm,
    b_hbm,
    meta,
    blocks,
    a_out,
    b_out,
    slot_at,
    ids,
    slot_of,
    lengths,
    x_ref,
    sems,
):
    width = x_hbm.shape[2]
    start = pl.multiple_of(lax.axis_index("tensor") * width, width)
    pairs = (
        (ids_hbm, ids),
        (slot_of_hbm, slot_of),
        (lengths_hbm, lengths),
        (x_hbm, x_ref),
        (a_hbm.at[:, pl.ds(start, width)], a_out),
        (b_hbm, b_out),
    )
    copies = [pltpu.make_async_copy(a, b, sems.at[k]) for k, (a, b) in enumerate(pairs)]
    for copy in copies:
        copy.start()
    rows = x_ref.shape[1]
    wide = x_ref.shape[2] // heads
    for copy in copies[:3]:
        copy.wait()
    row_at = rows
    order = rows + owners * CAP
    spans = order + rows
    for p in range(owners * CAP):
        meta[row_at + p] = -1
        slot_at[p] = -1
    for r in range(rows):
        slot = slot_of[ids[r]]
        first = over(slot, adapt) * CAP
        place = first + jnp.where(meta[row_at + first] >= 0, 1, 0)
        meta[row_at + place] = r
        slot_at[place] = rest(slot, adapt)
        meta[r] = place
    items = CAP * STEPS
    block = heads * items
    copies[3].wait()
    packed = exact(pack_matrix(meta, owners, heads, rows, False), stacked(x_ref, heads, wide))
    at = iota((block, adapt * rank), 0)
    lane_slot = over(iota((block, adapt * rank), 1), rank)
    first = rest(over(at, STEPS), CAP) == 0
    for i in range(owners):
        blocks[i, :, :wide] = packed[i * block : (i + 1) * block]
        slot = jnp.where(first, slot_at[i * CAP], slot_at[i * CAP + 1])
        blocks[i, :, wide:] = one_hot(lane_slot == slot)
    sizes = [lengths[r] for r in range(rows)]
    for r in range(rows):
        ahead = jnp.int32(0)
        for q in range(rows):
            if q != r:
                shorter = sizes[q] <= sizes[r] if q < r else sizes[q] < sizes[r]
                ahead = ahead + jnp.where(shorter, 1, 0)
        meta[order + ahead] = r
        meta[spans + r] = sizes[r]
    for copy in copies[4:]:
        copy.wait()


def project_kernel(owners, heads, wide, first, a_ref, blocks, *refs):
    core = lax.axis_index("tensor") if a_ref.shape[1] > heads * wide else 0
    if first:
        part_ref, mask_ref = refs
    else:
        mask_in, part_ref = refs
    grouped = regroup_matrix(owners, heads)
    items = owners * CAP * STEPS
    arrived = jnp.concatenate([blocks[i, :, :wide] for i in range(owners)], axis=0)
    arrived = exact(grouped, arrived)
    if first:
        masks = jnp.concatenate([blocks[i, :, wide:] for i in range(owners)], axis=0)
        mask = jnp.dot(grouped[:items], masks, preferred_element_type=F32)
        mask_ref[...] = mask
    else:
        mask = mask_in[...]
    total = jnp.zeros(mask.shape, F32)
    for c in range(heads):
        total = total + lax.dot_general(
            arrived[c * items : (c + 1) * items],
            a_ref[:, pl.ds(pl.multiple_of(core * (heads * wide) + c * wide, wide), wide)],
            (((1,), (1,)), ((), ())),
            preferred_element_type=F32,
        )
    part_ref[...] = total * mask


def expand_kernel(owners, heads, wide, mine, other, b_ref, *refs):
    blocks = refs[-1]
    low_rank = (mine[...] + other[...]).astype(BF16)
    pieces = []
    for c in range(heads):
        product = jnp.dot(
            low_rank, b_ref[:, c * wide : (c + 1) * wide], preferred_element_type=F32
        )
        pieces.append((2.0 * product).astype(BF16))
    back = exact(ungroup_matrix(owners, heads), jnp.concatenate(pieces, axis=0))
    block = heads * CAP * STEPS
    for i in range(owners):
        blocks[i] = back[i * block : (i + 1) * block]


def in_groups(row_of, span_of, rows, sizes, action):
    at = 0
    for count in [rows // 2] + [rows // 4] * 2:
        group = [row_of(at + j) for j in range(count)]
        amount = over(span_of(group[-1]) + (CHUNK - 1), CHUNK)
        for size in range(1, sizes + 1):

            @pl.when(amount == size)
            def _():
                action(group, size)

        at += count


def attend_kernel(
    owners,
    heads,
    meta,
    q_hbm,
    kn_hbm,
    vn_hbm,
    k_hbm,
    v_hbm,
    blocks,
    mixed_out,
    outgoing,
    spread_out,
    q_ref,
    kn_ref,
    vn_ref,
    k_ref,
    v_ref,
    mask_ref,
    q_buf,
    o_buf,
    k_sem,
    v_sem,
    sems,
):
    rows = q_hbm.shape[1]
    wide = q_hbm.shape[2] // heads
    groups = wide // HD
    pairs = heads * STEPS
    total = groups * pairs
    width = heads * HD
    fresh_rows = STEPS * rows

    singles = [pltpu.make_async_copy(q_hbm, q_ref, sems.at[0])]
    for k, (source, target) in enumerate(((kn_hbm, kn_ref), (vn_hbm, vn_ref))):
        for t in range(STEPS):
            part = target.at[pl.ds(t * rows, rows)]
            singles.append(pltpu.make_async_copy(source.at[t], part, sems.at[1 + k * STEPS + t]))
    for copy in singles:
        copy.start()

    def row_of(place):
        return meta[rows + owners * CAP + place]

    def span_of(row):
        return meta[2 * rows + owners * CAP + row]

    def copies(row, size):
        part = pl.ds(0, size * CHUNK)
        return (
            pltpu.make_async_copy(k_hbm.at[row, part], k_ref.at[row, part], k_sem.at[row]),
            pltpu.make_async_copy(v_hbm.at[row, part], v_ref.at[row, part], v_sem.at[row]),
        )

    def begin(rows_in, size):
        for row in rows_in:
            for copy in copies(row, size):
                copy.start()

    chunks = k_hbm.shape[1] // CHUNK
    in_groups(row_of, span_of, rows, chunks, begin)

    head_at = rest(over(iota((total, width), 0), STEPS), heads)
    mask_ref[...] = one_hot(head_at == over(iota((total, width), 1), HD))
    head_own = rest(over(iota((total, HD), 0), STEPS), heads)
    blank = jnp.zeros((CHUNK - fresh_rows, width), BF16)
    kn_ref[fresh_rows:, :] = blank
    vn_ref[fresh_rows:, :] = blank

    gather = jnp.concatenate(
        [by_row_matrix(heads, rows), unpack_matrix(meta, owners, heads, rows, True)], axis=1
    )
    for copy in singles:
        copy.wait()
    sources = [stacked(q_ref, heads, wide)] + [blocks[i] for i in range(owners)]
    q_buf[...] = jnp.dot(gather, jnp.concatenate(sources, axis=0), preferred_element_type=F32)

    factor = math.log2(math.e) / math.sqrt(HD)
    fresh_shape = (total, CHUNK)
    fresh_at = iota(fresh_shape, 1)
    fresh_step = over(fresh_at, rows)
    fresh_row = jnp.where(fresh_step <= rest(iota(fresh_shape, 0), STEPS), rest(fresh_at, rows), rows)
    contract = (((1,), (1,)), ((), ()))

    def attend(rows_in, size):
        for row in rows_in:
            for copy in copies(row, size):
                copy.wait()
        extent = size * CHUNK
        position = iota((total, extent), 1)
        starts = [pl.multiple_of(row * pairs, pairs) for row in rows_in]
        spreads = []
        for start in starts:
            flat = q_buf[pl.ds(start, pairs), :]
            one = jnp.concatenate(
                [flat[:, j * HD : (j + 1) * HD] for j in range(groups)], axis=0
            ).astype(BF16)
            spreads.append(jnp.concatenate([one] * heads, axis=1) * mask_ref[...])
        scores = []
        for row, spread in zip(rows_in, spreads):
            keys = jnp.concatenate([k_ref[row, :extent, :], kn_ref[...]], axis=0)
            score = lax.dot_general(spread, keys, contract, preferred_element_type=F32)
            cached = jnp.where(position < span_of(row), score[:, :extent], -jnp.inf)
            fresh = jnp.where(fresh_row == row, score[:, extent:], -jnp.inf)
            scores.append(jnp.concatenate([cached, fresh], axis=1))
        tops = [jnp.max(score, axis=1, keepdims=True) for score in scores]
        weights = [jnp.exp2((score - top) * factor) for score, top in zip(scores, tops)]
        shares = [1.0 / jnp.sum(weight, axis=1, keepdims=True) for weight in weights]
        for row, start, weight, share in zip(rows_in, starts, weights, shares):
            values = jnp.concatenate([v_ref[row, :extent, :], vn_ref[...]], axis=0)
            mixed = jnp.dot(weight.astype(BF16), values, preferred_element_type=F32)
            own = mixed[:, :HD]
            for c in range(1, heads):
                own = jnp.where(head_own == c, mixed[:, c * HD : (c + 1) * HD], own)
            own = own * share
            o_buf[pl.ds(start, pairs), :] = jnp.concatenate(
                [own[j * pairs : (j + 1) * pairs] for j in range(groups)], axis=1
            )

    in_groups(row_of, span_of, rows, chunks, attend)

    mixed = o_buf[...].astype(BF16)
    mixed_out[...] = mixed
    packed = exact(pack_matrix(meta, owners, heads, rows, True), mixed)
    block = heads * CAP * STEPS
    for i in range(owners):
        outgoing[i] = packed[i * block : (i + 1) * block]
    spread_out[...] = unpack_matrix(meta, owners, heads, rows, False)


def write_out(matrix, values, heads, out_hbm, out_ref, sems):
    rows = out_ref.shape[1]
    wide = out_ref.shape[2] // heads
    span = STEPS * rows
    copies = []
    for c in range(heads):
        ordered = exact(matrix[c * span : (c + 1) * span], values)
        for s in range(STEPS):
            out_ref[s, :, c * wide : (c + 1) * wide] = ordered[s * rows : (s + 1) * rows]
        part = (slice(None), slice(None), pl.ds(c * wide, wide))
        copies.append(pltpu.make_async_copy(out_ref.at[part], out_hbm.at[part], sems.at[c]))
        copies[-1].start()
    for copy in copies:
        copy.wait()


def finish_kernel(heads, mixed, part, out_hbm, after, out_ref, sems):
    after[...] = part[: after.shape[0], :]
    matrix = by_pair_matrix(heads, out_ref.shape[1])
    write_out(matrix, mixed[...], heads, out_hbm, out_ref, sems)


def collect_kernel(owners, heads, spread, blocks, out_hbm, out_ref, sems):
    arrived = jnp.concatenate([blocks[i] for i in range(owners)], axis=0)
    write_out(spread, arrived, heads, out_hbm, out_ref, sems)


def exchange(blocks):
    return lax.all_to_all(blocks, "store", split_axis=0, concat_axis=0, tiled=True)


def in_hbm(array):
    return pltpu.with_memory_space_constraint(array, pltpu.HBM)


def swap_cores(part):
    return lax.ppermute(part, "tensor", [(0, 1), (1, 0)])


def shards(
    x_in,
    q_base,
    k_new,
    v_new,
    cache_k,
    cache_v,
    lengths,
    adapter_ids,
    slot_of,
    a_query,
    b_query,
    a_output,
    b_output,
):
    owners = lax.axis_size("store")
    rows = x_in.shape[1]
    width = x_in.shape[2]
    heads = cache_k.shape[2] // HD
    wide = width // heads
    adapt, rank = a_query.shape[1:]
    lanes = adapt * rank
    block = heads * CAP * STEPS
    items = owners * CAP * STEPS
    def flat(a_store):
        return jnp.transpose(a_store, (1, 2, 0)).reshape(lanes, a_store.shape[0])

    shape = jax.ShapeDtypeStruct
    small = pltpu.CompilerParams(vmem_limit_bytes=16 * 1024 * 1024)

    sent = shape((owners, block, wide), BF16)
    meta, blocks, a_near, b_near = pl.pallas_call(
        functools.partial(dispatch_kernel, owners, heads, adapt, rank),
        out_shape=[
            shape((3 * rows + owners * CAP,), I32),
            shape((owners, block, wide + lanes), BF16),
            pltpu.VMEM((lanes, width), BF16),
            pltpu.VMEM((lanes, width), BF16),
        ],
        in_specs=[HBM] * 6,
        out_specs=[SMEM] + [VMEM] * 3,
        scratch_shapes=[
            pltpu.SMEM((owners * CAP,), I32),
            pltpu.SMEM(adapter_ids.shape, I32),
            pltpu.SMEM(slot_of.shape, I32),
            pltpu.SMEM(lengths.shape, I32),
            pltpu.VMEM(x_in.shape, BF16),
            pltpu.SemaphoreType.DMA((6,)),
        ],
        compiler_params=small,
        name="dispatch",
    )(
        *map(in_hbm, (adapter_ids, slot_of, lengths, x_in, flat(a_query))),
        in_hbm(b_query.reshape(lanes, width)),
    )

    arrived = exchange(blocks)
    part, mask = pl.pallas_call(
        functools.partial(project_kernel, owners, heads, wide, True),
        out_shape=[shape((items, lanes), F32)] * 2,
        in_specs=[VMEM] * 2,
        out_specs=[VMEM] * 2,
        compiler_params=small,
        name="project_query",
    )(a_near, arrived)

    def expand(part, other, b_store, name, *after):
        return pl.pallas_call(
            functools.partial(expand_kernel, owners, heads, wide),
            out_shape=sent,
            in_specs=[VMEM] * (3 + len(after)),
            out_specs=VMEM,
            compiler_params=small,
            name=name,
        )(part, other, b_store, *after)

    returned = exchange(expand(part, swap_cores(part), b_near, "expand_query"))

    mixed, outgoing, spread = pl.pallas_call(
        functools.partial(attend_kernel, owners, heads),
        out_shape=[
            shape((rows * STEPS * heads, wide), BF16),
            sent,
            shape((rows * STEPS * heads, owners * block), BF16),
        ],
        in_specs=[SMEM] + [HBM] * 5 + [VMEM],
        out_specs=[VMEM] * 3,
        scratch_shapes=[
            pltpu.VMEM(q_base.shape, BF16),
            pltpu.VMEM((CHUNK, heads * HD), BF16),
            pltpu.VMEM((CHUNK, heads * HD), BF16),
            pltpu.VMEM(cache_k.shape, BF16),
            pltpu.VMEM(cache_v.shape, BF16),
            pltpu.VMEM((STEPS * wide // HD * heads, heads * HD), BF16),
            pltpu.VMEM((rows * STEPS * heads, wide), F32),
            pltpu.VMEM((rows * STEPS * heads, wide), F32),
            pltpu.SemaphoreType.DMA((rows,)),
            pltpu.SemaphoreType.DMA((rows,)),
            pltpu.SemaphoreType.DMA((1 + 2 * STEPS,)),
        ],
        compiler_params=pltpu.CompilerParams(vmem_limit_bytes=32 * 1024 * 1024),
        name="attend",
    )(meta, *map(in_hbm, (q_base, k_new, v_new, cache_k, cache_v)), returned)

    arrived = exchange(outgoing)
    part = pl.pallas_call(
        functools.partial(project_kernel, owners, heads, wide, False),
        out_shape=shape((items, lanes), F32),
        in_specs=[VMEM] * 3,
        out_specs=VMEM,
        compiler_params=small,
        name="project_output",
    )(flat(a_output), arrived, mask)
    ordered = dict(
        scratch_shapes=[
            pltpu.VMEM((STEPS, rows, width), BF16),
            pltpu.SemaphoreType.DMA((heads,)),
        ],
        compiler_params=small,
    )
    other = swap_cores(part)
    attn_out, after = pl.pallas_call(
        functools.partial(finish_kernel, heads),
        out_shape=[shape((STEPS, rows, width), BF16), shape((8, lanes), F32)],
        in_specs=[VMEM] * 2,
        out_specs=[HBM, VMEM],
        name="finish",
        **ordered,
    )(mixed, part)
    returned = exchange(
        expand(part, other, b_output.reshape(lanes, width), "expand_output", after)
    )
    adapter_out = pl.pallas_call(
        functools.partial(collect_kernel, owners, heads),
        out_shape=shape((STEPS, rows, width), BF16),
        in_specs=[VMEM] * 2,
        out_specs=HBM,
        name="collect",
        **ordered,
    )(spread, returned)
    return (attn_out, adapter_out)


def solution(mesh):
    in_specs = (
        P(None, ("parts", "store"), "tensor"),
        P(None, ("parts", "store"), "tensor"),
        P(None, ("parts", "store"), "tensor"),
        P(None, ("parts", "store"), "tensor"),
        P(("parts", "store"), None, "tensor"),
        P(("parts", "store"), None, "tensor"),
        P(("parts", "store")),
        P(("parts", "store")),
        P("parts"),
        P(None, "store", None),
        P("store", None, "tensor"),
        P(None, "store", None),
        P("store", None, "tensor"),
    )
    out_specs = (P(None, ("parts", "store"), "tensor"), P(None, ("parts", "store"), "tensor"))
    return jax.shard_map(shards, mesh=mesh, in_specs=in_specs, out_specs=out_specs, check_vma=False)
```

```python
import functools
import math

import jax
import jax.numpy as jnp
from jax import lax
from jax.experimental import pallas as pl
from jax.experimental.pallas import tpu as pltpu
from jax.sharding import PartitionSpec as P

HD = 128
CAP = 2
STEPS = 2
CHUNK = 128
BF16 = jnp.bfloat16
F32 = jnp.float32
I32 = jnp.int32
VMEM = pl.BlockSpec(memory_space=pltpu.VMEM)
SMEM = pl.BlockSpec(memory_space=pltpu.SMEM)
HBM = pl.BlockSpec(memory_space=pltpu.HBM)


def iota(shape, dim):
    return lax.broadcasted_iota(I32, shape, dim)


def over(x, n):
    return lax.shift_right_logical(x, jnp.full_like(x, n.bit_length() - 1)) if n & (n - 1) == 0 else x // n


def rest(x, n):
    return x & (n - 1) if n & (n - 1) == 0 else x % n


def one_hot(hits):
    return jnp.where(hits, 1.0, 0.0).astype(BF16)


def stacked(ref, heads, wide):
    return jnp.concatenate(
        [ref[s, :, c * wide : (c + 1) * wide] for c in range(heads) for s in range(STEPS)], axis=0
    )


def pack_matrix(meta, owners, heads, rows, by_row):
    items = CAP * STEPS
    block = heads * items
    shape = (block, heads * STEPS * rows)
    at = iota(shape, 0)
    col = iota(shape, 1)
    head_step = over(at, items) * STEPS + rest(at, STEPS)
    offset = col - (head_step if by_row else head_step * rows)
    factor = heads * STEPS if by_row else 1
    first = rest(over(at, STEPS), CAP) == 0
    if not by_row:
        offset = jnp.where((offset >= 0) & (offset < rows), offset, -1)
    parts = []
    for i in range(owners):
        here = [meta[rows + i * CAP + k] for k in range(CAP)]
        spots = [jnp.where(h >= 0, h * factor, -rows * factor * heads * STEPS * 2) for h in here]
        parts.append(one_hot(offset == jnp.where(first, spots[0], spots[1])))
    return jnp.concatenate(parts, axis=0)


def unpack_matrix(meta, owners, heads, rows, by_row):
    items = CAP * STEPS
    block = heads * items
    pairs = heads * STEPS
    spots = [over(meta[r], CAP) * block + rest(meta[r], CAP) * STEPS for r in range(rows)]
    if by_row:
        shape = (pairs, owners * block)
        at = iota(shape, 0)
        col = iota(shape, 1) - (over(at, STEPS) * items + rest(at, STEPS))
        return jnp.concatenate([one_hot(col == spots[r]) for r in range(rows)], axis=0)
    shape = (rows, owners * block)
    at = iota(shape, 0)
    col = iota(shape, 1)
    spot = jnp.zeros(shape, I32)
    for r in range(rows):
        spot = jnp.where(at == r, spots[r], spot)
    offset = col - spot
    return jnp.concatenate(
        [one_hot(offset == c * items + s) for c in range(heads) for s in range(STEPS)], axis=0
    )


def by_row_matrix(heads, rows):
    pairs = heads * STEPS
    shape = (pairs * rows, pairs * rows)
    at = iota(shape, 0)
    return one_hot(iota(shape, 1) == rest(at, pairs) * rows + over(at, pairs))


def by_pair_matrix(heads, rows):
    pairs = heads * STEPS
    shape = (pairs * rows, pairs * rows)
    at = iota(shape, 0)
    return one_hot(iota(shape, 1) == rest(at, rows) * pairs + over(at, rows))


def regroup_matrix(owners, heads):
    items = CAP * STEPS
    total = owners * heads * items
    at = iota((total, total), 0)
    head = over(at, owners * items)
    owner = rest(over(at, items), owners)
    return one_hot(
        iota((total, total), 1) == owner * (heads * items) + head * items + rest(at, items)
    )


def ungroup_matrix(owners, heads):
    items = CAP * STEPS
    total = owners * heads * items
    at = iota((total, total), 0)
    owner = over(at, heads * items)
    head = rest(over(at, items), heads)
    return one_hot(
        iota((total, total), 1) == head * (owners * items) + owner * items + rest(at, items)
    )


def exact(matrix, values):
    return jnp.dot(matrix, values, preferred_element_type=F32).astype(BF16)


def dispatch_kernel(
    owners,
    heads,
    adapt,
    rank,
    ids_hbm,
    slot_of_hbm,
    lengths_hbm,
    x_hbm,
    a_hbm,
    b_hbm,
    meta,
    blocks,
    a_out,
    b_out,
    slot_at,
    ids,
    slot_of,
    lengths,
    x_ref,
    sems,
):
    width = x_hbm.shape[2]
    start = pl.multiple_of(lax.axis_index("tensor") * width, width)
    pairs = (
        (ids_hbm, ids),
        (slot_of_hbm, slot_of),
        (lengths_hbm, lengths),
        (x_hbm, x_ref),
        (a_hbm.at[:, pl.ds(start, width)], a_out),
        (b_hbm, b_out),
    )
    copies = [pltpu.make_async_copy(a, b, sems.at[k]) for k, (a, b) in enumerate(pairs)]
    for copy in copies:
        copy.start()
    rows = x_ref.shape[1]
    wide = x_ref.shape[2] // heads
    for copy in copies[:3]:
        copy.wait()
    row_at = rows
    order = rows + owners * CAP
    spans = order + rows
    for p in range(owners * CAP):
        meta[row_at + p] = -1
        slot_at[p] = -1
    for r in range(rows):
        slot = slot_of[ids[r]]
        first = over(slot, adapt) * CAP
        place = first + jnp.where(meta[row_at + first] >= 0, 1, 0)
        meta[row_at + place] = r
        slot_at[place] = rest(slot, adapt)
        meta[r] = place
    items = CAP * STEPS
    block = heads * items
    copies[3].wait()
    packed = exact(pack_matrix(meta, owners, heads, rows, False), stacked(x_ref, heads, wide))
    at = iota((block, adapt * rank), 0)
    lane_slot = over(iota((block, adapt * rank), 1), rank)
    first = rest(over(at, STEPS), CAP) == 0
    for i in range(owners):
        blocks[i, :, :wide] = packed[i * block : (i + 1) * block]
        slot = jnp.where(first, slot_at[i * CAP], slot_at[i * CAP + 1])
        blocks[i, :, wide:] = one_hot(lane_slot == slot)
    sizes = [lengths[r] for r in range(rows)]
    for r in range(rows):
        ahead = jnp.int32(0)
        for q in range(rows):
            if q != r:
                shorter = sizes[q] <= sizes[r] if q < r else sizes[q] < sizes[r]
                ahead = ahead + jnp.where(shorter, 1, 0)
        meta[order + ahead] = r
        meta[spans + r] = sizes[r]
    for copy in copies[4:]:
        copy.wait()


def project_kernel(owners, heads, wide, first, a_ref, blocks, *refs):
    core = lax.axis_index("tensor") if a_ref.shape[1] > heads * wide else 0
    if first:
        part_ref, mask_ref = refs
    else:
        mask_in, part_ref = refs
    grouped = regroup_matrix(owners, heads)
    items = owners * CAP * STEPS
    arrived = jnp.concatenate([blocks[i, :, :wide] for i in range(owners)], axis=0)
    arrived = exact(grouped, arrived)
    if first:
        masks = jnp.concatenate([blocks[i, :, wide:] for i in range(owners)], axis=0)
        mask = jnp.dot(grouped[:items], masks, preferred_element_type=F32)
        mask_ref[...] = mask
    else:
        mask = mask_in[...]
    total = jnp.zeros(mask.shape, F32)
    for c in range(heads):
        total = total + lax.dot_general(
            arrived[c * items : (c + 1) * items],
            a_ref[:, pl.ds(pl.multiple_of(core * (heads * wide) + c * wide, wide), wide)],
            (((1,), (1,)), ((), ())),
            preferred_element_type=F32,
        )
    part_ref[...] = total * mask


def expand_kernel(owners, heads, wide, mine, other, b_ref, *refs):
    blocks = refs[-1]
    low_rank = (mine[...] + other[...]).astype(BF16)
    pieces = []
    for c in range(heads):
        product = jnp.dot(
            low_rank, b_ref[:, c * wide : (c + 1) * wide], preferred_element_type=F32
        )
        pieces.append((2.0 * product).astype(BF16))
    back = exact(ungroup_matrix(owners, heads), jnp.concatenate(pieces, axis=0))
    block = heads * CAP * STEPS
    for i in range(owners):
        blocks[i] = back[i * block : (i + 1) * block]


def in_groups(row_of, span_of, rows, sizes, action):
    at = 0
    for count in [rows // 2] + [rows // 4] * 2:
        group = [row_of(at + j) for j in range(count)]
        amount = over(span_of(group[-1]) + (CHUNK - 1), CHUNK)
        for size in range(1, sizes + 1):

            @pl.when(amount == size)
            def _():
                action(group, size)

        at += count


def attend_kernel(
    owners,
    heads,
    meta,
    q_hbm,
    kn_hbm,
    vn_hbm,
    k_ref,
    v_ref,
    blocks,
    mixed_out,
    outgoing,
    spread_out,
    q_ref,
    kn_ref,
    vn_ref,
    mask_ref,
    q_buf,
    o_buf,
    sems,
):
    rows = q_hbm.shape[1]
    wide = q_hbm.shape[2] // heads
    groups = wide // HD
    pairs = heads * STEPS
    total = groups * pairs
    width = heads * HD
    fresh_rows = STEPS * rows

    singles = [pltpu.make_async_copy(q_hbm, q_ref, sems.at[0])]
    for k, (source, target) in enumerate(((kn_hbm, kn_ref), (vn_hbm, vn_ref))):
        for t in range(STEPS):
            part = target.at[pl.ds(t * rows, rows)]
            singles.append(pltpu.make_async_copy(source.at[t], part, sems.at[1 + k * STEPS + t]))
    for copy in singles:
        copy.start()

    def row_of(place):
        return meta[rows + owners * CAP + place]

    def span_of(row):
        return meta[2 * rows + owners * CAP + row]

    chunks = k_ref.shape[1] // CHUNK

    head_at = rest(over(iota((total, width), 0), STEPS), heads)
    mask_ref[...] = one_hot(head_at == over(iota((total, width), 1), HD))
    head_own = rest(over(iota((total, HD), 0), STEPS), heads)
    blank = jnp.zeros((CHUNK - fresh_rows, width), BF16)
    kn_ref[fresh_rows:, :] = blank
    vn_ref[fresh_rows:, :] = blank

    gather = jnp.concatenate(
        [by_row_matrix(heads, rows), unpack_matrix(meta, owners, heads, rows, True)], axis=1
    )
    for copy in singles:
        copy.wait()
    sources = [stacked(q_ref, heads, wide)] + [blocks[i] for i in range(owners)]
    q_buf[...] = jnp.dot(gather, jnp.concatenate(sources, axis=0), preferred_element_type=F32)

    factor = math.log2(math.e) / math.sqrt(HD)
    fresh_shape = (total, CHUNK)
    fresh_at = iota(fresh_shape, 1)
    fresh_step = over(fresh_at, rows)
    fresh_row = jnp.where(fresh_step <= rest(iota(fresh_shape, 0), STEPS), rest(fresh_at, rows), rows)
    contract = (((1,), (1,)), ((), ()))

    def attend(rows_in, size):
        extent = size * CHUNK
        position = iota((total, extent), 1)
        starts = [pl.multiple_of(row * pairs, pairs) for row in rows_in]
        spreads = []
        for start in starts:
            flat = q_buf[pl.ds(start, pairs), :]
            one = jnp.concatenate(
                [flat[:, j * HD : (j + 1) * HD] for j in range(groups)], axis=0
            ).astype(BF16)
            spreads.append(jnp.concatenate([one] * heads, axis=1) * mask_ref[...])
        scores = []
        for row, spread in zip(rows_in, spreads):
            keys = jnp.concatenate([k_ref[row, :extent, :], kn_ref[...]], axis=0)
            score = lax.dot_general(spread, keys, contract, preferred_element_type=F32)
            cached = jnp.where(position < span_of(row), score[:, :extent], -jnp.inf)
            fresh = jnp.where(fresh_row == row, score[:, extent:], -jnp.inf)
            scores.append(jnp.concatenate([cached, fresh], axis=1))
        tops = [jnp.max(score, axis=1, keepdims=True) for score in scores]
        weights = [jnp.exp2((score - top) * factor) for score, top in zip(scores, tops)]
        shares = [1.0 / jnp.sum(weight, axis=1, keepdims=True) for weight in weights]
        for row, start, weight, share in zip(rows_in, starts, weights, shares):
            values = jnp.concatenate([v_ref[row, :extent, :], vn_ref[...]], axis=0)
            mixed = jnp.dot(weight.astype(BF16), values, preferred_element_type=F32)
            own = mixed[:, :HD]
            for c in range(1, heads):
                own = jnp.where(head_own == c, mixed[:, c * HD : (c + 1) * HD], own)
            own = own * share
            o_buf[pl.ds(start, pairs), :] = jnp.concatenate(
                [own[j * pairs : (j + 1) * pairs] for j in range(groups)], axis=1
            )

    in_groups(row_of, span_of, rows, chunks, attend)

    mixed = o_buf[...].astype(BF16)
    mixed_out[...] = mixed
    packed = exact(pack_matrix(meta, owners, heads, rows, True), mixed)
    block = heads * CAP * STEPS
    for i in range(owners):
        outgoing[i] = packed[i * block : (i + 1) * block]
    spread_out[...] = unpack_matrix(meta, owners, heads, rows, False)


def write_out(matrix, values, heads, out_hbm, out_ref, sems):
    rows = out_ref.shape[1]
    wide = out_ref.shape[2] // heads
    span = STEPS * rows
    copies = []
    for c in range(heads):
        ordered = exact(matrix[c * span : (c + 1) * span], values)
        for s in range(STEPS):
            out_ref[s, :, c * wide : (c + 1) * wide] = ordered[s * rows : (s + 1) * rows]
        part = (slice(None), slice(None), pl.ds(c * wide, wide))
        copies.append(pltpu.make_async_copy(out_ref.at[part], out_hbm.at[part], sems.at[c]))
        copies[-1].start()
    for copy in copies:
        copy.wait()


def finish_kernel(heads, mixed, part, out_hbm, after, out_ref, sems):
    after[...] = part[: after.shape[0], :]
    matrix = by_pair_matrix(heads, out_ref.shape[1])
    write_out(matrix, mixed[...], heads, out_hbm, out_ref, sems)


def collect_kernel(owners, heads, spread, blocks, out_hbm, out_ref, sems):
    arrived = jnp.concatenate([blocks[i] for i in range(owners)], axis=0)
    write_out(spread, arrived, heads, out_hbm, out_ref, sems)


def exchange(blocks):
    return lax.all_to_all(blocks, "store", split_axis=0, concat_axis=0, tiled=True)


def in_hbm(array):
    return pltpu.with_memory_space_constraint(array, pltpu.HBM)


def swap_cores(part):
    return lax.ppermute(part, "tensor", [(0, 1), (1, 0)])


def shards(
    x_in,
    q_base,
    k_new,
    v_new,
    cache_k,
    cache_v,
    lengths,
    adapter_ids,
    slot_of,
    a_query,
    b_query,
    a_output,
    b_output,
):
    owners = lax.axis_size("store")
    rows = x_in.shape[1]
    width = x_in.shape[2]
    heads = cache_k.shape[2] // HD
    wide = width // heads
    adapt, rank = a_query.shape[1:]
    lanes = adapt * rank
    block = heads * CAP * STEPS
    items = owners * CAP * STEPS
    def flat(a_store):
        return jnp.transpose(a_store, (1, 2, 0)).reshape(lanes, a_store.shape[0])

    shape = jax.ShapeDtypeStruct
    small = pltpu.CompilerParams(vmem_limit_bytes=16 * 1024 * 1024)

    sent = shape((owners, block, wide), BF16)
    meta, blocks, a_near, b_near = pl.pallas_call(
        functools.partial(dispatch_kernel, owners, heads, adapt, rank),
        out_shape=[
            shape((3 * rows + owners * CAP,), I32),
            shape((owners, block, wide + lanes), BF16),
            pltpu.VMEM((lanes, width), BF16),
            pltpu.VMEM((lanes, width), BF16),
        ],
        in_specs=[HBM] * 6,
        out_specs=[SMEM] + [VMEM] * 3,
        scratch_shapes=[
            pltpu.SMEM((owners * CAP,), I32),
            pltpu.SMEM(adapter_ids.shape, I32),
            pltpu.SMEM(slot_of.shape, I32),
            pltpu.SMEM(lengths.shape, I32),
            pltpu.VMEM(x_in.shape, BF16),
            pltpu.SemaphoreType.DMA((6,)),
        ],
        compiler_params=small,
        name="dispatch",
    )(
        *map(in_hbm, (adapter_ids, slot_of, lengths, x_in, flat(a_query))),
        in_hbm(b_query.reshape(lanes, width)),
    )

    arrived = exchange(blocks)
    part, mask = pl.pallas_call(
        functools.partial(project_kernel, owners, heads, wide, True),
        out_shape=[shape((items, lanes), F32)] * 2,
        in_specs=[VMEM] * 2,
        out_specs=[VMEM] * 2,
        compiler_params=small,
        name="project_query",
    )(a_near, arrived)

    def expand(part, other, b_store, name, caches, *after):
        return pl.pallas_call(
            functools.partial(expand_kernel, owners, heads, wide),
            out_shape=sent,
            in_specs=[VMEM] * (3 + len(after)) + [HBM] * len(caches),
            out_specs=VMEM,
            compiler_params=small,
            name=name,
        )(part, other, b_store, *after, *caches)

    returned = exchange(expand(part, swap_cores(part), b_near, "expand_query", (in_hbm(cache_k), in_hbm(cache_v))))

    mixed, outgoing, spread = pl.pallas_call(
        functools.partial(attend_kernel, owners, heads),
        out_shape=[
            shape((rows * STEPS * heads, wide), BF16),
            sent,
            shape((rows * STEPS * heads, owners * block), BF16),
        ],
        in_specs=[SMEM] + [HBM] * 3 + [VMEM] * 3,
        out_specs=[VMEM] * 3,
        scratch_shapes=[
            pltpu.VMEM(q_base.shape, BF16),
            pltpu.VMEM((CHUNK, heads * HD), BF16),
            pltpu.VMEM((CHUNK, heads * HD), BF16),
            pltpu.VMEM((STEPS * wide // HD * heads, heads * HD), BF16),
            pltpu.VMEM((rows * STEPS * heads, wide), F32),
            pltpu.VMEM((rows * STEPS * heads, wide), F32),
            pltpu.SemaphoreType.DMA((1 + 2 * STEPS,)),
        ],
        compiler_params=pltpu.CompilerParams(vmem_limit_bytes=16 * 1024 * 1024),
        name="attend",
    )(meta, *map(in_hbm, (q_base, k_new, v_new)), cache_k, cache_v, returned)

    arrived = exchange(outgoing)
    part = pl.pallas_call(
        functools.partial(project_kernel, owners, heads, wide, False),
        out_shape=shape((items, lanes), F32),
        in_specs=[VMEM] * 3,
        out_specs=VMEM,
        compiler_params=small,
        name="project_output",
    )(flat(a_output), arrived, mask)
    ordered = dict(
        scratch_shapes=[
            pltpu.VMEM((STEPS, rows, width), BF16),
            pltpu.SemaphoreType.DMA((heads,)),
        ],
        compiler_params=small,
    )
    other = swap_cores(part)
    attn_out, after = pl.pallas_call(
        functools.partial(finish_kernel, heads),
        out_shape=[shape((STEPS, rows, width), BF16), shape((8, lanes), F32)],
        in_specs=[VMEM] * 2,
        out_specs=[HBM, VMEM],
        name="finish",
        **ordered,
    )(mixed, part)
    returned = exchange(
        expand(part, other, b_output.reshape(lanes, width), "expand_output", (), after)
    )
    adapter_out = pl.pallas_call(
        functools.partial(collect_kernel, owners, heads),
        out_shape=shape((STEPS, rows, width), BF16),
        in_specs=[VMEM] * 2,
        out_specs=HBM,
        name="collect",
        **ordered,
    )(spread, returned)
    return (attn_out, adapter_out)


def solution(mesh):
    in_specs = (
        P(None, ("parts", "store"), "tensor"),
        P(None, ("parts", "store"), "tensor"),
        P(None, ("parts", "store"), "tensor"),
        P(None, ("parts", "store"), "tensor"),
        P(("parts", "store"), None, "tensor"),
        P(("parts", "store"), None, "tensor"),
        P(("parts", "store")),
        P(("parts", "store")),
        P("parts"),
        P(None, "store", None),
        P("store", None, "tensor"),
        P(None, "store", None),
        P("store", None, "tensor"),
    )
    out_specs = (P(None, ("parts", "store"), "tensor"), P(None, ("parts", "store"), "tensor"))
    return jax.shard_map(shards, mesh=mesh, in_specs=in_specs, out_specs=out_specs, check_vma=False)
```

```python
import functools
import math

import jax
import jax.numpy as jnp
from jax import lax
from jax.experimental import pallas as pl
from jax.experimental.pallas import tpu as pltpu
from jax.sharding import PartitionSpec as P

HD = 128
CAP = 2
STEPS = 2
CHUNK = 128
BF16 = jnp.bfloat16
F32 = jnp.float32
I32 = jnp.int32
VMEM = pl.BlockSpec(memory_space=pltpu.VMEM)
SMEM = pl.BlockSpec(memory_space=pltpu.SMEM)
HBM = pl.BlockSpec(memory_space=pltpu.HBM)


def iota(shape, dim):
    return lax.broadcasted_iota(I32, shape, dim)


def over(x, n):
    return lax.shift_right_logical(x, jnp.full_like(x, n.bit_length() - 1)) if n & (n - 1) == 0 else x // n


def rest(x, n):
    return x & (n - 1) if n & (n - 1) == 0 else x % n


def one_hot(hits):
    return jnp.where(hits, 1.0, 0.0).astype(BF16)


def stacked(ref, heads, wide):
    return jnp.concatenate(
        [ref[s, :, c * wide : (c + 1) * wide] for c in range(heads) for s in range(STEPS)], axis=0
    )


def pack_matrix(meta, owners, heads, rows, by_row):
    items = CAP * STEPS
    block = heads * items
    shape = (block, heads * STEPS * rows)
    at = iota(shape, 0)
    col = iota(shape, 1)
    head_step = over(at, items) * STEPS + rest(at, STEPS)
    offset = col - (head_step if by_row else head_step * rows)
    factor = heads * STEPS if by_row else 1
    first = rest(over(at, STEPS), CAP) == 0
    if not by_row:
        offset = jnp.where((offset >= 0) & (offset < rows), offset, -1)
    parts = []
    for i in range(owners):
        here = [meta[rows + i * CAP + k] for k in range(CAP)]
        spots = [jnp.where(h >= 0, h * factor, -rows * factor * heads * STEPS * 2) for h in here]
        parts.append(one_hot(offset == jnp.where(first, spots[0], spots[1])))
    return jnp.concatenate(parts, axis=0)


def unpack_matrix(meta, owners, heads, rows, by_row):
    items = CAP * STEPS
    block = heads * items
    pairs = heads * STEPS
    spots = [over(meta[r], CAP) * block + rest(meta[r], CAP) * STEPS for r in range(rows)]
    if by_row:
        shape = (pairs, owners * block)
        at = iota(shape, 0)
        col = iota(shape, 1) - (over(at, STEPS) * items + rest(at, STEPS))
        return jnp.concatenate([one_hot(col == spots[r]) for r in range(rows)], axis=0)
    shape = (rows, owners * block)
    at = iota(shape, 0)
    col = iota(shape, 1)
    spot = jnp.zeros(shape, I32)
    for r in range(rows):
        spot = jnp.where(at == r, spots[r], spot)
    offset = col - spot
    return jnp.concatenate(
        [one_hot(offset == c * items + s) for c in range(heads) for s in range(STEPS)], axis=0
    )


def by_row_matrix(heads, rows):
    pairs = heads * STEPS
    shape = (pairs * rows, pairs * rows)
    at = iota(shape, 0)
    return one_hot(iota(shape, 1) == rest(at, pairs) * rows + over(at, pairs))


def by_pair_matrix(heads, rows):
    pairs = heads * STEPS
    shape = (pairs * rows, pairs * rows)
    at = iota(shape, 0)
    return one_hot(iota(shape, 1) == rest(at, rows) * pairs + over(at, rows))


def regroup_matrix(owners, heads):
    items = CAP * STEPS
    total = owners * heads * items
    at = iota((total, total), 0)
    head = over(at, owners * items)
    owner = rest(over(at, items), owners)
    return one_hot(
        iota((total, total), 1) == owner * (heads * items) + head * items + rest(at, items)
    )


def ungroup_matrix(owners, heads):
    items = CAP * STEPS
    total = owners * heads * items
    at = iota((total, total), 0)
    owner = over(at, heads * items)
    head = rest(over(at, items), heads)
    return one_hot(
        iota((total, total), 1) == head * (owners * items) + owner * items + rest(at, items)
    )


def exact(matrix, values):
    return jnp.dot(matrix, values, preferred_element_type=F32).astype(BF16)


def dispatch_kernel(
    owners,
    heads,
    adapt,
    rank,
    ids_hbm,
    slot_of_hbm,
    lengths_hbm,
    x_hbm,
    k_hbm,
    v_hbm,
    meta,
    blocks,
    slot_at,
    ids,
    slot_of,
    lengths,
    x_ref,
    sems,
):
    pairs = (
        (ids_hbm, ids),
        (slot_of_hbm, slot_of),
        (lengths_hbm, lengths),
        (x_hbm, x_ref),
    )
    copies = [pltpu.make_async_copy(a, b, sems.at[k]) for k, (a, b) in enumerate(pairs)]
    for copy in copies:
        copy.start()
    rows = x_ref.shape[1]
    wide = x_ref.shape[2] // heads
    for copy in copies[:3]:
        copy.wait()
    row_at = rows
    order = rows + owners * CAP
    spans = order + rows
    for p in range(owners * CAP):
        meta[row_at + p] = -1
        slot_at[p] = -1
    for r in range(rows):
        slot = slot_of[ids[r]]
        first = over(slot, adapt) * CAP
        place = first + jnp.where(meta[row_at + first] >= 0, 1, 0)
        meta[row_at + place] = r
        slot_at[place] = rest(slot, adapt)
        meta[r] = place
    items = CAP * STEPS
    block = heads * items
    copies[3].wait()
    packed = exact(pack_matrix(meta, owners, heads, rows, False), stacked(x_ref, heads, wide))
    at = iota((block, adapt * rank), 0)
    lane_slot = over(iota((block, adapt * rank), 1), rank)
    first = rest(over(at, STEPS), CAP) == 0
    for i in range(owners):
        blocks[i, :, :wide] = packed[i * block : (i + 1) * block]
        slot = jnp.where(first, slot_at[i * CAP], slot_at[i * CAP + 1])
        blocks[i, :, wide:] = one_hot(lane_slot == slot)
    sizes = [lengths[r] for r in range(rows)]
    for r in range(rows):
        ahead = jnp.int32(0)
        for q in range(rows):
            if q != r:
                shorter = sizes[q] <= sizes[r] if q < r else sizes[q] < sizes[r]
                ahead = ahead + jnp.where(shorter, 1, 0)
        meta[order + ahead] = r
        meta[spans + r] = sizes[r]


def project_kernel(owners, heads, wide, first, a_ref, blocks, *refs):
    core = lax.axis_index("tensor") if a_ref.shape[1] > heads * wide else 0
    if first:
        part_ref, mask_ref = refs
    else:
        mask_in, part_ref = refs
    grouped = regroup_matrix(owners, heads)
    items = owners * CAP * STEPS
    arrived = jnp.concatenate([blocks[i, :, :wide] for i in range(owners)], axis=0)
    arrived = exact(grouped, arrived)
    if first:
        masks = jnp.concatenate([blocks[i, :, wide:] for i in range(owners)], axis=0)
        mask = jnp.dot(grouped[:items], masks, preferred_element_type=F32)
        mask_ref[...] = mask
    else:
        mask = mask_in[...]
    total = jnp.zeros(mask.shape, F32)
    for c in range(heads):
        total = total + lax.dot_general(
            arrived[c * items : (c + 1) * items],
            a_ref[:, pl.ds(pl.multiple_of(core * (heads * wide) + c * wide, wide), wide)],
            (((1,), (1,)), ((), ())),
            preferred_element_type=F32,
        )
    part_ref[...] = total * mask


def expand_kernel(owners, heads, wide, mine, other, b_ref, *refs):
    blocks = refs[-1]
    low_rank = (mine[...] + other[...]).astype(BF16)
    pieces = []
    for c in range(heads):
        product = jnp.dot(
            low_rank, b_ref[:, c * wide : (c + 1) * wide], preferred_element_type=F32
        )
        pieces.append((2.0 * product).astype(BF16))
    back = exact(ungroup_matrix(owners, heads), jnp.concatenate(pieces, axis=0))
    block = heads * CAP * STEPS
    for i in range(owners):
        blocks[i] = back[i * block : (i + 1) * block]


def in_groups(row_of, span_of, rows, sizes, action):
    at = 0
    for count in [rows // 2] + [rows // 4] * 2:
        group = [row_of(at + j) for j in range(count)]
        amount = over(span_of(group[-1]) + (CHUNK - 1), CHUNK)
        for size in range(1, sizes + 1):

            @pl.when(amount == size)
            def _():
                action(group, size)

        at += count


def prepare_kernel(
    owners, heads, meta, q_ref, kn_ref, vn_ref, part, base_out, kn_out, vn_out, mask_out, gather_out, after
):
    rows = q_ref.shape[1]
    wide = q_ref.shape[2] // heads
    fresh_rows = STEPS * rows
    base_out[...] = exact(by_row_matrix(heads, rows), stacked(q_ref, heads, wide))
    blank = jnp.zeros((CHUNK - fresh_rows, heads * HD), BF16)
    for source, target in ((kn_ref, kn_out), (vn_ref, vn_out)):
        target[...] = jnp.concatenate([source[t] for t in range(STEPS)] + [blank], axis=0)
    head_at = rest(over(iota(mask_out.shape, 0), STEPS), heads)
    mask_out[...] = one_hot(head_at == over(iota(mask_out.shape, 1), HD))
    gather_out[...] = unpack_matrix(meta, owners, heads, rows, True)
    after[...] = part[: after.shape[0], :]


def attend_kernel(
    owners,
    heads,
    rows,
    meta,
    base_ref,
    kn_ref,
    vn_ref,
    mask_ref,
    gather_ref,
    k_ref,
    v_ref,
    blocks,
    mixed_out,
    outgoing,
    spread_out,
    q_buf,
    o_buf,
):
    wide = base_ref.shape[1]
    groups = wide // HD
    pairs = heads * STEPS
    total = groups * pairs
    chunks = k_ref.shape[1] // CHUNK

    def row_of(place):
        return meta[rows + owners * CAP + place]

    def span_of(row):
        return meta[2 * rows + owners * CAP + row]

    delta = jnp.dot(
        gather_ref[...],
        jnp.concatenate([blocks[i] for i in range(owners)], axis=0),
        preferred_element_type=F32,
    )
    q_buf[...] = base_ref[...].astype(F32) + delta

    head_own = rest(over(iota((total, HD), 0), STEPS), heads)
    factor = math.log2(math.e) / math.sqrt(HD)
    fresh_shape = (total, CHUNK)
    fresh_at = iota(fresh_shape, 1)
    fresh_step = over(fresh_at, rows)
    fresh_row = jnp.where(fresh_step <= rest(iota(fresh_shape, 0), STEPS), rest(fresh_at, rows), rows)
    contract = (((1,), (1,)), ((), ()))

    def attend(rows_in, size):
        extent = size * CHUNK
        position = iota((total, extent), 1)
        starts = [pl.multiple_of(row * pairs, pairs) for row in rows_in]
        spreads = []
        for start in starts:
            flat = q_buf[pl.ds(start, pairs), :]
            one = jnp.concatenate(
                [flat[:, j * HD : (j + 1) * HD] for j in range(groups)], axis=0
            ).astype(BF16)
            spreads.append(jnp.concatenate([one] * heads, axis=1) * mask_ref[...])
        scores = []
        for row, spread in zip(rows_in, spreads):
            keys = jnp.concatenate([k_ref[row, :extent, :], kn_ref[...]], axis=0)
            score = lax.dot_general(spread, keys, contract, preferred_element_type=F32)
            cached = jnp.where(position < span_of(row), score[:, :extent], -jnp.inf)
            fresh = jnp.where(fresh_row == row, score[:, extent:], -jnp.inf)
            scores.append(jnp.concatenate([cached, fresh], axis=1))
        tops = [jnp.max(score, axis=1, keepdims=True) for score in scores]
        weights = [jnp.exp2((score - top) * factor) for score, top in zip(scores, tops)]
        shares = [1.0 / jnp.sum(weight, axis=1, keepdims=True) for weight in weights]
        for row, start, weight, share in zip(rows_in, starts, weights, shares):
            values = jnp.concatenate([v_ref[row, :extent, :], vn_ref[...]], axis=0)
            mixed = jnp.dot(weight.astype(BF16), values, preferred_element_type=F32)
            own = mixed[:, :HD]
            for c in range(1, heads):
                own = jnp.where(head_own == c, mixed[:, c * HD : (c + 1) * HD], own)
            own = own * share
            o_buf[pl.ds(start, pairs), :] = jnp.concatenate(
                [own[j * pairs : (j + 1) * pairs] for j in range(groups)], axis=1
            )

    in_groups(row_of, span_of, rows, chunks, attend)

    mixed = o_buf[...].astype(BF16)
    mixed_out[...] = mixed
    packed = exact(pack_matrix(meta, owners, heads, rows, True), mixed)
    block = heads * CAP * STEPS
    for i in range(owners):
        outgoing[i] = packed[i * block : (i + 1) * block]
    spread_out[...] = unpack_matrix(meta, owners, heads, rows, False)


def write_out(matrix, values, heads, out_hbm, out_ref, sems):
    rows = out_ref.shape[1]
    wide = out_ref.shape[2] // heads
    span = STEPS * rows
    copies = []
    for c in range(heads):
        ordered = exact(matrix[c * span : (c + 1) * span], values)
        for s in range(STEPS):
            out_ref[s, :, c * wide : (c + 1) * wide] = ordered[s * rows : (s + 1) * rows]
        part = (slice(None), slice(None), pl.ds(c * wide, wide))
        copies.append(pltpu.make_async_copy(out_ref.at[part], out_hbm.at[part], sems.at[c]))
        copies[-1].start()
    for copy in copies:
        copy.wait()


def finish_kernel(heads, mixed, part, out_hbm, after, out_ref, sems):
    after[...] = part[: after.shape[0], :]
    matrix = by_pair_matrix(heads, out_ref.shape[1])
    write_out(matrix, mixed[...], heads, out_hbm, out_ref, sems)


def collect_kernel(owners, heads, spread, blocks, out_hbm, out_ref, sems):
    arrived = jnp.concatenate([blocks[i] for i in range(owners)], axis=0)
    write_out(spread, arrived, heads, out_hbm, out_ref, sems)


def exchange(blocks):
    return lax.all_to_all(blocks, "store", split_axis=0, concat_axis=0, tiled=True)


def in_hbm(array):
    return pltpu.with_memory_space_constraint(array, pltpu.HBM)


def swap_cores(part):
    return lax.ppermute(part, "tensor", [(0, 1), (1, 0)])


def shards(
    x_in,
    q_base,
    k_new,
    v_new,
    cache_k,
    cache_v,
    lengths,
    adapter_ids,
    slot_of,
    a_query,
    b_query,
    a_output,
    b_output,
):
    owners = lax.axis_size("store")
    rows = x_in.shape[1]
    width = x_in.shape[2]
    heads = cache_k.shape[2] // HD
    wide = width // heads
    adapt, rank = a_query.shape[1:]
    lanes = adapt * rank
    block = heads * CAP * STEPS
    items = owners * CAP * STEPS
    def flat(a_store):
        return jnp.transpose(a_store, (1, 2, 0)).reshape(lanes, a_store.shape[0])

    shape = jax.ShapeDtypeStruct
    small = pltpu.CompilerParams(vmem_limit_bytes=16 * 1024 * 1024)

    sent = shape((owners, block, wide), BF16)
    caches = (in_hbm(cache_k), in_hbm(cache_v))
    meta, blocks = pl.pallas_call(
        functools.partial(dispatch_kernel, owners, heads, adapt, rank),
        out_shape=[
            shape((3 * rows + owners * CAP,), I32),
            shape((owners, block, wide + lanes), BF16),
        ],
        in_specs=[HBM] * 6,
        out_specs=[SMEM, VMEM],
        scratch_shapes=[
            pltpu.SMEM((owners * CAP,), I32),
            pltpu.SMEM(adapter_ids.shape, I32),
            pltpu.SMEM(slot_of.shape, I32),
            pltpu.SMEM(lengths.shape, I32),
            pltpu.VMEM(x_in.shape, BF16),
            pltpu.SemaphoreType.DMA((4,)),
        ],
        compiler_params=small,
        name="dispatch",
    )(
        *map(in_hbm, (adapter_ids, slot_of, lengths, x_in)), *caches
    )

    arrived = exchange(blocks)
    part, mask = pl.pallas_call(
        functools.partial(project_kernel, owners, heads, wide, True),
        out_shape=[shape((items, lanes), F32)] * 2,
        in_specs=[VMEM] * 2,
        out_specs=[VMEM] * 2,
        compiler_params=small,
        name="project_query",
    )(flat(a_query), arrived)

    def expand(part, other, b_store, name, caches, *after):
        return pl.pallas_call(
            functools.partial(expand_kernel, owners, heads, wide),
            out_shape=sent,
            in_specs=[VMEM] * (3 + len(after)) + [HBM] * len(caches),
            out_specs=VMEM,
            compiler_params=small,
            name=name,
        )(part, other, b_store, *after, *caches)

    other = swap_cores(part)
    *prepared, after = pl.pallas_call(
        functools.partial(prepare_kernel, owners, heads),
        out_shape=[
            shape((rows * STEPS * heads, wide), BF16),
            shape((CHUNK, heads * HD), BF16),
            shape((CHUNK, heads * HD), BF16),
            shape((STEPS * wide // HD * heads, heads * HD), BF16),
            shape((rows * STEPS * heads, owners * block), BF16),
            shape((8, lanes), F32),
        ],
        in_specs=[SMEM] + [VMEM] * 4,
        out_specs=[VMEM] * 6,
        compiler_params=small,
        name="prepare",
    )(meta, q_base, k_new, v_new, part)
    returned = exchange(
        expand(part, other, b_query.reshape(lanes, width), "expand_query", caches, after)
    )

    mixed, outgoing, spread = pl.pallas_call(
        functools.partial(attend_kernel, owners, heads, rows),
        out_shape=[
            shape((rows * STEPS * heads, wide), BF16),
            sent,
            shape((rows * STEPS * heads, owners * block), BF16),
        ],
        in_specs=[SMEM] + [VMEM] * 8,
        out_specs=[VMEM] * 3,
        scratch_shapes=[
            pltpu.VMEM((rows * STEPS * heads, wide), F32),
            pltpu.VMEM((rows * STEPS * heads, wide), F32),
        ],
        compiler_params=small,
        name="attend",
    )(meta, *prepared, cache_k, cache_v, returned)

    arrived = exchange(outgoing)
    part = pl.pallas_call(
        functools.partial(project_kernel, owners, heads, wide, False),
        out_shape=shape((items, lanes), F32),
        in_specs=[VMEM] * 3,
        out_specs=VMEM,
        compiler_params=small,
        name="project_output",
    )(flat(a_output), arrived, mask)
    ordered = dict(
        scratch_shapes=[
            pltpu.VMEM((STEPS, rows, width), BF16),
            pltpu.SemaphoreType.DMA((heads,)),
        ],
        compiler_params=small,
    )
    other = swap_cores(part)
    attn_out, after = pl.pallas_call(
        functools.partial(finish_kernel, heads),
        out_shape=[shape((STEPS, rows, width), BF16), shape((8, lanes), F32)],
        in_specs=[VMEM] * 2,
        out_specs=[HBM, VMEM],
        name="finish",
        **ordered,
    )(mixed, part)
    returned = exchange(
        expand(part, other, b_output.reshape(lanes, width), "expand_output", (), after)
    )
    adapter_out = pl.pallas_call(
        functools.partial(collect_kernel, owners, heads),
        out_shape=shape((STEPS, rows, width), BF16),
        in_specs=[VMEM] * 2,
        out_specs=HBM,
        name="collect",
        **ordered,
    )(spread, returned)
    return (attn_out, adapter_out)


def solution(mesh):
    in_specs = (
        P(None, ("parts", "store"), "tensor"),
        P(None, ("parts", "store"), "tensor"),
        P(None, ("parts", "store"), "tensor"),
        P(None, ("parts", "store"), "tensor"),
        P(("parts", "store"), None, "tensor"),
        P(("parts", "store"), None, "tensor"),
        P(("parts", "store")),
        P(("parts", "store")),
        P("parts"),
        P(None, "store", None),
        P("store", None, "tensor"),
        P(None, "store", None),
        P("store", None, "tensor"),
    )
    out_specs = (P(None, ("parts", "store"), "tensor"), P(None, ("parts", "store"), "tensor"))
    return jax.shard_map(shards, mesh=mesh, in_specs=in_specs, out_specs=out_specs, check_vma=False)
```

```python
import functools
import math

import jax
import jax.numpy as jnp
from jax import lax
from jax.experimental import pallas as pl
from jax.experimental.pallas import tpu as pltpu
from jax.sharding import PartitionSpec as P

HD = 128
CAP = 2
STEPS = 2
CHUNK = 128
LAG = 2
BF16 = jnp.bfloat16
F32 = jnp.float32
I32 = jnp.int32
VMEM = pl.BlockSpec(memory_space=pltpu.VMEM)
SMEM = pl.BlockSpec(memory_space=pltpu.SMEM)
HBM = pl.BlockSpec(memory_space=pltpu.HBM)


def iota(shape, dim):
    return lax.broadcasted_iota(I32, shape, dim)


def over(x, n):
    return lax.shift_right_logical(x, jnp.full_like(x, n.bit_length() - 1)) if n & (n - 1) == 0 else x // n


def rest(x, n):
    return x & (n - 1) if n & (n - 1) == 0 else x % n


def one_hot(hits):
    return jnp.where(hits, 1.0, 0.0).astype(BF16)


def stacked(ref, heads, wide):
    return jnp.concatenate(
        [ref[s, :, c * wide : (c + 1) * wide] for c in range(heads) for s in range(STEPS)], axis=0
    )


def pack_matrix(meta, owners, heads, rows, by_row):
    items = CAP * STEPS
    block = heads * items
    shape = (block, heads * STEPS * rows)
    at = iota(shape, 0)
    col = iota(shape, 1)
    head_step = over(at, items) * STEPS + rest(at, STEPS)
    offset = col - (head_step if by_row else head_step * rows)
    factor = heads * STEPS if by_row else 1
    first = rest(over(at, STEPS), CAP) == 0
    if not by_row:
        offset = jnp.where((offset >= 0) & (offset < rows), offset, -1)
    parts = []
    for i in range(owners):
        here = [meta[rows + i * CAP + k] for k in range(CAP)]
        spots = [jnp.where(h >= 0, h * factor, -rows * factor * heads * STEPS * 2) for h in here]
        parts.append(one_hot(offset == jnp.where(first, spots[0], spots[1])))
    return jnp.concatenate(parts, axis=0)


def unpack_matrix(meta, owners, heads, rows, by_row):
    items = CAP * STEPS
    block = heads * items
    pairs = heads * STEPS
    spots = [over(meta[r], CAP) * block + rest(meta[r], CAP) * STEPS for r in range(rows)]
    if by_row:
        shape = (pairs, owners * block)
        at = iota(shape, 0)
        col = iota(shape, 1) - (over(at, STEPS) * items + rest(at, STEPS))
        return jnp.concatenate([one_hot(col == spots[r]) for r in range(rows)], axis=0)
    shape = (rows, owners * block)
    at = iota(shape, 0)
    col = iota(shape, 1)
    spot = jnp.zeros(shape, I32)
    for r in range(rows):
        spot = jnp.where(at == r, spots[r], spot)
    offset = col - spot
    return jnp.concatenate(
        [one_hot(offset == c * items + s) for c in range(heads) for s in range(STEPS)], axis=0
    )


def by_row_matrix(heads, rows):
    pairs = heads * STEPS
    shape = (pairs * rows, pairs * rows)
    at = iota(shape, 0)
    return one_hot(iota(shape, 1) == rest(at, pairs) * rows + over(at, pairs))


def by_pair_matrix(heads, rows):
    pairs = heads * STEPS
    shape = (pairs * rows, pairs * rows)
    at = iota(shape, 0)
    return one_hot(iota(shape, 1) == rest(at, rows) * pairs + over(at, rows))


def regroup_matrix(owners, heads):
    items = CAP * STEPS
    total = owners * heads * items
    at = iota((total, total), 0)
    head = over(at, owners * items)
    owner = rest(over(at, items), owners)
    return one_hot(
        iota((total, total), 1) == owner * (heads * items) + head * items + rest(at, items)
    )


def ungroup_matrix(owners, heads):
    items = CAP * STEPS
    total = owners * heads * items
    at = iota((total, total), 0)
    owner = over(at, heads * items)
    head = rest(over(at, items), heads)
    return one_hot(
        iota((total, total), 1) == head * (owners * items) + owner * items + rest(at, items)
    )


def exact(matrix, values):
    return jnp.dot(matrix, values, preferred_element_type=F32).astype(BF16)


def dispatch_kernel(
    owners,
    heads,
    adapt,
    rank,
    ids_hbm,
    slot_of_hbm,
    lengths_hbm,
    x_hbm,
    k_hbm,
    v_hbm,
    meta,
    blocks,
    slot_at,
    ids,
    slot_of,
    lengths,
    x_ref,
    sems,
):
    pairs = (
        (ids_hbm, ids),
        (slot_of_hbm, slot_of),
        (lengths_hbm, lengths),
        (x_hbm, x_ref),
    )
    copies = [pltpu.make_async_copy(a, b, sems.at[k]) for k, (a, b) in enumerate(pairs)]
    for copy in copies:
        copy.start()
    rows = x_ref.shape[1]
    wide = x_ref.shape[2] // heads
    for copy in copies[:3]:
        copy.wait()
    row_at = rows
    spans = rows + owners * CAP
    for p in range(owners * CAP):
        meta[row_at + p] = -1
        slot_at[p] = -1
    for r in range(rows):
        slot = slot_of[ids[r]]
        first = over(slot, adapt) * CAP
        place = first + jnp.where(meta[row_at + first] >= 0, 1, 0)
        meta[row_at + place] = r
        slot_at[place] = rest(slot, adapt)
        meta[r] = place
        meta[spans + r] = lengths[r]
    items = CAP * STEPS
    block = heads * items
    copies[3].wait()
    packed = exact(pack_matrix(meta, owners, heads, rows, False), stacked(x_ref, heads, wide))
    at = iota((block, adapt * rank), 0)
    lane_slot = over(iota((block, adapt * rank), 1), rank)
    first = rest(over(at, STEPS), CAP) == 0
    for i in range(owners):
        blocks[i, :, :wide] = packed[i * block : (i + 1) * block]
        slot = jnp.where(first, slot_at[i * CAP], slot_at[i * CAP + 1])
        blocks[i, :, wide:] = one_hot(lane_slot == slot)


def project_kernel(owners, heads, wide, first, a_ref, blocks, *refs):
    core = lax.axis_index("tensor") if a_ref.shape[1] > heads * wide else 0
    if first:
        part_ref, mask_ref = refs
    else:
        mask_in, part_ref = refs
    grouped = regroup_matrix(owners, heads)
    items = owners * CAP * STEPS
    arrived = jnp.concatenate([blocks[i, :, :wide] for i in range(owners)], axis=0)
    arrived = exact(grouped, arrived)
    if first:
        masks = jnp.concatenate([blocks[i, :, wide:] for i in range(owners)], axis=0)
        mask = jnp.dot(grouped[:items], masks, preferred_element_type=F32)
        mask_ref[...] = mask
    else:
        mask = mask_in[...]
    total = jnp.zeros(mask.shape, F32)
    for c in range(heads):
        total = total + lax.dot_general(
            arrived[c * items : (c + 1) * items],
            a_ref[:, pl.ds(pl.multiple_of(core * (heads * wide) + c * wide, wide), wide)],
            (((1,), (1,)), ((), ())),
            preferred_element_type=F32,
        )
    part_ref[...] = total * mask


def expand_kernel(owners, heads, wide, mine, other, b_ref, *refs):
    blocks = refs[-1]
    low_rank = (mine[...] + other[...]).astype(BF16)
    pieces = []
    for c in range(heads):
        product = jnp.dot(
            low_rank, b_ref[:, c * wide : (c + 1) * wide], preferred_element_type=F32
        )
        pieces.append((2.0 * product).astype(BF16))
    back = exact(ungroup_matrix(owners, heads), jnp.concatenate(pieces, axis=0))
    block = heads * CAP * STEPS
    for i in range(owners):
        blocks[i] = back[i * block : (i + 1) * block]


def by_shape(amount_of, rows, most, action):
    half, quarter = rows // 2, rows // 4
    middle = max(most // 2, 1)
    low = amount_of(half - 1)
    high = amount_of(half + quarter - 1)
    one, two = low <= 1, low <= middle
    shapes = (
        (one & (high <= middle), (1, middle, most)),
        (one & (high > middle), (1, most, most)),
        (two & (low > 1), (middle, most, most)),
        (low > middle, (most, most, most)),
    )
    for fits, (a, b, c) in shapes:

        @pl.when(fits)
        def _():
            action([a] * half + [b] * quarter + [c] * quarter)


def prepare_kernel(
    owners,
    heads,
    meta,
    q_ref,
    kn_ref,
    vn_ref,
    part,
    order,
    base_out,
    kn_out,
    vn_out,
    mask_out,
    gather_out,
    pack_out,
    after,
):
    rows = q_ref.shape[1]
    wide = q_ref.shape[2] // heads
    fresh_rows = STEPS * rows
    base_out[...] = exact(by_row_matrix(heads, rows), stacked(q_ref, heads, wide))
    blank = jnp.zeros((CHUNK - fresh_rows, heads * HD), BF16)
    for source, target in ((kn_ref, kn_out), (vn_ref, vn_out)):
        target[...] = jnp.concatenate([source[t] for t in range(STEPS)] + [blank], axis=0)
    head_at = rest(over(iota(mask_out.shape, 0), STEPS), heads)
    mask_out[...] = one_hot(head_at == over(iota(mask_out.shape, 1), HD))
    gather_out[...] = unpack_matrix(meta, owners, heads, rows, True)
    pack_out[...] = pack_matrix(meta, owners, heads, rows, True)
    sizes = [meta[rows + owners * CAP + r] for r in range(rows)]
    for r in range(rows):
        ahead = jnp.int32(0)
        for q in range(rows):
            if q != r:
                shorter = sizes[q] <= sizes[r] if q < r else sizes[q] < sizes[r]
                ahead = ahead + jnp.where(shorter, 1, 0)
        order[ahead] = r
    after[...] = part[: after.shape[0], :]


def attend_kernel(
    owners,
    heads,
    rows,
    meta,
    order,
    base_ref,
    kn_ref,
    vn_ref,
    mask_ref,
    gather_ref,
    pack_ref,
    k_ref,
    v_ref,
    blocks,
    mixed_out,
    outgoing,
    q_buf,
    o_buf,
):
    wide = base_ref.shape[1]
    groups = wide // HD
    pairs = heads * STEPS
    total = groups * pairs

    def span_of(row):
        return meta[rows + owners * CAP + row]

    delta = jnp.dot(
        gather_ref[...],
        jnp.concatenate([blocks[i] for i in range(owners)], axis=0),
        preferred_element_type=F32,
    )
    q_buf[...] = base_ref[...].astype(F32) + delta

    head_own = rest(over(iota((total, HD), 0), STEPS), heads)
    factor = math.log2(math.e) / math.sqrt(HD)
    fresh_shape = (total, CHUNK)
    fresh_at = iota(fresh_shape, 1)
    fresh_step = over(fresh_at, rows)
    fresh_row = jnp.where(fresh_step <= rest(iota(fresh_shape, 0), STEPS), rest(fresh_at, rows), rows)
    contract = (((1,), (1,)), ((), ()))

    def scores_of(row, extent):
        flat = q_buf[pl.ds(pl.multiple_of(row * pairs, pairs), pairs), :]
        one = jnp.concatenate([flat[:, j * HD : (j + 1) * HD] for j in range(groups)], axis=0)
        spread = jnp.concatenate([one.astype(BF16)] * heads, axis=1) * mask_ref[...]
        keys = jnp.concatenate([k_ref[row, :extent, :], kn_ref[...]], axis=0)
        score = lax.dot_general(spread, keys, contract, preferred_element_type=F32)
        cached = jnp.where(iota((total, extent), 1) < span_of(row), score[:, :extent], -jnp.inf)
        fresh = jnp.where(fresh_row == row, score[:, extent:], -jnp.inf)
        return jnp.concatenate([cached, fresh], axis=1)

    def softmax_of(score):
        top = jnp.max(score, axis=1, keepdims=True)
        weight = jnp.exp2((score - top) * factor)
        return weight.astype(BF16), 1.0 / jnp.sum(weight, axis=1, keepdims=True)

    def mix(row, extent, weight, share):
        values = jnp.concatenate([v_ref[row, :extent, :], vn_ref[...]], axis=0)
        mixed = jnp.dot(weight, values, preferred_element_type=F32)
        own = mixed[:, :HD]
        for c in range(1, heads):
            own = jnp.where(head_own == c, mixed[:, c * HD : (c + 1) * HD], own)
        own = own * share
        o_buf[pl.ds(pl.multiple_of(row * pairs, pairs), pairs), :] = jnp.concatenate(
            [own[j * pairs : (j + 1) * pairs] for j in range(groups)], axis=1
        )

    def attend(sizes):
        ordered = [order[k] for k in range(rows)]
        extents = [size * CHUNK for size in sizes]
        scores, weights = {}, {}
        for t in range(rows + 2 * LAG):
            if t < rows:
                scores[t] = scores_of(ordered[t], extents[t])
            if 0 <= t - LAG < rows:
                weights[t - LAG] = softmax_of(scores.pop(t - LAG))
            if 0 <= t - 2 * LAG < rows:
                done = t - 2 * LAG
                mix(ordered[done], extents[done], *weights.pop(done))

    def amount_of(place):
        return over(span_of(order[place]) + (CHUNK - 1), CHUNK)

    by_shape(amount_of, rows, k_ref.shape[1] // CHUNK, attend)

    mixed = o_buf[...].astype(BF16)
    mixed_out[...] = mixed
    packed = exact(pack_ref[...], mixed)
    block = heads * CAP * STEPS
    for i in range(owners):
        outgoing[i] = packed[i * block : (i + 1) * block]


def write_out(matrix, values, heads, out_hbm, out_ref, sems):
    rows = out_ref.shape[1]
    wide = out_ref.shape[2] // heads
    span = STEPS * rows
    copies = []
    for c in range(heads):
        ordered = exact(matrix[c * span : (c + 1) * span], values)
        for s in range(STEPS):
            out_ref[s, :, c * wide : (c + 1) * wide] = ordered[s * rows : (s + 1) * rows]
        part = (slice(None), slice(None), pl.ds(c * wide, wide))
        copies.append(pltpu.make_async_copy(out_ref.at[part], out_hbm.at[part], sems.at[c]))
        copies[-1].start()
    for copy in copies:
        copy.wait()


def finish_kernel(heads, mixed, gather_ref, part, out_hbm, after, spread_out, out_ref, sems):
    after[...] = part[: after.shape[0], :]
    matrix = by_pair_matrix(heads, out_ref.shape[1])
    spread_out[...] = exact(matrix, gather_ref[...])
    write_out(matrix, mixed[...], heads, out_hbm, out_ref, sems)


def collect_kernel(owners, heads, spread, blocks, out_hbm, out_ref, sems):
    arrived = jnp.concatenate([blocks[i] for i in range(owners)], axis=0)
    write_out(spread, arrived, heads, out_hbm, out_ref, sems)


def exchange(blocks):
    return lax.all_to_all(blocks, "store", split_axis=0, concat_axis=0, tiled=True)


def in_hbm(array):
    return pltpu.with_memory_space_constraint(array, pltpu.HBM)


def swap_cores(part):
    return lax.ppermute(part, "tensor", [(0, 1), (1, 0)])


def shards(
    x_in,
    q_base,
    k_new,
    v_new,
    cache_k,
    cache_v,
    lengths,
    adapter_ids,
    slot_of,
    a_query,
    b_query,
    a_output,
    b_output,
):
    owners = lax.axis_size("store")
    rows = x_in.shape[1]
    width = x_in.shape[2]
    heads = cache_k.shape[2] // HD
    wide = width // heads
    adapt, rank = a_query.shape[1:]
    lanes = adapt * rank
    block = heads * CAP * STEPS
    items = owners * CAP * STEPS
    def flat(a_store):
        return jnp.transpose(a_store, (1, 2, 0)).reshape(lanes, a_store.shape[0])

    shape = jax.ShapeDtypeStruct
    small = pltpu.CompilerParams(vmem_limit_bytes=16 * 1024 * 1024)

    sent = shape((owners, block, wide), BF16)
    caches = (in_hbm(cache_k), in_hbm(cache_v))
    meta, blocks = pl.pallas_call(
        functools.partial(dispatch_kernel, owners, heads, adapt, rank),
        out_shape=[
            shape((2 * rows + owners * CAP,), I32),
            shape((owners, block, wide + lanes), BF16),
        ],
        in_specs=[HBM] * 6,
        out_specs=[SMEM, VMEM],
        scratch_shapes=[
            pltpu.SMEM((owners * CAP,), I32),
            pltpu.SMEM(adapter_ids.shape, I32),
            pltpu.SMEM(slot_of.shape, I32),
            pltpu.SMEM(lengths.shape, I32),
            pltpu.VMEM(x_in.shape, BF16),
            pltpu.SemaphoreType.DMA((4,)),
        ],
        compiler_params=small,
        name="dispatch",
    )(
        *map(in_hbm, (adapter_ids, slot_of, lengths, x_in)), *caches
    )

    arrived = exchange(blocks)
    part, mask = pl.pallas_call(
        functools.partial(project_kernel, owners, heads, wide, True),
        out_shape=[shape((items, lanes), F32)] * 2,
        in_specs=[VMEM] * 2,
        out_specs=[VMEM] * 2,
        compiler_params=small,
        name="project_query",
    )(flat(a_query), arrived)

    def expand(part, other, b_store, name, caches, *after):
        return pl.pallas_call(
            functools.partial(expand_kernel, owners, heads, wide),
            out_shape=sent,
            in_specs=[VMEM] * (3 + len(after)) + [HBM] * len(caches),
            out_specs=VMEM,
            compiler_params=small,
            name=name,
        )(part, other, b_store, *after, *caches)

    other = swap_cores(part)
    order, *prepared, after = pl.pallas_call(
        functools.partial(prepare_kernel, owners, heads),
        out_shape=[
            shape((rows,), I32),
            shape((rows * STEPS * heads, wide), BF16),
            shape((CHUNK, heads * HD), BF16),
            shape((CHUNK, heads * HD), BF16),
            shape((STEPS * wide // HD * heads, heads * HD), BF16),
            shape((rows * STEPS * heads, owners * block), BF16),
            shape((owners * block, rows * STEPS * heads), BF16),
            shape((8, lanes), F32),
        ],
        in_specs=[SMEM] + [VMEM] * 4,
        out_specs=[SMEM] + [VMEM] * 7,
        compiler_params=small,
        name="prepare",
    )(meta, q_base, k_new, v_new, part)
    returned = exchange(
        expand(part, other, b_query.reshape(lanes, width), "expand_query", caches, after)
    )

    mixed, outgoing = pl.pallas_call(
        functools.partial(attend_kernel, owners, heads, rows),
        out_shape=[
            shape((rows * STEPS * heads, wide), BF16),
            sent,
        ],
        in_specs=[SMEM] * 2 + [VMEM] * 9,
        out_specs=[VMEM] * 2,
        scratch_shapes=[
            pltpu.VMEM((rows * STEPS * heads, wide), F32),
            pltpu.VMEM((rows * STEPS * heads, wide), F32),
        ],
        compiler_params=small,
        name="attend",
    )(meta, order, *prepared, cache_k, cache_v, returned)

    arrived = exchange(outgoing)
    part = pl.pallas_call(
        functools.partial(project_kernel, owners, heads, wide, False),
        out_shape=shape((items, lanes), F32),
        in_specs=[VMEM] * 3,
        out_specs=VMEM,
        compiler_params=small,
        name="project_output",
    )(flat(a_output), arrived, mask)
    ordered = dict(
        scratch_shapes=[
            pltpu.VMEM((STEPS, rows, width), BF16),
            pltpu.SemaphoreType.DMA((heads,)),
        ],
        compiler_params=small,
    )
    other = swap_cores(part)
    attn_out, after, spread = pl.pallas_call(
        functools.partial(finish_kernel, heads),
        out_shape=[
            shape((STEPS, rows, width), BF16),
            shape((8, lanes), F32),
            shape((rows * STEPS * heads, owners * block), BF16),
        ],
        in_specs=[VMEM] * 3,
        out_specs=[HBM, VMEM, VMEM],
        name="finish",
        **ordered,
    )(mixed, prepared[4], part)
    returned = exchange(
        expand(part, other, b_output.reshape(lanes, width), "expand_output", (), after)
    )
    adapter_out = pl.pallas_call(
        functools.partial(collect_kernel, owners, heads),
        out_shape=shape((STEPS, rows, width), BF16),
        in_specs=[VMEM] * 2,
        out_specs=HBM,
        name="collect",
        **ordered,
    )(spread, returned)
    return (attn_out, adapter_out)


def solution(mesh):
    in_specs = (
        P(None, ("parts", "store"), "tensor"),
        P(None, ("parts", "store"), "tensor"),
        P(None, ("parts", "store"), "tensor"),
        P(None, ("parts", "store"), "tensor"),
        P(("parts", "store"), None, "tensor"),
        P(("parts", "store"), None, "tensor"),
        P(("parts", "store")),
        P(("parts", "store")),
        P("parts"),
        P(None, "store", None),
        P("store", None, "tensor"),
        P(None, "store", None),
        P("store", None, "tensor"),
    )
    out_specs = (P(None, ("parts", "store"), "tensor"), P(None, ("parts", "store"), "tensor"))
    return jax.shard_map(shards, mesh=mesh, in_specs=in_specs, out_specs=out_specs, check_vma=False)
```

```python
import functools
import math

import jax
import jax.numpy as jnp
from jax import lax
from jax.experimental import pallas as pl
from jax.experimental.pallas import tpu as pltpu
from jax.sharding import PartitionSpec as P

HD = 128
CAP = 2
STEPS = 2
LAG = 2
BF16 = jnp.bfloat16
F32 = jnp.float32
I32 = jnp.int32
VMEM = pl.BlockSpec(memory_space=pltpu.VMEM)
SMEM = pl.BlockSpec(memory_space=pltpu.SMEM)
HBM = pl.BlockSpec(memory_space=pltpu.HBM)


def iota(shape, dim):
    return lax.broadcasted_iota(I32, shape, dim)


def over(x, n):
    return lax.shift_right_logical(x, jnp.full_like(x, n.bit_length() - 1)) if n & (n - 1) == 0 else x // n


def rest(x, n):
    return x & (n - 1) if n & (n - 1) == 0 else x % n


def one_hot(hits):
    return jnp.where(hits, 1.0, 0.0).astype(BF16)


def stacked(ref, heads, wide):
    return jnp.concatenate(
        [ref[s, :, c * wide : (c + 1) * wide] for c in range(heads) for s in range(STEPS)], axis=0
    )


def pack_matrix(meta, owners, heads, rows, by_row):
    items = CAP * STEPS
    block = heads * items
    shape = (block, heads * STEPS * rows)
    at = iota(shape, 0)
    col = iota(shape, 1)
    head_step = over(at, items) * STEPS + rest(at, STEPS)
    offset = col - (head_step if by_row else head_step * rows)
    factor = heads * STEPS if by_row else 1
    first = rest(over(at, STEPS), CAP) == 0
    if not by_row:
        offset = jnp.where((offset >= 0) & (offset < rows), offset, -1)
    parts = []
    for i in range(owners):
        here = [meta[rows + i * CAP + k] for k in range(CAP)]
        spots = [jnp.where(h >= 0, h * factor, -rows * factor * heads * STEPS * 2) for h in here]
        parts.append(one_hot(offset == jnp.where(first, spots[0], spots[1])))
    return jnp.concatenate(parts, axis=0)


def unpack_matrix(meta, owners, heads, rows, by_row):
    items = CAP * STEPS
    block = heads * items
    pairs = heads * STEPS
    spots = [over(meta[r], CAP) * block + rest(meta[r], CAP) * STEPS for r in range(rows)]
    if by_row:
        shape = (pairs, owners * block)
        at = iota(shape, 0)
        col = iota(shape, 1) - (over(at, STEPS) * items + rest(at, STEPS))
        return jnp.concatenate([one_hot(col == spots[r]) for r in range(rows)], axis=0)
    shape = (rows, owners * block)
    at = iota(shape, 0)
    col = iota(shape, 1)
    spot = jnp.zeros(shape, I32)
    for r in range(rows):
        spot = jnp.where(at == r, spots[r], spot)
    offset = col - spot
    return jnp.concatenate(
        [one_hot(offset == c * items + s) for c in range(heads) for s in range(STEPS)], axis=0
    )


def by_row_matrix(heads, rows):
    pairs = heads * STEPS
    shape = (pairs * rows, pairs * rows)
    at = iota(shape, 0)
    return one_hot(iota(shape, 1) == rest(at, pairs) * rows + over(at, pairs))


def by_pair_matrix(heads, rows):
    pairs = heads * STEPS
    shape = (pairs * rows, pairs * rows)
    at = iota(shape, 0)
    return one_hot(iota(shape, 1) == rest(at, rows) * pairs + over(at, rows))


def regroup_matrix(owners, heads):
    items = CAP * STEPS
    total = owners * heads * items
    at = iota((total, total), 0)
    head = over(at, owners * items)
    owner = rest(over(at, items), owners)
    return one_hot(
        iota((total, total), 1) == owner * (heads * items) + head * items + rest(at, items)
    )


def ungroup_matrix(owners, heads):
    items = CAP * STEPS
    total = owners * heads * items
    at = iota((total, total), 0)
    owner = over(at, heads * items)
    head = rest(over(at, items), heads)
    return one_hot(
        iota((total, total), 1) == head * (owners * items) + owner * items + rest(at, items)
    )


def exact(matrix, values):
    return jnp.dot(matrix, values, preferred_element_type=F32).astype(BF16)


def dispatch_kernel(
    owners,
    heads,
    adapt,
    rank,
    ids_hbm,
    slot_of_hbm,
    lengths_hbm,
    x_hbm,
    k_hbm,
    v_hbm,
    meta,
    blocks,
    slot_at,
    ids,
    slot_of,
    lengths,
    x_ref,
    sems,
):
    pairs = (
        (ids_hbm, ids),
        (slot_of_hbm, slot_of),
        (lengths_hbm, lengths),
        (x_hbm, x_ref),
    )
    copies = [pltpu.make_async_copy(a, b, sems.at[k]) for k, (a, b) in enumerate(pairs)]
    for copy in copies:
        copy.start()
    rows = x_ref.shape[1]
    wide = x_ref.shape[2] // heads
    for copy in copies[:3]:
        copy.wait()
    row_at = rows
    spans = rows + owners * CAP
    for p in range(owners * CAP):
        meta[row_at + p] = -1
        slot_at[p] = -1
    for r in range(rows):
        slot = slot_of[ids[r]]
        first = over(slot, adapt) * CAP
        place = first + jnp.where(meta[row_at + first] >= 0, 1, 0)
        meta[row_at + place] = r
        slot_at[place] = rest(slot, adapt)
        meta[r] = place
        meta[spans + r] = lengths[r]
    items = CAP * STEPS
    block = heads * items
    copies[3].wait()
    packed = exact(pack_matrix(meta, owners, heads, rows, False), stacked(x_ref, heads, wide))
    at = iota((block, adapt * rank), 0)
    lane_slot = over(iota((block, adapt * rank), 1), rank)
    first = rest(over(at, STEPS), CAP) == 0
    for i in range(owners):
        blocks[i, :, :wide] = packed[i * block : (i + 1) * block]
        slot = jnp.where(first, slot_at[i * CAP], slot_at[i * CAP + 1])
        blocks[i, :, wide:] = one_hot(lane_slot == slot)


def project_kernel(owners, heads, wide, first, a_ref, blocks, *refs):
    core = lax.axis_index("tensor") if a_ref.shape[1] > heads * wide else 0
    if first:
        part_ref, mask_ref = refs
    else:
        mask_in, part_ref = refs
    grouped = regroup_matrix(owners, heads)
    items = owners * CAP * STEPS
    arrived = jnp.concatenate([blocks[i, :, :wide] for i in range(owners)], axis=0)
    arrived = exact(grouped, arrived)
    if first:
        masks = jnp.concatenate([blocks[i, :, wide:] for i in range(owners)], axis=0)
        mask = jnp.dot(grouped[:items], masks, preferred_element_type=F32)
        mask_ref[...] = mask
    else:
        mask = mask_in[...]
    total = jnp.zeros(mask.shape, F32)
    for c in range(heads):
        total = total + lax.dot_general(
            arrived[c * items : (c + 1) * items],
            a_ref[:, pl.ds(pl.multiple_of(core * (heads * wide) + c * wide, wide), wide)],
            (((1,), (1,)), ((), ())),
            preferred_element_type=F32,
        )
    part_ref[...] = total * mask


def expand_kernel(owners, heads, wide, mine, other, b_ref, *refs):
    blocks = refs[-1]
    low_rank = (mine[...] + other[...]).astype(BF16)
    pieces = []
    for c in range(heads):
        product = jnp.dot(
            low_rank, b_ref[:, c * wide : (c + 1) * wide], preferred_element_type=F32
        )
        pieces.append((2.0 * product).astype(BF16))
    back = exact(ungroup_matrix(owners, heads), jnp.concatenate(pieces, axis=0))
    block = heads * CAP * STEPS
    for i in range(owners):
        blocks[i] = back[i * block : (i + 1) * block]


def by_shape(span_at, rows, most, action):
    half, quarter = rows // 2, rows // 4
    lower = ((most // 8, most // 4), (most // 4, most // 4), (most // 4, most // 2), (most, most))
    upper = ((most // 4, most), (most // 2, most), (most * 3 // 4, most), (most, most))
    for at, shapes in ((0, lower), (half, upper)):
        first, last = span_at(at + quarter - 1), span_at(at + half - 1)
        open_yet = True
        for a, b in shapes:
            fits = (first <= a) & (last <= b) & open_yet
            open_yet = open_yet & ~((first <= a) & (last <= b))

            @pl.when(fits)
            def _():
                action(at, [a] * quarter + [b] * quarter)


def prepare_kernel(
    owners,
    heads,
    meta,
    q_ref,
    kn_ref,
    vn_ref,
    part,
    order,
    base_out,
    kn_out,
    vn_out,
    mask_out,
    gather_out,
    pack_out,
    after,
):
    rows = q_ref.shape[1]
    wide = q_ref.shape[2] // heads
    base_out[...] = exact(by_row_matrix(heads, rows), stacked(q_ref, heads, wide))
    for source, target in ((kn_ref, kn_out), (vn_ref, vn_out)):
        target[...] = jnp.concatenate([source[t] for t in range(STEPS)], axis=0)
    head_at = rest(over(iota(mask_out.shape, 0), STEPS), heads)
    mask_out[...] = one_hot(head_at == over(iota(mask_out.shape, 1), HD))
    gather_out[...] = unpack_matrix(meta, owners, heads, rows, True)
    pack_out[...] = pack_matrix(meta, owners, heads, rows, True)
    sizes = [meta[rows + owners * CAP + r] for r in range(rows)]
    ahead = [jnp.int32(0)] * rows
    for r in range(rows):
        for q in range(r):
            shorter = jnp.where(sizes[q] <= sizes[r], 1, 0)
            ahead[r] = ahead[r] + shorter
            ahead[q] = ahead[q] + (1 - shorter)
    for r in range(rows):
        order[ahead[r]] = r
    after[...] = part[: after.shape[0], :]


def attend_kernel(
    owners,
    heads,
    rows,
    meta,
    order,
    base_ref,
    kn_ref,
    vn_ref,
    mask_ref,
    gather_ref,
    pack_ref,
    k_ref,
    v_ref,
    blocks,
    mixed_out,
    outgoing,
    q_buf,
    o_buf,
):
    wide = base_ref.shape[1]
    groups = wide // HD
    pairs = heads * STEPS
    total = groups * pairs

    def span_of(row):
        return meta[rows + owners * CAP + row]

    delta = jnp.dot(
        gather_ref[...],
        jnp.concatenate([blocks[i] for i in range(owners)], axis=0),
        preferred_element_type=F32,
    )
    q_buf[...] = base_ref[...].astype(F32) + delta

    head_own = rest(over(iota((total, HD), 0), STEPS), heads)
    factor = math.log2(math.e) / math.sqrt(HD)
    fresh_shape = (total, STEPS * rows)
    fresh_at = iota(fresh_shape, 1)
    fresh_step = over(fresh_at, rows)
    fresh_row = jnp.where(fresh_step <= rest(iota(fresh_shape, 0), STEPS), rest(fresh_at, rows), rows)
    contract = (((1,), (1,)), ((), ()))

    def scores_of(row, extent):
        flat = q_buf[pl.ds(pl.multiple_of(row * pairs, pairs), pairs), :]
        one = jnp.concatenate([flat[:, j * HD : (j + 1) * HD] for j in range(groups)], axis=0)
        spread = jnp.concatenate([one.astype(BF16)] * heads, axis=1) * mask_ref[...]
        keys = jnp.concatenate([k_ref[row, :extent, :], kn_ref[...]], axis=0)
        score = lax.dot_general(spread, keys, contract, preferred_element_type=F32)
        cached = jnp.where(iota((total, extent), 1) < span_of(row), score[:, :extent], -jnp.inf)
        fresh = jnp.where(fresh_row == row, score[:, extent:], -jnp.inf)
        return jnp.concatenate([cached, fresh], axis=1)

    def softmax_of(score):
        top = jnp.max(score, axis=1, keepdims=True)
        weight = jnp.exp2((score - top) * factor)
        return weight.astype(BF16), 1.0 / jnp.sum(weight, axis=1, keepdims=True)

    def mix(row, extent, weight, share):
        values = jnp.concatenate([v_ref[row, :extent, :], vn_ref[...]], axis=0)
        mixed = jnp.dot(weight, values, preferred_element_type=F32)
        own = mixed[:, :HD]
        for c in range(1, heads):
            own = jnp.where(head_own == c, mixed[:, c * HD : (c + 1) * HD], own)
        own = own * share
        o_buf[pl.ds(pl.multiple_of(row * pairs, pairs), pairs), :] = jnp.concatenate(
            [own[j * pairs : (j + 1) * pairs] for j in range(groups)], axis=1
        )

    def attend(at, extents):
        count = len(extents)
        ordered = [order[at + k] for k in range(count)]
        scores, weights = {}, {}
        for t in range(count + 2 * LAG):
            if t < count:
                scores[t] = scores_of(ordered[t], extents[t])
            if 0 <= t - LAG < count:
                weights[t - LAG] = softmax_of(scores.pop(t - LAG))
            if 0 <= t - 2 * LAG < count:
                done = t - 2 * LAG
                mix(ordered[done], extents[done], *weights.pop(done))

    by_shape(lambda place: span_of(order[place]), rows, k_ref.shape[1], attend)

    mixed = o_buf[...].astype(BF16)
    mixed_out[...] = mixed
    packed = exact(pack_ref[...], mixed)
    block = heads * CAP * STEPS
    for i in range(owners):
        outgoing[i] = packed[i * block : (i + 1) * block]


def write_out(matrix, values, heads, out_hbm, out_ref, sems):
    rows = out_ref.shape[1]
    wide = out_ref.shape[2] // heads
    span = STEPS * rows
    copies = []
    for c in range(heads):
        ordered = exact(matrix[c * span : (c + 1) * span], values)
        for s in range(STEPS):
            out_ref[s, :, c * wide : (c + 1) * wide] = ordered[s * rows : (s + 1) * rows]
        part = (slice(None), slice(None), pl.ds(c * wide, wide))
        copies.append(pltpu.make_async_copy(out_ref.at[part], out_hbm.at[part], sems.at[c]))
        copies[-1].start()
    for copy in copies:
        copy.wait()


def finish_kernel(heads, mixed, gather_ref, part, out_hbm, after, spread_out, out_ref, sems):
    after[...] = part[: after.shape[0], :]
    matrix = by_pair_matrix(heads, out_ref.shape[1])
    spread_out[...] = exact(matrix, gather_ref[...])
    write_out(matrix, mixed[...], heads, out_hbm, out_ref, sems)


def collect_kernel(owners, heads, spread, blocks, out_hbm, out_ref, sems):
    arrived = jnp.concatenate([blocks[i] for i in range(owners)], axis=0)
    write_out(spread, arrived, heads, out_hbm, out_ref, sems)


def exchange(blocks):
    return lax.all_to_all(blocks, "store", split_axis=0, concat_axis=0, tiled=True)


def in_hbm(array):
    return pltpu.with_memory_space_constraint(array, pltpu.HBM)


def swap_cores(part):
    return lax.ppermute(part, "tensor", [(0, 1), (1, 0)])


def shards(
    x_in,
    q_base,
    k_new,
    v_new,
    cache_k,
    cache_v,
    lengths,
    adapter_ids,
    slot_of,
    a_query,
    b_query,
    a_output,
    b_output,
):
    owners = lax.axis_size("store")
    rows = x_in.shape[1]
    width = x_in.shape[2]
    heads = cache_k.shape[2] // HD
    wide = width // heads
    adapt, rank = a_query.shape[1:]
    lanes = adapt * rank
    block = heads * CAP * STEPS
    items = owners * CAP * STEPS
    def flat(a_store):
        return jnp.transpose(a_store, (1, 2, 0)).reshape(lanes, a_store.shape[0])

    shape = jax.ShapeDtypeStruct
    small = pltpu.CompilerParams(vmem_limit_bytes=16 * 1024 * 1024)

    sent = shape((owners, block, wide), BF16)
    caches = (in_hbm(cache_k), in_hbm(cache_v))
    meta, blocks = pl.pallas_call(
        functools.partial(dispatch_kernel, owners, heads, adapt, rank),
        out_shape=[
            shape((2 * rows + owners * CAP,), I32),
            shape((owners, block, wide + lanes), BF16),
        ],
        in_specs=[HBM] * 6,
        out_specs=[SMEM, VMEM],
        scratch_shapes=[
            pltpu.SMEM((owners * CAP,), I32),
            pltpu.SMEM(adapter_ids.shape, I32),
            pltpu.SMEM(slot_of.shape, I32),
            pltpu.SMEM(lengths.shape, I32),
            pltpu.VMEM(x_in.shape, BF16),
            pltpu.SemaphoreType.DMA((4,)),
        ],
        compiler_params=small,
        name="dispatch",
    )(
        *map(in_hbm, (adapter_ids, slot_of, lengths, x_in)), *caches
    )

    arrived = exchange(blocks)
    part, mask = pl.pallas_call(
        functools.partial(project_kernel, owners, heads, wide, True),
        out_shape=[shape((items, lanes), F32)] * 2,
        in_specs=[VMEM] * 2,
        out_specs=[VMEM] * 2,
        compiler_params=small,
        name="project_query",
    )(flat(a_query), arrived)

    def expand(part, other, b_store, name, caches, *after):
        return pl.pallas_call(
            functools.partial(expand_kernel, owners, heads, wide),
            out_shape=sent,
            in_specs=[VMEM] * (3 + len(after)) + [HBM] * len(caches),
            out_specs=VMEM,
            compiler_params=small,
            name=name,
        )(part, other, b_store, *after, *caches)

    other = swap_cores(part)
    order, *prepared, after = pl.pallas_call(
        functools.partial(prepare_kernel, owners, heads),
        out_shape=[
            shape((rows,), I32),
            shape((rows * STEPS * heads, wide), BF16),
            shape((STEPS * rows, heads * HD), BF16),
            shape((STEPS * rows, heads * HD), BF16),
            shape((STEPS * wide // HD * heads, heads * HD), BF16),
            shape((rows * STEPS * heads, owners * block), BF16),
            shape((owners * block, rows * STEPS * heads), BF16),
            shape((8, lanes), F32),
        ],
        in_specs=[SMEM] + [VMEM] * 4,
        out_specs=[SMEM] + [VMEM] * 7,
        compiler_params=small,
        name="prepare",
    )(meta, q_base, k_new, v_new, part)
    returned = exchange(
        expand(part, other, b_query.reshape(lanes, width), "expand_query", caches, after)
    )

    mixed, outgoing = pl.pallas_call(
        functools.partial(attend_kernel, owners, heads, rows),
        out_shape=[
            shape((rows * STEPS * heads, wide), BF16),
            sent,
        ],
        in_specs=[SMEM] * 2 + [VMEM] * 9,
        out_specs=[VMEM] * 2,
        scratch_shapes=[
            pltpu.VMEM((rows * STEPS * heads, wide), F32),
            pltpu.VMEM((rows * STEPS * heads, wide), F32),
        ],
        compiler_params=small,
        name="attend",
    )(meta, order, *prepared, cache_k, cache_v, returned)

    arrived = exchange(outgoing)
    part = pl.pallas_call(
        functools.partial(project_kernel, owners, heads, wide, False),
        out_shape=shape((items, lanes), F32),
        in_specs=[VMEM] * 3,
        out_specs=VMEM,
        compiler_params=small,
        name="project_output",
    )(flat(a_output), arrived, mask)
    ordered = dict(
        scratch_shapes=[
            pltpu.VMEM((STEPS, rows, width), BF16),
            pltpu.SemaphoreType.DMA((heads,)),
        ],
        compiler_params=small,
    )
    other = swap_cores(part)
    attn_out, after, spread = pl.pallas_call(
        functools.partial(finish_kernel, heads),
        out_shape=[
            shape((STEPS, rows, width), BF16),
            shape((8, lanes), F32),
            shape((rows * STEPS * heads, owners * block), BF16),
        ],
        in_specs=[VMEM] * 3,
        out_specs=[HBM, VMEM, VMEM],
        name="finish",
        **ordered,
    )(mixed, prepared[4], part)
    returned = exchange(
        expand(part, other, b_output.reshape(lanes, width), "expand_output", (), after)
    )
    adapter_out = pl.pallas_call(
        functools.partial(collect_kernel, owners, heads),
        out_shape=shape((STEPS, rows, width), BF16),
        in_specs=[VMEM] * 2,
        out_specs=HBM,
        name="collect",
        **ordered,
    )(spread, returned)
    return (attn_out, adapter_out)


def solution(mesh):
    in_specs = (
        P(None, ("parts", "store"), "tensor"),
        P(None, ("parts", "store"), "tensor"),
        P(None, ("parts", "store"), "tensor"),
        P(None, ("parts", "store"), "tensor"),
        P(("parts", "store"), None, "tensor"),
        P(("parts", "store"), None, "tensor"),
        P(("parts", "store")),
        P(("parts", "store")),
        P("parts"),
        P(None, "store", None),
        P("store", None, "tensor"),
        P(None, "store", None),
        P("store", None, "tensor"),
    )
    out_specs = (P(None, ("parts", "store"), "tensor"), P(None, ("parts", "store"), "tensor"))
    return jax.shard_map(shards, mesh=mesh, in_specs=in_specs, out_specs=out_specs, check_vma=False)
```

```python
import functools
import math

import jax
import jax.numpy as jnp
from jax import lax
from jax.experimental import pallas as pl
from jax.experimental.pallas import tpu as pltpu
from jax.sharding import PartitionSpec as P

HD = 128
CAP = 2
STEPS = 2
LAG = 2
BF16 = jnp.bfloat16
F32 = jnp.float32
I32 = jnp.int32
VMEM = pl.BlockSpec(memory_space=pltpu.VMEM)
SMEM = pl.BlockSpec(memory_space=pltpu.SMEM)
HBM = pl.BlockSpec(memory_space=pltpu.HBM)


def iota(shape, dim):
    return lax.broadcasted_iota(I32, shape, dim)


def over(x, n):
    return lax.shift_right_logical(x, jnp.full_like(x, n.bit_length() - 1)) if n & (n - 1) == 0 else x // n


def rest(x, n):
    return x & (n - 1) if n & (n - 1) == 0 else x % n


def one_hot(hits):
    return jnp.where(hits, 1.0, 0.0).astype(BF16)


def stacked(ref, heads, wide):
    return jnp.concatenate(
        [ref[s, :, c * wide : (c + 1) * wide] for c in range(heads) for s in range(STEPS)], axis=0
    )


def pack_matrix(meta, owners, heads, rows, by_row):
    items = CAP * STEPS
    block = heads * items
    shape = (block, heads * STEPS * rows)
    at = iota(shape, 0)
    col = iota(shape, 1)
    head_step = over(at, items) * STEPS + rest(at, STEPS)
    offset = col - (head_step if by_row else head_step * rows)
    factor = heads * STEPS if by_row else 1
    first = rest(over(at, STEPS), CAP) == 0
    if not by_row:
        offset = jnp.where((offset >= 0) & (offset < rows), offset, -1)
    parts = []
    for i in range(owners):
        here = [meta[rows + i * CAP + k] for k in range(CAP)]
        spots = [jnp.where(h >= 0, h * factor, -rows * factor * heads * STEPS * 2) for h in here]
        parts.append(one_hot(offset == jnp.where(first, spots[0], spots[1])))
    return jnp.concatenate(parts, axis=0)


def unpack_matrix(meta, owners, heads, rows, by_row):
    items = CAP * STEPS
    block = heads * items
    pairs = heads * STEPS
    spots = [over(meta[r], CAP) * block + rest(meta[r], CAP) * STEPS for r in range(rows)]
    if by_row:
        shape = (pairs, owners * block)
        at = iota(shape, 0)
        col = iota(shape, 1) - (over(at, STEPS) * items + rest(at, STEPS))
        return jnp.concatenate([one_hot(col == spots[r]) for r in range(rows)], axis=0)
    shape = (rows, owners * block)
    at = iota(shape, 0)
    col = iota(shape, 1)
    spot = jnp.zeros(shape, I32)
    for r in range(rows):
        spot = jnp.where(at == r, spots[r], spot)
    offset = col - spot
    return jnp.concatenate(
        [one_hot(offset == c * items + s) for c in range(heads) for s in range(STEPS)], axis=0
    )


def by_row_matrix(heads, rows):
    pairs = heads * STEPS
    shape = (pairs * rows, pairs * rows)
    at = iota(shape, 0)
    return one_hot(iota(shape, 1) == rest(at, pairs) * rows + over(at, pairs))


def by_pair_matrix(heads, rows):
    pairs = heads * STEPS
    shape = (pairs * rows, pairs * rows)
    at = iota(shape, 0)
    return one_hot(iota(shape, 1) == rest(at, rows) * pairs + over(at, rows))


def regroup_matrix(owners, heads):
    items = CAP * STEPS
    total = owners * heads * items
    at = iota((total, total), 0)
    head = over(at, owners * items)
    owner = rest(over(at, items), owners)
    return one_hot(
        iota((total, total), 1) == owner * (heads * items) + head * items + rest(at, items)
    )


def ungroup_matrix(owners, heads):
    items = CAP * STEPS
    total = owners * heads * items
    at = iota((total, total), 0)
    owner = over(at, heads * items)
    head = rest(over(at, items), heads)
    return one_hot(
        iota((total, total), 1) == head * (owners * items) + owner * items + rest(at, items)
    )


def exact(matrix, values):
    return jnp.dot(matrix, values, preferred_element_type=F32).astype(BF16)


def dispatch_kernel(
    owners,
    heads,
    adapt,
    rank,
    ids_hbm,
    slot_of_hbm,
    lengths_hbm,
    x_hbm,
    k_hbm,
    v_hbm,
    meta,
    blocks,
    slot_at,
    ids,
    slot_of,
    lengths,
    x_ref,
    sems,
):
    pairs = (
        (ids_hbm, ids),
        (slot_of_hbm, slot_of),
        (lengths_hbm, lengths),
        (x_hbm, x_ref),
    )
    copies = [pltpu.make_async_copy(a, b, sems.at[k]) for k, (a, b) in enumerate(pairs)]
    for copy in copies:
        copy.start()
    rows = x_ref.shape[1]
    wide = x_ref.shape[2] // heads
    for copy in copies[:3]:
        copy.wait()
    row_at = rows
    spans = rows + owners * CAP
    for p in range(owners * CAP):
        meta[row_at + p] = -1
        slot_at[p] = -1
    for r in range(rows):
        slot = slot_of[ids[r]]
        owner = over(slot, adapt)
        half = over(owner, 2)
        first = jnp.where(rest(owner, 2) == 0, half, owners - 1 - half) * CAP
        place = first + jnp.where(meta[row_at + first] >= 0, 1, 0)
        meta[row_at + place] = r
        slot_at[place] = rest(slot, adapt)
        meta[r] = place
        meta[spans + r] = lengths[r]
    items = CAP * STEPS
    block = heads * items
    copies[3].wait()
    packed = exact(pack_matrix(meta, owners, heads, rows, False), stacked(x_ref, heads, wide))
    at = iota((block, adapt * rank), 0)
    lane_slot = over(iota((block, adapt * rank), 1), rank)
    first = rest(over(at, STEPS), CAP) == 0
    for i in range(owners):
        blocks[i, :, :wide] = packed[i * block : (i + 1) * block]
        slot = jnp.where(first, slot_at[i * CAP], slot_at[i * CAP + 1])
        blocks[i, :, wide:] = one_hot(lane_slot == slot)


def project_kernel(owners, heads, wide, first, a_ref, blocks, *refs):
    core = lax.axis_index("tensor") if a_ref.shape[1] > heads * wide else 0
    if first:
        part_ref, mask_ref = refs
    else:
        mask_in, part_ref = refs
    grouped = regroup_matrix(owners, heads)
    items = owners * CAP * STEPS
    arrived = jnp.concatenate([blocks[i, :, :wide] for i in range(owners)], axis=0)
    arrived = exact(grouped, arrived)
    if first:
        masks = jnp.concatenate([blocks[i, :, wide:] for i in range(owners)], axis=0)
        mask = jnp.dot(grouped[:items], masks, preferred_element_type=F32)
        mask_ref[...] = mask
    else:
        mask = mask_in[...]
    total = jnp.zeros(mask.shape, F32)
    for c in range(heads):
        total = total + lax.dot_general(
            arrived[c * items : (c + 1) * items],
            a_ref[:, pl.ds(pl.multiple_of(core * (heads * wide) + c * wide, wide), wide)],
            (((1,), (1,)), ((), ())),
            preferred_element_type=F32,
        )
    part_ref[...] = total * mask


def expand_kernel(owners, heads, wide, mine, other, b_ref, *refs):
    blocks = refs[-1]
    low_rank = (mine[...] + other[...]).astype(BF16)
    pieces = []
    for c in range(heads):
        product = jnp.dot(
            low_rank, b_ref[:, c * wide : (c + 1) * wide], preferred_element_type=F32
        )
        pieces.append((2.0 * product).astype(BF16))
    back = exact(ungroup_matrix(owners, heads), jnp.concatenate(pieces, axis=0))
    block = heads * CAP * STEPS
    for i in range(owners):
        blocks[i] = back[i * block : (i + 1) * block]


def by_shape(span_at, rows, most, action):
    half, quarter = rows // 2, rows // 4
    lower = ((most // 8, most // 4), (most // 4, most // 4), (most // 4, most // 2), (most, most))
    upper = ((most // 4, most), (most // 2, most), (most * 3 // 4, most), (most, most))
    for at, shapes in ((0, lower), (half, upper)):
        first, last = span_at(at + quarter - 1), span_at(at + half - 1)
        open_yet = True
        for a, b in shapes:
            fits = (first <= a) & (last <= b) & open_yet
            open_yet = open_yet & ~((first <= a) & (last <= b))

            @pl.when(fits)
            def _():
                action(at, [a] * quarter + [b] * quarter)


def prepare_kernel(
    owners,
    heads,
    meta,
    q_ref,
    kn_ref,
    vn_ref,
    part,
    order,
    base_out,
    kn_out,
    vn_out,
    mask_out,
    gather_out,
    pack_out,
    after,
):
    rows = q_ref.shape[1]
    wide = q_ref.shape[2] // heads
    base_out[...] = exact(by_row_matrix(heads, rows), stacked(q_ref, heads, wide))
    for source, target in ((kn_ref, kn_out), (vn_ref, vn_out)):
        target[...] = jnp.concatenate([source[t] for t in range(STEPS)], axis=0)
    head_at = rest(over(iota(mask_out.shape, 0), STEPS), heads)
    mask_out[...] = one_hot(head_at == over(iota(mask_out.shape, 1), HD))
    gather_out[...] = unpack_matrix(meta, owners, heads, rows, True)
    pack_out[...] = pack_matrix(meta, owners, heads, rows, True)
    sizes = [meta[rows + owners * CAP + r] for r in range(rows)]
    ahead = [jnp.int32(0)] * rows
    for r in range(rows):
        for q in range(r):
            shorter = jnp.where(sizes[q] <= sizes[r], 1, 0)
            ahead[r] = ahead[r] + shorter
            ahead[q] = ahead[q] + (1 - shorter)
    for r in range(rows):
        order[ahead[r]] = r
    after[...] = part[: after.shape[0], :]


def attend_kernel(
    owners,
    heads,
    rows,
    meta,
    order,
    base_ref,
    kn_ref,
    vn_ref,
    mask_ref,
    gather_ref,
    pack_ref,
    k_ref,
    v_ref,
    blocks,
    mixed_out,
    outgoing,
    q_buf,
    o_buf,
):
    wide = base_ref.shape[1]
    groups = wide // HD
    pairs = heads * STEPS
    total = groups * pairs

    def span_of(row):
        return meta[rows + owners * CAP + row]

    delta = jnp.dot(
        gather_ref[...],
        jnp.concatenate([blocks[i] for i in range(owners)], axis=0),
        preferred_element_type=F32,
    )
    q_buf[...] = base_ref[...].astype(F32) + delta

    head_own = rest(over(iota((total, HD), 0), STEPS), heads)
    factor = math.log2(math.e) / math.sqrt(HD)
    fresh_shape = (total, STEPS * rows)
    fresh_at = iota(fresh_shape, 1)
    fresh_step = over(fresh_at, rows)
    fresh_row = jnp.where(fresh_step <= rest(iota(fresh_shape, 0), STEPS), rest(fresh_at, rows), rows)
    contract = (((1,), (1,)), ((), ()))

    def scores_of(row, extent):
        flat = q_buf[pl.ds(pl.multiple_of(row * pairs, pairs), pairs), :]
        one = jnp.concatenate([flat[:, j * HD : (j + 1) * HD] for j in range(groups)], axis=0)
        spread = jnp.concatenate([one.astype(BF16)] * heads, axis=1) * mask_ref[...]
        keys = jnp.concatenate([k_ref[row, :extent, :], kn_ref[...]], axis=0)
        score = lax.dot_general(spread, keys, contract, preferred_element_type=F32)
        cached = jnp.where(iota((total, extent), 1) < span_of(row), score[:, :extent], -jnp.inf)
        fresh = jnp.where(fresh_row == row, score[:, extent:], -jnp.inf)
        return jnp.concatenate([cached, fresh], axis=1)

    def softmax_of(score):
        top = jnp.max(score, axis=1, keepdims=True)
        weight = jnp.exp2((score - top) * factor)
        return weight.astype(BF16), 1.0 / jnp.sum(weight, axis=1, keepdims=True)

    def mix(row, extent, weight, share):
        values = jnp.concatenate([v_ref[row, :extent, :], vn_ref[...]], axis=0)
        mixed = jnp.dot(weight, values, preferred_element_type=F32)
        own = mixed[:, :HD]
        for c in range(1, heads):
            own = jnp.where(head_own == c, mixed[:, c * HD : (c + 1) * HD], own)
        own = own * share
        o_buf[pl.ds(pl.multiple_of(row * pairs, pairs), pairs), :] = jnp.concatenate(
            [own[j * pairs : (j + 1) * pairs] for j in range(groups)], axis=1
        )

    def attend(at, extents):
        count = len(extents)
        ordered = [order[at + k] for k in range(count)]
        scores, weights = {}, {}
        for t in range(count + 2 * LAG):
            if t < count:
                scores[t] = scores_of(ordered[t], extents[t])
            if 0 <= t - LAG < count:
                weights[t - LAG] = softmax_of(scores.pop(t - LAG))
            if 0 <= t - 2 * LAG < count:
                done = t - 2 * LAG
                mix(ordered[done], extents[done], *weights.pop(done))

    by_shape(lambda place: span_of(order[place]), rows, k_ref.shape[1], attend)

    mixed = o_buf[...].astype(BF16)
    mixed_out[...] = mixed
    packed = exact(pack_ref[...], mixed)
    block = heads * CAP * STEPS
    for i in range(owners):
        outgoing[i] = packed[i * block : (i + 1) * block]


def write_out(matrix, values, heads, out_hbm, out_ref, sems):
    rows = out_ref.shape[1]
    wide = out_ref.shape[2] // heads
    span = STEPS * rows
    copies = []
    for c in range(heads):
        ordered = exact(matrix[c * span : (c + 1) * span], values)
        for s in range(STEPS):
            out_ref[s, :, c * wide : (c + 1) * wide] = ordered[s * rows : (s + 1) * rows]
        part = (slice(None), slice(None), pl.ds(c * wide, wide))
        copies.append(pltpu.make_async_copy(out_ref.at[part], out_hbm.at[part], sems.at[c]))
        copies[-1].start()
    for copy in copies:
        copy.wait()


def finish_kernel(heads, mixed, gather_ref, part, out_hbm, after, spread_out, out_ref, sems):
    after[...] = part[: after.shape[0], :]
    matrix = by_pair_matrix(heads, out_ref.shape[1])
    spread_out[...] = exact(matrix, gather_ref[...])
    write_out(matrix, mixed[...], heads, out_hbm, out_ref, sems)


def collect_kernel(owners, heads, spread, blocks, out_hbm, out_ref, sems):
    arrived = jnp.concatenate([blocks[i] for i in range(owners)], axis=0)
    write_out(spread, arrived, heads, out_hbm, out_ref, sems)


def exchange(blocks):
    owners = blocks.shape[0]
    cycle = list(range(0, owners, 2)) + list(range(owners - 1, 0, -2))
    return lax.all_to_all(
        blocks, "store", split_axis=0, concat_axis=0, axis_index_groups=[cycle], tiled=True
    )


def in_hbm(array):
    return pltpu.with_memory_space_constraint(array, pltpu.HBM)


def swap_cores(part):
    return lax.ppermute(part, "tensor", [(0, 1), (1, 0)])


def shards(
    x_in,
    q_base,
    k_new,
    v_new,
    cache_k,
    cache_v,
    lengths,
    adapter_ids,
    slot_of,
    a_query,
    b_query,
    a_output,
    b_output,
):
    owners = lax.axis_size("store")
    rows = x_in.shape[1]
    width = x_in.shape[2]
    heads = cache_k.shape[2] // HD
    wide = width // heads
    adapt, rank = a_query.shape[1:]
    lanes = adapt * rank
    block = heads * CAP * STEPS
    items = owners * CAP * STEPS
    def flat(a_store):
        return jnp.transpose(a_store, (1, 2, 0)).reshape(lanes, a_store.shape[0])

    shape = jax.ShapeDtypeStruct
    small = pltpu.CompilerParams(vmem_limit_bytes=16 * 1024 * 1024)

    sent = shape((owners, block, wide), BF16)
    caches = (in_hbm(cache_k), in_hbm(cache_v))
    meta, blocks = pl.pallas_call(
        functools.partial(dispatch_kernel, owners, heads, adapt, rank),
        out_shape=[
            shape((2 * rows + owners * CAP,), I32),
            shape((owners, block, wide + lanes), BF16),
        ],
        in_specs=[HBM] * 6,
        out_specs=[SMEM, VMEM],
        scratch_shapes=[
            pltpu.SMEM((owners * CAP,), I32),
            pltpu.SMEM(adapter_ids.shape, I32),
            pltpu.SMEM(slot_of.shape, I32),
            pltpu.SMEM(lengths.shape, I32),
            pltpu.VMEM(x_in.shape, BF16),
            pltpu.SemaphoreType.DMA((4,)),
        ],
        compiler_params=small,
        name="dispatch",
    )(
        *map(in_hbm, (adapter_ids, slot_of, lengths, x_in)), *caches
    )

    arrived = exchange(blocks)
    part, mask = pl.pallas_call(
        functools.partial(project_kernel, owners, heads, wide, True),
        out_shape=[shape((items, lanes), F32)] * 2,
        in_specs=[VMEM] * 2,
        out_specs=[VMEM] * 2,
        compiler_params=small,
        name="project_query",
    )(flat(a_query), arrived)

    def expand(part, other, b_store, name, caches, *after):
        return pl.pallas_call(
            functools.partial(expand_kernel, owners, heads, wide),
            out_shape=sent,
            in_specs=[VMEM] * (3 + len(after)) + [HBM] * len(caches),
            out_specs=VMEM,
            compiler_params=small,
            name=name,
        )(part, other, b_store, *after, *caches)

    other = swap_cores(part)
    order, *prepared, after = pl.pallas_call(
        functools.partial(prepare_kernel, owners, heads),
        out_shape=[
            shape((rows,), I32),
            shape((rows * STEPS * heads, wide), BF16),
            shape((STEPS * rows, heads * HD), BF16),
            shape((STEPS * rows, heads * HD), BF16),
            shape((STEPS * wide // HD * heads, heads * HD), BF16),
            shape((rows * STEPS * heads, owners * block), BF16),
            shape((owners * block, rows * STEPS * heads), BF16),
            shape((8, lanes), F32),
        ],
        in_specs=[SMEM] + [VMEM] * 4,
        out_specs=[SMEM] + [VMEM] * 7,
        compiler_params=small,
        name="prepare",
    )(meta, q_base, k_new, v_new, part)
    returned = exchange(
        expand(part, other, b_query.reshape(lanes, width), "expand_query", caches, after)
    )

    mixed, outgoing = pl.pallas_call(
        functools.partial(attend_kernel, owners, heads, rows),
        out_shape=[
            shape((rows * STEPS * heads, wide), BF16),
            sent,
        ],
        in_specs=[SMEM] * 2 + [VMEM] * 9,
        out_specs=[VMEM] * 2,
        scratch_shapes=[
            pltpu.VMEM((rows * STEPS * heads, wide), F32),
            pltpu.VMEM((rows * STEPS * heads, wide), F32),
        ],
        compiler_params=small,
        name="attend",
    )(meta, order, *prepared, cache_k, cache_v, returned)

    arrived = exchange(outgoing)
    part = pl.pallas_call(
        functools.partial(project_kernel, owners, heads, wide, False),
        out_shape=shape((items, lanes), F32),
        in_specs=[VMEM] * 3,
        out_specs=VMEM,
        compiler_params=small,
        name="project_output",
    )(flat(a_output), arrived, mask)
    ordered = dict(
        scratch_shapes=[
            pltpu.VMEM((STEPS, rows, width), BF16),
            pltpu.SemaphoreType.DMA((heads,)),
        ],
        compiler_params=small,
    )
    other = swap_cores(part)
    attn_out, after, spread = pl.pallas_call(
        functools.partial(finish_kernel, heads),
        out_shape=[
            shape((STEPS, rows, width), BF16),
            shape((8, lanes), F32),
            shape((rows * STEPS * heads, owners * block), BF16),
        ],
        in_specs=[VMEM] * 3,
        out_specs=[HBM, VMEM, VMEM],
        name="finish",
        **ordered,
    )(mixed, prepared[4], part)
    returned = exchange(
        expand(part, other, b_output.reshape(lanes, width), "expand_output", (), after)
    )
    adapter_out = pl.pallas_call(
        functools.partial(collect_kernel, owners, heads),
        out_shape=shape((STEPS, rows, width), BF16),
        in_specs=[VMEM] * 2,
        out_specs=HBM,
        name="collect",
        **ordered,
    )(spread, returned)
    return (attn_out, adapter_out)


def solution(mesh):
    in_specs = (
        P(None, ("parts", "store"), "tensor"),
        P(None, ("parts", "store"), "tensor"),
        P(None, ("parts", "store"), "tensor"),
        P(None, ("parts", "store"), "tensor"),
        P(("parts", "store"), None, "tensor"),
        P(("parts", "store"), None, "tensor"),
        P(("parts", "store")),
        P(("parts", "store")),
        P("parts"),
        P(None, "store", None),
        P("store", None, "tensor"),
        P(None, "store", None),
        P("store", None, "tensor"),
    )
    out_specs = (P(None, ("parts", "store"), "tensor"), P(None, ("parts", "store"), "tensor"))
    return jax.shard_map(shards, mesh=mesh, in_specs=in_specs, out_specs=out_specs, check_vma=False)
```

```python
import functools
import math

import jax
import jax.numpy as jnp
from jax import lax
from jax.experimental import pallas as pl
from jax.experimental.pallas import tpu as pltpu
from jax.sharding import PartitionSpec as P

HD = 128
CAP = 2
STEPS = 2
LAG = 2
SPLIT = 2
BF16 = jnp.bfloat16
F32 = jnp.float32
I32 = jnp.int32
VMEM = pl.BlockSpec(memory_space=pltpu.VMEM)
SMEM = pl.BlockSpec(memory_space=pltpu.SMEM)
HBM = pl.BlockSpec(memory_space=pltpu.HBM)


def iota(shape, dim):
    return lax.broadcasted_iota(I32, shape, dim)


def over(x, n):
    return lax.shift_right_logical(x, jnp.full_like(x, n.bit_length() - 1)) if n & (n - 1) == 0 else x // n


def rest(x, n):
    return x & (n - 1) if n & (n - 1) == 0 else x % n


def one_hot(hits):
    return jnp.where(hits, 1.0, 0.0).astype(BF16)


def stacked(ref, heads, wide):
    return jnp.concatenate(
        [ref[s, :, c * wide : (c + 1) * wide] for c in range(heads) for s in range(STEPS)], axis=0
    )


def pack_matrix(meta, owners, heads, rows, by_row):
    items = CAP * STEPS
    block = heads * items
    shape = (block, heads * STEPS * rows)
    at = iota(shape, 0)
    col = iota(shape, 1)
    head_step = over(at, items) * STEPS + rest(at, STEPS)
    offset = col - (head_step if by_row else head_step * rows)
    factor = heads * STEPS if by_row else 1
    first = rest(over(at, STEPS), CAP) == 0
    if not by_row:
        offset = jnp.where((offset >= 0) & (offset < rows), offset, -1)
    parts = []
    for i in range(owners):
        here = [meta[rows + i * CAP + k] for k in range(CAP)]
        spots = [jnp.where(h >= 0, h * factor, -rows * factor * heads * STEPS * 2) for h in here]
        parts.append(one_hot(offset == jnp.where(first, spots[0], spots[1])))
    return jnp.concatenate(parts, axis=0)


def unpack_matrix(meta, owners, heads, rows, by_row):
    items = CAP * STEPS
    block = heads * items
    pairs = heads * STEPS
    spots = [over(meta[r], CAP) * block + rest(meta[r], CAP) * STEPS for r in range(rows)]
    if by_row:
        shape = (pairs, owners * block)
        at = iota(shape, 0)
        col = iota(shape, 1) - (over(at, STEPS) * items + rest(at, STEPS))
        return jnp.concatenate([one_hot(col == spots[r]) for r in range(rows)], axis=0)
    shape = (rows, owners * block)
    at = iota(shape, 0)
    col = iota(shape, 1)
    spot = jnp.zeros(shape, I32)
    for r in range(rows):
        spot = jnp.where(at == r, spots[r], spot)
    offset = col - spot
    return jnp.concatenate(
        [one_hot(offset == c * items + s) for c in range(heads) for s in range(STEPS)], axis=0
    )


def by_row_matrix(heads, rows):
    pairs = heads * STEPS
    shape = (pairs * rows, pairs * rows)
    at = iota(shape, 0)
    return one_hot(iota(shape, 1) == rest(at, pairs) * rows + over(at, pairs))


def by_pair_matrix(heads, rows):
    pairs = heads * STEPS
    shape = (pairs * rows, pairs * rows)
    at = iota(shape, 0)
    return one_hot(iota(shape, 1) == rest(at, rows) * pairs + over(at, rows))


def regroup_matrix(owners, heads):
    items = CAP * STEPS
    total = owners * heads * items
    at = iota((total, total), 0)
    head = over(at, owners * items)
    owner = rest(over(at, items), owners)
    return one_hot(
        iota((total, total), 1) == owner * (heads * items) + head * items + rest(at, items)
    )


def ungroup_matrix(owners, heads):
    items = CAP * STEPS
    total = owners * heads * items
    at = iota((total, total), 0)
    owner = over(at, heads * items)
    head = rest(over(at, items), heads)
    return one_hot(
        iota((total, total), 1) == head * (owners * items) + owner * items + rest(at, items)
    )


def exact(matrix, values):
    return jnp.dot(matrix, values, preferred_element_type=F32).astype(BF16)


def dispatch_kernel(
    owners,
    heads,
    adapt,
    rank,
    ids_hbm,
    slot_of_hbm,
    lengths_hbm,
    x_hbm,
    k_hbm,
    v_hbm,
    k_again,
    v_again,
    meta,
    blocks,
    slot_at,
    ids,
    slot_of,
    lengths,
    x_ref,
    sems,
):
    pairs = (
        (ids_hbm, ids),
        (slot_of_hbm, slot_of),
        (lengths_hbm, lengths),
        (x_hbm, x_ref),
    )
    copies = [pltpu.make_async_copy(a, b, sems.at[k]) for k, (a, b) in enumerate(pairs)]
    for copy in copies:
        copy.start()
    rows = x_ref.shape[1]
    wide = x_ref.shape[2] // heads
    for copy in copies[:3]:
        copy.wait()
    row_at = rows
    spans = rows + owners * CAP
    for p in range(owners * CAP):
        meta[row_at + p] = -1
        slot_at[p] = -1
    for r in range(rows):
        slot = slot_of[ids[r]]
        owner = over(slot, adapt)
        half = over(owner, 2)
        first = jnp.where(rest(owner, 2) == 0, half, owners - 1 - half) * CAP
        place = first + jnp.where(meta[row_at + first] >= 0, 1, 0)
        meta[row_at + place] = r
        slot_at[place] = rest(slot, adapt)
        meta[r] = place
        meta[spans + r] = lengths[r]
    items = CAP * STEPS
    block = heads * items
    copies[3].wait()
    packed = exact(pack_matrix(meta, owners, heads, rows, False), stacked(x_ref, heads, wide))
    at = iota((block, adapt * rank), 0)
    lane_slot = over(iota((block, adapt * rank), 1), rank)
    first = rest(over(at, STEPS), CAP) == 0
    for i in range(owners):
        blocks[i, :, :wide] = packed[i * block : (i + 1) * block]
        slot = jnp.where(first, slot_at[i * CAP], slot_at[i * CAP + 1])
        blocks[i, :, wide:] = one_hot(lane_slot == slot)


def project_kernel(owners, heads, wide, first, a_ref, blocks, *refs):
    core = lax.axis_index("tensor") if a_ref.shape[1] > heads * wide else 0
    if first:
        part_ref, mask_ref = refs
    else:
        mask_in, part_ref = refs
    grouped = regroup_matrix(owners, heads)
    items = owners * CAP * STEPS
    arrived = jnp.concatenate([blocks[i, :, :wide] for i in range(owners)], axis=0)
    arrived = exact(grouped, arrived)
    if first:
        masks = jnp.concatenate([blocks[i, :, wide:] for i in range(owners)], axis=0)
        mask = jnp.dot(grouped[:items], masks, preferred_element_type=F32)
        mask_ref[...] = mask
    else:
        mask = mask_in[...]
    total = jnp.zeros(mask.shape, F32)
    for c in range(heads):
        total = total + lax.dot_general(
            arrived[c * items : (c + 1) * items],
            a_ref[:, pl.ds(pl.multiple_of(core * (heads * wide) + c * wide, wide), wide)],
            (((1,), (1,)), ((), ())),
            preferred_element_type=F32,
        )
    part_ref[...] = total * mask


def expand_kernel(owners, heads, wide, mine, other, b_ref, *refs):
    blocks = refs[-1]
    low_rank = (mine[...] + other[...]).astype(BF16)
    pieces = []
    for c in range(heads):
        product = jnp.dot(
            low_rank, b_ref[:, c * wide : (c + 1) * wide], preferred_element_type=F32
        )
        pieces.append((2.0 * product).astype(BF16))
    back = exact(ungroup_matrix(owners, heads), jnp.concatenate(pieces, axis=0))
    block = heads * CAP * STEPS
    for i in range(owners):
        blocks[i] = back[i * block : (i + 1) * block]


def by_shape(span_at, rows, most, action):
    half, quarter = rows // 2, rows // 4
    lower = ((most // 8, most // 4), (most // 4, most // 4), (most // 4, most // 2), (most, most))
    upper = ((most // 4, most), (most // 2, most), (most * 3 // 4, most), (most, most))
    for at, shapes in ((0, lower), (half, upper)):
        first, last = span_at(at + quarter - 1), span_at(at + half - 1)
        open_yet = True
        for a, b in shapes:
            fits = (first <= a) & (last <= b) & open_yet
            open_yet = open_yet & ~((first <= a) & (last <= b))

            @pl.when(fits)
            def _():
                action(at, [a] * quarter + [b] * quarter)


def prepare_kernel(
    owners,
    heads,
    meta,
    q_ref,
    kn_ref,
    vn_ref,
    part,
    order,
    base_out,
    kn_out,
    vn_out,
    mask_out,
    gather_out,
    pack_out,
    after,
):
    rows = q_ref.shape[1]
    wide = q_ref.shape[2] // heads
    base_out[...] = exact(by_row_matrix(heads, rows), stacked(q_ref, heads, wide))
    for source, target in ((kn_ref, kn_out), (vn_ref, vn_out)):
        target[...] = jnp.concatenate([source[t] for t in range(STEPS)], axis=0)
    head_at = rest(over(iota(mask_out.shape, 0), STEPS), heads)
    mask_out[...] = one_hot(head_at == over(iota(mask_out.shape, 1), HD))
    gather_out[...] = unpack_matrix(meta, owners, heads, rows, True)
    pack_out[...] = pack_matrix(meta, owners, heads, rows, True)
    sizes = [meta[rows + owners * CAP + r] for r in range(rows)]
    ahead = [jnp.int32(0)] * rows
    for r in range(rows):
        for q in range(r):
            shorter = jnp.where(sizes[q] <= sizes[r], 1, 0)
            ahead[r] = ahead[r] + shorter
            ahead[q] = ahead[q] + (1 - shorter)
    for r in range(rows):
        order[ahead[r]] = r
    after[...] = part[: after.shape[0], :]


def attend_kernel(
    owners,
    heads,
    rows,
    meta,
    order,
    base_ref,
    kn_ref,
    vn_ref,
    mask_ref,
    gather_ref,
    pack_ref,
    k_ref,
    v_ref,
    blocks,
    mixed_out,
    outgoing,
    q_buf,
    o_buf,
):
    wide = base_ref.shape[1]
    groups = wide // HD
    pairs = heads * STEPS
    total = groups * pairs

    def span_of(row):
        return meta[rows + owners * CAP + row]

    delta = jnp.dot(
        gather_ref[...],
        jnp.concatenate([blocks[i] for i in range(owners)], axis=0),
        preferred_element_type=F32,
    )
    q_buf[...] = base_ref[...].astype(F32) + delta

    head_own = rest(over(iota((total, HD), 0), STEPS), heads)
    factor = math.log2(math.e) / math.sqrt(HD)
    fresh_shape = (total, STEPS * rows)
    fresh_at = iota(fresh_shape, 1)
    fresh_step = over(fresh_at, rows)
    fresh_row = jnp.where(fresh_step <= rest(iota(fresh_shape, 0), STEPS), rest(fresh_at, rows), rows)
    contract = (((1,), (1,)), ((), ()))

    def scores_of(row, extent):
        flat = q_buf[pl.ds(pl.multiple_of(row * pairs, pairs), pairs), :]
        one = jnp.concatenate([flat[:, j * HD : (j + 1) * HD] for j in range(groups)], axis=0)
        spread = jnp.concatenate([one.astype(BF16)] * heads, axis=1) * mask_ref[...]
        keys = jnp.concatenate([k_ref[row, :extent, :], kn_ref[...]], axis=0)
        score = lax.dot_general(spread, keys, contract, preferred_element_type=F32)
        cached = jnp.where(iota((total, extent), 1) < span_of(row), score[:, :extent], -jnp.inf)
        fresh = jnp.where(fresh_row == row, score[:, extent:], -jnp.inf)
        return jnp.concatenate([cached, fresh], axis=1)

    def softmax_of(score):
        top = jnp.max(score, axis=1, keepdims=True)
        weight = jnp.exp2((score - top) * factor)
        return weight.astype(BF16), 1.0 / jnp.sum(weight, axis=1, keepdims=True)

    def mix(row, extent, weight, share):
        values = jnp.concatenate([v_ref[row, :extent, :], vn_ref[...]], axis=0)
        mixed = jnp.dot(weight, values, preferred_element_type=F32)
        own = mixed[:, :HD]
        for c in range(1, heads):
            own = jnp.where(head_own == c, mixed[:, c * HD : (c + 1) * HD], own)
        own = own * share
        o_buf[pl.ds(pl.multiple_of(row * pairs, pairs), pairs), :] = jnp.concatenate(
            [own[j * pairs : (j + 1) * pairs] for j in range(groups)], axis=1
        )

    def attend(at, extents):
        count = len(extents)
        ordered = [order[at + k] for k in range(count)]
        scores, weights = {}, {}
        for t in range(count + 2 * LAG):
            if t < count:
                scores[t] = scores_of(ordered[t], extents[t])
            if 0 <= t - LAG < count:
                weights[t - LAG] = softmax_of(scores.pop(t - LAG))
            if 0 <= t - 2 * LAG < count:
                done = t - 2 * LAG
                mix(ordered[done], extents[done], *weights.pop(done))

    by_shape(lambda place: span_of(order[place]), rows, k_ref.shape[1], attend)

    mixed = o_buf[...].astype(BF16)
    mixed_out[...] = mixed
    packed = exact(pack_ref[...], mixed)
    block = heads * CAP * STEPS
    for i in range(owners):
        outgoing[i] = packed[i * block : (i + 1) * block]


def write_out(matrix, values, heads, out_hbm, out_ref, sems):
    rows = out_ref.shape[1]
    wide = out_ref.shape[2] // heads
    span = STEPS * rows
    copies = []
    for c in range(heads):
        ordered = exact(matrix[c * span : (c + 1) * span], values)
        for s in range(STEPS):
            out_ref[s, :, c * wide : (c + 1) * wide] = ordered[s * rows : (s + 1) * rows]
        part = (slice(None), slice(None), pl.ds(c * wide, wide))
        copies.append(pltpu.make_async_copy(out_ref.at[part], out_hbm.at[part], sems.at[c]))
        copies[-1].start()
    for copy in copies:
        copy.wait()


def finish_kernel(heads, mixed, gather_ref, part, out_hbm, after, spread_out, out_ref, sems):
    after[...] = part[: after.shape[0], :]
    matrix = by_pair_matrix(heads, out_ref.shape[1])
    spread_out[...] = exact(matrix, gather_ref[...])
    write_out(matrix, mixed[...], heads, out_hbm, out_ref, sems)


def collect_kernel(owners, heads, spread, blocks, out_hbm, out_ref, sems):
    arrived = jnp.concatenate([blocks[i] for i in range(owners)], axis=0)
    write_out(spread, arrived, heads, out_hbm, out_ref, sems)


def exchange(blocks):
    owners = blocks.shape[0]
    cycle = list(range(0, owners, 2)) + list(range(owners - 1, 0, -2))
    return lax.all_to_all(
        blocks, "store", split_axis=0, concat_axis=0, axis_index_groups=[cycle], tiled=True
    )


def in_hbm(array):
    return pltpu.with_memory_space_constraint(array, pltpu.HBM)


def swap_cores(part):
    return lax.ppermute(part, "tensor", [(0, 1), (1, 0)])


def shards(
    x_in,
    q_base,
    k_new,
    v_new,
    cache_k,
    cache_v,
    lengths,
    adapter_ids,
    slot_of,
    a_query,
    b_query,
    a_output,
    b_output,
):
    owners = lax.axis_size("store")
    rows = x_in.shape[1]
    width = x_in.shape[2]
    heads = cache_k.shape[2] // HD
    wide = width // heads
    adapt, rank = a_query.shape[1:]
    lanes = adapt * rank
    block = heads * CAP * STEPS
    items = owners * CAP * STEPS
    def flat(a_store):
        return jnp.transpose(a_store, (1, 2, 0)).reshape(lanes, a_store.shape[0])

    shape = jax.ShapeDtypeStruct
    small = pltpu.CompilerParams(vmem_limit_bytes=16 * 1024 * 1024)

    sent = shape((owners, block, wide), BF16)
    caches = (in_hbm(cache_k), in_hbm(cache_v))
    meta, blocks = pl.pallas_call(
        functools.partial(dispatch_kernel, owners, SPLIT, adapt, rank),
        out_shape=[
            shape((2 * rows + owners * CAP,), I32),
            shape((owners, SPLIT * CAP * STEPS, width // SPLIT + lanes), BF16),
        ],
        in_specs=[HBM] * 8,
        out_specs=[SMEM, VMEM],
        scratch_shapes=[
            pltpu.SMEM((owners * CAP,), I32),
            pltpu.SMEM(adapter_ids.shape, I32),
            pltpu.SMEM(slot_of.shape, I32),
            pltpu.SMEM(lengths.shape, I32),
            pltpu.VMEM(x_in.shape, BF16),
            pltpu.SemaphoreType.DMA((4,)),
        ],
        compiler_params=small,
        name="dispatch",
    )(
        *map(in_hbm, (adapter_ids, slot_of, lengths, x_in)), *caches, *caches
    )

    arrived = exchange(blocks)
    part, mask = pl.pallas_call(
        functools.partial(project_kernel, owners, SPLIT, width // SPLIT, True),
        out_shape=[shape((items, lanes), F32)] * 2,
        in_specs=[VMEM] * 2,
        out_specs=[VMEM] * 2,
        compiler_params=small,
        name="project_query",
    )(flat(a_query), arrived)

    def expand(part, other, b_store, name, caches, *after):
        return pl.pallas_call(
            functools.partial(expand_kernel, owners, heads, wide),
            out_shape=sent,
            in_specs=[VMEM] * (3 + len(after)) + [HBM] * len(caches),
            out_specs=VMEM,
            compiler_params=small,
            name=name,
        )(part, other, b_store, *after, *caches)

    other = swap_cores(part)
    order, *prepared, after = pl.pallas_call(
        functools.partial(prepare_kernel, owners, heads),
        out_shape=[
            shape((rows,), I32),
            shape((rows * STEPS * heads, wide), BF16),
            shape((STEPS * rows, heads * HD), BF16),
            shape((STEPS * rows, heads * HD), BF16),
            shape((STEPS * wide // HD * heads, heads * HD), BF16),
            shape((rows * STEPS * heads, owners * block), BF16),
            shape((owners * block, rows * STEPS * heads), BF16),
            shape((8, lanes), F32),
        ],
        in_specs=[SMEM] + [VMEM] * 4,
        out_specs=[SMEM] + [VMEM] * 7,
        compiler_params=small,
        name="prepare",
    )(meta, q_base, k_new, v_new, part)
    returned = exchange(
        expand(part, other, b_query.reshape(lanes, width), "expand_query", (), after)
    )

    mixed, outgoing = pl.pallas_call(
        functools.partial(attend_kernel, owners, heads, rows),
        out_shape=[
            shape((rows * STEPS * heads, wide), BF16),
            sent,
        ],
        in_specs=[SMEM] * 2 + [VMEM] * 9,
        out_specs=[VMEM] * 2,
        scratch_shapes=[
            pltpu.VMEM((rows * STEPS * heads, wide), F32),
            pltpu.VMEM((rows * STEPS * heads, wide), F32),
        ],
        compiler_params=small,
        name="attend",
    )(meta, order, *prepared, cache_k, cache_v, returned)

    arrived = exchange(outgoing)
    part = pl.pallas_call(
        functools.partial(project_kernel, owners, heads, wide, False),
        out_shape=shape((items, lanes), F32),
        in_specs=[VMEM] * 3,
        out_specs=VMEM,
        compiler_params=small,
        name="project_output",
    )(flat(a_output), arrived, mask)
    ordered = dict(
        scratch_shapes=[
            pltpu.VMEM((STEPS, rows, width), BF16),
            pltpu.SemaphoreType.DMA((heads,)),
        ],
        compiler_params=small,
    )
    other = swap_cores(part)
    attn_out, after, spread = pl.pallas_call(
        functools.partial(finish_kernel, heads),
        out_shape=[
            shape((STEPS, rows, width), BF16),
            shape((8, lanes), F32),
            shape((rows * STEPS * heads, owners * block), BF16),
        ],
        in_specs=[VMEM] * 3,
        out_specs=[HBM, VMEM, VMEM],
        name="finish",
        **ordered,
    )(mixed, prepared[4], part)
    returned = exchange(
        expand(part, other, b_output.reshape(lanes, width), "expand_output", (), after)
    )
    adapter_out = pl.pallas_call(
        functools.partial(collect_kernel, owners, heads),
        out_shape=shape((STEPS, rows, width), BF16),
        in_specs=[VMEM] * 2,
        out_specs=HBM,
        name="collect",
        **ordered,
    )(spread, returned)
    return (attn_out, adapter_out)


def solution(mesh):
    in_specs = (
        P(None, ("parts", "store"), "tensor"),
        P(None, ("parts", "store"), "tensor"),
        P(None, ("parts", "store"), "tensor"),
        P(None, ("parts", "store"), "tensor"),
        P(("parts", "store"), None, "tensor"),
        P(("parts", "store"), None, "tensor"),
        P(("parts", "store")),
        P(("parts", "store")),
        P("parts"),
        P(None, "store", None),
        P("store", None, "tensor"),
        P(None, "store", None),
        P("store", None, "tensor"),
    )
    out_specs = (P(None, ("parts", "store"), "tensor"), P(None, ("parts", "store"), "tensor"))
    return jax.shard_map(shards, mesh=mesh, in_specs=in_specs, out_specs=out_specs, check_vma=False)
```

```python
import functools
import math

import jax
import jax.numpy as jnp
from jax import lax
from jax.experimental import pallas as pl
from jax.experimental.pallas import tpu as pltpu
from jax.sharding import PartitionSpec as P

HD = 128
CAP = 2
STEPS = 2
LAG = 2
SPLIT = 2
BF16 = jnp.bfloat16
F32 = jnp.float32
I32 = jnp.int32
VMEM = pl.BlockSpec(memory_space=pltpu.VMEM)
SMEM = pl.BlockSpec(memory_space=pltpu.SMEM)
HBM = pl.BlockSpec(memory_space=pltpu.HBM)


def iota(shape, dim):
    return lax.broadcasted_iota(I32, shape, dim)


def over(x, n):
    return lax.shift_right_logical(x, jnp.full_like(x, n.bit_length() - 1)) if n & (n - 1) == 0 else x // n


def rest(x, n):
    return x & (n - 1) if n & (n - 1) == 0 else x % n


def one_hot(hits):
    return jnp.where(hits, 1.0, 0.0).astype(BF16)


def stacked(ref, heads, wide):
    return jnp.concatenate(
        [ref[s, :, c * wide : (c + 1) * wide] for c in range(heads) for s in range(STEPS)], axis=0
    )


def pack_matrix(meta, owners, heads, rows, by_row):
    items = CAP * STEPS
    block = heads * items
    shape = (block, heads * STEPS * rows)
    at = iota(shape, 0)
    col = iota(shape, 1)
    head_step = over(at, items) * STEPS + rest(at, STEPS)
    offset = col - (head_step if by_row else head_step * rows)
    factor = heads * STEPS if by_row else 1
    first = rest(over(at, STEPS), CAP) == 0
    if not by_row:
        offset = jnp.where((offset >= 0) & (offset < rows), offset, -1)
    parts = []
    for i in range(owners):
        here = [meta[rows + i * CAP + k] for k in range(CAP)]
        spots = [jnp.where(h >= 0, h * factor, -rows * factor * heads * STEPS * 2) for h in here]
        parts.append(one_hot(offset == jnp.where(first, spots[0], spots[1])))
    return jnp.concatenate(parts, axis=0)


def unpack_matrix(meta, owners, heads, rows, by_row):
    items = CAP * STEPS
    block = heads * items
    pairs = heads * STEPS
    spots = [over(meta[r], CAP) * block + rest(meta[r], CAP) * STEPS for r in range(rows)]
    if by_row:
        shape = (pairs, owners * block)
        at = iota(shape, 0)
        col = iota(shape, 1) - (over(at, STEPS) * items + rest(at, STEPS))
        return jnp.concatenate([one_hot(col == spots[r]) for r in range(rows)], axis=0)
    shape = (rows, owners * block)
    at = iota(shape, 0)
    col = iota(shape, 1)
    spot = jnp.zeros(shape, I32)
    for r in range(rows):
        spot = jnp.where(at == r, spots[r], spot)
    offset = col - spot
    return jnp.concatenate(
        [one_hot(offset == c * items + s) for c in range(heads) for s in range(STEPS)], axis=0
    )


def by_row_matrix(heads, rows):
    pairs = heads * STEPS
    shape = (pairs * rows, pairs * rows)
    at = iota(shape, 0)
    return one_hot(iota(shape, 1) == rest(at, pairs) * rows + over(at, pairs))


def by_pair_matrix(heads, rows):
    pairs = heads * STEPS
    shape = (pairs * rows, pairs * rows)
    at = iota(shape, 0)
    return one_hot(iota(shape, 1) == rest(at, rows) * pairs + over(at, rows))


def turned(place, owners, core):
    return place + rest(core, 2) * (owners - 1 - 2 * place)


def regroup_matrix(owners, heads, core):
    items = CAP * STEPS
    total = owners * heads * items
    at = iota((total, total), 0)
    head = over(at, owners * items)
    owner = turned(rest(over(at, items), owners), owners, core)
    return one_hot(
        iota((total, total), 1) == owner * (heads * items) + head * items + rest(at, items)
    )


def ungroup_matrix(owners, heads, core):
    items = CAP * STEPS
    total = owners * heads * items
    at = iota((total, total), 0)
    owner = turned(over(at, heads * items), owners, core)
    head = rest(over(at, items), heads)
    return one_hot(
        iota((total, total), 1) == head * (owners * items) + owner * items + rest(at, items)
    )


def exact(matrix, values):
    return jnp.dot(matrix, values, preferred_element_type=F32).astype(BF16)


def dispatch_kernel(
    owners,
    heads,
    adapt,
    rank,
    ids_hbm,
    slot_of_hbm,
    lengths_hbm,
    x_hbm,
    k_hbm,
    v_hbm,
    k_again,
    v_again,
    meta,
    blocks,
    slot_at,
    ids,
    slot_of,
    lengths,
    x_ref,
    sems,
):
    pairs = (
        (ids_hbm, ids),
        (slot_of_hbm, slot_of),
        (lengths_hbm, lengths),
        (x_hbm, x_ref),
    )
    copies = [pltpu.make_async_copy(a, b, sems.at[k]) for k, (a, b) in enumerate(pairs)]
    for copy in copies:
        copy.start()
    rows = x_ref.shape[1]
    wide = x_ref.shape[2] // heads
    for copy in copies[:3]:
        copy.wait()
    core = lax.axis_index("tensor")
    row_at = rows
    spans = rows + owners * CAP
    for p in range(owners * CAP):
        meta[row_at + p] = -1
        slot_at[p] = -1
    for r in range(rows):
        slot = slot_of[ids[r]]
        owner = over(slot, adapt)
        half = over(owner, 2)
        first = turned(jnp.where(rest(owner, 2) == 0, half, owners - 1 - half), owners, core) * CAP
        place = first + jnp.where(meta[row_at + first] >= 0, 1, 0)
        meta[row_at + place] = r
        slot_at[place] = rest(slot, adapt)
        meta[r] = place
        meta[spans + r] = lengths[r]
    items = CAP * STEPS
    block = heads * items
    copies[3].wait()
    packed = exact(pack_matrix(meta, owners, heads, rows, False), stacked(x_ref, heads, wide))
    at = iota((block, adapt * rank), 0)
    lane_slot = over(iota((block, adapt * rank), 1), rank)
    first = rest(over(at, STEPS), CAP) == 0
    for i in range(owners):
        blocks[i, :, :wide] = packed[i * block : (i + 1) * block]
        slot = jnp.where(first, slot_at[i * CAP], slot_at[i * CAP + 1])
        blocks[i, :, wide:] = one_hot(lane_slot == slot)


def project_kernel(owners, heads, wide, first, a_ref, blocks, *refs):
    core = lax.axis_index("tensor")
    if first:
        part_ref, mask_ref = refs
    else:
        mask_in, part_ref = refs
    grouped = regroup_matrix(owners, heads, core)
    items = owners * CAP * STEPS
    arrived = jnp.concatenate([blocks[i, :, :wide] for i in range(owners)], axis=0)
    arrived = exact(grouped, arrived)
    if first:
        masks = jnp.concatenate([blocks[i, :, wide:] for i in range(owners)], axis=0)
        mask = jnp.dot(grouped[:items], masks, preferred_element_type=F32)
        mask_ref[...] = mask
    else:
        mask = mask_in[...]
    total = jnp.zeros(mask.shape, F32)
    for c in range(heads):
        total = total + lax.dot_general(
            arrived[c * items : (c + 1) * items],
            a_ref[:, pl.ds(pl.multiple_of(core * (heads * wide) + c * wide, wide), wide)],
            (((1,), (1,)), ((), ())),
            preferred_element_type=F32,
        )
    part_ref[...] = total * mask


def expand_kernel(owners, heads, wide, mine, other, b_ref, *refs):
    blocks = refs[-1]
    low_rank = (mine[...] + other[...]).astype(BF16)
    pieces = []
    for c in range(heads):
        product = jnp.dot(
            low_rank, b_ref[:, c * wide : (c + 1) * wide], preferred_element_type=F32
        )
        pieces.append((2.0 * product).astype(BF16))
    back = exact(ungroup_matrix(owners, heads, lax.axis_index("tensor")), jnp.concatenate(pieces, axis=0))
    block = heads * CAP * STEPS
    for i in range(owners):
        blocks[i] = back[i * block : (i + 1) * block]


def by_shape(span_at, rows, most, action):
    half, quarter = rows // 2, rows // 4
    lower = ((most // 8, most // 4), (most // 4, most // 4), (most // 4, most // 2), (most, most))
    upper = ((most // 4, most), (most // 2, most), (most * 3 // 4, most), (most, most))
    for at, shapes in ((0, lower), (half, upper)):
        first, last = span_at(at + quarter - 1), span_at(at + half - 1)
        open_yet = True
        for a, b in shapes:
            fits = (first <= a) & (last <= b) & open_yet
            open_yet = open_yet & ~((first <= a) & (last <= b))

            @pl.when(fits)
            def _():
                action(at, [a] * quarter + [b] * quarter)


def prepare_kernel(
    owners,
    heads,
    meta,
    q_ref,
    kn_ref,
    vn_ref,
    part,
    order,
    base_out,
    kn_out,
    vn_out,
    mask_out,
    gather_out,
    pack_out,
    after,
):
    rows = q_ref.shape[1]
    wide = q_ref.shape[2] // heads
    base_out[...] = exact(by_row_matrix(heads, rows), stacked(q_ref, heads, wide))
    for source, target in ((kn_ref, kn_out), (vn_ref, vn_out)):
        target[...] = jnp.concatenate([source[t] for t in range(STEPS)], axis=0)
    head_at = rest(over(iota(mask_out.shape, 0), STEPS), heads)
    mask_out[...] = one_hot(head_at == over(iota(mask_out.shape, 1), HD))
    gather_out[...] = unpack_matrix(meta, owners, heads, rows, True)
    pack_out[...] = pack_matrix(meta, owners, heads, rows, True)
    sizes = [meta[rows + owners * CAP + r] for r in range(rows)]
    ahead = [jnp.int32(0)] * rows
    for r in range(rows):
        for q in range(r):
            shorter = jnp.where(sizes[q] <= sizes[r], 1, 0)
            ahead[r] = ahead[r] + shorter
            ahead[q] = ahead[q] + (1 - shorter)
    for r in range(rows):
        order[ahead[r]] = r
    after[...] = part[: after.shape[0], :]


def attend_kernel(
    owners,
    heads,
    rows,
    meta,
    order,
    base_ref,
    kn_ref,
    vn_ref,
    mask_ref,
    gather_ref,
    pack_ref,
    k_ref,
    v_ref,
    blocks,
    mixed_out,
    outgoing,
    q_buf,
    o_buf,
):
    wide = base_ref.shape[1]
    groups = wide // HD
    pairs = heads * STEPS
    total = groups * pairs

    def span_of(row):
        return meta[rows + owners * CAP + row]

    delta = jnp.dot(
        gather_ref[...],
        jnp.concatenate([blocks[i] for i in range(owners)], axis=0),
        preferred_element_type=F32,
    )
    q_buf[...] = base_ref[...].astype(F32) + delta

    head_own = rest(over(iota((total, HD), 0), STEPS), heads)
    factor = math.log2(math.e) / math.sqrt(HD)
    fresh_shape = (total, STEPS * rows)
    fresh_at = iota(fresh_shape, 1)
    fresh_step = over(fresh_at, rows)
    fresh_row = jnp.where(fresh_step <= rest(iota(fresh_shape, 0), STEPS), rest(fresh_at, rows), rows)
    contract = (((1,), (1,)), ((), ()))

    def scores_of(row, extent):
        flat = q_buf[pl.ds(pl.multiple_of(row * pairs, pairs), pairs), :]
        one = jnp.concatenate([flat[:, j * HD : (j + 1) * HD] for j in range(groups)], axis=0)
        spread = jnp.concatenate([one.astype(BF16)] * heads, axis=1) * mask_ref[...]
        keys = jnp.concatenate([k_ref[row, :extent, :], kn_ref[...]], axis=0)
        score = lax.dot_general(spread, keys, contract, preferred_element_type=F32)
        cached = jnp.where(iota((total, extent), 1) < span_of(row), score[:, :extent], -jnp.inf)
        fresh = jnp.where(fresh_row == row, score[:, extent:], -jnp.inf)
        return jnp.concatenate([cached, fresh], axis=1)

    def softmax_of(score):
        top = jnp.max(score, axis=1, keepdims=True)
        weight = jnp.exp2((score - top) * factor)
        return weight.astype(BF16), 1.0 / jnp.sum(weight, axis=1, keepdims=True)

    def mix(row, extent, weight, share):
        values = jnp.concatenate([v_ref[row, :extent, :], vn_ref[...]], axis=0)
        mixed = jnp.dot(weight, values, preferred_element_type=F32)
        own = mixed[:, :HD]
        for c in range(1, heads):
            own = jnp.where(head_own == c, mixed[:, c * HD : (c + 1) * HD], own)
        own = own * share
        o_buf[pl.ds(pl.multiple_of(row * pairs, pairs), pairs), :] = jnp.concatenate(
            [own[j * pairs : (j + 1) * pairs] for j in range(groups)], axis=1
        )

    def attend(at, extents):
        count = len(extents)
        ordered = [order[at + k] for k in range(count)]
        scores, weights = {}, {}
        for t in range(count + 2 * LAG):
            if t < count:
                scores[t] = scores_of(ordered[t], extents[t])
            if 0 <= t - LAG < count:
                weights[t - LAG] = softmax_of(scores.pop(t - LAG))
            if 0 <= t - 2 * LAG < count:
                done = t - 2 * LAG
                mix(ordered[done], extents[done], *weights.pop(done))

    by_shape(lambda place: span_of(order[place]), rows, k_ref.shape[1], attend)

    mixed = o_buf[...].astype(BF16)
    mixed_out[...] = mixed
    packed = exact(pack_ref[...], mixed)
    block = heads * CAP * STEPS
    for i in range(owners):
        outgoing[i] = packed[i * block : (i + 1) * block]


def write_out(matrix, values, heads, out_hbm, out_ref, sems):
    rows = out_ref.shape[1]
    wide = out_ref.shape[2] // heads
    span = STEPS * rows
    copies = []
    for c in range(heads):
        ordered = exact(matrix[c * span : (c + 1) * span], values)
        for s in range(STEPS):
            out_ref[s, :, c * wide : (c + 1) * wide] = ordered[s * rows : (s + 1) * rows]
        part = (slice(None), slice(None), pl.ds(c * wide, wide))
        copies.append(pltpu.make_async_copy(out_ref.at[part], out_hbm.at[part], sems.at[c]))
        copies[-1].start()
    for copy in copies:
        copy.wait()


def finish_kernel(heads, mixed, gather_ref, part, out_hbm, after, spread_out, out_ref, sems):
    after[...] = part[: after.shape[0], :]
    matrix = by_pair_matrix(heads, out_ref.shape[1])
    spread_out[...] = exact(matrix, gather_ref[...])
    write_out(matrix, mixed[...], heads, out_hbm, out_ref, sems)


def collect_kernel(owners, heads, spread, blocks, out_hbm, out_ref, sems):
    arrived = jnp.concatenate([blocks[i] for i in range(owners)], axis=0)
    write_out(spread, arrived, heads, out_hbm, out_ref, sems)


def exchange(blocks):
    owners = blocks.shape[0]
    cores = lax.axis_size("tensor")
    cycle = list(range(0, owners, 2)) + list(range(owners - 1, 0, -2))
    groups = [
        [s * cores + core for s in (cycle if core % 2 == 0 else cycle[::-1])]
        for core in range(cores)
    ]
    return lax.all_to_all(
        blocks,
        ("store", "tensor"),
        split_axis=0,
        concat_axis=0,
        axis_index_groups=groups,
        tiled=True,
    )


def in_hbm(array):
    return pltpu.with_memory_space_constraint(array, pltpu.HBM)


def swap_cores(part):
    return lax.ppermute(part, "tensor", [(0, 1), (1, 0)])


def shards(
    x_in,
    q_base,
    k_new,
    v_new,
    cache_k,
    cache_v,
    lengths,
    adapter_ids,
    slot_of,
    a_query,
    b_query,
    a_output,
    b_output,
):
    owners = lax.axis_size("store")
    rows = x_in.shape[1]
    width = x_in.shape[2]
    heads = cache_k.shape[2] // HD
    wide = width // heads
    adapt, rank = a_query.shape[1:]
    lanes = adapt * rank
    block = heads * CAP * STEPS
    items = owners * CAP * STEPS
    def flat(a_store):
        return jnp.transpose(a_store, (1, 2, 0)).reshape(lanes, a_store.shape[0])

    shape = jax.ShapeDtypeStruct
    small = pltpu.CompilerParams(vmem_limit_bytes=16 * 1024 * 1024)

    sent = shape((owners, block, wide), BF16)
    caches = (in_hbm(cache_k), in_hbm(cache_v))
    meta, blocks = pl.pallas_call(
        functools.partial(dispatch_kernel, owners, SPLIT, adapt, rank),
        out_shape=[
            shape((2 * rows + owners * CAP,), I32),
            shape((owners, SPLIT * CAP * STEPS, width // SPLIT + lanes), BF16),
        ],
        in_specs=[HBM] * 8,
        out_specs=[SMEM, VMEM],
        scratch_shapes=[
            pltpu.SMEM((owners * CAP,), I32),
            pltpu.SMEM(adapter_ids.shape, I32),
            pltpu.SMEM(slot_of.shape, I32),
            pltpu.SMEM(lengths.shape, I32),
            pltpu.VMEM(x_in.shape, BF16),
            pltpu.SemaphoreType.DMA((4,)),
        ],
        compiler_params=small,
        name="dispatch",
    )(
        *map(in_hbm, (adapter_ids, slot_of, lengths, x_in)), *caches, *caches
    )

    arrived = exchange(blocks)
    part, mask = pl.pallas_call(
        functools.partial(project_kernel, owners, SPLIT, width // SPLIT, True),
        out_shape=[shape((items, lanes), F32)] * 2,
        in_specs=[VMEM] * 2,
        out_specs=[VMEM] * 2,
        compiler_params=small,
        name="project_query",
    )(flat(a_query), arrived)

    def expand(part, other, b_store, name, caches, *after):
        return pl.pallas_call(
            functools.partial(expand_kernel, owners, heads, wide),
            out_shape=sent,
            in_specs=[VMEM] * (3 + len(after)) + [HBM] * len(caches),
            out_specs=VMEM,
            compiler_params=small,
            name=name,
        )(part, other, b_store, *after, *caches)

    other = swap_cores(part)
    order, *prepared, after = pl.pallas_call(
        functools.partial(prepare_kernel, owners, heads),
        out_shape=[
            shape((rows,), I32),
            shape((rows * STEPS * heads, wide), BF16),
            shape((STEPS * rows, heads * HD), BF16),
            shape((STEPS * rows, heads * HD), BF16),
            shape((STEPS * wide // HD * heads, heads * HD), BF16),
            shape((rows * STEPS * heads, owners * block), BF16),
            shape((owners * block, rows * STEPS * heads), BF16),
            shape((8, lanes), F32),
        ],
        in_specs=[SMEM] + [VMEM] * 4,
        out_specs=[SMEM] + [VMEM] * 7,
        compiler_params=small,
        name="prepare",
    )(meta, q_base, k_new, v_new, part)
    returned = exchange(
        expand(part, other, b_query.reshape(lanes, width), "expand_query", (), after)
    )

    mixed, outgoing = pl.pallas_call(
        functools.partial(attend_kernel, owners, heads, rows),
        out_shape=[
            shape((rows * STEPS * heads, wide), BF16),
            sent,
        ],
        in_specs=[SMEM] * 2 + [VMEM] * 9,
        out_specs=[VMEM] * 2,
        scratch_shapes=[
            pltpu.VMEM((rows * STEPS * heads, wide), F32),
            pltpu.VMEM((rows * STEPS * heads, wide), F32),
        ],
        compiler_params=small,
        name="attend",
    )(meta, order, *prepared, cache_k, cache_v, returned)

    arrived = exchange(outgoing)
    part = pl.pallas_call(
        functools.partial(project_kernel, owners, heads, wide, False),
        out_shape=shape((items, lanes), F32),
        in_specs=[VMEM] * 3,
        out_specs=VMEM,
        compiler_params=small,
        name="project_output",
    )(flat(a_output), arrived, mask)
    ordered = dict(
        scratch_shapes=[
            pltpu.VMEM((STEPS, rows, width), BF16),
            pltpu.SemaphoreType.DMA((heads,)),
        ],
        compiler_params=small,
    )
    other = swap_cores(part)
    attn_out, after, spread = pl.pallas_call(
        functools.partial(finish_kernel, heads),
        out_shape=[
            shape((STEPS, rows, width), BF16),
            shape((8, lanes), F32),
            shape((rows * STEPS * heads, owners * block), BF16),
        ],
        in_specs=[VMEM] * 3,
        out_specs=[HBM, VMEM, VMEM],
        name="finish",
        **ordered,
    )(mixed, prepared[4], part)
    returned = exchange(
        expand(part, other, b_output.reshape(lanes, width), "expand_output", (), after)
    )
    adapter_out = pl.pallas_call(
        functools.partial(collect_kernel, owners, heads),
        out_shape=shape((STEPS, rows, width), BF16),
        in_specs=[VMEM] * 2,
        out_specs=HBM,
        name="collect",
        **ordered,
    )(spread, returned)
    return (attn_out, adapter_out)


def solution(mesh):
    in_specs = (
        P(None, ("parts", "store"), "tensor"),
        P(None, ("parts", "store"), "tensor"),
        P(None, ("parts", "store"), "tensor"),
        P(None, ("parts", "store"), "tensor"),
        P(("parts", "store"), None, "tensor"),
        P(("parts", "store"), None, "tensor"),
        P(("parts", "store")),
        P(("parts", "store")),
        P("parts"),
        P(None, "store", None),
        P("store", None, "tensor"),
        P(None, "store", None),
        P("store", None, "tensor"),
    )
    out_specs = (P(None, ("parts", "store"), "tensor"), P(None, ("parts", "store"), "tensor"))
    return jax.shard_map(shards, mesh=mesh, in_specs=in_specs, out_specs=out_specs, check_vma=False)
```

```python
import functools
import math

import jax
import jax.numpy as jnp
from jax import lax
from jax.experimental import pallas as pl
from jax.experimental.pallas import tpu as pltpu
from jax.sharding import PartitionSpec as P

HD = 128
CAP = 2
STEPS = 2
LAG = 2
SPLIT = 2
BF16 = jnp.bfloat16
F32 = jnp.float32
I32 = jnp.int32
VMEM = pl.BlockSpec(memory_space=pltpu.VMEM)
SMEM = pl.BlockSpec(memory_space=pltpu.SMEM)
HBM = pl.BlockSpec(memory_space=pltpu.HBM)


def iota(shape, dim):
    return lax.broadcasted_iota(I32, shape, dim)


def over(x, n):
    return lax.shift_right_logical(x, jnp.full_like(x, n.bit_length() - 1)) if n & (n - 1) == 0 else x // n


def rest(x, n):
    return x & (n - 1) if n & (n - 1) == 0 else x % n


def one_hot(hits):
    return jnp.where(hits, 1.0, 0.0).astype(BF16)


def stacked(ref, heads, wide):
    return jnp.concatenate(
        [ref[s, :, c * wide : (c + 1) * wide] for c in range(heads) for s in range(STEPS)], axis=0
    )


def pack_matrix(meta, owners, heads, rows, by_row):
    items = CAP * STEPS
    block = heads * items
    shape = (block, heads * STEPS * rows)
    at = iota(shape, 0)
    col = iota(shape, 1)
    head_step = over(at, items) * STEPS + rest(at, STEPS)
    offset = col - (head_step if by_row else head_step * rows)
    factor = heads * STEPS if by_row else 1
    first = rest(over(at, STEPS), CAP) == 0
    if not by_row:
        offset = jnp.where((offset >= 0) & (offset < rows), offset, -1)
    parts = []
    for i in range(owners):
        here = [meta[rows + i * CAP + k] for k in range(CAP)]
        spots = [jnp.where(h >= 0, h * factor, -rows * factor * heads * STEPS * 2) for h in here]
        parts.append(one_hot(offset == jnp.where(first, spots[0], spots[1])))
    return jnp.concatenate(parts, axis=0)


def unpack_matrix(meta, owners, heads, rows, by_row):
    items = CAP * STEPS
    block = heads * items
    pairs = heads * STEPS
    spots = [over(meta[r], CAP) * block + rest(meta[r], CAP) * STEPS for r in range(rows)]
    if by_row:
        shape = (pairs, owners * block)
        at = iota(shape, 0)
        col = iota(shape, 1) - (over(at, STEPS) * items + rest(at, STEPS))
        return jnp.concatenate([one_hot(col == spots[r]) for r in range(rows)], axis=0)
    shape = (rows, owners * block)
    at = iota(shape, 0)
    col = iota(shape, 1)
    spot = jnp.zeros(shape, I32)
    for r in range(rows):
        spot = jnp.where(at == r, spots[r], spot)
    offset = col - spot
    return jnp.concatenate(
        [one_hot(offset == c * items + s) for c in range(heads) for s in range(STEPS)], axis=0
    )


def by_row_matrix(heads, rows):
    pairs = heads * STEPS
    shape = (pairs * rows, pairs * rows)
    at = iota(shape, 0)
    return one_hot(iota(shape, 1) == rest(at, pairs) * rows + over(at, pairs))


def by_pair_matrix(heads, rows):
    pairs = heads * STEPS
    shape = (pairs * rows, pairs * rows)
    at = iota(shape, 0)
    return one_hot(iota(shape, 1) == rest(at, rows) * pairs + over(at, rows))


def stride_of(owners):
    return 3 if owners % 3 else 1


def turned(place, owners, core):
    return place + rest(core, 2) * (owners - 1 - 2 * place)


def regroup_matrix(owners, heads, core):
    items = CAP * STEPS
    total = owners * heads * items
    at = iota((total, total), 0)
    head = over(at, owners * items)
    owner = turned(rest(over(at, items), owners), owners, core)
    return one_hot(
        iota((total, total), 1) == owner * (heads * items) + head * items + rest(at, items)
    )


def ungroup_matrix(owners, heads, core):
    items = CAP * STEPS
    total = owners * heads * items
    at = iota((total, total), 0)
    owner = turned(over(at, heads * items), owners, core)
    head = rest(over(at, items), heads)
    return one_hot(
        iota((total, total), 1) == head * (owners * items) + owner * items + rest(at, items)
    )


def exact(matrix, values):
    return jnp.dot(matrix, values, preferred_element_type=F32).astype(BF16)


def dispatch_kernel(
    owners,
    heads,
    adapt,
    rank,
    ids_hbm,
    slot_of_hbm,
    lengths_hbm,
    x_hbm,
    k_hbm,
    v_hbm,
    k_again,
    v_again,
    meta,
    blocks,
    slot_at,
    ids,
    slot_of,
    lengths,
    x_ref,
    sems,
):
    pairs = (
        (ids_hbm, ids),
        (slot_of_hbm, slot_of),
        (lengths_hbm, lengths),
        (x_hbm, x_ref),
    )
    copies = [pltpu.make_async_copy(a, b, sems.at[k]) for k, (a, b) in enumerate(pairs)]
    for copy in copies:
        copy.start()
    rows = x_ref.shape[1]
    wide = x_ref.shape[2] // heads
    for copy in copies[:3]:
        copy.wait()
    core = lax.axis_index("tensor")
    row_at = rows
    spans = rows + owners * CAP
    for p in range(owners * CAP):
        meta[row_at + p] = -1
        slot_at[p] = -1
    for r in range(rows):
        slot = slot_of[ids[r]]
        owner = over(slot, adapt)
        half = over(owner, 2)
        along = jnp.where(rest(owner, 2) == 0, half, owners - 1 - half)
        along = rest(along * pow(stride_of(owners), -1, owners), owners)
        first = turned(along, owners, core) * CAP
        place = first + jnp.where(meta[row_at + first] >= 0, 1, 0)
        meta[row_at + place] = r
        slot_at[place] = rest(slot, adapt)
        meta[r] = place
        meta[spans + r] = lengths[r]
    items = CAP * STEPS
    block = heads * items
    copies[3].wait()
    packed = exact(pack_matrix(meta, owners, heads, rows, False), stacked(x_ref, heads, wide))
    at = iota((block, adapt * rank), 0)
    lane_slot = over(iota((block, adapt * rank), 1), rank)
    first = rest(over(at, STEPS), CAP) == 0
    for i in range(owners):
        blocks[i, :, :wide] = packed[i * block : (i + 1) * block]
        slot = jnp.where(first, slot_at[i * CAP], slot_at[i * CAP + 1])
        blocks[i, :, wide:] = one_hot(lane_slot == slot)


def project_kernel(owners, heads, wide, first, a_ref, blocks, *refs):
    core = lax.axis_index("tensor")
    if first:
        part_ref, mask_ref = refs
    else:
        mask_in, part_ref = refs
    grouped = regroup_matrix(owners, heads, core)
    items = owners * CAP * STEPS
    arrived = jnp.concatenate([blocks[i, :, :wide] for i in range(owners)], axis=0)
    arrived = exact(grouped, arrived)
    if first:
        masks = jnp.concatenate([blocks[i, :, wide:] for i in range(owners)], axis=0)
        mask = jnp.dot(grouped[:items], masks, preferred_element_type=F32)
        mask_ref[...] = mask
    else:
        mask = mask_in[...]
    total = jnp.zeros(mask.shape, F32)
    for c in range(heads):
        total = total + lax.dot_general(
            arrived[c * items : (c + 1) * items],
            a_ref[:, pl.ds(pl.multiple_of(core * (heads * wide) + c * wide, wide), wide)],
            (((1,), (1,)), ((), ())),
            preferred_element_type=F32,
        )
    part_ref[...] = total * mask


def expand_kernel(owners, heads, wide, mine, other, b_ref, *refs):
    blocks = refs[-1]
    low_rank = (mine[...] + other[...]).astype(BF16)
    pieces = []
    for c in range(heads):
        product = jnp.dot(
            low_rank, b_ref[:, c * wide : (c + 1) * wide], preferred_element_type=F32
        )
        pieces.append((2.0 * product).astype(BF16))
    back = exact(ungroup_matrix(owners, heads, lax.axis_index("tensor")), jnp.concatenate(pieces, axis=0))
    block = heads * CAP * STEPS
    for i in range(owners):
        blocks[i] = back[i * block : (i + 1) * block]


def by_shape(span_at, rows, most, action):
    half, quarter = rows // 2, rows // 4
    lower = ((most // 8, most // 4), (most // 4, most // 4), (most // 4, most // 2), (most, most))
    upper = ((most // 4, most), (most // 2, most), (most * 3 // 4, most), (most, most))
    for at, shapes in ((0, lower), (half, upper)):
        first, last = span_at(at + quarter - 1), span_at(at + half - 1)
        open_yet = True
        for a, b in shapes:
            fits = (first <= a) & (last <= b) & open_yet
            open_yet = open_yet & ~((first <= a) & (last <= b))

            @pl.when(fits)
            def _():
                action(at, [a] * quarter + [b] * quarter)


def prepare_kernel(
    owners,
    heads,
    meta,
    q_ref,
    kn_ref,
    vn_ref,
    part,
    order,
    base_out,
    kn_out,
    vn_out,
    mask_out,
    gather_out,
    pack_out,
    after,
):
    rows = q_ref.shape[1]
    wide = q_ref.shape[2] // heads
    base_out[...] = exact(by_row_matrix(heads, rows), stacked(q_ref, heads, wide))
    for source, target in ((kn_ref, kn_out), (vn_ref, vn_out)):
        target[...] = jnp.concatenate([source[t] for t in range(STEPS)], axis=0)
    head_at = rest(over(iota(mask_out.shape, 0), STEPS), heads)
    mask_out[...] = one_hot(head_at == over(iota(mask_out.shape, 1), HD))
    gather_out[...] = unpack_matrix(meta, owners, heads, rows, True)
    pack_out[...] = pack_matrix(meta, owners, heads, rows, True)
    sizes = [meta[rows + owners * CAP + r] for r in range(rows)]
    ahead = [jnp.int32(0)] * rows
    for r in range(rows):
        for q in range(r):
            shorter = jnp.where(sizes[q] <= sizes[r], 1, 0)
            ahead[r] = ahead[r] + shorter
            ahead[q] = ahead[q] + (1 - shorter)
    for r in range(rows):
        order[ahead[r]] = r
        order[rows + r] = sizes[r]
    after[...] = part[: after.shape[0], :]


def attend_kernel(
    owners,
    heads,
    rows,
    order,
    base_ref,
    kn_ref,
    vn_ref,
    mask_ref,
    gather_ref,
    pack_ref,
    k_ref,
    v_ref,
    blocks,
    mixed_out,
    outgoing,
    q_buf,
    o_buf,
):
    wide = base_ref.shape[1]
    groups = wide // HD
    pairs = heads * STEPS
    total = groups * pairs

    def span_of(row):
        return order[rows + row]

    delta = jnp.dot(
        gather_ref[...],
        jnp.concatenate([blocks[i] for i in range(owners)], axis=0),
        preferred_element_type=F32,
    )
    q_buf[...] = base_ref[...].astype(F32) + delta

    head_own = rest(over(iota((total, HD), 0), STEPS), heads)
    factor = math.log2(math.e) / math.sqrt(HD)
    fresh_shape = (total, STEPS * rows)
    fresh_at = iota(fresh_shape, 1)
    fresh_step = over(fresh_at, rows)
    fresh_row = jnp.where(fresh_step <= rest(iota(fresh_shape, 0), STEPS), rest(fresh_at, rows), rows)
    contract = (((1,), (1,)), ((), ()))

    def scores_of(row, extent):
        flat = q_buf[pl.ds(pl.multiple_of(row * pairs, pairs), pairs), :]
        one = jnp.concatenate([flat[:, j * HD : (j + 1) * HD] for j in range(groups)], axis=0)
        spread = jnp.concatenate([one.astype(BF16)] * heads, axis=1) * mask_ref[...]
        keys = jnp.concatenate([k_ref[row, :extent, :], kn_ref[...]], axis=0)
        score = lax.dot_general(spread, keys, contract, preferred_element_type=F32)
        cached = jnp.where(iota((total, extent), 1) < span_of(row), score[:, :extent], -jnp.inf)
        fresh = jnp.where(fresh_row == row, score[:, extent:], -jnp.inf)
        return jnp.concatenate([cached, fresh], axis=1)

    def softmax_of(score):
        top = jnp.max(score, axis=1, keepdims=True)
        weight = jnp.exp2((score - top) * factor)
        return weight.astype(BF16), 1.0 / jnp.sum(weight, axis=1, keepdims=True)

    def mix(row, extent, weight, share):
        values = jnp.concatenate([v_ref[row, :extent, :], vn_ref[...]], axis=0)
        mixed = jnp.dot(weight, values, preferred_element_type=F32)
        own = mixed[:, :HD]
        for c in range(1, heads):
            own = jnp.where(head_own == c, mixed[:, c * HD : (c + 1) * HD], own)
        own = own * share
        o_buf[pl.ds(pl.multiple_of(row * pairs, pairs), pairs), :] = jnp.concatenate(
            [own[j * pairs : (j + 1) * pairs] for j in range(groups)], axis=1
        )

    def attend(at, extents):
        count = len(extents)
        ordered = [order[at + k] for k in range(count)]
        scores, weights = {}, {}
        for t in range(count + 2 * LAG):
            if t < count:
                scores[t] = scores_of(ordered[t], extents[t])
            if 0 <= t - LAG < count:
                weights[t - LAG] = softmax_of(scores.pop(t - LAG))
            if 0 <= t - 2 * LAG < count:
                done = t - 2 * LAG
                mix(ordered[done], extents[done], *weights.pop(done))

    by_shape(lambda place: span_of(order[place]), rows, k_ref.shape[1], attend)

    mixed = o_buf[...].astype(BF16)
    mixed_out[...] = mixed
    packed = exact(pack_ref[...], mixed)
    block = heads * CAP * STEPS
    for i in range(owners):
        outgoing[i] = packed[i * block : (i + 1) * block]


def write_out(matrix, values, heads, out_hbm, out_ref, sems):
    rows = out_ref.shape[1]
    wide = out_ref.shape[2] // heads
    span = STEPS * rows
    copies = []
    for c in range(heads):
        ordered = exact(matrix[c * span : (c + 1) * span], values)
        for s in range(STEPS):
            out_ref[s, :, c * wide : (c + 1) * wide] = ordered[s * rows : (s + 1) * rows]
        part = (slice(None), slice(None), pl.ds(c * wide, wide))
        copies.append(pltpu.make_async_copy(out_ref.at[part], out_hbm.at[part], sems.at[c]))
        copies[-1].start()
    for copy in copies:
        copy.wait()


def finish_kernel(heads, mixed, gather_ref, part, out_hbm, after, spread_out, out_ref, sems):
    after[...] = part[: after.shape[0], :]
    matrix = by_pair_matrix(heads, out_ref.shape[1])
    spread_out[...] = exact(matrix, gather_ref[...])
    write_out(matrix, mixed[...], heads, out_hbm, out_ref, sems)


def collect_kernel(owners, heads, spread, blocks, out_hbm, out_ref, sems):
    arrived = jnp.concatenate([blocks[i] for i in range(owners)], axis=0)
    write_out(spread, arrived, heads, out_hbm, out_ref, sems)


def exchange(blocks):
    owners = blocks.shape[0]
    cores = lax.axis_size("tensor")
    cycle = list(range(0, owners, 2)) + list(range(owners - 1, 0, -2))
    cycle = [cycle[i * stride_of(owners) % owners] for i in range(owners)]
    groups = [
        [s * cores + core for s in (cycle if core % 2 == 0 else cycle[::-1])]
        for core in range(cores)
    ]
    return lax.all_to_all(
        blocks,
        ("store", "tensor"),
        split_axis=0,
        concat_axis=0,
        axis_index_groups=groups,
        tiled=True,
    )


def in_hbm(array):
    return pltpu.with_memory_space_constraint(array, pltpu.HBM)


def swap_cores(part):
    return lax.ppermute(part, "tensor", [(0, 1), (1, 0)])


def shards(
    x_in,
    q_base,
    k_new,
    v_new,
    cache_k,
    cache_v,
    lengths,
    adapter_ids,
    slot_of,
    a_query,
    b_query,
    a_output,
    b_output,
):
    owners = lax.axis_size("store")
    rows = x_in.shape[1]
    width = x_in.shape[2]
    heads = cache_k.shape[2] // HD
    wide = width // heads
    adapt, rank = a_query.shape[1:]
    lanes = adapt * rank
    block = heads * CAP * STEPS
    items = owners * CAP * STEPS
    def flat(a_store):
        return jnp.transpose(a_store, (1, 2, 0)).reshape(lanes, a_store.shape[0])

    shape = jax.ShapeDtypeStruct
    small = pltpu.CompilerParams(vmem_limit_bytes=16 * 1024 * 1024)

    sent = shape((owners, block, wide), BF16)
    caches = (in_hbm(cache_k), in_hbm(cache_v))
    meta, blocks = pl.pallas_call(
        functools.partial(dispatch_kernel, owners, SPLIT, adapt, rank),
        out_shape=[
            shape((2 * rows + owners * CAP,), I32),
            shape((owners, SPLIT * CAP * STEPS, width // SPLIT + lanes), BF16),
        ],
        in_specs=[HBM] * 8,
        out_specs=[SMEM, VMEM],
        scratch_shapes=[
            pltpu.SMEM((owners * CAP,), I32),
            pltpu.SMEM(adapter_ids.shape, I32),
            pltpu.SMEM(slot_of.shape, I32),
            pltpu.SMEM(lengths.shape, I32),
            pltpu.VMEM(x_in.shape, BF16),
            pltpu.SemaphoreType.DMA((4,)),
        ],
        compiler_params=small,
        name="dispatch",
    )(
        *map(in_hbm, (adapter_ids, slot_of, lengths, x_in)), *caches, *caches
    )

    arrived = exchange(blocks)
    part, mask = pl.pallas_call(
        functools.partial(project_kernel, owners, SPLIT, width // SPLIT, True),
        out_shape=[shape((items, lanes), F32)] * 2,
        in_specs=[VMEM] * 2,
        out_specs=[VMEM] * 2,
        compiler_params=small,
        name="project_query",
    )(flat(a_query), arrived)

    def expand(part, other, b_store, name, caches, *after):
        return pl.pallas_call(
            functools.partial(expand_kernel, owners, heads, wide),
            out_shape=sent,
            in_specs=[VMEM] * (3 + len(after)) + [HBM] * len(caches),
            out_specs=VMEM,
            compiler_params=small,
            name=name,
        )(part, other, b_store, *after, *caches)

    other = swap_cores(part)
    order, *prepared, after = pl.pallas_call(
        functools.partial(prepare_kernel, owners, heads),
        out_shape=[
            shape((2 * rows,), I32),
            shape((rows * STEPS * heads, wide), BF16),
            shape((STEPS * rows, heads * HD), BF16),
            shape((STEPS * rows, heads * HD), BF16),
            shape((STEPS * wide // HD * heads, heads * HD), BF16),
            shape((rows * STEPS * heads, owners * block), BF16),
            shape((owners * block, rows * STEPS * heads), BF16),
            shape((8, lanes), F32),
        ],
        in_specs=[SMEM] + [VMEM] * 4,
        out_specs=[SMEM] + [VMEM] * 7,
        compiler_params=small,
        name="prepare",
    )(meta, q_base, k_new, v_new, part)
    returned = exchange(
        expand(part, other, b_query.reshape(lanes, width), "expand_query", (), after)
    )

    mixed, outgoing = pl.pallas_call(
        functools.partial(attend_kernel, owners, heads, rows),
        out_shape=[
            shape((rows * STEPS * heads, wide), BF16),
            sent,
        ],
        in_specs=[SMEM] + [VMEM] * 9,
        out_specs=[VMEM] * 2,
        scratch_shapes=[
            pltpu.VMEM((rows * STEPS * heads, wide), F32),
            pltpu.VMEM((rows * STEPS * heads, wide), F32),
        ],
        compiler_params=small,
        name="attend",
    )(order, *prepared, cache_k, cache_v, returned)

    arrived = exchange(outgoing)
    part = pl.pallas_call(
        functools.partial(project_kernel, owners, heads, wide, False),
        out_shape=shape((items, lanes), F32),
        in_specs=[VMEM] * 3,
        out_specs=VMEM,
        compiler_params=small,
        name="project_output",
    )(flat(a_output), arrived, mask)
    ordered = dict(
        scratch_shapes=[
            pltpu.VMEM((STEPS, rows, width), BF16),
            pltpu.SemaphoreType.DMA((heads,)),
        ],
        compiler_params=small,
    )
    other = swap_cores(part)
    attn_out, after, spread = pl.pallas_call(
        functools.partial(finish_kernel, heads),
        out_shape=[
            shape((STEPS, rows, width), BF16),
            shape((8, lanes), F32),
            shape((rows * STEPS * heads, owners * block), BF16),
        ],
        in_specs=[VMEM] * 3,
        out_specs=[HBM, VMEM, VMEM],
        name="finish",
        **ordered,
    )(mixed, prepared[4], part)
    returned = exchange(
        expand(part, other, b_output.reshape(lanes, width), "expand_output", (), after)
    )
    adapter_out = pl.pallas_call(
        functools.partial(collect_kernel, owners, heads),
        out_shape=shape((STEPS, rows, width), BF16),
        in_specs=[VMEM] * 2,
        out_specs=HBM,
        name="collect",
        **ordered,
    )(spread, returned)
    return (attn_out, adapter_out)


def solution(mesh):
    in_specs = (
        P(None, ("parts", "store"), "tensor"),
        P(None, ("parts", "store"), "tensor"),
        P(None, ("parts", "store"), "tensor"),
        P(None, ("parts", "store"), "tensor"),
        P(("parts", "store"), None, "tensor"),
        P(("parts", "store"), None, "tensor"),
        P(("parts", "store")),
        P(("parts", "store")),
        P("parts"),
        P(None, "store", None),
        P("store", None, "tensor"),
        P(None, "store", None),
        P("store", None, "tensor"),
    )
    out_specs = (P(None, ("parts", "store"), "tensor"), P(None, ("parts", "store"), "tensor"))
    return jax.shard_map(shards, mesh=mesh, in_specs=in_specs, out_specs=out_specs, check_vma=False)
```

```python
import functools
import math

import jax
import jax.numpy as jnp
from jax import lax
from jax.experimental import pallas as pl
from jax.experimental.pallas import tpu as pltpu
from jax.sharding import PartitionSpec as P

HD = 128
CAP = 2
STEPS = 2
LAG = 2
SPLIT = 2
BF16 = jnp.bfloat16
F32 = jnp.float32
I32 = jnp.int32
VMEM = pl.BlockSpec(memory_space=pltpu.VMEM)
SMEM = pl.BlockSpec(memory_space=pltpu.SMEM)
HBM = pl.BlockSpec(memory_space=pltpu.HBM)


def iota(shape, dim):
    return lax.broadcasted_iota(I32, shape, dim)


def over(x, n):
    return lax.shift_right_logical(x, jnp.full_like(x, n.bit_length() - 1)) if n & (n - 1) == 0 else x // n


def rest(x, n):
    return x & (n - 1) if n & (n - 1) == 0 else x % n


def one_hot(hits):
    return jnp.where(hits, 1.0, 0.0).astype(BF16)


def stacked(ref, heads, wide):
    return jnp.concatenate(
        [ref[s, :, c * wide : (c + 1) * wide] for c in range(heads) for s in range(STEPS)], axis=0
    )


def pack_matrix(meta, owners, heads, rows, by_row):
    items = CAP * STEPS
    block = heads * items
    shape = (block, heads * STEPS * rows)
    at = iota(shape, 0)
    col = iota(shape, 1)
    head_step = over(at, items) * STEPS + rest(at, STEPS)
    offset = col - (head_step if by_row else head_step * rows)
    factor = heads * STEPS if by_row else 1
    first = rest(over(at, STEPS), CAP) == 0
    if not by_row:
        offset = jnp.where((offset >= 0) & (offset < rows), offset, -1)
    parts = []
    for i in range(owners):
        here = [meta[rows + i * CAP + k] for k in range(CAP)]
        spots = [jnp.where(h >= 0, h * factor, -rows * factor * heads * STEPS * 2) for h in here]
        parts.append(one_hot(offset == jnp.where(first, spots[0], spots[1])))
    return jnp.concatenate(parts, axis=0)


def unpack_matrix(meta, owners, heads, rows, by_row):
    items = CAP * STEPS
    block = heads * items
    pairs = heads * STEPS
    spots = [over(meta[r], CAP) * block + rest(meta[r], CAP) * STEPS for r in range(rows)]
    if by_row:
        shape = (pairs, owners * block)
        at = iota(shape, 0)
        col = iota(shape, 1) - (over(at, STEPS) * items + rest(at, STEPS))
        return jnp.concatenate([one_hot(col == spots[r]) for r in range(rows)], axis=0)
    shape = (rows, owners * block)
    at = iota(shape, 0)
    col = iota(shape, 1)
    spot = jnp.zeros(shape, I32)
    for r in range(rows):
        spot = jnp.where(at == r, spots[r], spot)
    offset = col - spot
    return jnp.concatenate(
        [one_hot(offset == c * items + s) for c in range(heads) for s in range(STEPS)], axis=0
    )


def by_row_matrix(heads, rows):
    pairs = heads * STEPS
    shape = (pairs * rows, pairs * rows)
    at = iota(shape, 0)
    return one_hot(iota(shape, 1) == rest(at, pairs) * rows + over(at, pairs))


def by_pair_matrix(heads, rows):
    pairs = heads * STEPS
    shape = (pairs * rows, pairs * rows)
    at = iota(shape, 0)
    return one_hot(iota(shape, 1) == rest(at, rows) * pairs + over(at, rows))


def stride_of(owners):
    return 3 if owners % 3 else 1


def turned(place, owners, core):
    return place + rest(core, 2) * (owners - 1 - 2 * place)


def regroup_matrix(owners, heads, core):
    items = CAP * STEPS
    total = owners * heads * items
    at = iota((total, total), 0)
    head = over(at, owners * items)
    owner = turned(rest(over(at, items), owners), owners, core)
    return one_hot(
        iota((total, total), 1) == owner * (heads * items) + head * items + rest(at, items)
    )


def ungroup_matrix(owners, heads, core):
    items = CAP * STEPS
    total = owners * heads * items
    at = iota((total, total), 0)
    owner = turned(over(at, heads * items), owners, core)
    head = rest(over(at, items), heads)
    return one_hot(
        iota((total, total), 1) == head * (owners * items) + owner * items + rest(at, items)
    )


def exact(matrix, values):
    return jnp.dot(matrix, values, preferred_element_type=F32).astype(BF16)


def dispatch_kernel(
    owners,
    heads,
    adapt,
    rank,
    ids_hbm,
    slot_of_hbm,
    lengths_hbm,
    x_hbm,
    k_hbm,
    v_hbm,
    k_again,
    v_again,
    meta,
    blocks,
    slot_at,
    ids,
    slot_of,
    lengths,
    x_ref,
    sems,
):
    pairs = (
        (ids_hbm, ids),
        (slot_of_hbm, slot_of),
        (lengths_hbm, lengths),
        (x_hbm, x_ref),
    )
    copies = [pltpu.make_async_copy(a, b, sems.at[k]) for k, (a, b) in enumerate(pairs)]
    for copy in copies:
        copy.start()
    rows = x_ref.shape[1]
    wide = x_ref.shape[2] // heads
    for copy in copies[:3]:
        copy.wait()
    core = lax.axis_index("tensor")
    row_at = rows
    order = rows + owners * CAP
    spans = order + rows
    for p in range(owners * CAP):
        meta[row_at + p] = -1
        slot_at[p] = -1
    for r in range(rows):
        slot = slot_of[ids[r]]
        owner = over(slot, adapt)
        half = over(owner, 2)
        along = jnp.where(rest(owner, 2) == 0, half, owners - 1 - half)
        along = rest(along * pow(stride_of(owners), -1, owners), owners)
        first = turned(along, owners, core) * CAP
        place = first + jnp.where(meta[row_at + first] >= 0, 1, 0)
        meta[row_at + place] = r
        slot_at[place] = rest(slot, adapt)
        meta[r] = place
    sizes = [lengths[r] for r in range(rows)]
    ahead = [jnp.int32(0)] * rows
    for r in range(rows):
        for q in range(r):
            shorter = jnp.where(sizes[q] <= sizes[r], 1, 0)
            ahead[r] = ahead[r] + shorter
            ahead[q] = ahead[q] + (1 - shorter)
    for r in range(rows):
        meta[order + ahead[r]] = r
        meta[spans + r] = sizes[r]
    items = CAP * STEPS
    block = heads * items
    copies[3].wait()
    packed = exact(pack_matrix(meta, owners, heads, rows, False), stacked(x_ref, heads, wide))
    at = iota((block, adapt * rank), 0)
    lane_slot = over(iota((block, adapt * rank), 1), rank)
    first = rest(over(at, STEPS), CAP) == 0
    for i in range(owners):
        blocks[i, :, :wide] = packed[i * block : (i + 1) * block]
        slot = jnp.where(first, slot_at[i * CAP], slot_at[i * CAP + 1])
        blocks[i, :, wide:] = one_hot(lane_slot == slot)


def project_kernel(owners, heads, wide, first, a_ref, blocks, *refs):
    core = lax.axis_index("tensor")
    if first:
        part_ref, mask_ref = refs
    else:
        mask_in, part_ref = refs
    grouped = regroup_matrix(owners, heads, core)
    items = owners * CAP * STEPS
    arrived = jnp.concatenate([blocks[i, :, :wide] for i in range(owners)], axis=0)
    arrived = exact(grouped, arrived)
    if first:
        masks = jnp.concatenate([blocks[i, :, wide:] for i in range(owners)], axis=0)
        mask = jnp.dot(grouped[:items], masks, preferred_element_type=F32)
        mask_ref[...] = mask
    else:
        mask = mask_in[...]
    total = jnp.zeros(mask.shape, F32)
    for c in range(heads):
        total = total + lax.dot_general(
            arrived[c * items : (c + 1) * items],
            a_ref[:, pl.ds(pl.multiple_of(core * (heads * wide) + c * wide, wide), wide)],
            (((1,), (1,)), ((), ())),
            preferred_element_type=F32,
        )
    part_ref[...] = total * mask


def expand_kernel(owners, heads, wide, mine, other, b_ref, *refs):
    blocks = refs[-1]
    low_rank = (mine[...] + other[...]).astype(BF16)
    pieces = []
    for c in range(heads):
        product = jnp.dot(
            low_rank, b_ref[:, c * wide : (c + 1) * wide], preferred_element_type=F32
        )
        pieces.append((2.0 * product).astype(BF16))
    back = exact(ungroup_matrix(owners, heads, lax.axis_index("tensor")), jnp.concatenate(pieces, axis=0))
    block = heads * CAP * STEPS
    for i in range(owners):
        blocks[i] = back[i * block : (i + 1) * block]


def by_shape(span_at, rows, most, action):
    half, quarter = rows // 2, rows // 4
    lower = ((most // 8, most // 4), (most // 4, most // 4), (most // 4, most // 2), (most, most))
    upper = ((most // 4, most), (most // 2, most), (most * 3 // 4, most), (most, most))
    for at, shapes in ((0, lower), (half, upper)):
        first, last = span_at(at + quarter - 1), span_at(at + half - 1)
        open_yet = True
        for a, b in shapes:
            fits = (first <= a) & (last <= b) & open_yet
            open_yet = open_yet & ~((first <= a) & (last <= b))

            @pl.when(fits)
            def _():
                action(at, [a] * quarter + [b] * quarter)


def prepare_kernel(
    owners,
    heads,
    meta,
    q_ref,
    kn_ref,
    vn_ref,
    part,
    base_out,
    kn_out,
    vn_out,
    mask_out,
    gather_out,
    pack_out,
    after,
):
    rows = q_ref.shape[1]
    wide = q_ref.shape[2] // heads
    base_out[...] = exact(by_row_matrix(heads, rows), stacked(q_ref, heads, wide))
    for source, target in ((kn_ref, kn_out), (vn_ref, vn_out)):
        target[...] = jnp.concatenate([source[t] for t in range(STEPS)], axis=0)
    head_at = rest(over(iota(mask_out.shape, 0), STEPS), heads)
    mask_out[...] = one_hot(head_at == over(iota(mask_out.shape, 1), HD))
    gather_out[...] = unpack_matrix(meta, owners, heads, rows, True)
    pack_out[...] = pack_matrix(meta, owners, heads, rows, True)
    after[...] = part[: after.shape[0], :]


def attend_kernel(
    owners,
    heads,
    rows,
    meta,
    base_ref,
    kn_ref,
    vn_ref,
    mask_ref,
    gather_ref,
    pack_ref,
    k_ref,
    v_ref,
    blocks,
    mixed_out,
    outgoing,
    q_buf,
    o_buf,
):
    wide = base_ref.shape[1]
    groups = wide // HD
    pairs = heads * STEPS
    total = groups * pairs

    def span_of(row):
        return meta[2 * rows + owners * CAP + row]

    def row_at(place):
        return meta[rows + owners * CAP + place]

    delta = jnp.dot(
        gather_ref[...],
        jnp.concatenate([blocks[i] for i in range(owners)], axis=0),
        preferred_element_type=F32,
    )
    q_buf[...] = base_ref[...].astype(F32) + delta

    head_own = rest(over(iota((total, HD), 0), STEPS), heads)
    factor = math.log2(math.e) / math.sqrt(HD)
    fresh_shape = (total, STEPS * rows)
    fresh_at = iota(fresh_shape, 1)
    fresh_step = over(fresh_at, rows)
    fresh_row = jnp.where(fresh_step <= rest(iota(fresh_shape, 0), STEPS), rest(fresh_at, rows), rows)
    contract = (((1,), (1,)), ((), ()))

    def scores_of(row, extent):
        flat = q_buf[pl.ds(pl.multiple_of(row * pairs, pairs), pairs), :]
        one = jnp.concatenate([flat[:, j * HD : (j + 1) * HD] for j in range(groups)], axis=0)
        spread = jnp.concatenate([one.astype(BF16)] * heads, axis=1) * mask_ref[...]
        keys = jnp.concatenate([k_ref[row, :extent, :], kn_ref[...]], axis=0)
        score = lax.dot_general(spread, keys, contract, preferred_element_type=F32)
        cached = jnp.where(iota((total, extent), 1) < span_of(row), score[:, :extent], -jnp.inf)
        fresh = jnp.where(fresh_row == row, score[:, extent:], -jnp.inf)
        return jnp.concatenate([cached, fresh], axis=1)

    def softmax_of(score):
        top = jnp.max(score, axis=1, keepdims=True)
        weight = jnp.exp2((score - top) * factor)
        return weight.astype(BF16), 1.0 / jnp.sum(weight, axis=1, keepdims=True)

    def mix(row, extent, weight, share):
        values = jnp.concatenate([v_ref[row, :extent, :], vn_ref[...]], axis=0)
        mixed = jnp.dot(weight, values, preferred_element_type=F32)
        own = mixed[:, :HD]
        for c in range(1, heads):
            own = jnp.where(head_own == c, mixed[:, c * HD : (c + 1) * HD], own)
        own = own * share
        o_buf[pl.ds(pl.multiple_of(row * pairs, pairs), pairs), :] = jnp.concatenate(
            [own[j * pairs : (j + 1) * pairs] for j in range(groups)], axis=1
        )

    def attend(at, extents):
        count = len(extents)
        ordered = [row_at(at + k) for k in range(count)]
        scores, weights = {}, {}
        for t in range(count + 2 * LAG):
            if t < count:
                scores[t] = scores_of(ordered[t], extents[t])
            if 0 <= t - LAG < count:
                weights[t - LAG] = softmax_of(scores.pop(t - LAG))
            if 0 <= t - 2 * LAG < count:
                done = t - 2 * LAG
                mix(ordered[done], extents[done], *weights.pop(done))

    by_shape(lambda place: span_of(row_at(place)), rows, k_ref.shape[1], attend)

    mixed = o_buf[...].astype(BF16)
    mixed_out[...] = mixed
    packed = exact(pack_ref[...], mixed)
    block = heads * CAP * STEPS
    for i in range(owners):
        outgoing[i] = packed[i * block : (i + 1) * block]


def write_out(matrix, values, heads, out_hbm, out_ref, sems):
    rows = out_ref.shape[1]
    wide = out_ref.shape[2] // heads
    span = STEPS * rows
    copies = []
    for c in range(heads):
        ordered = exact(matrix[c * span : (c + 1) * span], values)
        for s in range(STEPS):
            out_ref[s, :, c * wide : (c + 1) * wide] = ordered[s * rows : (s + 1) * rows]
        part = (slice(None), slice(None), pl.ds(c * wide, wide))
        copies.append(pltpu.make_async_copy(out_ref.at[part], out_hbm.at[part], sems.at[c]))
        copies[-1].start()
    for copy in copies:
        copy.wait()


def finish_kernel(heads, mixed, gather_ref, part, out_hbm, after, spread_out, out_ref, sems):
    after[...] = part[: after.shape[0], :]
    matrix = by_pair_matrix(heads, out_ref.shape[1])
    spread_out[...] = exact(matrix, gather_ref[...])
    write_out(matrix, mixed[...], heads, out_hbm, out_ref, sems)


def collect_kernel(owners, heads, spread, blocks, out_hbm, out_ref, sems):
    arrived = jnp.concatenate([blocks[i] for i in range(owners)], axis=0)
    write_out(spread, arrived, heads, out_hbm, out_ref, sems)


def exchange(blocks):
    owners = blocks.shape[0]
    cores = lax.axis_size("tensor")
    cycle = list(range(0, owners, 2)) + list(range(owners - 1, 0, -2))
    cycle = [cycle[i * stride_of(owners) % owners] for i in range(owners)]
    groups = [
        [s * cores + core for s in (cycle if core % 2 == 0 else cycle[::-1])]
        for core in range(cores)
    ]
    return lax.all_to_all(
        blocks,
        ("store", "tensor"),
        split_axis=0,
        concat_axis=0,
        axis_index_groups=groups,
        tiled=True,
    )


def in_hbm(array):
    return pltpu.with_memory_space_constraint(array, pltpu.HBM)


def swap_cores(part):
    return lax.ppermute(part, "tensor", [(0, 1), (1, 0)])


def shards(
    x_in,
    q_base,
    k_new,
    v_new,
    cache_k,
    cache_v,
    lengths,
    adapter_ids,
    slot_of,
    a_query,
    b_query,
    a_output,
    b_output,
):
    owners = lax.axis_size("store")
    rows = x_in.shape[1]
    width = x_in.shape[2]
    heads = cache_k.shape[2] // HD
    wide = width // heads
    adapt, rank = a_query.shape[1:]
    lanes = adapt * rank
    block = heads * CAP * STEPS
    items = owners * CAP * STEPS
    def flat(a_store):
        return jnp.transpose(a_store, (1, 2, 0)).reshape(lanes, a_store.shape[0])

    shape = jax.ShapeDtypeStruct
    small = pltpu.CompilerParams(vmem_limit_bytes=16 * 1024 * 1024)

    sent = shape((owners, block, wide), BF16)
    caches = (in_hbm(cache_k), in_hbm(cache_v))
    meta, blocks = pl.pallas_call(
        functools.partial(dispatch_kernel, owners, SPLIT, adapt, rank),
        out_shape=[
            shape((3 * rows + owners * CAP,), I32),
            shape((owners, SPLIT * CAP * STEPS, width // SPLIT + lanes), BF16),
        ],
        in_specs=[HBM] * 8,
        out_specs=[SMEM, VMEM],
        scratch_shapes=[
            pltpu.SMEM((owners * CAP,), I32),
            pltpu.SMEM(adapter_ids.shape, I32),
            pltpu.SMEM(slot_of.shape, I32),
            pltpu.SMEM(lengths.shape, I32),
            pltpu.VMEM(x_in.shape, BF16),
            pltpu.SemaphoreType.DMA((4,)),
        ],
        compiler_params=small,
        name="dispatch",
    )(
        *map(in_hbm, (adapter_ids, slot_of, lengths, x_in)), *caches, *caches
    )

    arrived = exchange(blocks)
    part, mask = pl.pallas_call(
        functools.partial(project_kernel, owners, SPLIT, width // SPLIT, True),
        out_shape=[shape((items, lanes), F32)] * 2,
        in_specs=[VMEM] * 2,
        out_specs=[VMEM] * 2,
        compiler_params=small,
        name="project_query",
    )(flat(a_query), arrived)

    def expand(part, other, b_store, name, caches, *after):
        return pl.pallas_call(
            functools.partial(expand_kernel, owners, heads, wide),
            out_shape=sent,
            in_specs=[VMEM] * (3 + len(after)) + [HBM] * len(caches),
            out_specs=VMEM,
            compiler_params=small,
            name=name,
        )(part, other, b_store, *after, *caches)

    other = swap_cores(part)
    *prepared, after = pl.pallas_call(
        functools.partial(prepare_kernel, owners, heads),
        out_shape=[
            shape((rows * STEPS * heads, wide), BF16),
            shape((STEPS * rows, heads * HD), BF16),
            shape((STEPS * rows, heads * HD), BF16),
            shape((STEPS * wide // HD * heads, heads * HD), BF16),
            shape((rows * STEPS * heads, owners * block), BF16),
            shape((owners * block, rows * STEPS * heads), BF16),
            shape((8, lanes), F32),
        ],
        in_specs=[SMEM] + [VMEM] * 4,
        out_specs=[VMEM] * 7,
        compiler_params=small,
        name="prepare",
    )(meta, q_base, k_new, v_new, part)
    returned = exchange(
        expand(part, other, b_query.reshape(lanes, width), "expand_query", (), after)
    )

    mixed, outgoing = pl.pallas_call(
        functools.partial(attend_kernel, owners, heads, rows),
        out_shape=[
            shape((rows * STEPS * heads, wide), BF16),
            sent,
        ],
        in_specs=[SMEM] + [VMEM] * 9,
        out_specs=[VMEM] * 2,
        scratch_shapes=[
            pltpu.VMEM((rows * STEPS * heads, wide), F32),
            pltpu.VMEM((rows * STEPS * heads, wide), F32),
        ],
        compiler_params=small,
        name="attend",
    )(meta, *prepared, cache_k, cache_v, returned)

    arrived = exchange(outgoing)
    part = pl.pallas_call(
        functools.partial(project_kernel, owners, heads, wide, False),
        out_shape=shape((items, lanes), F32),
        in_specs=[VMEM] * 3,
        out_specs=VMEM,
        compiler_params=small,
        name="project_output",
    )(flat(a_output), arrived, mask)
    ordered = dict(
        scratch_shapes=[
            pltpu.VMEM((STEPS, rows, width), BF16),
            pltpu.SemaphoreType.DMA((heads,)),
        ],
        compiler_params=small,
    )
    other = swap_cores(part)
    attn_out, after, spread = pl.pallas_call(
        functools.partial(finish_kernel, heads),
        out_shape=[
            shape((STEPS, rows, width), BF16),
            shape((8, lanes), F32),
            shape((rows * STEPS * heads, owners * block), BF16),
        ],
        in_specs=[VMEM] * 3,
        out_specs=[HBM, VMEM, VMEM],
        name="finish",
        **ordered,
    )(mixed, prepared[4], part)
    returned = exchange(
        expand(part, other, b_output.reshape(lanes, width), "expand_output", (), after)
    )
    adapter_out = pl.pallas_call(
        functools.partial(collect_kernel, owners, heads),
        out_shape=shape((STEPS, rows, width), BF16),
        in_specs=[VMEM] * 2,
        out_specs=HBM,
        name="collect",
        **ordered,
    )(spread, returned)
    return (attn_out, adapter_out)


def solution(mesh):
    in_specs = (
        P(None, ("parts", "store"), "tensor"),
        P(None, ("parts", "store"), "tensor"),
        P(None, ("parts", "store"), "tensor"),
        P(None, ("parts", "store"), "tensor"),
        P(("parts", "store"), None, "tensor"),
        P(("parts", "store"), None, "tensor"),
        P(("parts", "store")),
        P(("parts", "store")),
        P("parts"),
        P(None, "store", None),
        P("store", None, "tensor"),
        P(None, "store", None),
        P("store", None, "tensor"),
    )
    out_specs = (P(None, ("parts", "store"), "tensor"), P(None, ("parts", "store"), "tensor"))
    return jax.shard_map(shards, mesh=mesh, in_specs=in_specs, out_specs=out_specs, check_vma=False)
```

```python
import functools
import math

import jax
import jax.numpy as jnp
from jax import lax
from jax.experimental import pallas as pl
from jax.experimental.pallas import tpu as pltpu
from jax.sharding import PartitionSpec as P

HD = 128
CAP = 2
STEPS = 2
LAG = 2
SPLIT = 2
BF16 = jnp.bfloat16
F32 = jnp.float32
I32 = jnp.int32
VMEM = pl.BlockSpec(memory_space=pltpu.VMEM)
SMEM = pl.BlockSpec(memory_space=pltpu.SMEM)
HBM = pl.BlockSpec(memory_space=pltpu.HBM)


def iota(shape, dim):
    return lax.broadcasted_iota(I32, shape, dim)


def over(x, n):
    return lax.shift_right_logical(x, jnp.full_like(x, n.bit_length() - 1)) if n & (n - 1) == 0 else x // n


def rest(x, n):
    return x & (n - 1) if n & (n - 1) == 0 else x % n


def one_hot(hits):
    return jnp.where(hits, 1.0, 0.0).astype(BF16)


def stacked(ref, heads, wide):
    return jnp.concatenate(
        [ref[s, :, c * wide : (c + 1) * wide] for c in range(heads) for s in range(STEPS)], axis=0
    )


def pack_matrix(meta, owners, heads, rows, by_row):
    items = CAP * STEPS
    block = heads * items
    shape = (block, heads * STEPS * rows)
    at = iota(shape, 0)
    col = iota(shape, 1)
    head_step = over(at, items) * STEPS + rest(at, STEPS)
    offset = col - (head_step if by_row else head_step * rows)
    factor = heads * STEPS if by_row else 1
    first = rest(over(at, STEPS), CAP) == 0
    if not by_row:
        offset = jnp.where((offset >= 0) & (offset < rows), offset, -1)
    parts = []
    for i in range(owners):
        here = [meta[rows + i * CAP + k] for k in range(CAP)]
        spots = [jnp.where(h >= 0, h * factor, -rows * factor * heads * STEPS * 2) for h in here]
        parts.append(one_hot(offset == jnp.where(first, spots[0], spots[1])))
    return jnp.concatenate(parts, axis=0)


def unpack_matrix(meta, owners, heads, rows, by_row):
    items = CAP * STEPS
    block = heads * items
    pairs = heads * STEPS
    spots = [over(meta[r], CAP) * block + rest(meta[r], CAP) * STEPS for r in range(rows)]
    if by_row:
        shape = (pairs, owners * block)
        at = iota(shape, 0)
        col = iota(shape, 1) - (over(at, STEPS) * items + rest(at, STEPS))
        return jnp.concatenate([one_hot(col == spots[r]) for r in range(rows)], axis=0)
    shape = (rows, owners * block)
    at = iota(shape, 0)
    col = iota(shape, 1)
    spot = jnp.zeros(shape, I32)
    for r in range(rows):
        spot = jnp.where(at == r, spots[r], spot)
    offset = col - spot
    return jnp.concatenate(
        [one_hot(offset == c * items + s) for c in range(heads) for s in range(STEPS)], axis=0
    )


def by_row_matrix(heads, rows):
    pairs = heads * STEPS
    shape = (pairs * rows, pairs * rows)
    at = iota(shape, 0)
    return one_hot(iota(shape, 1) == rest(at, pairs) * rows + over(at, pairs))


def by_pair_matrix(heads, rows):
    pairs = heads * STEPS
    shape = (pairs * rows, pairs * rows)
    at = iota(shape, 0)
    return one_hot(iota(shape, 1) == rest(at, rows) * pairs + over(at, rows))


def stride_of(owners):
    return 3 if owners % 3 else 1


def to_block(place, owners, core):
    other = owners - 1 - rest(place * stride_of(owners), owners)
    return place + rest(core, 2) * (other - place)


def to_place(block, owners, core):
    other = rest((owners - 1 - block) * pow(stride_of(owners), -1, owners), owners)
    return block + rest(core, 2) * (other - block)


def regroup_matrix(owners, heads, core):
    items = CAP * STEPS
    total = owners * heads * items
    at = iota((total, total), 0)
    head = over(at, owners * items)
    owner = to_block(rest(over(at, items), owners), owners, core)
    return one_hot(
        iota((total, total), 1) == owner * (heads * items) + head * items + rest(at, items)
    )


def ungroup_matrix(owners, heads, core):
    items = CAP * STEPS
    total = owners * heads * items
    at = iota((total, total), 0)
    owner = to_place(over(at, heads * items), owners, core)
    head = rest(over(at, items), heads)
    return one_hot(
        iota((total, total), 1) == head * (owners * items) + owner * items + rest(at, items)
    )


def exact(matrix, values):
    return jnp.dot(matrix, values, preferred_element_type=F32).astype(BF16)


def dispatch_kernel(
    owners,
    heads,
    adapt,
    rank,
    ids_hbm,
    slot_of_hbm,
    lengths_hbm,
    x_hbm,
    k_hbm,
    v_hbm,
    k_again,
    v_again,
    meta,
    blocks,
    slot_at,
    ids,
    slot_of,
    lengths,
    x_ref,
    sems,
):
    pairs = (
        (ids_hbm, ids),
        (slot_of_hbm, slot_of),
        (lengths_hbm, lengths),
        (x_hbm, x_ref),
    )
    copies = [pltpu.make_async_copy(a, b, sems.at[k]) for k, (a, b) in enumerate(pairs)]
    for copy in copies:
        copy.start()
    rows = x_ref.shape[1]
    wide = x_ref.shape[2] // heads
    for copy in copies[:3]:
        copy.wait()
    core = lax.axis_index("tensor")
    row_at = rows
    order = rows + owners * CAP
    spans = order + rows
    for p in range(owners * CAP):
        meta[row_at + p] = -1
        slot_at[p] = -1
    for r in range(rows):
        slot = slot_of[ids[r]]
        owner = over(slot, adapt)
        half = over(owner, 2)
        along = jnp.where(rest(owner, 2) == 0, half, owners - 1 - half)
        along = rest(along * pow(stride_of(owners), -1, owners), owners)
        first = to_block(along, owners, core) * CAP
        place = first + jnp.where(meta[row_at + first] >= 0, 1, 0)
        meta[row_at + place] = r
        slot_at[place] = rest(slot, adapt)
        meta[r] = place
    sizes = [lengths[r] for r in range(rows)]
    ahead = [jnp.int32(0)] * rows
    for r in range(rows):
        for q in range(r):
            shorter = jnp.where(sizes[q] <= sizes[r], 1, 0)
            ahead[r] = ahead[r] + shorter
            ahead[q] = ahead[q] + (1 - shorter)
    for r in range(rows):
        meta[order + ahead[r]] = r
        meta[spans + r] = sizes[r]
    items = CAP * STEPS
    block = heads * items
    copies[3].wait()
    packed = exact(pack_matrix(meta, owners, heads, rows, False), stacked(x_ref, heads, wide))
    at = iota((block, adapt * rank), 0)
    lane_slot = over(iota((block, adapt * rank), 1), rank)
    first = rest(over(at, STEPS), CAP) == 0
    for i in range(owners):
        blocks[i, :, :wide] = packed[i * block : (i + 1) * block]
        slot = jnp.where(first, slot_at[i * CAP], slot_at[i * CAP + 1])
        blocks[i, :, wide:] = one_hot(lane_slot == slot)


def project_kernel(owners, heads, wide, first, a_ref, blocks, *refs):
    core = lax.axis_index("tensor")
    if first:
        part_ref, mask_ref = refs
    else:
        mask_in, part_ref = refs
    grouped = regroup_matrix(owners, heads, core)
    items = owners * CAP * STEPS
    arrived = jnp.concatenate([blocks[i, :, :wide] for i in range(owners)], axis=0)
    arrived = exact(grouped, arrived)
    if first:
        masks = jnp.concatenate([blocks[i, :, wide:] for i in range(owners)], axis=0)
        mask = jnp.dot(grouped[:items], masks, preferred_element_type=F32)
        mask_ref[...] = mask
    else:
        mask = mask_in[...]
    total = jnp.zeros(mask.shape, F32)
    for c in range(heads):
        total = total + lax.dot_general(
            arrived[c * items : (c + 1) * items],
            a_ref[:, pl.ds(pl.multiple_of(core * (heads * wide) + c * wide, wide), wide)],
            (((1,), (1,)), ((), ())),
            preferred_element_type=F32,
        )
    part_ref[...] = total * mask


def expand_kernel(owners, heads, wide, mine, other, b_ref, *refs):
    blocks = refs[-1]
    low_rank = (mine[...] + other[...]).astype(BF16)
    pieces = []
    for c in range(heads):
        product = jnp.dot(
            low_rank, b_ref[:, c * wide : (c + 1) * wide], preferred_element_type=F32
        )
        pieces.append((2.0 * product).astype(BF16))
    back = exact(ungroup_matrix(owners, heads, lax.axis_index("tensor")), jnp.concatenate(pieces, axis=0))
    block = heads * CAP * STEPS
    for i in range(owners):
        blocks[i] = back[i * block : (i + 1) * block]


def by_shape(span_at, rows, most, action):
    half, quarter = rows // 2, rows // 4
    lower = ((most // 8, most // 4), (most // 4, most // 4), (most // 4, most // 2), (most, most))
    upper = ((most // 4, most), (most // 2, most), (most * 3 // 4, most), (most, most))
    for at, shapes in ((0, lower), (half, upper)):
        first, last = span_at(at + quarter - 1), span_at(at + half - 1)
        open_yet = True
        for a, b in shapes:
            fits = (first <= a) & (last <= b) & open_yet
            open_yet = open_yet & ~((first <= a) & (last <= b))

            @pl.when(fits)
            def _():
                action(at, [a] * quarter + [b] * quarter)


def prepare_kernel(
    owners,
    heads,
    meta,
    q_ref,
    kn_ref,
    vn_ref,
    part,
    base_out,
    kn_out,
    vn_out,
    mask_out,
    gather_out,
    pack_out,
    after,
):
    rows = q_ref.shape[1]
    wide = q_ref.shape[2] // heads
    base_out[...] = exact(by_row_matrix(heads, rows), stacked(q_ref, heads, wide))
    for source, target in ((kn_ref, kn_out), (vn_ref, vn_out)):
        target[...] = jnp.concatenate([source[t] for t in range(STEPS)], axis=0)
    head_at = rest(over(iota(mask_out.shape, 0), STEPS), heads)
    mask_out[...] = one_hot(head_at == over(iota(mask_out.shape, 1), HD))
    gather_out[...] = unpack_matrix(meta, owners, heads, rows, True)
    pack_out[...] = pack_matrix(meta, owners, heads, rows, True)
    after[...] = part[: after.shape[0], :]


def attend_kernel(
    owners,
    heads,
    rows,
    meta,
    base_ref,
    kn_ref,
    vn_ref,
    mask_ref,
    gather_ref,
    pack_ref,
    k_ref,
    v_ref,
    blocks,
    mixed_out,
    outgoing,
    q_buf,
    o_buf,
):
    wide = base_ref.shape[1]
    groups = wide // HD
    pairs = heads * STEPS
    total = groups * pairs

    def span_of(row):
        return meta[2 * rows + owners * CAP + row]

    def row_at(place):
        return meta[rows + owners * CAP + place]

    delta = jnp.dot(
        gather_ref[...],
        jnp.concatenate([blocks[i] for i in range(owners)], axis=0),
        preferred_element_type=F32,
    )
    q_buf[...] = base_ref[...].astype(F32) + delta

    head_own = rest(over(iota((total, HD), 0), STEPS), heads)
    factor = math.log2(math.e) / math.sqrt(HD)
    fresh_shape = (total, STEPS * rows)
    fresh_at = iota(fresh_shape, 1)
    fresh_step = over(fresh_at, rows)
    fresh_row = jnp.where(fresh_step <= rest(iota(fresh_shape, 0), STEPS), rest(fresh_at, rows), rows)
    contract = (((1,), (1,)), ((), ()))

    def scores_of(row, extent):
        flat = q_buf[pl.ds(pl.multiple_of(row * pairs, pairs), pairs), :]
        one = jnp.concatenate([flat[:, j * HD : (j + 1) * HD] for j in range(groups)], axis=0)
        spread = jnp.concatenate([one.astype(BF16)] * heads, axis=1) * mask_ref[...]
        keys = jnp.concatenate([k_ref[row, :extent, :], kn_ref[...]], axis=0)
        score = lax.dot_general(spread, keys, contract, preferred_element_type=F32)
        cached = jnp.where(iota((total, extent), 1) < span_of(row), score[:, :extent], -jnp.inf)
        fresh = jnp.where(fresh_row == row, score[:, extent:], -jnp.inf)
        return jnp.concatenate([cached, fresh], axis=1)

    def softmax_of(score):
        top = jnp.max(score, axis=1, keepdims=True)
        weight = jnp.exp2((score - top) * factor)
        return weight.astype(BF16), 1.0 / jnp.sum(weight, axis=1, keepdims=True)

    def mix(row, extent, weight, share):
        values = jnp.concatenate([v_ref[row, :extent, :], vn_ref[...]], axis=0)
        mixed = jnp.dot(weight, values, preferred_element_type=F32)
        own = mixed[:, :HD]
        for c in range(1, heads):
            own = jnp.where(head_own == c, mixed[:, c * HD : (c + 1) * HD], own)
        own = own * share
        o_buf[pl.ds(pl.multiple_of(row * pairs, pairs), pairs), :] = jnp.concatenate(
            [own[j * pairs : (j + 1) * pairs] for j in range(groups)], axis=1
        )

    def attend(at, extents):
        count = len(extents)
        ordered = [row_at(at + k) for k in range(count)]
        scores, weights = {}, {}
        for t in range(count + 2 * LAG):
            if t < count:
                scores[t] = scores_of(ordered[t], extents[t])
            if 0 <= t - LAG < count:
                weights[t - LAG] = softmax_of(scores.pop(t - LAG))
            if 0 <= t - 2 * LAG < count:
                done = t - 2 * LAG
                mix(ordered[done], extents[done], *weights.pop(done))

    by_shape(lambda place: span_of(row_at(place)), rows, k_ref.shape[1], attend)

    mixed = o_buf[...].astype(BF16)
    mixed_out[...] = mixed
    packed = exact(pack_ref[...], mixed)
    block = heads * CAP * STEPS
    for i in range(owners):
        outgoing[i] = packed[i * block : (i + 1) * block]


def write_out(matrix, values, heads, out_hbm, out_ref, sems):
    rows = out_ref.shape[1]
    wide = out_ref.shape[2] // heads
    span = STEPS * rows
    copies = []
    for c in range(heads):
        ordered = exact(matrix[c * span : (c + 1) * span], values)
        for s in range(STEPS):
            out_ref[s, :, c * wide : (c + 1) * wide] = ordered[s * rows : (s + 1) * rows]
        part = (slice(None), slice(None), pl.ds(c * wide, wide))
        copies.append(pltpu.make_async_copy(out_ref.at[part], out_hbm.at[part], sems.at[c]))
        copies[-1].start()
    for copy in copies:
        copy.wait()


def finish_kernel(heads, mixed, gather_ref, part, out_hbm, after, spread_out, out_ref, sems):
    after[...] = part[: after.shape[0], :]
    matrix = by_pair_matrix(heads, out_ref.shape[1])
    spread_out[...] = exact(matrix, gather_ref[...])
    write_out(matrix, mixed[...], heads, out_hbm, out_ref, sems)


def collect_kernel(owners, heads, spread, blocks, out_hbm, out_ref, sems):
    arrived = jnp.concatenate([blocks[i] for i in range(owners)], axis=0)
    write_out(spread, arrived, heads, out_hbm, out_ref, sems)


def exchange(blocks):
    owners = blocks.shape[0]
    cores = lax.axis_size("tensor")
    cycle = list(range(0, owners, 2)) + list(range(owners - 1, 0, -2))
    strided = [cycle[i * stride_of(owners) % owners] for i in range(owners)]
    groups = [
        [s * cores + core for s in (strided if core % 2 == 0 else cycle[::-1])]
        for core in range(cores)
    ]
    return lax.all_to_all(
        blocks,
        ("store", "tensor"),
        split_axis=0,
        concat_axis=0,
        axis_index_groups=groups,
        tiled=True,
    )


def in_hbm(array):
    return pltpu.with_memory_space_constraint(array, pltpu.HBM)


def swap_cores(part):
    return lax.ppermute(part, "tensor", [(0, 1), (1, 0)])


def shards(
    x_in,
    q_base,
    k_new,
    v_new,
    cache_k,
    cache_v,
    lengths,
    adapter_ids,
    slot_of,
    a_query,
    b_query,
    a_output,
    b_output,
):
    owners = lax.axis_size("store")
    rows = x_in.shape[1]
    width = x_in.shape[2]
    heads = cache_k.shape[2] // HD
    wide = width // heads
    adapt, rank = a_query.shape[1:]
    lanes = adapt * rank
    block = heads * CAP * STEPS
    items = owners * CAP * STEPS
    def flat(a_store):
        return jnp.transpose(a_store, (1, 2, 0)).reshape(lanes, a_store.shape[0])

    shape = jax.ShapeDtypeStruct
    small = pltpu.CompilerParams(vmem_limit_bytes=16 * 1024 * 1024)

    sent = shape((owners, block, wide), BF16)
    caches = (in_hbm(cache_k), in_hbm(cache_v))
    meta, blocks = pl.pallas_call(
        functools.partial(dispatch_kernel, owners, SPLIT, adapt, rank),
        out_shape=[
            shape((3 * rows + owners * CAP,), I32),
            shape((owners, SPLIT * CAP * STEPS, width // SPLIT + lanes), BF16),
        ],
        in_specs=[HBM] * 8,
        out_specs=[SMEM, VMEM],
        scratch_shapes=[
            pltpu.SMEM((owners * CAP,), I32),
            pltpu.SMEM(adapter_ids.shape, I32),
            pltpu.SMEM(slot_of.shape, I32),
            pltpu.SMEM(lengths.shape, I32),
            pltpu.VMEM(x_in.shape, BF16),
            pltpu.SemaphoreType.DMA((4,)),
        ],
        compiler_params=small,
        name="dispatch",
    )(
        *map(in_hbm, (adapter_ids, slot_of, lengths, x_in)), *caches, *caches
    )

    arrived = exchange(blocks)
    part, mask = pl.pallas_call(
        functools.partial(project_kernel, owners, SPLIT, width // SPLIT, True),
        out_shape=[shape((items, lanes), F32)] * 2,
        in_specs=[VMEM] * 2,
        out_specs=[VMEM] * 2,
        compiler_params=small,
        name="project_query",
    )(flat(a_query), arrived)

    def expand(part, other, b_store, name, caches, *after):
        return pl.pallas_call(
            functools.partial(expand_kernel, owners, heads, wide),
            out_shape=sent,
            in_specs=[VMEM] * (3 + len(after)) + [HBM] * len(caches),
            out_specs=VMEM,
            compiler_params=small,
            name=name,
        )(part, other, b_store, *after, *caches)

    other = swap_cores(part)
    *prepared, after = pl.pallas_call(
        functools.partial(prepare_kernel, owners, heads),
        out_shape=[
            shape((rows * STEPS * heads, wide), BF16),
            shape((STEPS * rows, heads * HD), BF16),
            shape((STEPS * rows, heads * HD), BF16),
            shape((STEPS * wide // HD * heads, heads * HD), BF16),
            shape((rows * STEPS * heads, owners * block), BF16),
            shape((owners * block, rows * STEPS * heads), BF16),
            shape((8, lanes), F32),
        ],
        in_specs=[SMEM] + [VMEM] * 4,
        out_specs=[VMEM] * 7,
        compiler_params=small,
        name="prepare",
    )(meta, q_base, k_new, v_new, part)
    returned = exchange(
        expand(part, other, b_query.reshape(lanes, width), "expand_query", (), after)
    )

    mixed, outgoing = pl.pallas_call(
        functools.partial(attend_kernel, owners, heads, rows),
        out_shape=[
            shape((rows * STEPS * heads, wide), BF16),
            sent,
        ],
        in_specs=[SMEM] + [VMEM] * 9,
        out_specs=[VMEM] * 2,
        scratch_shapes=[
            pltpu.VMEM((rows * STEPS * heads, wide), F32),
            pltpu.VMEM((rows * STEPS * heads, wide), F32),
        ],
        compiler_params=small,
        name="attend",
    )(meta, *prepared, cache_k, cache_v, returned)

    arrived = exchange(outgoing)
    part = pl.pallas_call(
        functools.partial(project_kernel, owners, heads, wide, False),
        out_shape=shape((items, lanes), F32),
        in_specs=[VMEM] * 3,
        out_specs=VMEM,
        compiler_params=small,
        name="project_output",
    )(flat(a_output), arrived, mask)
    ordered = dict(
        scratch_shapes=[
            pltpu.VMEM((STEPS, rows, width), BF16),
            pltpu.SemaphoreType.DMA((heads,)),
        ],
        compiler_params=small,
    )
    other = swap_cores(part)
    attn_out, after, spread = pl.pallas_call(
        functools.partial(finish_kernel, heads),
        out_shape=[
            shape((STEPS, rows, width), BF16),
            shape((8, lanes), F32),
            shape((rows * STEPS * heads, owners * block), BF16),
        ],
        in_specs=[VMEM] * 3,
        out_specs=[HBM, VMEM, VMEM],
        name="finish",
        **ordered,
    )(mixed, prepared[4], part)
    returned = exchange(
        expand(part, other, b_output.reshape(lanes, width), "expand_output", (), after)
    )
    adapter_out = pl.pallas_call(
        functools.partial(collect_kernel, owners, heads),
        out_shape=shape((STEPS, rows, width), BF16),
        in_specs=[VMEM] * 2,
        out_specs=HBM,
        name="collect",
        **ordered,
    )(spread, returned)
    return (attn_out, adapter_out)


def solution(mesh):
    in_specs = (
        P(None, ("parts", "store"), "tensor"),
        P(None, ("parts", "store"), "tensor"),
        P(None, ("parts", "store"), "tensor"),
        P(None, ("parts", "store"), "tensor"),
        P(("parts", "store"), None, "tensor"),
        P(("parts", "store"), None, "tensor"),
        P(("parts", "store")),
        P(("parts", "store")),
        P("parts"),
        P(None, "store", None),
        P("store", None, "tensor"),
        P(None, "store", None),
        P("store", None, "tensor"),
    )
    out_specs = (P(None, ("parts", "store"), "tensor"), P(None, ("parts", "store"), "tensor"))
    return jax.shard_map(shards, mesh=mesh, in_specs=in_specs, out_specs=out_specs, check_vma=False)
```

```python
import functools
import math

import jax
import jax.numpy as jnp
from jax import lax
from jax.experimental import pallas as pl
from jax.experimental.pallas import tpu as pltpu
from jax.sharding import PartitionSpec as P

HD = 128
CAP = 2
STEPS = 2
LAG = 2
SPLIT = 4
BF16 = jnp.bfloat16
F32 = jnp.float32
I32 = jnp.int32
VMEM = pl.BlockSpec(memory_space=pltpu.VMEM)
SMEM = pl.BlockSpec(memory_space=pltpu.SMEM)
HBM = pl.BlockSpec(memory_space=pltpu.HBM)


def iota(shape, dim):
    return lax.broadcasted_iota(I32, shape, dim)


def over(x, n):
    return lax.shift_right_logical(x, jnp.full_like(x, n.bit_length() - 1)) if n & (n - 1) == 0 else x // n


def rest(x, n):
    return x & (n - 1) if n & (n - 1) == 0 else x % n


def one_hot(hits):
    return jnp.where(hits, 1.0, 0.0).astype(BF16)


def stacked(ref, heads, wide):
    return jnp.concatenate(
        [ref[s, :, c * wide : (c + 1) * wide] for c in range(heads) for s in range(STEPS)], axis=0
    )


def pack_matrix(meta, owners, heads, rows, by_row):
    items = CAP * STEPS
    block = heads * items
    shape = (block, heads * STEPS * rows)
    at = iota(shape, 0)
    col = iota(shape, 1)
    head_step = over(at, items) * STEPS + rest(at, STEPS)
    offset = col - (head_step if by_row else head_step * rows)
    factor = heads * STEPS if by_row else 1
    first = rest(over(at, STEPS), CAP) == 0
    if not by_row:
        offset = jnp.where((offset >= 0) & (offset < rows), offset, -1)
    parts = []
    for i in range(owners):
        here = [meta[rows + i * CAP + k] for k in range(CAP)]
        spots = [jnp.where(h >= 0, h * factor, -rows * factor * heads * STEPS * 2) for h in here]
        parts.append(one_hot(offset == jnp.where(first, spots[0], spots[1])))
    return jnp.concatenate(parts, axis=0)


def unpack_matrix(meta, owners, heads, rows, by_row):
    items = CAP * STEPS
    block = heads * items
    pairs = heads * STEPS
    spots = [over(meta[r], CAP) * block + rest(meta[r], CAP) * STEPS for r in range(rows)]
    if by_row:
        shape = (pairs, owners * block)
        at = iota(shape, 0)
        col = iota(shape, 1) - (over(at, STEPS) * items + rest(at, STEPS))
        return jnp.concatenate([one_hot(col == spots[r]) for r in range(rows)], axis=0)
    shape = (rows, owners * block)
    at = iota(shape, 0)
    col = iota(shape, 1)
    spot = jnp.zeros(shape, I32)
    for r in range(rows):
        spot = jnp.where(at == r, spots[r], spot)
    offset = col - spot
    return jnp.concatenate(
        [one_hot(offset == c * items + s) for c in range(heads) for s in range(STEPS)], axis=0
    )


def by_row_matrix(heads, rows):
    pairs = heads * STEPS
    shape = (pairs * rows, pairs * rows)
    at = iota(shape, 0)
    return one_hot(iota(shape, 1) == rest(at, pairs) * rows + over(at, pairs))


def by_pair_matrix(heads, rows):
    pairs = heads * STEPS
    shape = (pairs * rows, pairs * rows)
    at = iota(shape, 0)
    return one_hot(iota(shape, 1) == rest(at, rows) * pairs + over(at, rows))


def stride_of(owners):
    return 3 if owners % 3 else 1


def turned(place, owners, core):
    return place + rest(core, 2) * (owners - 1 - 2 * place)


def regroup_matrix(owners, heads, core):
    items = CAP * STEPS
    total = owners * heads * items
    at = iota((total, total), 0)
    head = over(at, owners * items)
    owner = turned(rest(over(at, items), owners), owners, core)
    return one_hot(
        iota((total, total), 1) == owner * (heads * items) + head * items + rest(at, items)
    )


def ungroup_matrix(owners, heads, core):
    items = CAP * STEPS
    total = owners * heads * items
    at = iota((total, total), 0)
    owner = turned(over(at, heads * items), owners, core)
    head = rest(over(at, items), heads)
    return one_hot(
        iota((total, total), 1) == head * (owners * items) + owner * items + rest(at, items)
    )


def exact(matrix, values):
    return jnp.dot(matrix, values, preferred_element_type=F32).astype(BF16)


def dispatch_kernel(
    owners,
    heads,
    adapt,
    rank,
    ids_hbm,
    slot_of_hbm,
    lengths_hbm,
    x_hbm,
    k_hbm,
    v_hbm,
    k_again,
    v_again,
    meta,
    blocks,
    slot_at,
    ids,
    slot_of,
    lengths,
    x_ref,
    sems,
):
    pairs = (
        (ids_hbm, ids),
        (slot_of_hbm, slot_of),
        (lengths_hbm, lengths),
        (x_hbm, x_ref),
    )
    copies = [pltpu.make_async_copy(a, b, sems.at[k]) for k, (a, b) in enumerate(pairs)]
    for copy in copies:
        copy.start()
    rows = x_ref.shape[1]
    wide = x_ref.shape[2] // heads
    for copy in copies[:3]:
        copy.wait()
    core = lax.axis_index("tensor")
    row_at = rows
    order = rows + owners * CAP
    spans = order + rows
    for p in range(owners * CAP):
        meta[row_at + p] = -1
        slot_at[p] = -1
    for r in range(rows):
        slot = slot_of[ids[r]]
        owner = over(slot, adapt)
        half = over(owner, 2)
        along = jnp.where(rest(owner, 2) == 0, half, owners - 1 - half)
        along = rest(along * pow(stride_of(owners), -1, owners), owners)
        first = turned(along, owners, core) * CAP
        place = first + jnp.where(meta[row_at + first] >= 0, 1, 0)
        meta[row_at + place] = r
        slot_at[place] = rest(slot, adapt)
        meta[r] = place
    sizes = [lengths[r] for r in range(rows)]
    ahead = [jnp.int32(0)] * rows
    for r in range(rows):
        for q in range(r):
            shorter = jnp.where(sizes[q] <= sizes[r], 1, 0)
            ahead[r] = ahead[r] + shorter
            ahead[q] = ahead[q] + (1 - shorter)
    for r in range(rows):
        meta[order + ahead[r]] = r
        meta[spans + r] = sizes[r]
    items = CAP * STEPS
    block = heads * items
    copies[3].wait()
    packed = exact(pack_matrix(meta, owners, heads, rows, False), stacked(x_ref, heads, wide))
    at = iota((block, adapt * rank), 0)
    lane_slot = over(iota((block, adapt * rank), 1), rank)
    first = rest(over(at, STEPS), CAP) == 0
    for i in range(owners):
        blocks[i, :, :wide] = packed[i * block : (i + 1) * block]
        slot = jnp.where(first, slot_at[i * CAP], slot_at[i * CAP + 1])
        blocks[i, :, wide:] = one_hot(lane_slot == slot)


def project_kernel(owners, heads, wide, first, a_ref, blocks, *refs):
    core = lax.axis_index("tensor")
    if first:
        part_ref, mask_ref = refs
    else:
        mask_in, part_ref = refs
    grouped = regroup_matrix(owners, heads, core)
    items = owners * CAP * STEPS
    arrived = jnp.concatenate([blocks[i, :, :wide] for i in range(owners)], axis=0)
    arrived = exact(grouped, arrived)
    if first:
        masks = jnp.concatenate([blocks[i, :, wide:] for i in range(owners)], axis=0)
        mask = jnp.dot(grouped[:items], masks, preferred_element_type=F32)
        mask_ref[...] = mask
    else:
        mask = mask_in[...]
    total = jnp.zeros(mask.shape, F32)
    for c in range(heads):
        total = total + lax.dot_general(
            arrived[c * items : (c + 1) * items],
            a_ref[:, pl.ds(pl.multiple_of(core * (heads * wide) + c * wide, wide), wide)],
            (((1,), (1,)), ((), ())),
            preferred_element_type=F32,
        )
    part_ref[...] = total * mask


def expand_kernel(owners, heads, wide, mine, other, b_ref, *refs):
    blocks = refs[-1]
    low_rank = (mine[...] + other[...]).astype(BF16)
    pieces = []
    for c in range(heads):
        product = jnp.dot(
            low_rank, b_ref[:, c * wide : (c + 1) * wide], preferred_element_type=F32
        )
        pieces.append((2.0 * product).astype(BF16))
    back = exact(ungroup_matrix(owners, heads, lax.axis_index("tensor")), jnp.concatenate(pieces, axis=0))
    block = heads * CAP * STEPS
    for i in range(owners):
        blocks[i] = back[i * block : (i + 1) * block]


def by_shape(span_at, rows, most, action):
    half, quarter = rows // 2, rows // 4
    lower = ((most // 8, most // 4), (most // 4, most // 4), (most // 4, most // 2), (most, most))
    upper = ((most // 4, most), (most // 2, most), (most * 3 // 4, most), (most, most))
    for at, shapes in ((0, lower), (half, upper)):
        first, last = span_at(at + quarter - 1), span_at(at + half - 1)
        open_yet = True
        for a, b in shapes:
            fits = (first <= a) & (last <= b) & open_yet
            open_yet = open_yet & ~((first <= a) & (last <= b))

            @pl.when(fits)
            def _():
                action(at, [a] * quarter + [b] * quarter)


def prepare_kernel(
    owners,
    heads,
    meta,
    q_ref,
    kn_ref,
    vn_ref,
    part,
    base_out,
    kn_out,
    vn_out,
    mask_out,
    gather_out,
    pack_out,
    after,
):
    rows = q_ref.shape[1]
    wide = q_ref.shape[2] // heads
    base_out[...] = exact(by_row_matrix(heads, rows), stacked(q_ref, heads, wide))
    for source, target in ((kn_ref, kn_out), (vn_ref, vn_out)):
        target[...] = jnp.concatenate([source[t] for t in range(STEPS)], axis=0)
    head_at = rest(over(iota(mask_out.shape, 0), STEPS), heads)
    mask_out[...] = one_hot(head_at == over(iota(mask_out.shape, 1), HD))
    gather_out[...] = unpack_matrix(meta, owners, heads, rows, True)
    pack_out[...] = pack_matrix(meta, owners, heads, rows, True)
    after[...] = part[: after.shape[0], :]


def attend_kernel(
    owners,
    heads,
    rows,
    meta,
    base_ref,
    kn_ref,
    vn_ref,
    mask_ref,
    gather_ref,
    pack_ref,
    k_ref,
    v_ref,
    blocks,
    mixed_out,
    outgoing,
    q_buf,
    o_buf,
):
    wide = base_ref.shape[1]
    groups = wide // HD
    pairs = heads * STEPS
    total = groups * pairs

    def span_of(row):
        return meta[2 * rows + owners * CAP + row]

    def row_at(place):
        return meta[rows + owners * CAP + place]

    delta = jnp.dot(
        gather_ref[...],
        jnp.concatenate([blocks[i] for i in range(owners)], axis=0),
        preferred_element_type=F32,
    )
    q_buf[...] = base_ref[...].astype(F32) + delta

    head_own = rest(over(iota((total, HD), 0), STEPS), heads)
    factor = math.log2(math.e) / math.sqrt(HD)
    fresh_shape = (total, STEPS * rows)
    fresh_at = iota(fresh_shape, 1)
    fresh_step = over(fresh_at, rows)
    fresh_row = jnp.where(fresh_step <= rest(iota(fresh_shape, 0), STEPS), rest(fresh_at, rows), rows)
    contract = (((1,), (1,)), ((), ()))

    def scores_of(row, extent):
        flat = q_buf[pl.ds(pl.multiple_of(row * pairs, pairs), pairs), :]
        one = jnp.concatenate([flat[:, j * HD : (j + 1) * HD] for j in range(groups)], axis=0)
        spread = jnp.concatenate([one.astype(BF16)] * heads, axis=1) * mask_ref[...]
        keys = jnp.concatenate([k_ref[row, :extent, :], kn_ref[...]], axis=0)
        score = lax.dot_general(spread, keys, contract, preferred_element_type=F32)
        cached = jnp.where(iota((total, extent), 1) < span_of(row), score[:, :extent], -jnp.inf)
        fresh = jnp.where(fresh_row == row, score[:, extent:], -jnp.inf)
        return jnp.concatenate([cached, fresh], axis=1)

    def softmax_of(score):
        top = jnp.max(score, axis=1, keepdims=True)
        weight = jnp.exp2((score - top) * factor)
        return weight.astype(BF16), 1.0 / jnp.sum(weight, axis=1, keepdims=True)

    def mix(row, extent, weight, share):
        values = jnp.concatenate([v_ref[row, :extent, :], vn_ref[...]], axis=0)
        mixed = jnp.dot(weight, values, preferred_element_type=F32)
        own = mixed[:, :HD]
        for c in range(1, heads):
            own = jnp.where(head_own == c, mixed[:, c * HD : (c + 1) * HD], own)
        own = own * share
        o_buf[pl.ds(pl.multiple_of(row * pairs, pairs), pairs), :] = jnp.concatenate(
            [own[j * pairs : (j + 1) * pairs] for j in range(groups)], axis=1
        )

    def attend(at, extents):
        count = len(extents)
        ordered = [row_at(at + k) for k in range(count)]
        scores, weights = {}, {}
        for t in range(count + 2 * LAG):
            if t < count:
                scores[t] = scores_of(ordered[t], extents[t])
            if 0 <= t - LAG < count:
                weights[t - LAG] = softmax_of(scores.pop(t - LAG))
            if 0 <= t - 2 * LAG < count:
                done = t - 2 * LAG
                mix(ordered[done], extents[done], *weights.pop(done))

    by_shape(lambda place: span_of(row_at(place)), rows, k_ref.shape[1], attend)

    mixed = o_buf[...].astype(BF16)
    mixed_out[...] = mixed
    packed = exact(pack_ref[...], mixed)
    block = heads * CAP * STEPS
    for i in range(owners):
        outgoing[i] = packed[i * block : (i + 1) * block]


def write_out(matrix, values, heads, out_hbm, out_ref, sems):
    rows = out_ref.shape[1]
    wide = out_ref.shape[2] // heads
    span = STEPS * rows
    copies = []
    for c in range(heads):
        ordered = exact(matrix[c * span : (c + 1) * span], values)
        for s in range(STEPS):
            out_ref[s, :, c * wide : (c + 1) * wide] = ordered[s * rows : (s + 1) * rows]
        part = (slice(None), slice(None), pl.ds(c * wide, wide))
        copies.append(pltpu.make_async_copy(out_ref.at[part], out_hbm.at[part], sems.at[c]))
        copies[-1].start()
    for copy in copies:
        copy.wait()


def finish_kernel(heads, mixed, gather_ref, part, out_hbm, after, spread_out, out_ref, sems):
    after[...] = part[: after.shape[0], :]
    matrix = by_pair_matrix(heads, out_ref.shape[1])
    spread_out[...] = exact(matrix, gather_ref[...])
    write_out(matrix, mixed[...], heads, out_hbm, out_ref, sems)


def collect_kernel(owners, heads, spread, blocks, out_hbm, out_ref, sems):
    arrived = jnp.concatenate([blocks[i] for i in range(owners)], axis=0)
    write_out(spread, arrived, heads, out_hbm, out_ref, sems)


def exchange(blocks):
    owners = blocks.shape[0]
    cores = lax.axis_size("tensor")
    cycle = list(range(0, owners, 2)) + list(range(owners - 1, 0, -2))
    cycle = [cycle[i * stride_of(owners) % owners] for i in range(owners)]
    groups = [
        [s * cores + core for s in (cycle if core % 2 == 0 else cycle[::-1])]
        for core in range(cores)
    ]
    return lax.all_to_all(
        blocks,
        ("store", "tensor"),
        split_axis=0,
        concat_axis=0,
        axis_index_groups=groups,
        tiled=True,
    )


def in_hbm(array):
    return pltpu.with_memory_space_constraint(array, pltpu.HBM)


def swap_cores(part):
    return lax.ppermute(part, "tensor", [(0, 1), (1, 0)])


def shards(
    x_in,
    q_base,
    k_new,
    v_new,
    cache_k,
    cache_v,
    lengths,
    adapter_ids,
    slot_of,
    a_query,
    b_query,
    a_output,
    b_output,
):
    owners = lax.axis_size("store")
    rows = x_in.shape[1]
    width = x_in.shape[2]
    heads = cache_k.shape[2] // HD
    wide = width // heads
    adapt, rank = a_query.shape[1:]
    lanes = adapt * rank
    block = heads * CAP * STEPS
    items = owners * CAP * STEPS
    def flat(a_store):
        return jnp.transpose(a_store, (1, 2, 0)).reshape(lanes, a_store.shape[0])

    shape = jax.ShapeDtypeStruct
    small = pltpu.CompilerParams(vmem_limit_bytes=16 * 1024 * 1024)

    sent = shape((owners, block, wide), BF16)
    caches = (in_hbm(cache_k), in_hbm(cache_v))
    meta, blocks = pl.pallas_call(
        functools.partial(dispatch_kernel, owners, SPLIT, adapt, rank),
        out_shape=[
            shape((3 * rows + owners * CAP,), I32),
            shape((owners, SPLIT * CAP * STEPS, width // SPLIT + lanes), BF16),
        ],
        in_specs=[HBM] * 8,
        out_specs=[SMEM, VMEM],
        scratch_shapes=[
            pltpu.SMEM((owners * CAP,), I32),
            pltpu.SMEM(adapter_ids.shape, I32),
            pltpu.SMEM(slot_of.shape, I32),
            pltpu.SMEM(lengths.shape, I32),
            pltpu.VMEM(x_in.shape, BF16),
            pltpu.SemaphoreType.DMA((4,)),
        ],
        compiler_params=small,
        name="dispatch",
    )(
        *map(in_hbm, (adapter_ids, slot_of, lengths, x_in)), *caches, *caches
    )

    arrived = exchange(blocks)
    part, mask = pl.pallas_call(
        functools.partial(project_kernel, owners, SPLIT, width // SPLIT, True),
        out_shape=[shape((items, lanes), F32)] * 2,
        in_specs=[VMEM] * 2,
        out_specs=[VMEM] * 2,
        compiler_params=small,
        name="project_query",
    )(flat(a_query), arrived)

    def expand(part, other, b_store, name, caches, *after):
        return pl.pallas_call(
            functools.partial(expand_kernel, owners, heads, wide),
            out_shape=sent,
            in_specs=[VMEM] * (3 + len(after)) + [HBM] * len(caches),
            out_specs=VMEM,
            compiler_params=small,
            name=name,
        )(part, other, b_store, *after, *caches)

    other = swap_cores(part)
    *prepared, after = pl.pallas_call(
        functools.partial(prepare_kernel, owners, heads),
        out_shape=[
            shape((rows * STEPS * heads, wide), BF16),
            shape((STEPS * rows, heads * HD), BF16),
            shape((STEPS * rows, heads * HD), BF16),
            shape((STEPS * wide // HD * heads, heads * HD), BF16),
            shape((rows * STEPS * heads, owners * block), BF16),
            shape((owners * block, rows * STEPS * heads), BF16),
            shape((8, lanes), F32),
        ],
        in_specs=[SMEM] + [VMEM] * 4,
        out_specs=[VMEM] * 7,
        compiler_params=small,
        name="prepare",
    )(meta, q_base, k_new, v_new, part)
    returned = exchange(
        expand(part, other, b_query.reshape(lanes, width), "expand_query", (), after)
    )

    mixed, outgoing = pl.pallas_call(
        functools.partial(attend_kernel, owners, heads, rows),
        out_shape=[
            shape((rows * STEPS * heads, wide), BF16),
            sent,
        ],
        in_specs=[SMEM] + [VMEM] * 9,
        out_specs=[VMEM] * 2,
        scratch_shapes=[
            pltpu.VMEM((rows * STEPS * heads, wide), F32),
            pltpu.VMEM((rows * STEPS * heads, wide), F32),
        ],
        compiler_params=small,
        name="attend",
    )(meta, *prepared, cache_k, cache_v, returned)

    arrived = exchange(outgoing)
    part = pl.pallas_call(
        functools.partial(project_kernel, owners, heads, wide, False),
        out_shape=shape((items, lanes), F32),
        in_specs=[VMEM] * 3,
        out_specs=VMEM,
        compiler_params=small,
        name="project_output",
    )(flat(a_output), arrived, mask)
    ordered = dict(
        scratch_shapes=[
            pltpu.VMEM((STEPS, rows, width), BF16),
            pltpu.SemaphoreType.DMA((heads,)),
        ],
        compiler_params=small,
    )
    other = swap_cores(part)
    attn_out, after, spread = pl.pallas_call(
        functools.partial(finish_kernel, heads),
        out_shape=[
            shape((STEPS, rows, width), BF16),
            shape((8, lanes), F32),
            shape((rows * STEPS * heads, owners * block), BF16),
        ],
        in_specs=[VMEM] * 3,
        out_specs=[HBM, VMEM, VMEM],
        name="finish",
        **ordered,
    )(mixed, prepared[4], part)
    returned = exchange(
        expand(part, other, b_output.reshape(lanes, width), "expand_output", (), after)
    )
    adapter_out = pl.pallas_call(
        functools.partial(collect_kernel, owners, heads),
        out_shape=shape((STEPS, rows, width), BF16),
        in_specs=[VMEM] * 2,
        out_specs=HBM,
        name="collect",
        **ordered,
    )(spread, returned)
    return (attn_out, adapter_out)


def solution(mesh):
    in_specs = (
        P(None, ("parts", "store"), "tensor"),
        P(None, ("parts", "store"), "tensor"),
        P(None, ("parts", "store"), "tensor"),
        P(None, ("parts", "store"), "tensor"),
        P(("parts", "store"), None, "tensor"),
        P(("parts", "store"), None, "tensor"),
        P(("parts", "store")),
        P(("parts", "store")),
        P("parts"),
        P(None, "store", None),
        P("store", None, "tensor"),
        P(None, "store", None),
        P("store", None, "tensor"),
    )
    out_specs = (P(None, ("parts", "store"), "tensor"), P(None, ("parts", "store"), "tensor"))
    return jax.shard_map(shards, mesh=mesh, in_specs=in_specs, out_specs=out_specs, check_vma=False)
```
